32 devices in a mesh: seq: 8 (over z, y), tp: 4 (over x, core).
Axes of the slice: x: 2, y: 2, z: 4, core: 2. Of those that a mesh axis runs over, the one named last changes fastest.
Arguments:
- tokens: bfloat16 [8192, 2048], P('seq', 'tp')
- bounds: int32 [8], P('seq'), may hold values from 0 to 1024, as said below
- cotangent: bfloat16 [8192, 2048], P('seq', 'tp'), may hold values from -6 to 6
- entry_weight: float32 [2048, 3, 2048], P('seq', None, 'tp'), may hold values from -0.125 to 0.125
- entry_first: float32 [2048, 3, 2048], P('seq', None, 'tp'), may hold values from -96 to 96
- entry_second: float32 [2048, 3, 2048], P('seq', None, 'tp'), may hold values from 983.04 to 3932.16
- exit_weight: float32 [2048, 2048], P('seq', 'tp'), may hold values from -0.125 to 0.125
- exit_first: float32 [2048, 2048], P('seq', 'tp'), may hold values from -96 to 96
- exit_second: float32 [2048, 2048], P('seq', 'tp'), may hold values from 983.04 to 3932.16
- expand_weight: float32 [2048, 2, 8192], P('seq', None, 'tp'), may hold values from -0.125 to 0.125
- expand_first: float32 [2048, 2, 8192], P('seq', None, 'tp'), may hold values from -32 to 32
- expand_second: float32 [2048, 2, 8192], P('seq', None, 'tp'), may hold values from 155.648 to 622.592
- shrink_weight: float32 [2048, 8192], P('seq', 'tp'), may hold values from -0.125 to 0.125
- shrink_first: float32 [2048, 8192], P('seq', 'tp'), may hold values from -32 to 32
- shrink_second: float32 [2048, 8192], P('seq', 'tp'), may hold values from 155.648 to 622.592
- conv_kernel: float32 [3, 2048], P(None, ('tp', 'seq')), may hold values from -3 to 3
- conv_first: float32 [3, 2048], P(None, ('tp', 'seq')), may hold values from -128 to 128
- conv_second: float32 [3, 2048], P(None, ('tp', 'seq')), may hold values from 1720.32 to 6881.28
- norm_gains: float32 [2, 2048], P(None, ('tp', 'seq')), may hold values from 0.5 to 1.5
- gain_first: float32 [2, 2048], P(None, ('tp', 'seq')), may hold values from -96 to 96
- gain_second: float32 [2, 2048], P(None, ('tp', 'seq')), may hold values from 983.04 to 3932.16
Outputs:
- mixed: bfloat16 [8192, 2048], P('seq', 'tp')
- tokens_grad: float32 [8192, 2048], P('seq', 'tp')
- entry_next: float32 [2048, 3, 2048], P('seq', None, 'tp')
- entry_first_next: float32 [2048, 3, 2048], P('seq', None, 'tp')
- entry_second_next: float32 [2048, 3, 2048], P('seq', None, 'tp')
- exit_next: float32 [2048, 2048], P('seq', 'tp')
- exit_first_next: float32 [2048, 2048], P('seq', 'tp')
- exit_second_next: float32 [2048, 2048], P('seq', 'tp')
- expand_next: float32 [2048, 2, 8192], P('seq', None, 'tp')
- expand_first_next: float32 [2048, 2, 8192], P('seq', None, 'tp')
- expand_second_next: float32 [2048, 2, 8192], P('seq', None, 'tp')
- shrink_next: float32 [2048, 8192], P('seq', 'tp')
- shrink_first_next: float32 [2048, 8192], P('seq', 'tp')
- shrink_second_next: float32 [2048, 8192], P('seq', 'tp')
- conv_next: float32 [3, 2048], P(None, ('tp', 'seq'))
- conv_first_next: float32 [3, 2048], P(None, ('tp', 'seq'))
- conv_second_next: float32 [3, 2048], P(None, ('tp', 'seq'))
- gains_next: float32 [2, 2048], P(None, ('tp', 'seq'))
- gains_first_next: float32 [2, 2048], P(None, ('tp', 'seq'))
- gains_second_next: float32 [2, 2048], P(None, ('tp', 'seq'))
The draws below stay inside these ranges and needn't reach their ends.
Inputs may be any that keep to these rules, and one draw needn't show every extreme that they name: bounds[i] is the offset within group i at which a new sequence begins, 1024 where none does; group 0 begins one at offset 0, every other group at an offset of 2 to 1022 or not at all, and some group other than the first holds none.
All inputs are finite; a program needn't handle non-finite values.
Results may differ from the reference program's by a relative error of at most 0.012.
The reference program's roundings to bfloat16 on the way count: a program that leaves them out, or rounds other values in their place, can miss the bound.
Values may be sent and summed in bfloat16 or wider, within the bound.
A program may use at most 256 MiB of HBM per device.

```python
import math
import jax
import jax.numpy as jnp
from jax import lax

D = 2048
FF = 8192
TOK_DEV = 1024
STEP = 10
TOKENS = 8192
N_SEQ = 8


def draw_tokens(key, part):
    key = jax.random.fold_in(key, 11)
    column = jnp.arange(D, dtype=jnp.float32) / (D - 1)
    base = jnp.clip(jax.random.normal(key, (TOKENS, D), jnp.float32), -6.0, 6.0)
    rising = 0.6 * 3.0 ** column
    return (base * rising).astype(jnp.bfloat16)


def draw_bounds(key, part):
    key = jax.random.fold_in(key, 23)
    key_place, key_pick, key_keep = jax.random.split(key, 3)
    placed = jax.random.randint(key_place, (N_SEQ,), 2, TOK_DEV - 1)
    picked = jax.random.randint(key_pick, (N_SEQ,), 0, 4)
    keeper = jax.random.randint(key_keep, (), 1, N_SEQ)
    group_index = jnp.arange(N_SEQ, dtype=jnp.int32)
    result = jnp.where(picked == 0, placed, TOK_DEV)
    result = jnp.where(group_index == keeper, TOK_DEV, result)
    result = jnp.where(group_index == 0, 0, result)
    return result.astype(jnp.int32)


def levels(stream_key, extent, cuts, smallest, largest):
    level = 1.0
    for dim, blocks in cuts:
        draws = jax.random.uniform(jax.random.fold_in(jax.random.fold_in(stream_key, 6), dim), (blocks,), jnp.float32, smallest / len(cuts), largest / len(cuts))
        level = level * jnp.repeat(jnp.exp(draws), extent[dim] // blocks).reshape((-1,) + (1,) * (len(extent) - 1 - dim))
    return level


def scatter_about(stream_key, shape, width, most, shards=(), kind=jnp.bfloat16):
    array = width * jax.random.normal(stream_key, shape, jnp.float32)
    if shards:
        array = array * levels(stream_key, shape, shards, -0.22, 0.18)
    return jnp.clip(array, -most, most).astype(kind)


def setup_inputs(seed: int = 0) -> dict:
    keys = jax.random.split(jax.random.key(seed), 22)
    tokens = draw_tokens(jax.random.fold_in(keys[21], 71), 0)
    bounds = draw_bounds(jax.random.fold_in(keys[21], 71), 0)
    cotangent = scatter_about(keys[2], (TOKENS, D), 1.0, 6.0, ((0, 8), (1, 4)))
    entry_weight = scatter_about(keys[3], (D, 3, D), D ** -0.5, 0.125, ((0, 8), (2, 4)), jnp.float32)
    entry_first = scatter_about(keys[4], (D, 3, D), (0.17 * TOKENS ** 0.5), 96.0, ((0, 8), (2, 4)), jnp.float32)
    entry_second = jnp.clip(jnp.exp(math.log(3932.16) - 1.3862944 * jax.random.uniform(keys[5], (D, 3, D), jnp.float32) ** levels(keys[5], (D, 3, D), ((0, 8), (2, 4)), -0.2, 0.2)), 983.04, 3932.16)
    exit_weight = scatter_about(keys[6], (D, D), D ** -0.5, 0.125, ((0, 8), (1, 4)), jnp.float32)
    exit_first = scatter_about(keys[7], (D, D), (0.17 * TOKENS ** 0.5), 96.0, ((0, 8), (1, 4)), jnp.float32)
    exit_second = jnp.clip(jnp.exp(math.log(3932.16) - 1.3862944 * jax.random.uniform(keys[8], (D, D), jnp.float32) ** levels(keys[8], (D, D), ((0, 8), (1, 4)), -0.2, 0.2)), 983.04, 3932.16)
    expand_weight = scatter_about(keys[9], (D, 2, FF), D ** -0.5, 0.125, ((0, 8), (2, 4)), jnp.float32)
    expand_first = scatter_about(keys[10], (D, 2, FF), (0.067 * TOKENS ** 0.5), 32.0, ((0, 8), (2, 4)), jnp.float32)
    expand_second = jnp.clip(jnp.exp(math.log(622.592) - 1.3862944 * jax.random.uniform(keys[11], (D, 2, FF), jnp.float32) ** levels(keys[11], (D, 2, FF), ((0, 8), (2, 4)), -0.2, 0.2)), 155.648, 622.592)
    shrink_weight = scatter_about(keys[12], (D, FF), (FF // 4) ** -0.5, 0.125, ((0, 8), (1, 4)), jnp.float32)
    shrink_first = scatter_about(keys[13], (D, FF), (0.067 * TOKENS ** 0.5), 32.0, ((0, 8), (1, 4)), jnp.float32)
    shrink_second = jnp.clip(jnp.exp(math.log(622.592) - 1.3862944 * jax.random.uniform(keys[14], (D, FF), jnp.float32) ** levels(keys[14], (D, FF), ((0, 8), (1, 4)), -0.2, 0.2)), 155.648, 622.592)
    conv_kernel = scatter_about(keys[15], (3, D), 0.5, 3.0, ((1, 32),), jnp.float32)
    conv_first = scatter_about(keys[16], (3, D), (0.22 * TOKENS ** 0.5), 128.0, ((1, 32),), jnp.float32)
    conv_second = jnp.clip(jnp.exp(math.log(6881.28) - 1.3862944 * jax.random.uniform(keys[17], (3, D), jnp.float32) ** levels(keys[17], (3, D), ((1, 32),), -0.2, 0.2)), 1720.32, 6881.28)
    norm_gains = jnp.clip(1.0 + 0.1 * jax.random.normal(keys[18], (2, D), jnp.float32), 0.5, 1.5)
    gain_first = scatter_about(keys[19], (2, D), (0.17 * TOKENS ** 0.5), 96.0, ((1, 32),), jnp.float32)
    gain_second = jnp.clip(jnp.exp(math.log(3932.16) - 1.3862944 * jax.random.uniform(keys[20], (2, D), jnp.float32) ** levels(keys[20], (2, D), ((1, 32),), -0.2, 0.2)), 983.04, 3932.16)
    return dict(tokens=tokens, bounds=bounds, cotangent=cotangent, entry_weight=entry_weight, entry_first=entry_first, entry_second=entry_second, exit_weight=exit_weight, exit_first=exit_first, exit_second=exit_second, expand_weight=expand_weight, expand_first=expand_first, expand_second=expand_second, shrink_weight=shrink_weight, shrink_first=shrink_first, shrink_second=shrink_second, conv_kernel=conv_kernel, conv_first=conv_first, conv_second=conv_second, norm_gains=norm_gains, gain_first=gain_first, gain_second=gain_second)


EPSILON = 1e-05
BETA_ONE = 0.9
BETA_TWO = 0.95
ADAM_EPSILON = 1e-08
WEIGHT_DECAY = 0.1
RATE_WIDE = 0.04
RATE_CONV = 0.5
RATE_GAIN = 0.4
HIGHEST_PRECISION = lax.Precision.HIGHEST

@jax.custom_vjp
def low(v):
    return lax.optimization_barrier(v.astype(jnp.bfloat16)).astype(jnp.float32)

@jax.custom_vjp
def low_back(v):
    return v

def low_keep(v):
    return (low(v), None)

def low_pass(kept, grad):
    return (grad,)

def back_keep(v):
    return (v, None)

def back_low(kept, grad):
    return (low(grad),)
low.defvjp(low_keep, low_pass)
low_back.defvjp(back_keep, back_low)

def rms_scale(values):
    return lax.rsqrt(lax.optimization_barrier(jnp.mean(values * values, axis=-1, keepdims=True)) + EPSILON)

def layer(tokens_f, entry_weight, exit_weight, expand_weight, shrink_weight, conv_kernel, norm_gains, see_one, see_two):
    entry_low = low(entry_weight)
    exit_low = low(exit_weight)
    expand_low = low(expand_weight)
    shrink_low = low(shrink_weight)
    kernel = low(conv_kernel)
    gains = low(norm_gains)
    block_rows = 4096 if TOKENS % 4096 == 0 else TOKENS
    count = TOKENS // block_rows

    def block_step(carry, inputs):
        rows_in, mask_one, mask_two = inputs
        normed_one = low(rows_in * rms_scale(rows_in) * gains[0])
        projected = jnp.einsum('td,dkc->tkc', normed_one, entry_low, precision=HIGHEST_PRECISION)
        input_gate = low_back(projected[:, 0])
        output_gate = low_back(projected[:, 1])
        values_rows = low_back(projected[:, 2])
        gated_rows = low(input_gate * values_rows)
        extended = jnp.concatenate([carry, gated_rows], axis=0)
        conv_out = kernel[2] * extended[2:] + kernel[1] * extended[1:-1] * mask_one[:, None] + kernel[0] * extended[:-2] * mask_two[:, None]
        mixer_rows = low(output_gate * conv_out)
        branch = low_back(jnp.dot(mixer_rows, exit_low.T, precision=HIGHEST_PRECISION))
        residual = rows_in + branch
        normed_two = low(residual * rms_scale(residual) * gains[1])
        expanded = jnp.einsum('td,dkf->tkf', normed_two, expand_low, precision=HIGHEST_PRECISION)
        gate_rows = low_back(expanded[:, 0])
        up_rows = low_back(expanded[:, 1])
        activation = low(jax.nn.silu(gate_rows) * up_rows)
        output = residual + jnp.dot(activation, shrink_low.T, precision=HIGHEST_PRECISION)
        return (extended[-2:], output)
    start_carry = jnp.zeros((2, D), jnp.float32)
    pieces = (tokens_f.reshape(count, block_rows, D), see_one.reshape(count, block_rows), see_two.reshape(count, block_rows))
    carry_out, outputs = lax.scan(jax.checkpoint(block_step), start_carry, pieces)
    return outputs.reshape(TOKENS, D)

def adam_update(weight, first, second, grad, rate, decay):
    first_next = BETA_ONE * first + (1.0 - BETA_ONE) * grad
    second_next = BETA_TWO * second + (1.0 - BETA_TWO) * grad * grad
    corrected = first_next / (1.0 - BETA_ONE ** STEP)
    spread = jnp.sqrt(second_next / (1.0 - BETA_TWO ** STEP)) + ADAM_EPSILON
    return (weight - rate * (corrected / spread + decay * weight), first_next, second_next)

def reference(tokens, bounds, cotangent, entry_weight, entry_first, entry_second, exit_weight, exit_first, exit_second, expand_weight, expand_first, expand_second, shrink_weight, shrink_first, shrink_second, conv_kernel, conv_first, conv_second, norm_gains, gain_first, gain_second):
    positions = jnp.arange(TOKENS, dtype=jnp.int32)
    group_index = positions // TOK_DEV
    offsets = positions % TOK_DEV
    starts = (offsets == bounds[group_index]).astype(jnp.float32)
    before = jnp.concatenate([jnp.zeros((1,), jnp.float32), starts[:-1]])
    see_one = 1.0 - starts
    see_two = (1.0 - starts) * (1.0 - before)
    tokens_f = tokens.astype(jnp.float32)

    def forward(rows_in, entry_w, exit_w, expand_w, shrink_w, kernel_w, gains_w):
        return layer(rows_in, entry_w, exit_w, expand_w, shrink_w, kernel_w, gains_w, see_one, see_two)
    output, pull = jax.vjp(forward, tokens_f, entry_weight, exit_weight, expand_weight, shrink_weight, conv_kernel, norm_gains)
    tokens_grad, entry_grad, exit_grad, expand_grad, shrink_grad, kernel_grad, gains_grad = pull(cotangent.astype(jnp.float32))
    entry_next, entry_first_next, entry_second_next = adam_update(entry_weight, entry_first, entry_second, entry_grad, RATE_WIDE, WEIGHT_DECAY)
    exit_next, exit_first_next, exit_second_next = adam_update(exit_weight, exit_first, exit_second, exit_grad, RATE_WIDE, WEIGHT_DECAY)
    expand_next, expand_first_next, expand_second_next = adam_update(expand_weight, expand_first, expand_second, expand_grad, RATE_WIDE, WEIGHT_DECAY)
    shrink_next, shrink_first_next, shrink_second_next = adam_update(shrink_weight, shrink_first, shrink_second, shrink_grad, RATE_WIDE, WEIGHT_DECAY)
    conv_next, conv_first_next, conv_second_next = adam_update(conv_kernel, conv_first, conv_second, kernel_grad, RATE_CONV, 0.0)
    gains_next, gains_first_next, gains_second_next = adam_update(norm_gains, gain_first, gain_second, gains_grad, RATE_GAIN, 0.0)
    return (output.astype(jnp.bfloat16), tokens_grad, entry_next, entry_first_next, entry_second_next, exit_next, exit_first_next, exit_second_next, expand_next, expand_first_next, expand_second_next, shrink_next, shrink_first_next, shrink_second_next, conv_next, conv_first_next, conv_second_next, gains_next, gains_first_next, gains_second_next)
```

```python
import functools

import jax
import jax.numpy as jnp
from jax import lax
from jax.experimental import pallas as pl
from jax.experimental.pallas import tpu as pltpu
from jax.sharding import PartitionSpec as P

D = 2048
STEP = 10


EPSILON = 1e-05
BETA_ONE = 0.9
BETA_TWO = 0.95
ADAM_EPSILON = 1e-08
WEIGHT_DECAY = 0.1
RATE_WIDE = 0.04
RATE_CONV = 0.5
RATE_GAIN = 0.4

MESH = pl.DeviceIdType.MESH
LOW = jnp.bfloat16
VMEM_BYTES = 60 * 1024 * 1024


def ring_place(index, count):
    side = index % 2
    level = index // 2
    return level * (1 - side) + (count - 1 - level) * side


def ring_index(place, count):
    back = place // (count // 2)
    return (1 - back) * (2 * place) + back * (2 * (count - 1 - place) + 1)


def ring_ends(count):
    place = ring_place(lax.axis_index("seq"), count)
    ahead = ring_index((place + 1) % count, count)
    behind = ring_index((place + count - 1) % count, count)
    return place, ahead, behind


def greet(ahead, behind, column):
    barrier = pltpu.get_barrier_semaphore()
    for other in (ahead, behind):
        pl.semaphore_signal(barrier, inc=1, device_id=(other, column), device_id_type=MESH)
    pl.semaphore_wait(barrier, 2)


def gather_kernel(count, arrays, *refs):
    shard_refs = refs[:arrays]
    full_refs = refs[arrays : 2 * arrays]
    send_sem, recv_sem, own_sem = refs[2 * arrays :]
    column = lax.axis_index("tp")
    place, ahead, behind = ring_ends(count)
    greet(ahead, behind, column)

    def copy(array, step, way):
        owner = ring_index((place + count - step) % count if way == 0 else (place + step) % count, count)
        half = shard_refs[array].shape[0] // 2
        part = pl.ds(way * half, half)
        return pltpu.make_async_remote_copy(
            src_ref=full_refs[array].at[owner, part],
            dst_ref=full_refs[array].at[owner, part],
            send_sem=send_sem.at[array, way, step],
            recv_sem=recv_sem.at[array, way, step],
            device_id=(ahead if way == 0 else behind, column),
            device_id_type=MESH,
        )

    def first(array, way):
        half = shard_refs[array].shape[0] // 2
        part = pl.ds(way * half, half)
        return pltpu.make_async_remote_copy(
            src_ref=shard_refs[array].at[part],
            dst_ref=full_refs[array].at[lax.axis_index("seq"), part],
            send_sem=send_sem.at[array, way, 0],
            recv_sem=recv_sem.at[array, way, 0],
            device_id=(ahead if way == 0 else behind, column),
            device_id_type=MESH,
        )

    def own(array):
        return pltpu.make_async_copy(
            shard_refs[array], full_refs[array].at[lax.axis_index("seq")], own_sem.at[array]
        )

    for array in range(arrays):
        for way in range(2):
            first(array, way).start()
    for array in range(arrays):
        own(array).start()

    def hop(step, carry):
        for array in range(arrays):
            for way in range(2):
                copy(array, step - 1, way).wait_recv()
                copy(array, step, way).start()
        return carry

    lax.fori_loop(1, count - 1, hop, 0)
    for array in range(arrays):
        for way in range(2):
            copy(array, count - 2, way).wait_recv()

    def sent(step, carry):
        for array in range(arrays):
            for way in range(2):
                copy(array, step, way).wait_send()
        return carry

    lax.fori_loop(0, count - 1, sent, 0)
    for array in range(arrays):
        own(array).wait()


def ring_gather(shards, collective):
    count = lax.axis_size("seq")
    arrays = len(shards)
    moved = sum(shard.size for shard in shards) * 2 * count
    fulls = pl.pallas_call(
        functools.partial(gather_kernel, count, arrays),
        out_shape=[jax.ShapeDtypeStruct((count,) + shard.shape, shard.dtype) for shard in shards],
        in_specs=[pl.BlockSpec(memory_space=pl.ANY)] * arrays,
        out_specs=[pl.BlockSpec(memory_space=pl.ANY)] * arrays,
        scratch_shapes=[
            pltpu.SemaphoreType.DMA((arrays, 2, count - 1)),
            pltpu.SemaphoreType.DMA((arrays, 2, count - 1)),
            pltpu.SemaphoreType.DMA((arrays,)),
        ],
        compiler_params=pltpu.CompilerParams(
            collective_id=collective, has_side_effects=True, vmem_limit_bytes=VMEM_BYTES
        ),
        cost_estimate=pl.CostEstimate(flops=0, bytes_accessed=30 * moved, transcendentals=0),
        name="ring_gather",
    )(*shards)
    return [full.reshape(count * full.shape[1], full.shape[2]) for full in fulls]


def chunks_of(width):
    return 2 if width % 256 == 0 and width > 256 else 1


def scatter_kernel(count, arrays, *refs):
    left_refs = refs[:arrays]
    right_refs = refs[arrays : 2 * arrays]
    out_refs = refs[2 * arrays : 3 * arrays]
    scratch = refs[3 * arrays :]
    lefts = scratch[:arrays]
    rights = scratch[arrays : 2 * arrays]
    slots = scratch[2 * arrays : 3 * arrays]
    finals = scratch[3 * arrays : 4 * arrays]
    send_sem, recv_sem, load_sem, done_sem = scratch[4 * arrays :]
    column = lax.axis_index("tp")
    place, ahead, behind = ring_ends(count)
    loads = []
    for array in range(arrays):
        loads.append(pltpu.make_async_copy(left_refs[array], lefts[array], load_sem.at[array, 0]))
        loads.append(pltpu.make_async_copy(right_refs[array], rights[array], load_sem.at[array, 1]))
    for load in loads:
        load.start()
    greet(ahead, behind, column)

    def pieces(array):
        half = rights[array].shape[1] // 2
        parts = chunks_of(half)
        width = half // parts
        return [(way, part, way * half + part * width, part * width, width) for part in range(parts) for way in range(2)]

    def term(array, step, way, start, width):
        owner = ring_index((place + 2 * count - 1 - step) % count if way == 0 else (place + 1 + step) % count, count)
        rows = finals[array].shape[0]
        left = lefts[array][pl.ds(pl.multiple_of(owner * rows, 16), rows), :]
        return jnp.dot(left, rights[array][:, start : start + width], preferred_element_type=jnp.float32)

    def copy(array, step, way, part, inner, width):
        held = slots[array].at[way, step, :, pl.ds(inner, width)]
        return pltpu.make_async_remote_copy(
            src_ref=held,
            dst_ref=slots[array].at[way, step + 1, :, pl.ds(inner, width)],
            send_sem=send_sem.at[array, way, part, step],
            recv_sem=recv_sem.at[array, way, part, step],
            device_id=(ahead if way == 0 else behind, column),
            device_id_type=MESH,
        )

    for array in range(arrays):
        loads[2 * array].wait()
        loads[2 * array + 1].wait()
        for way, part, start, inner, width in pieces(array):
            slots[array][way, 0, :, inner : inner + width] = term(array, 0, way, start, width).astype(LOW)
            copy(array, 0, way, part, inner, width).start()

    def hop(step, carry):
        for array in range(arrays):
            for way, part, start, inner, width in pieces(array):
                mine = term(array, step, way, start, width)
                copy(array, step - 1, way, part, inner, width).wait_recv()
                held = slots[array].at[way, step, :, pl.ds(inner, width)]
                held[...] = (held[...].astype(jnp.float32) + mine).astype(LOW)
                copy(array, step, way, part, inner, width).start()
        return carry

    lax.fori_loop(1, count - 1, hop, 0)
    stores = []
    for array in range(arrays):
        for way, part, start, inner, width in pieces(array):
            mine = term(array, count - 1, way, start, width)
            copy(array, count - 2, way, part, inner, width).wait_recv()
            held = slots[array][way, count - 1, :, inner : inner + width]
            finals[array][:, start : start + width] = held.astype(jnp.float32) + mine
        store = pltpu.make_async_copy(finals[array], out_refs[array], done_sem.at[array])
        store.start()
        stores.append(store)

    def sent(step, carry):
        for array in range(arrays):
            for way, part, start, inner, width in pieces(array):
                copy(array, step, way, part, inner, width).wait_send()
        return carry

    lax.fori_loop(0, count - 1, sent, 0)
    for store in stores:
        store.wait()


def ring_scatter(pairs, collective):
    count = lax.axis_size("seq")
    arrays = len(pairs)
    lefts = [left for left, right in pairs]
    rights = [right for left, right in pairs]
    rows = [left.shape[0] // count for left in lefts]
    widths = [right.shape[1] for right in rights]
    moved = sum(left.shape[0] * width * 2 for left, width in zip(lefts, widths))
    flops = sum(2 * left.shape[0] * left.shape[1] * width for left, width in zip(lefts, widths))
    return pl.pallas_call(
        functools.partial(scatter_kernel, count, arrays),
        out_shape=[jax.ShapeDtypeStruct((row, width), jnp.float32) for row, width in zip(rows, widths)],
        in_specs=[pl.BlockSpec(memory_space=pl.ANY)] * (2 * arrays),
        out_specs=[pl.BlockSpec(memory_space=pl.ANY)] * arrays,
        scratch_shapes=[pltpu.VMEM(left.shape, left.dtype) for left in lefts]
        + [pltpu.VMEM(right.shape, right.dtype) for right in rights]
        + [pltpu.VMEM((2, count, row, width // 2), LOW) for row, width in zip(rows, widths)]
        + [pltpu.VMEM((row, width), jnp.float32) for row, width in zip(rows, widths)]
        + [
            pltpu.SemaphoreType.DMA((arrays, 2, 2, count - 1)),
            pltpu.SemaphoreType.DMA((arrays, 2, 2, count - 1)),
            pltpu.SemaphoreType.DMA((arrays, 2)),
            pltpu.SemaphoreType.DMA((arrays,)),
        ],
        compiler_params=pltpu.CompilerParams(
            collective_id=collective, has_side_effects=True, vmem_limit_bytes=VMEM_BYTES
        ),
        cost_estimate=pl.CostEstimate(flops=flops, bytes_accessed=30 * moved, transcendentals=0),
        name="ring_scatter",
    )(*lefts, *rights)


def from_behind(block, axis, distance):
    devices = range(lax.axis_size(axis))
    route = [(i - distance, i) for i in devices if i - distance in devices]
    return lax.ppermute(block, axis, route)


def contract_rows(left, right):
    return lax.dot_general(
        left, right, (((0,), (0,)), ((), ())), preferred_element_type=jnp.float32
    )


def contract_cols(left, right):
    return lax.dot_general(
        left, right, (((1,), (1,)), ((), ())), preferred_element_type=jnp.float32
    )


def gather_features(own):
    return lax.all_gather(own.T, "tp", axis=0, tiled=True)


def reduce_branch(term):
    return lax.psum_scatter(term.astype(LOW), "tp", scatter_dimension=1, tiled=True).astype(jnp.float32)


def norm_forward(values, gain_row):
    row_total = lax.psum(jnp.sum(values * values, axis=1, keepdims=True), "tp")
    row_scale = lax.rsqrt(row_total / D + EPSILON)
    own_normed = (values * row_scale * gain_row).astype(LOW)
    return gather_features(own_normed), row_scale


def norm_backward(grad_normed, kept_rows, row_scale, kept_gain):
    inner_sum = lax.psum(jnp.sum(grad_normed * kept_gain * kept_rows, axis=1, keepdims=True), "tp")
    rows_grad = row_scale * kept_gain * grad_normed - kept_rows * row_scale**3 * inner_sum / D
    return (rows_grad, jnp.sum(grad_normed * kept_rows * row_scale, axis=0))


def adam_update(weight, first, second, grad, rate, decay):
    first_next = BETA_ONE * first + (1.0 - BETA_ONE) * grad
    second_next = BETA_TWO * second + (1.0 - BETA_TWO) * grad * grad
    corrected = first_next / (1.0 - BETA_ONE**STEP)
    spread = jnp.sqrt(second_next / (1.0 - BETA_TWO**STEP)) + ADAM_EPSILON
    return (weight - rate * (corrected / spread + decay * weight), first_next, second_next)


def shards(
    tokens,
    bounds,
    cotangent,
    entry_weight,
    entry_first,
    entry_second,
    exit_weight,
    exit_first,
    exit_second,
    expand_weight,
    expand_first,
    expand_second,
    shrink_weight,
    shrink_first,
    shrink_second,
    conv_kernel,
    conv_first,
    conv_second,
    norm_gains,
    gain_first,
    gain_second,
):
    rows_dev = tokens.shape[0]
    channels = tokens.shape[1]
    hidden = shrink_weight.shape[1]
    small = jnp.concatenate([conv_kernel, norm_gains], axis=0).astype(LOW)
    small_full = lax.all_gather(small, "seq", axis=1, tiled=True).astype(jnp.float32)
    kernel = small_full[:3]
    gains_row = small_full[3:]
    entry_low = entry_weight.reshape(entry_weight.shape[0], 3 * channels).astype(LOW)
    gate_low = expand_weight[:, 0].astype(LOW)
    up_low = expand_weight[:, 1].astype(LOW)

    position = jnp.arange(rows_dev, dtype=jnp.int32)[:, None]
    boundary = bounds[0]
    see_one = (position != boundary).astype(jnp.float32)
    see_two = see_one * (position - 1 != boundary).astype(jnp.float32)
    tokens_f = tokens.astype(jnp.float32)

    normed_one, scale_one = norm_forward(tokens_f, gains_row[0])
    entry_full, exit_full = ring_gather([entry_low, exit_weight.astype(LOW)], 0)
    projected = contract_rows(normed_one, entry_full)
    input_gate = projected[:, :channels]
    output_gate = projected[:, channels : 2 * channels]
    values_rows = projected[:, 2 * channels :]
    gated_rows = (input_gate * values_rows).astype(LOW)
    previous = from_behind(gated_rows[-2:], "seq", 1)
    extended = jnp.concatenate([previous, gated_rows], axis=0).astype(jnp.float32)
    conv_out = (
        kernel[2] * extended[2:]
        + kernel[1] * extended[1:-1] * see_one
        + kernel[0] * extended[:-2] * see_two
    )
    mixer_rows = (output_gate * conv_out).astype(LOW)
    branch = reduce_branch(contract_cols(mixer_rows, exit_full))
    (gate_full,) = ring_gather([gate_low], 1)
    residual = tokens_f + branch
    normed_two, scale_two = norm_forward(residual, gains_row[1])
    (up_full,) = ring_gather([up_low], 2)
    cot_full = gather_features(cotangent)
    (shrink_full,) = ring_gather([shrink_weight.astype(LOW)], 3)
    gate_rows = contract_rows(normed_two, gate_full)
    up_rows = contract_rows(normed_two, up_full)
    sigmoid_gate = jax.nn.sigmoid(gate_rows)
    silu_gate = gate_rows * sigmoid_gate
    activation = (silu_gate * up_rows).astype(LOW)

    act_grad = contract_rows(cot_full, shrink_full)
    gate_grad = (
        act_grad * up_rows * sigmoid_gate * (1.0 + gate_rows * (1.0 - sigmoid_gate))
    ).astype(LOW)
    up_grad = (act_grad * silu_gate).astype(LOW)
    two_term = contract_cols(gate_grad, gate_full) + contract_cols(up_grad, up_full)
    grad_normed_two = reduce_branch(two_term)
    (shrink_part,) = ring_scatter([(cot_full, activation)], 4)
    mixed = (residual + reduce_branch(contract_cols(activation, shrink_full))).astype(LOW)
    residual_norm_grad, gain_two_grad = norm_backward(grad_normed_two, residual, scale_two, gains_row[1])
    residual_grad = cotangent.astype(jnp.float32) + residual_norm_grad
    branch_full = gather_features(residual_grad.astype(LOW))
    (gate_part,) = ring_scatter([(normed_two, gate_grad)], 5)
    mixer_grad = contract_rows(branch_full, exit_full)
    out_gate_grad = (mixer_grad * conv_out).astype(LOW)
    conv_grad = mixer_grad * output_gate
    lag_zero = conv_grad * kernel[2]
    lag_one = conv_grad * see_one * kernel[1]
    lag_two = conv_grad * see_two * kernel[0]
    padded_grad = (
        jnp.pad(lag_zero, ((2, 0), (0, 0)))
        + jnp.pad(lag_one, ((1, 1), (0, 0)))
        + jnp.pad(lag_two, ((0, 2), (0, 0)))
    )
    returned = from_behind(padded_grad[:2], "seq", -1)
    gated_grad = padded_grad[2:] + jnp.pad(returned, ((rows_dev - 2, 0), (0, 0)))
    kernel_grad = jnp.stack(
        [
            jnp.sum(conv_grad * see_two * extended[:-2], axis=0),
            jnp.sum(conv_grad * see_one * extended[1:-1], axis=0),
            jnp.sum(conv_grad * extended[2:], axis=0),
        ]
    )
    in_gate_grad = (gated_grad * values_rows).astype(LOW)
    values_grad = (gated_grad * input_gate).astype(LOW)
    projected_grad = jnp.concatenate([in_gate_grad, out_gate_grad, values_grad], axis=1)
    one_term = contract_cols(projected_grad, entry_full)
    grad_normed_one = reduce_branch(one_term)
    (up_part,) = ring_scatter([(normed_two, up_grad)], 6)
    tokens_norm_grad, gain_one_grad = norm_backward(grad_normed_one, tokens_f, scale_one, gains_row[0])
    tokens_grad = residual_grad + tokens_norm_grad
    small_grad = jnp.concatenate([kernel_grad, gain_one_grad[None], gain_two_grad[None]], axis=0)
    small_part = lax.psum_scatter(small_grad, "seq", scatter_dimension=1, tiled=True)
    kernel_part = small_part[:3]
    gains_part = small_part[3:]
    entry_part, exit_part = ring_scatter([(normed_one, projected_grad), (branch_full, mixer_rows)], 7)
    entry_part = entry_part.reshape(entry_weight.shape)
    expand_part = jnp.stack([gate_part, up_part], axis=1)
    entry_next, entry_first_next, entry_second_next = adam_update(
        entry_weight, entry_first, entry_second, entry_part, RATE_WIDE, WEIGHT_DECAY
    )
    exit_next, exit_first_next, exit_second_next = adam_update(
        exit_weight, exit_first, exit_second, exit_part, RATE_WIDE, WEIGHT_DECAY
    )
    expand_next, expand_first_next, expand_second_next = adam_update(
        expand_weight, expand_first, expand_second, expand_part, RATE_WIDE, WEIGHT_DECAY
    )
    shrink_next, shrink_first_next, shrink_second_next = adam_update(
        shrink_weight, shrink_first, shrink_second, shrink_part, RATE_WIDE, WEIGHT_DECAY
    )
    conv_next, conv_first_next, conv_second_next = adam_update(
        conv_kernel, conv_first, conv_second, kernel_part, RATE_CONV, 0.0
    )
    gains_next, gains_first_next, gains_second_next = adam_update(
        norm_gains, gain_first, gain_second, gains_part, RATE_GAIN, 0.0
    )
    return (
        mixed,
        tokens_grad,
        entry_next,
        entry_first_next,
        entry_second_next,
        exit_next,
        exit_first_next,
        exit_second_next,
        expand_next,
        expand_first_next,
        expand_second_next,
        shrink_next,
        shrink_first_next,
        shrink_second_next,
        conv_next,
        conv_first_next,
        conv_second_next,
        gains_next,
        gains_first_next,
        gains_second_next,
    )


def solution(mesh):
    rows = P("seq", "tp")
    stacked = P("seq", None, "tp")
    small = P(None, ("tp", "seq"))
    return jax.shard_map(
        shards,
        mesh=mesh,
        in_specs=(rows, P("seq"), rows) + (stacked,) * 3 + (rows,) * 3 + (stacked,) * 3 + (rows,) * 3 + (small,) * 6,
        out_specs=(rows, rows) + (stacked,) * 3 + (rows,) * 3 + (stacked,) * 3 + (rows,) * 3 + (small,) * 6,
        check_vma=False,
    )
```

```python
import functools

import jax
import jax.numpy as jnp
from jax import lax
from jax.experimental import pallas as pl
from jax.experimental.pallas import tpu as pltpu
from jax.sharding import PartitionSpec as P

D = 2048
STEP = 10


EPSILON = 1e-05
BETA_ONE = 0.9
BETA_TWO = 0.95
ADAM_EPSILON = 1e-08
WEIGHT_DECAY = 0.1
RATE_WIDE = 0.04
RATE_CONV = 0.5
RATE_GAIN = 0.4

MESH = pl.DeviceIdType.MESH
LOW = jnp.bfloat16
VMEM_BYTES = 60 * 1024 * 1024


def ring_place(index, count):
    side = index % 2
    level = index // 2
    return level * (1 - side) + (count - 1 - level) * side


def ring_index(place, count):
    back = place // (count // 2)
    return (1 - back) * (2 * place) + back * (2 * (count - 1 - place) + 1)


def ring_ends(count):
    place = ring_place(lax.axis_index("seq"), count)
    ahead = ring_index((place + 1) % count, count)
    behind = ring_index((place + count - 1) % count, count)
    return place, ahead, behind


def greet(ahead, behind, column):
    barrier = pltpu.get_barrier_semaphore()
    for other in (ahead, behind):
        pl.semaphore_signal(barrier, inc=1, device_id=(other, column), device_id_type=MESH)
    pl.semaphore_wait(barrier, 2)


def gather_kernel(count, arrays, *refs):
    shard_refs = refs[:arrays]
    full_refs = refs[arrays : 2 * arrays]
    send_sem, recv_sem, own_sem = refs[2 * arrays :]
    column = lax.axis_index("tp")
    place, ahead, behind = ring_ends(count)
    greet(ahead, behind, column)

    def copy(array, step, way):
        owner = ring_index((place + count - step) % count if way == 0 else (place + step) % count, count)
        half = shard_refs[array].shape[0] // 2
        part = pl.ds(way * half, half)
        return pltpu.make_async_remote_copy(
            src_ref=full_refs[array].at[owner, part],
            dst_ref=full_refs[array].at[owner, part],
            send_sem=send_sem.at[array, way, step],
            recv_sem=recv_sem.at[array, way, step],
            device_id=(ahead if way == 0 else behind, column),
            device_id_type=MESH,
        )

    def first(array, way):
        half = shard_refs[array].shape[0] // 2
        part = pl.ds(way * half, half)
        return pltpu.make_async_remote_copy(
            src_ref=shard_refs[array].at[part],
            dst_ref=full_refs[array].at[lax.axis_index("seq"), part],
            send_sem=send_sem.at[array, way, 0],
            recv_sem=recv_sem.at[array, way, 0],
            device_id=(ahead if way == 0 else behind, column),
            device_id_type=MESH,
        )

    def own(array):
        return pltpu.make_async_copy(
            shard_refs[array], full_refs[array].at[lax.axis_index("seq")], own_sem.at[array]
        )

    for array in range(arrays):
        for way in range(2):
            first(array, way).start()
    for array in range(arrays):
        own(array).start()

    def hop(step, carry):
        for array in range(arrays):
            for way in range(2):
                copy(array, step - 1, way).wait_recv()
                copy(array, step, way).start()
        return carry

    lax.fori_loop(1, count - 1, hop, 0)
    for array in range(arrays):
        for way in range(2):
            copy(array, count - 2, way).wait_recv()

    def sent(step, carry):
        for array in range(arrays):
            for way in range(2):
                copy(array, step, way).wait_send()
        return carry

    lax.fori_loop(0, count - 1, sent, 0)
    for array in range(arrays):
        own(array).wait()


def ring_gather(shards, collective):
    count = lax.axis_size("seq")
    arrays = len(shards)
    moved = sum(shard.size for shard in shards) * 2 * count
    fulls = pl.pallas_call(
        functools.partial(gather_kernel, count, arrays),
        out_shape=[jax.ShapeDtypeStruct((count,) + shard.shape, shard.dtype) for shard in shards],
        in_specs=[pl.BlockSpec(memory_space=pl.ANY)] * arrays,
        out_specs=[pl.BlockSpec(memory_space=pl.ANY)] * arrays,
        scratch_shapes=[
            pltpu.SemaphoreType.DMA((arrays, 2, count - 1)),
            pltpu.SemaphoreType.DMA((arrays, 2, count - 1)),
            pltpu.SemaphoreType.DMA((arrays,)),
        ],
        compiler_params=pltpu.CompilerParams(
            collective_id=collective, has_side_effects=True, vmem_limit_bytes=VMEM_BYTES
        ),
        cost_estimate=pl.CostEstimate(flops=0, bytes_accessed=30 * moved, transcendentals=0),
        name="ring_gather",
    )(*shards)
    return [full.reshape(count * full.shape[1], full.shape[2]) for full in fulls]


def chunks_of(width):
    return 2 if width % 256 == 0 and width > 256 else 1


def scatter_kernel(count, arrays, *refs):
    left_refs = refs[:arrays]
    right_refs = refs[arrays : 2 * arrays]
    out_refs = refs[2 * arrays : 3 * arrays]
    scratch = refs[3 * arrays :]
    lefts = scratch[:arrays]
    rights = scratch[arrays : 2 * arrays]
    slots = scratch[2 * arrays : 3 * arrays]
    finals = scratch[3 * arrays : 4 * arrays]
    send_sem, recv_sem, load_sem, done_sem = scratch[4 * arrays :]
    column = lax.axis_index("tp")
    place, ahead, behind = ring_ends(count)
    loads = []
    for array in range(arrays):
        loads.append(pltpu.make_async_copy(left_refs[array], lefts[array], load_sem.at[array, 0]))
        loads.append(pltpu.make_async_copy(right_refs[array], rights[array], load_sem.at[array, 1]))
    for load in loads:
        load.start()
    greet(ahead, behind, column)

    def pieces(array):
        half = rights[array].shape[1] // 2
        parts = chunks_of(half)
        width = half // parts
        return [(way, part, way * half + part * width, part * width, width) for part in range(parts) for way in range(2)]

    def term(array, step, way, start, width):
        owner = ring_index((place + 2 * count - 1 - step) % count if way == 0 else (place + 1 + step) % count, count)
        rows = finals[array].shape[0]
        left = lefts[array][pl.ds(pl.multiple_of(owner * rows, 16), rows), :]
        return jnp.dot(left, rights[array][:, start : start + width], preferred_element_type=jnp.float32)

    def copy(array, step, way, part, inner, width):
        held = slots[array].at[way, step, :, pl.ds(inner, width)]
        return pltpu.make_async_remote_copy(
            src_ref=held,
            dst_ref=slots[array].at[way, step + 1, :, pl.ds(inner, width)],
            send_sem=send_sem.at[array, way, part, step],
            recv_sem=recv_sem.at[array, way, part, step],
            device_id=(ahead if way == 0 else behind, column),
            device_id_type=MESH,
        )

    for array in range(arrays):
        loads[2 * array].wait()
        loads[2 * array + 1].wait()
        for way, part, start, inner, width in pieces(array):
            slots[array][way, 0, :, inner : inner + width] = term(array, 0, way, start, width).astype(LOW)
            copy(array, 0, way, part, inner, width).start()

    def hop(step, carry):
        for array in range(arrays):
            for way, part, start, inner, width in pieces(array):
                mine = term(array, step, way, start, width)
                copy(array, step - 1, way, part, inner, width).wait_recv()
                held = slots[array].at[way, step, :, pl.ds(inner, width)]
                held[...] = (held[...].astype(jnp.float32) + mine).astype(LOW)
                copy(array, step, way, part, inner, width).start()
        return carry

    lax.fori_loop(1, count - 1, hop, 0)
    stores = []
    for array in range(arrays):
        for way, part, start, inner, width in pieces(array):
            mine = term(array, count - 1, way, start, width)
            copy(array, count - 2, way, part, inner, width).wait_recv()
            held = slots[array][way, count - 1, :, inner : inner + width]
            finals[array][:, start : start + width] = held.astype(jnp.float32) + mine
        store = pltpu.make_async_copy(finals[array], out_refs[array], done_sem.at[array])
        store.start()
        stores.append(store)

    def sent(step, carry):
        for array in range(arrays):
            for way, part, start, inner, width in pieces(array):
                copy(array, step, way, part, inner, width).wait_send()
        return carry

    lax.fori_loop(0, count - 1, sent, 0)
    for store in stores:
        store.wait()


def ring_scatter(pairs, collective):
    count = lax.axis_size("seq")
    arrays = len(pairs)
    lefts = [left for left, right in pairs]
    rights = [right for left, right in pairs]
    rows = [left.shape[0] // count for left in lefts]
    widths = [right.shape[1] for right in rights]
    moved = sum(left.shape[0] * width * 2 for left, width in zip(lefts, widths))
    flops = sum(2 * left.shape[0] * left.shape[1] * width for left, width in zip(lefts, widths))
    return pl.pallas_call(
        functools.partial(scatter_kernel, count, arrays),
        out_shape=[jax.ShapeDtypeStruct((row, width), jnp.float32) for row, width in zip(rows, widths)],
        in_specs=[pl.BlockSpec(memory_space=pl.ANY)] * (2 * arrays),
        out_specs=[pl.BlockSpec(memory_space=pl.ANY)] * arrays,
        scratch_shapes=[pltpu.VMEM(left.shape, left.dtype) for left in lefts]
        + [pltpu.VMEM(right.shape, right.dtype) for right in rights]
        + [pltpu.VMEM((2, count, row, width // 2), LOW) for row, width in zip(rows, widths)]
        + [pltpu.VMEM((row, width), jnp.float32) for row, width in zip(rows, widths)]
        + [
            pltpu.SemaphoreType.DMA((arrays, 2, 2, count - 1)),
            pltpu.SemaphoreType.DMA((arrays, 2, 2, count - 1)),
            pltpu.SemaphoreType.DMA((arrays, 2)),
            pltpu.SemaphoreType.DMA((arrays,)),
        ],
        compiler_params=pltpu.CompilerParams(
            collective_id=collective, has_side_effects=True, vmem_limit_bytes=VMEM_BYTES
        ),
        cost_estimate=pl.CostEstimate(flops=flops, bytes_accessed=30 * moved, transcendentals=0),
        name="ring_scatter",
    )(*lefts, *rights)


def from_behind(block, axis, distance):
    devices = range(lax.axis_size(axis))
    route = [(i - distance, i) for i in devices if i - distance in devices]
    return lax.ppermute(block, axis, route)


def contract_rows(left, right):
    return lax.dot_general(
        left, right, (((0,), (0,)), ((), ())), preferred_element_type=jnp.float32
    )


def contract_cols(left, right):
    return lax.dot_general(
        left, right, (((1,), (1,)), ((), ())), preferred_element_type=jnp.float32
    )


def tie(*values):
    return lax.optimization_barrier(values)


def gather_rows(own):
    return lax.all_gather(own, "tp", axis=0, tiled=True)


def gather_features(own):
    return gather_rows(own.T)


def reduce_branch(term):
    return lax.psum_scatter(term, "tp", scatter_dimension=1, tiled=True).astype(jnp.float32)


def norm_forward(values, gain_row):
    row_total = lax.psum(jnp.sum(values * values, axis=1, keepdims=True), "tp")
    row_scale = lax.rsqrt(row_total / D + EPSILON)
    return (values * row_scale * gain_row).astype(LOW), row_scale


def norm_backward(grad_normed, kept_rows, row_scale, kept_gain):
    inner_sum = lax.psum(jnp.sum(grad_normed * kept_gain * kept_rows, axis=1, keepdims=True), "tp")
    rows_grad = row_scale * kept_gain * grad_normed - kept_rows * row_scale**3 * inner_sum / D
    return (rows_grad, jnp.sum(grad_normed * kept_rows * row_scale, axis=0))


def adam_update(weight, first, second, grad, rate, decay):
    first_next = BETA_ONE * first + (1.0 - BETA_ONE) * grad
    second_next = BETA_TWO * second + (1.0 - BETA_TWO) * grad * grad
    corrected = first_next / (1.0 - BETA_ONE**STEP)
    spread = jnp.sqrt(second_next / (1.0 - BETA_TWO**STEP)) + ADAM_EPSILON
    return (weight - rate * (corrected / spread + decay * weight), first_next, second_next)


def shards(
    tokens,
    bounds,
    cotangent,
    entry_weight,
    entry_first,
    entry_second,
    exit_weight,
    exit_first,
    exit_second,
    expand_weight,
    expand_first,
    expand_second,
    shrink_weight,
    shrink_first,
    shrink_second,
    conv_kernel,
    conv_first,
    conv_second,
    norm_gains,
    gain_first,
    gain_second,
):
    rows_dev = tokens.shape[0]
    channels = tokens.shape[1]
    count = lax.axis_size("seq")
    small = jnp.concatenate([conv_kernel, norm_gains], axis=0)
    small = jnp.pad(small, ((0, 32 - small.shape[0]), (0, 128 - small.shape[1]))).astype(LOW)
    entry_low = entry_weight.reshape(entry_weight.shape[0], 3 * channels).astype(LOW)
    gate_low = expand_weight[:, 0].astype(LOW)
    up_low = expand_weight[:, 1].astype(LOW)

    position = jnp.arange(rows_dev, dtype=jnp.int32)[:, None]
    boundary = bounds[0]
    see_one = (position != boundary).astype(jnp.float32)
    see_two = see_one * (position - 1 != boundary).astype(jnp.float32)
    tokens_f = tokens.astype(jnp.float32)

    tokens_full = gather_features(tokens)
    entry_full, exit_full, small_full = ring_gather([entry_low, exit_weight.astype(LOW), small], 0)
    tokens_full, entry_full, small_full = tie(tokens_full, entry_full, small_full)
    small_full = small_full.reshape(count, 32, 128)[:, :5, : conv_kernel.shape[1]]
    small_full = small_full.swapaxes(0, 1).reshape(5, channels).astype(jnp.float32)
    kernel = small_full[:3]
    gains_row = small_full[3:]
    gain_one_full = lax.all_gather(gains_row[0].astype(LOW), "tp", axis=0, tiled=True).astype(jnp.float32)

    tokens_full = tokens_full.astype(jnp.float32)
    scale_row = lax.rsqrt(jnp.sum(tokens_full * tokens_full, axis=0, keepdims=True) / D + EPSILON)
    normed_one = (tokens_full * scale_row * gain_one_full[:, None]).astype(LOW)
    scale_one = scale_row.reshape(rows_dev, 1)
    projected = contract_rows(normed_one, entry_full)
    input_gate = projected[:, :channels]
    output_gate = projected[:, channels : 2 * channels]
    values_rows = projected[:, 2 * channels :]
    gated_rows = (input_gate * values_rows).astype(LOW)
    previous = from_behind(gated_rows[-2:], "seq", 1)
    extended = jnp.concatenate([previous, gated_rows], axis=0).astype(jnp.float32)
    conv_out = (
        kernel[2] * extended[2:]
        + kernel[1] * extended[1:-1] * see_one
        + kernel[0] * extended[:-2] * see_two
    )
    mixer_rows = (output_gate * conv_out).astype(LOW)
    branch_term, gate_low = tie(contract_cols(mixer_rows, exit_full).astype(LOW), gate_low)
    (gate_full,) = ring_gather([gate_low], 1)
    branch, gate_full = tie(reduce_branch(branch_term), gate_full)
    residual = tokens_f + branch
    own_normed_two, scale_two = norm_forward(residual, gains_row[1])
    own_normed_two, up_low = tie(own_normed_two.T, up_low)
    (up_full,) = ring_gather([up_low], 2)
    normed_two, up_full = tie(gather_rows(own_normed_two), up_full)
    cot_own, shrink_low, normed_two = tie(cotangent.T, shrink_weight.astype(LOW), normed_two)
    (shrink_full,) = ring_gather([shrink_low], 3)
    cot_full, shrink_full = tie(gather_rows(cot_own), shrink_full)
    gate_rows = contract_rows(normed_two, gate_full)
    up_rows = contract_rows(normed_two, up_full)
    sigmoid_gate = jax.nn.sigmoid(gate_rows)
    silu_gate = gate_rows * sigmoid_gate
    activation = (silu_gate * up_rows).astype(LOW)

    act_grad = contract_rows(cot_full, shrink_full)
    gate_grad = (
        act_grad * up_rows * sigmoid_gate * (1.0 + gate_rows * (1.0 - sigmoid_gate))
    ).astype(LOW)
    up_grad = (act_grad * silu_gate).astype(LOW)
    two_term = contract_cols(gate_grad, gate_full) + contract_cols(up_grad, up_full)
    two_term, activation = tie(two_term.astype(LOW), activation)
    (shrink_part,) = ring_scatter([(cot_full, activation)], 4)
    grad_normed_two, shrink_part = tie(reduce_branch(two_term), shrink_part)
    residual_norm_grad, gain_two_grad = norm_backward(grad_normed_two, residual, scale_two, gains_row[1])
    residual_grad = cotangent.astype(jnp.float32) + residual_norm_grad
    mixed_term = contract_cols(activation, shrink_full).astype(LOW)
    branch_own, mixed_term, gate_grad = tie(residual_grad.astype(LOW).T, mixed_term, gate_grad)
    (gate_part,) = ring_scatter([(normed_two, gate_grad)], 5)
    branch_full, gate_part, mixed_branch = tie(gather_rows(branch_own), gate_part, reduce_branch(mixed_term))
    mixed = (residual + mixed_branch).astype(LOW)
    mixer_grad = contract_rows(branch_full, exit_full)
    out_gate_grad = (mixer_grad * conv_out).astype(LOW)
    conv_grad = mixer_grad * output_gate
    lag_zero = conv_grad * kernel[2]
    lag_one = conv_grad * see_one * kernel[1]
    lag_two = conv_grad * see_two * kernel[0]
    padded_grad = (
        jnp.pad(lag_zero, ((2, 0), (0, 0)))
        + jnp.pad(lag_one, ((1, 1), (0, 0)))
        + jnp.pad(lag_two, ((0, 2), (0, 0)))
    )
    returned = from_behind(padded_grad[:2], "seq", -1)
    gated_grad = padded_grad[2:] + jnp.pad(returned, ((rows_dev - 2, 0), (0, 0)))
    kernel_grad = jnp.stack(
        [
            jnp.sum(conv_grad * see_two * extended[:-2], axis=0),
            jnp.sum(conv_grad * see_one * extended[1:-1], axis=0),
            jnp.sum(conv_grad * extended[2:], axis=0),
        ]
    )
    in_gate_grad = (gated_grad * values_rows).astype(LOW)
    values_grad = (gated_grad * input_gate).astype(LOW)
    projected_grad = jnp.concatenate([in_gate_grad, out_gate_grad, values_grad], axis=1)
    one_term, up_grad = tie(contract_cols(projected_grad, entry_full).astype(LOW), up_grad)
    (up_part,) = ring_scatter([(normed_two, up_grad)], 6)
    grad_normed_one, up_part = tie(reduce_branch(one_term), up_part)
    tokens_norm_grad, gain_one_grad = norm_backward(grad_normed_one, tokens_f, scale_one, gains_row[0])
    tokens_grad = residual_grad + tokens_norm_grad
    small_grad = jnp.concatenate([kernel_grad, gain_one_grad[None], gain_two_grad[None]], axis=0)
    small_grad = lax.psum(small_grad, "seq")
    small_part = lax.dynamic_slice_in_dim(
        small_grad, lax.axis_index("seq") * conv_kernel.shape[1], conv_kernel.shape[1], axis=1
    )
    kernel_part = small_part[:3]
    gains_part = small_part[3:]
    projected_grad, small_part = tie(projected_grad, small_part)
    entry_part, exit_part = ring_scatter([(normed_one, projected_grad), (branch_full, mixer_rows)], 7)
    entry_part = entry_part.reshape(entry_weight.shape)
    expand_part = jnp.stack([gate_part, up_part], axis=1)
    entry_next, entry_first_next, entry_second_next = adam_update(
        entry_weight, entry_first, entry_second, entry_part, RATE_WIDE, WEIGHT_DECAY
    )
    exit_next, exit_first_next, exit_second_next = adam_update(
        exit_weight, exit_first, exit_second, exit_part, RATE_WIDE, WEIGHT_DECAY
    )
    expand_next, expand_first_next, expand_second_next = adam_update(
        expand_weight, expand_first, expand_second, expand_part, RATE_WIDE, WEIGHT_DECAY
    )
    shrink_next, shrink_first_next, shrink_second_next = adam_update(
        shrink_weight, shrink_first, shrink_second, shrink_part, RATE_WIDE, WEIGHT_DECAY
    )
    conv_next, conv_first_next, conv_second_next = adam_update(
        conv_kernel, conv_first, conv_second, kernel_part, RATE_CONV, 0.0
    )
    gains_next, gains_first_next, gains_second_next = adam_update(
        norm_gains, gain_first, gain_second, gains_part, RATE_GAIN, 0.0
    )
    return (
        mixed,
        tokens_grad,
        entry_next,
        entry_first_next,
        entry_second_next,
        exit_next,
        exit_first_next,
        exit_second_next,
        expand_next,
        expand_first_next,
        expand_second_next,
        shrink_next,
        shrink_first_next,
        shrink_second_next,
        conv_next,
        conv_first_next,
        conv_second_next,
        gains_next,
        gains_first_next,
        gains_second_next,
    )


def solution(mesh):
    rows = P("seq", "tp")
    stacked = P("seq", None, "tp")
    small = P(None, ("tp", "seq"))
    return jax.shard_map(
        shards,
        mesh=mesh,
        in_specs=(rows, P("seq"), rows) + (stacked,) * 3 + (rows,) * 3 + (stacked,) * 3 + (rows,) * 3 + (small,) * 6,
        out_specs=(rows, rows) + (stacked,) * 3 + (rows,) * 3 + (stacked,) * 3 + (rows,) * 3 + (small,) * 6,
        check_vma=False,
    )
```

```python
import functools

import jax
import jax.numpy as jnp
from jax import lax
from jax.experimental import pallas as pl
from jax.experimental.layout import Layout, with_layout_constraint
from jax.experimental.pallas import tpu as pltpu
from jax.sharding import PartitionSpec as P

D = 2048
STEP = 10


EPSILON = 1e-05
BETA_ONE = 0.9
BETA_TWO = 0.95
ADAM_EPSILON = 1e-08
WEIGHT_DECAY = 0.1
RATE_WIDE = 0.04
RATE_CONV = 0.5
RATE_GAIN = 0.4

MESH = pl.DeviceIdType.MESH
LOW = jnp.bfloat16
VMEM_BYTES = 60 * 1024 * 1024


def ring_place(index, count):
    side = index % 2
    level = index // 2
    return level * (1 - side) + (count - 1 - level) * side


def ring_index(place, count):
    back = place // (count // 2)
    return (1 - back) * (2 * place) + back * (2 * (count - 1 - place) + 1)


def ring_ends(count):
    place = ring_place(lax.axis_index("seq"), count)
    ahead = ring_index((place + 1) % count, count)
    behind = ring_index((place + count - 1) % count, count)
    return place, ahead, behind


def greet(peers):
    barrier = pltpu.get_barrier_semaphore()
    for peer in peers:
        pl.semaphore_signal(barrier, inc=1, device_id=peer, device_id_type=MESH)
    pl.semaphore_wait(barrier, len(peers))


def split(items, sizes):
    parts, start = [], 0
    for size in sizes:
        parts.append(items[start : start + size])
        start += size
    return parts


class GatherRing:
    name = "ring_gather"

    def __init__(self, shards):
        self.count = lax.axis_size("seq")
        self.inputs = list(shards)
        self.arrays = len(shards)
        self.rows = [shard.shape[0] for shard in shards]
        self.parts = 2 if min(self.rows) % 64 == 0 else 1
        self.ticks = (self.count - 2) * self.parts
        self.out_shapes = [jax.ShapeDtypeStruct((self.count,) + shard.shape, shard.dtype) for shard in shards]
        sems = pltpu.SemaphoreType.DMA((self.arrays, 2, self.parts, self.count - 1))
        self.scratch = [sems, sems, pltpu.SemaphoreType.DMA((self.arrays,))]
        self.flops = 0
        self.bytes = 20 * sum(shard.size for shard in shards) * 2 * self.count

    def bind(self, ins, outs, scratch):
        self.shard_refs, self.full_refs = ins, outs
        self.send_sem, self.recv_sem, self.own_sem = scratch
        self.column = lax.axis_index("tp")
        self.place, self.ahead, self.behind = ring_ends(self.count)

    def pieces(self):
        return [(array, way) for array in range(self.arrays) for way in range(2)]

    def copy(self, array, way, part, step, first=False):
        move = (self.place + self.count - step) if way == 0 else (self.place + step)
        owner = ring_index(move % self.count, self.count)
        size = self.rows[array] // 2 // self.parts
        rows = pl.ds(pl.multiple_of(way * (self.rows[array] // 2) + part * size, 16), size)
        there = self.full_refs[array].at[owner, rows]
        return pltpu.make_async_remote_copy(
            src_ref=self.shard_refs[array].at[rows] if first else there,
            dst_ref=there,
            send_sem=self.send_sem.at[array, way, part, step],
            recv_sem=self.recv_sem.at[array, way, part, step],
            device_id=(self.ahead if way == 0 else self.behind, self.column),
            device_id_type=MESH,
        )

    def own(self, array):
        there = self.full_refs[array].at[lax.axis_index("seq")]
        return pltpu.make_async_copy(self.shard_refs[array], there, self.own_sem.at[array])

    def peers(self):
        return [(self.ahead, self.column), (self.behind, self.column)]

    def prepare(self):
        pass

    def start(self):
        for part in range(self.parts):
            for array, way in self.pieces():
                self.copy(array, way, part, 0, True).start()
        for array in range(self.arrays):
            self.own(array).start()

    def tick(self, index):
        step, part = 1 + index // self.parts, index % self.parts
        for array, way in self.pieces():
            self.copy(array, way, part, step - 1).wait_recv()
            self.copy(array, way, part, step).start()

    def finish(self):
        for part in range(self.parts):
            for array, way in self.pieces():
                self.copy(array, way, part, self.count - 2).wait_recv()

        def sent(step, carry):
            for part in range(self.parts):
                for array, way in self.pieces():
                    self.copy(array, way, part, step).wait_send()
            return carry

        lax.fori_loop(0, self.count - 1, sent, 0)
        for array in range(self.arrays):
            self.own(array).wait()


class ScatterRing:
    name = "ring_scatter"

    def __init__(self, pairs):
        self.count = count = lax.axis_size("seq")
        lefts = [left for left, right in pairs]
        rights = [right for left, right in pairs]
        self.inputs = lefts + rights
        self.arrays = len(pairs)
        self.rows = [left.shape[0] // count for left in lefts]
        self.columns = [right.shape[1] for right in rights]
        self.parts = 2 if min(self.columns) % 512 == 0 else 1
        self.ticks = (count - 2) * self.parts
        self.out_shapes = [
            jax.ShapeDtypeStruct((row, width), jnp.float32) for row, width in zip(self.rows, self.columns)
        ]
        sems = pltpu.SemaphoreType.DMA((self.arrays, 2, self.parts, count - 1))
        self.scratch = (
            [pltpu.VMEM(left.shape, left.dtype) for left in lefts]
            + [pltpu.VMEM(right.shape, right.dtype) for right in rights]
            + [pltpu.VMEM((2, count, row, width // 2), LOW) for row, width in zip(self.rows, self.columns)]
            + [pltpu.VMEM((row, width), jnp.float32) for row, width in zip(self.rows, self.columns)]
            + [sems, sems, pltpu.SemaphoreType.DMA((self.arrays, 2)), pltpu.SemaphoreType.DMA((self.arrays,))]
        )
        self.flops = sum(2 * left.size * width for left, width in zip(lefts, self.columns))
        self.bytes = 20 * sum(left.shape[0] * width * 2 for left, width in zip(lefts, self.columns))

    def bind(self, ins, outs, scratch):
        arrays = self.arrays
        self.in_refs, self.out_refs = ins, outs
        self.lefts, self.rights, self.slots, self.finals = split(scratch, [arrays] * 4)
        self.send_sem, self.recv_sem, self.load_sem, self.done_sem = scratch[4 * arrays :]
        self.column = lax.axis_index("tp")
        self.place, self.ahead, self.behind = ring_ends(self.count)

    def pieces(self):
        return [(array, way) for array in range(self.arrays) for way in range(2)]

    def span(self, array, way, part):
        half = self.columns[array] // 2
        width = half // self.parts
        inner = part * width
        return way * half + inner, inner, width

    def term(self, array, way, part, step):
        move = (self.place + 2 * self.count - 1 - step) if way == 0 else (self.place + 1 + step)
        owner = ring_index(move % self.count, self.count)
        rows = self.rows[array]
        start, _, width = self.span(array, way, part)
        left = self.lefts[array][pl.ds(pl.multiple_of(owner * rows, 16), rows), :]
        right = self.rights[array][:, pl.ds(pl.multiple_of(start, 128), width)]
        return jnp.dot(left, right, preferred_element_type=jnp.float32)

    def held(self, array, way, part, step):
        _, inner, width = self.span(array, way, part)
        return self.slots[array].at[way, step, :, pl.ds(pl.multiple_of(inner, 128), width)]

    def copy(self, array, way, part, step):
        return pltpu.make_async_remote_copy(
            src_ref=self.held(array, way, part, step),
            dst_ref=self.held(array, way, part, step + 1),
            send_sem=self.send_sem.at[array, way, part, step],
            recv_sem=self.recv_sem.at[array, way, part, step],
            device_id=(self.ahead if way == 0 else self.behind, self.column),
            device_id_type=MESH,
        )

    def loads(self):
        return [
            pltpu.make_async_copy(
                self.in_refs[array + side * self.arrays],
                (self.rights if side else self.lefts)[array],
                self.load_sem.at[array, side],
            )
            for array in range(self.arrays)
            for side in range(2)
        ]

    def peers(self):
        return [(self.ahead, self.column), (self.behind, self.column)]

    def prepare(self):
        for load in self.loads():
            load.start()

    def start(self):
        for load in self.loads():
            load.wait()
        for part in range(self.parts):
            for array, way in self.pieces():
                self.held(array, way, part, 0)[...] = self.term(array, way, part, 0).astype(LOW)
                self.copy(array, way, part, 0).start()

    def tick(self, index):
        step, part = 1 + index // self.parts, index % self.parts
        for array, way in self.pieces():
            mine = self.term(array, way, part, step)
            self.copy(array, way, part, step - 1).wait_recv()
            held = self.held(array, way, part, step)
            held[...] = (held[...].astype(jnp.float32) + mine).astype(LOW)
            self.copy(array, way, part, step).start()

    def finish(self):
        last = self.count - 1
        for part in range(self.parts):
            for array, way in self.pieces():
                start, _, width = self.span(array, way, part)
                mine = self.term(array, way, part, last)
                self.copy(array, way, part, last - 1).wait_recv()
                self.finals[array][:, start : start + width] = (
                    self.held(array, way, part, last)[...].astype(jnp.float32) + mine
                )
        stores = [
            pltpu.make_async_copy(self.finals[array], self.out_refs[array], self.done_sem.at[array])
            for array in range(self.arrays)
        ]
        for store in stores:
            store.start()

        def sent(step, carry):
            for part in range(self.parts):
                for array, way in self.pieces():
                    self.copy(array, way, part, step).wait_send()
            return carry

        lax.fori_loop(0, last, sent, 0)
        for store in stores:
            store.wait()


class NoJob:
    inputs, out_shapes, scratch, tiles, flops = [], [], [], 0, 0

    def bind(self, ins, outs, scratch):
        pass

    def peers(self):
        return []

    def start(self):
        pass

    def finish(self):
        pass


class Job:
    wide = 256

    def __init__(self, whole, tiled, outs, tiles, flops):
        self.whole, self.tiled = whole, tiled
        self.inputs = list(whole) + [array for array, axis in tiled]
        self.axes = [axis for array, axis in tiled]
        self.out_shapes = [jax.ShapeDtypeStruct(shape, dtype) for shape, dtype in outs]
        self.tiles = tiles
        self.flops = flops
        self.scratch = (
            [pltpu.VMEM(array.shape, array.dtype) for array in self.inputs]
            + [pltpu.VMEM(shape, dtype) for shape, dtype in outs]
            + [
                pltpu.SemaphoreType.DMA((len(whole),)),
                pltpu.SemaphoreType.DMA((len(tiled), tiles)),
                pltpu.SemaphoreType.DMA((len(outs), tiles)),
            ]
        )

    def bind(self, ins, outs, scratch):
        self.in_refs, self.out_refs = ins, outs
        sizes = [len(self.whole), len(self.tiled), len(outs)]
        self.whole_v, self.tiled_v, self.outs_v = split(scratch, sizes)
        self.whole_sem, self.tiled_sem, self.out_sem = scratch[sum(sizes) :]

    def peers(self):
        return []

    def window(self, axis, index):
        span = pl.ds(pl.multiple_of(index * self.wide, 128), self.wide)
        return (span,) if axis == 0 else (slice(None), span)

    def whole_load(self, which):
        return pltpu.make_async_copy(self.in_refs[which], self.whole_v[which], self.whole_sem.at[which])

    def tiled_load(self, which, index):
        window = self.window(self.axes[which], index)
        there = self.in_refs[len(self.whole) + which].at[window]
        return pltpu.make_async_copy(there, self.tiled_v[which].at[window], self.tiled_sem.at[which, index])

    def out_window(self, index):
        return self.window(1, index)

    def store(self, which, index):
        window = self.out_window(index)
        return pltpu.make_async_copy(
            self.outs_v[which].at[window], self.out_refs[which].at[window], self.out_sem.at[which, index]
        )

    def start(self):
        for which in range(len(self.whole)):
            self.whole_load(which).start()

        def begin(index, carry):
            for which in range(len(self.tiled)):
                self.tiled_load(which, index).start()
            return carry

        lax.fori_loop(0, self.tiles, begin, 0)

    def tile(self, index):
        @pl.when(index == 0)
        def _():
            for which in range(len(self.whole)):
                self.whole_load(which).wait()

        for which in range(len(self.tiled)):
            self.tiled_load(which, index).wait()
        tiles = [ref[self.window(axis, index)] for ref, axis in zip(self.tiled_v, self.axes)]
        for which, value in enumerate(self.compute(self.whole_v, tiles)):
            self.outs_v[which][self.out_window(index)] = value
            self.store(which, index).start()

    def finish(self):
        def end(index, carry):
            for which in range(len(self.outs_v)):
                self.store(which, index).wait()
            return carry

        lax.fori_loop(0, self.tiles, end, 0)


def blocks_dot(blocks, weight):
    parts, _, depth = blocks.shape
    total = None
    for part in range(parts):
        term = jnp.dot(blocks[part], weight[part * depth : (part + 1) * depth], preferred_element_type=jnp.float32)
        total = term if total is None else total + term
    return total


class ExpandJob(Job):
    def __init__(self, normed, gate_full, up_full):
        rows, width = normed.shape[1], gate_full.shape[1]
        outs = [((rows, width), jnp.float32), ((rows, width), jnp.float32), ((rows, width), LOW)]
        super().__init__(
            [normed], [(gate_full, 1), (up_full, 1)], outs, width // self.wide, 4 * rows * gate_full.size
        )

    def compute(self, whole, tiles):
        gate_rows = blocks_dot(whole[0], tiles[0])
        up_rows = blocks_dot(whole[0], tiles[1])
        return gate_rows, up_rows, (gate_rows * jax.nn.sigmoid(gate_rows) * up_rows).astype(LOW)


class HiddenGradJob(Job):
    def __init__(self, cot, shrink_full, gate_rows, up_rows):
        rows, width = gate_rows.shape
        outs = [((rows, width), LOW), ((rows, width), LOW)]
        tiled = [(shrink_full, 1), (gate_rows, 1), (up_rows, 1)]
        super().__init__([cot], tiled, outs, width // self.wide, 2 * rows * shrink_full.size)

    def compute(self, whole, tiles):
        _, gate_rows, up_rows = tiles
        act_grad = blocks_dot(whole[0], tiles[0])
        sigmoid_gate = jax.nn.sigmoid(gate_rows)
        gate_grad = act_grad * up_rows * sigmoid_gate * (1.0 + gate_rows * (1.0 - sigmoid_gate))
        return gate_grad.astype(LOW), (act_grad * (gate_rows * sigmoid_gate)).astype(LOW)


class WidthJob(Job):
    def __init__(self, lefts, weights):
        rows, width = lefts[0].shape[0], weights[0].shape[0]
        flops = 2 * rows * sum(weight.size for weight in weights)
        self.own = width // lax.axis_size("tp")
        self.height = rows
        out = ((rows * lax.axis_size("tp"), self.own), LOW)
        super().__init__(lefts, [(weight, 0) for weight in weights], [out], width // self.wide, flops)

    def out_window(self, index):
        return owner_window(index, self.wide, self.own, self.height)

    def compute(self, whole, tiles):
        total = None
        for left, weight in zip(whole, tiles):
            term = contract_cols(left[...], weight)
            total = term if total is None else total + term
        return (total.astype(LOW),)


def owner_window(index, wide, own, height):
    each = own // wide
    rows = pl.ds(pl.multiple_of(index // each * height, 16), height)
    return rows, pl.ds(pl.multiple_of(index % each * wide, 128), wide)


class MixerJob:
    def __init__(self, inputs, outs, extra, phases, flops):
        self.inputs = list(inputs)
        self.out_shapes = [jax.ShapeDtypeStruct(shape, dtype) for shape, dtype in outs]
        self.phases = phases
        self.tiles = sum(phases)
        self.flops = flops
        self.scratch = (
            [pltpu.VMEM(array.shape, array.dtype) for array in self.inputs]
            + [pltpu.VMEM(shape, dtype) for shape, dtype in outs]
            + extra
            + [
                pltpu.SemaphoreType.DMA((len(self.inputs),)),
                pltpu.SemaphoreType.DMA((len(outs),)),
                pltpu.SemaphoreType.DMA((2,)),
            ]
        )

    def bind(self, ins, outs, scratch):
        self.in_refs, self.out_refs = ins, outs
        extra = len(scratch) - len(ins) - len(outs) - 3
        self.ins_v, self.outs_v, self.extra_v = split(scratch, [len(ins), len(outs), extra])
        self.in_sem, self.out_sem, self.pass_sem = scratch[-3:]
        self.count = lax.axis_size("seq")
        self.seq = lax.axis_index("seq")
        self.column = lax.axis_index("tp")

    def peers(self):
        after = (self.seq + 1) % self.count
        before = (self.seq + self.count - 1) % self.count
        return [(after, self.column), (before, self.column)]

    def load(self, which):
        return pltpu.make_async_copy(self.in_refs[which], self.ins_v[which], self.in_sem.at[which])

    def store(self, which):
        return pltpu.make_async_copy(self.outs_v[which], self.out_refs[which], self.out_sem.at[which])

    def passing(self, source, target, forward):
        step = 1 if forward else self.count - 1
        return pltpu.make_async_remote_copy(
            src_ref=source,
            dst_ref=target,
            send_sem=self.pass_sem.at[0],
            recv_sem=self.pass_sem.at[1],
            device_id=((self.seq + step) % self.count, self.column),
            device_id_type=MESH,
        )

    def start(self):
        for which in range(len(self.inputs)):
            self.load(which).start()

    def tile(self, index):
        begin = 0
        for phase, tiles in enumerate(self.phases):
            here = index - begin

            @pl.when((here >= 0) & (here < tiles))
            def _(phase=phase, here=here, tiles=tiles):
                @pl.when(here == 0)
                def _():
                    self.before(phase)

                self.work(phase, here)

                @pl.when(here == tiles - 1)
                def _():
                    self.after(phase)

            begin += tiles

    def finish(self):
        for which in range(len(self.out_shapes)):
            self.store(which).wait()


def visible(bound_row, shape):
    position = lax.broadcasted_iota(jnp.int32, shape, 0)
    see_one = position != bound_row
    return position, see_one, see_one & (position - 1 != bound_row)


def lagged(rows, halo, position):
    last, second = halo[15:16].astype(jnp.float32), halo[14:15].astype(jnp.float32)
    one = jnp.where(position == 0, last, pltpu.roll(rows, 1, 0))
    two = jnp.where(position == 0, second, jnp.where(position == 1, last, pltpu.roll(rows, 2, 0)))
    return one, two


class EntryJob(MixerJob):
    def __init__(self, tokens, gains, entry_full, exit_full, taps, bound):
        parts, rows, own = tokens.shape
        width, columns = exit_full.shape
        self.rows, self.columns, self.own = rows, columns, own
        self.width = width
        outs = [
            ((rows, 3 * columns), jnp.float32),
            ((rows, columns), jnp.float32),
            ((rows, columns), LOW),
            ((16, columns), LOW),
            ((rows, columns), LOW),
            ((parts * rows, own), LOW),
            ((rows, 128), jnp.float32),
            ((width, rows), LOW),
        ]
        phases = [rows // 256, 3 * columns // 256, 1, columns // 128, width // 256]
        flops = 2 * rows * (entry_full.size + exit_full.size)
        super().__init__([tokens, gains, entry_full, exit_full, taps, bound], outs, [], phases, flops)

    def halo(self):
        return self.passing(self.outs_v[2].at[pl.ds(self.rows - 16, 16)], self.outs_v[3], True)

    def before(self, phase):
        if phase == 0:
            for which in (0, 1):
                self.load(which).wait()
        if phase == 1:
            self.store(6).start()
            self.store(7).start()
            self.load(2).wait()
        if phase == 3:
            for which in (4, 5):
                self.load(which).wait()
            self.halo().wait_recv()
            self.store(3).start()
        if phase == 4:
            self.load(3).wait()

    def after(self, phase):
        if phase == 1:
            self.store(0).start()
        if phase == 2:
            self.halo().start()
            self.store(2).start()
        if phase == 3:
            self.store(1).start()
            self.store(4).start()
        if phase == 4:
            self.store(5).start()

    def finish(self):
        self.halo().wait_send()
        super().finish()

    def work(self, phase, index):
        tokens, gains, entry, exits, taps, bound = self.ins_v
        projected, conv, gated, halo, mixer, term, scales, turned_rows = self.outs_v
        columns = self.columns
        if phase == 0:
            rows = pl.ds(pl.multiple_of(index * 256, 256), 256)
            values = [tokens[part, rows, :].astype(jnp.float32) for part in range(tokens.shape[0])]
            total = sum(jnp.sum(value * value, axis=1, keepdims=True) for value in values)
            scale = lax.rsqrt(total / D + EPSILON)
            scales[rows, :] = jnp.broadcast_to(scale, (256, 128))
            for part, value in enumerate(values):
                normed = (value * scale * gains[part, 0:1, :]).astype(LOW)
                tokens[part, rows, :] = normed
                turned_rows[part * self.own : (part + 1) * self.own, rows] = normed.T
        if phase == 1:
            span = pl.ds(pl.multiple_of(index * 256, 256), 256)
            projected[:, span] = blocks_dot(tokens, entry[:, span])
        if phase == 2:
            gated[...] = (projected[:, :columns] * projected[:, 2 * columns :]).astype(LOW)
        if phase == 3:
            span = pl.ds(pl.multiple_of(index * 128, 128), 128)
            middle = pl.ds(pl.multiple_of(columns + index * 128, 128), 128)
            rows = gated[:, span].astype(jnp.float32)
            position, see_one, see_two = visible(bound[0:1, :], rows.shape)
            before = halo[:, span].astype(jnp.float32) * jnp.where(self.seq > 0, 1.0, 0.0)
            one, two = lagged(rows, before, position)
            total = (
                taps[2:3, span] * rows
                + taps[1:2, span] * jnp.where(see_one, one, 0.0)
                + taps[0:1, span] * jnp.where(see_two, two, 0.0)
            )
            conv[:, span] = total
            mixer[:, span] = (projected[:, middle] * total).astype(LOW)
        if phase == 4:
            features = pl.ds(pl.multiple_of(index * 256, 256), 256)
            window = owner_window(index, 256, self.own, self.rows)
            term[window] = contract_cols(mixer[...], exits[features, :]).astype(LOW)


class MixerGradJob(MixerJob):
    def __init__(self, branch, exit_full, entry_full, projected, conv, gated, halo, taps, bound):
        parts, rows, own = branch.shape
        width, columns = exit_full.shape
        self.rows, self.columns, self.own = rows, columns, own
        outs = [((rows, 3 * columns), LOW), ((parts * rows, own), LOW), ((8, columns), jnp.float32)]
        extra = [
            pltpu.VMEM((rows, columns), jnp.float32),
            pltpu.VMEM((8, columns), jnp.float32),
            pltpu.VMEM((8, columns), jnp.float32),
        ]
        phases = [columns // 256, 1, columns // 128, width // 256]
        flops = 2 * rows * (entry_full.size + exit_full.size)
        inputs = [branch, exit_full, entry_full, projected, conv, gated, halo, taps, bound]
        super().__init__(inputs, outs, extra, phases, flops)

    def back(self):
        return self.passing(self.extra_v[1], self.extra_v[2], False)

    def before(self, phase):
        if phase == 0:
            for which in (0, 1, 3, 4):
                self.load(which).wait()
        if phase == 1:
            for which in (7, 8):
                self.load(which).wait()
        if phase == 2:
            for which in (5, 6):
                self.load(which).wait()
            self.back().wait_recv()
        if phase == 3:
            self.load(2).wait()

    def after(self, phase):
        if phase == 1:
            self.back().start()
        if phase == 2:
            self.store(0).start()
            self.store(2).start()
        if phase == 3:
            self.store(1).start()

    def finish(self):
        self.back().wait_send()
        super().finish()

    def work(self, phase, index):
        branch, exits, entry, projected, conv, gated, halo, taps, bound = self.ins_v
        grads, term, taps_grad = self.outs_v
        conv_grad, sent, returned = self.extra_v
        columns, height = self.columns, self.rows
        if phase == 0:
            span = pl.ds(pl.multiple_of(index * 256, 256), 256)
            middle = pl.ds(pl.multiple_of(columns + index * 256, 256), 256)
            mixer_grad = blocks_dot(branch, exits[:, span])
            grads[:, middle] = (mixer_grad * conv[:, span]).astype(LOW)
            conv_grad[:, span] = mixer_grad * projected[:, middle]
        if phase == 1:
            for start in range(0, columns, 128):
                span = slice(start, start + 128)
                rows = conv_grad[0:8, span]
                position, see_one, see_two = visible(bound[0:1, :], rows.shape)
                one = pltpu.roll(jnp.where(see_one, rows, 0.0) * taps[1:2, span], 1, 0)
                two = jnp.where(see_two, rows, 0.0) * taps[0:1, span]
                sent[:, span] = two + jnp.where(position == 0, 0.0, one)
            taps_grad[...] = jnp.zeros_like(taps_grad)
        if phase == 2:
            span = pl.ds(pl.multiple_of(index * 128, 128), 128)
            last = pl.ds(pl.multiple_of(2 * columns + index * 128, 128), 128)
            rows = conv_grad[:, span]
            position, see_one, see_two = visible(bound[0:1, :], rows.shape)
            seen_one, seen_two = jnp.where(see_one, rows, 0.0), jnp.where(see_two, rows, 0.0)
            one = pltpu.roll(seen_one * taps[1:2, span], height - 1, 0)
            two = pltpu.roll(seen_two * taps[0:1, span], height - 2, 0)
            after = returned[:, span] * jnp.where(self.seq < self.count - 1, 1.0, 0.0)
            gated_grad = (
                rows * taps[2:3, span]
                + jnp.where(position == height - 1, after[1:2], one)
                + jnp.where(position < height - 2, two, jnp.where(position == height - 2, after[0:1], 0.0))
            )
            grads[:, span] = (gated_grad * projected[:, last]).astype(LOW)
            grads[:, last] = (gated_grad * projected[:, span]).astype(LOW)
            own_rows = gated[:, span].astype(jnp.float32)
            before = halo[:, span].astype(jnp.float32) * jnp.where(self.seq > 0, 1.0, 0.0)
            lag_one, lag_two = lagged(own_rows, before, position)
            taps_grad[0:1, span] = jnp.sum(seen_two * lag_two, axis=0, keepdims=True)
            taps_grad[1:2, span] = jnp.sum(seen_one * lag_one, axis=0, keepdims=True)
            taps_grad[2:3, span] = jnp.sum(rows * own_rows, axis=0, keepdims=True)
        if phase == 3:
            features = pl.ds(pl.multiple_of(index * 256, 256), 256)
            window = owner_window(index, 256, self.own, height)
            term[window] = contract_cols(grads[...], entry[features, :]).astype(LOW)


class SmallSumJob:
    tiles, flops = 0, 0

    def __init__(self, blocks):
        count = lax.axis_size("seq")
        self.inputs = [blocks]
        self.out_shapes = [jax.ShapeDtypeStruct(blocks.shape[1:], blocks.dtype)]
        self.scratch = [
            pltpu.VMEM(blocks.shape, blocks.dtype),
            pltpu.VMEM(blocks.shape, blocks.dtype),
            pltpu.VMEM(blocks.shape[1:], blocks.dtype),
            pltpu.SemaphoreType.DMA((2,)),
            pltpu.SemaphoreType.DMA((count,)),
            pltpu.SemaphoreType.DMA((count,)),
        ]

    def bind(self, ins, outs, scratch):
        self.source, self.target = ins[0], outs[0]
        self.own, self.slots, self.total, self.local_sem, self.send_sem, self.recv_sem = scratch
        self.count = lax.axis_size("seq")
        self.seq = lax.axis_index("seq")
        self.column = lax.axis_index("tp")

    def peers(self):
        return [((self.seq + far) % self.count, self.column) for far in range(1, self.count)]

    def copy(self, far):
        other = (self.seq + far) % self.count
        return pltpu.make_async_remote_copy(
            src_ref=self.own.at[other],
            dst_ref=self.slots.at[far],
            send_sem=self.send_sem.at[far],
            recv_sem=self.recv_sem.at[far],
            device_id=(other, self.column),
            device_id_type=MESH,
        )

    def start(self):
        load = pltpu.make_async_copy(self.source, self.own, self.local_sem.at[0])
        load.start()
        load.wait()

        def begin(far, carry):
            self.copy(far).start()
            return carry

        lax.fori_loop(1, self.count, begin, 0)

    def finish(self):
        self.total[...] = self.own[self.seq]

        def add(far, carry):
            self.copy(far).wait_recv()
            self.total[...] += self.slots[far]
            return carry

        lax.fori_loop(1, self.count, add, 0)
        store = pltpu.make_async_copy(self.total, self.target, self.local_sem.at[1])
        store.start()

        def sent(far, carry):
            self.copy(far).wait_send()
            return carry

        lax.fori_loop(1, self.count, sent, 0)
        store.wait()


def ring_kernel(ring, job, *refs):
    sizes = [len(group) for group in (ring.inputs, job.inputs, ring.out_shapes, job.out_shapes, ring.scratch, job.scratch)]
    ring_in, job_in, ring_out, job_out, ring_scratch, job_scratch = split(refs, sizes)
    ring.bind(ring_in, ring_out, ring_scratch)
    job.bind(job_in, job_out, job_scratch)
    ring.prepare()
    greet(ring.peers() + job.peers())
    ring.start()
    job.start()
    each = -(-job.tiles // ring.ticks)

    def step(index, carry):
        for inner in range(each):
            tile = index * each + inner

            @pl.when(tile < job.tiles)
            def _(tile=tile):
                job.tile(tile)

        ring.tick(index)
        return carry

    lax.fori_loop(0, ring.ticks, step, 0)
    ring.finish()
    job.finish()


def run_ring(ring, job, collective):
    inputs = ring.inputs + job.inputs
    outs = ring.out_shapes + job.out_shapes
    return pl.pallas_call(
        functools.partial(ring_kernel, ring, job),
        out_shape=outs,
        in_specs=[pl.BlockSpec(memory_space=pl.ANY)] * len(inputs),
        out_specs=[pl.BlockSpec(memory_space=pl.ANY)] * len(outs),
        scratch_shapes=ring.scratch + job.scratch,
        compiler_params=pltpu.CompilerParams(
            collective_id=collective, has_side_effects=True, vmem_limit_bytes=VMEM_BYTES
        ),
        cost_estimate=pl.CostEstimate(flops=ring.flops + job.flops, bytes_accessed=ring.bytes, transcendentals=0),
        name=ring.name,
    )(*inputs)


def flat(full):
    return full.reshape(full.shape[0] * full.shape[1], full.shape[2])


def contract_rows(left, right):
    return lax.dot_general(
        left, right, (((0,), (0,)), ((), ())), preferred_element_type=jnp.float32
    )


def contract_cols(left, right):
    return lax.dot_general(
        left, right, (((1,), (1,)), ((), ())), preferred_element_type=jnp.float32
    )


def tie(*values):
    return lax.optimization_barrier(values)


def gather_rows(own):
    return lax.all_gather(own, "tp", axis=0, tiled=True)


def turned(own):
    return with_layout_constraint(own.T, Layout(major_to_minor=(0, 1)))


def gather_blocks(own):
    return gather_rows(own).reshape(-1, *own.shape)


def reduce_branch(term):
    return lax.psum_scatter(term, "tp", scatter_dimension=0, tiled=True).astype(jnp.float32)


def share_small(own):
    count = lax.axis_size("tp")
    pieces = [own] + [
        lax.ppermute(own, "tp", [(i, (i + far) % count) for i in range(count)]) for far in range(1, count)
    ]
    place = lax.axis_index("tp")
    return jnp.stack([lax.dynamic_index_in_dim(jnp.stack(pieces), (place - part) % count, 0, False) for part in range(count)])


def norm_forward(values, gain_row):
    row_total = lax.psum(jnp.sum(values * values, axis=1, keepdims=True), "tp")
    row_scale = lax.rsqrt(row_total / D + EPSILON)
    return (values * row_scale * gain_row).astype(LOW), row_scale


def norm_backward(grad_normed, kept_rows, row_scale, kept_gain):
    inner_sum = lax.psum(jnp.sum(grad_normed * kept_gain * kept_rows, axis=1, keepdims=True), "tp")
    rows_grad = row_scale * kept_gain * grad_normed - kept_rows * row_scale**3 * inner_sum / D
    return (rows_grad, jnp.sum(grad_normed * kept_rows * row_scale, axis=0))


def adam_update(weight, first, second, grad, rate, decay):
    first_next = BETA_ONE * first + (1.0 - BETA_ONE) * grad
    second_next = BETA_TWO * second + (1.0 - BETA_TWO) * grad * grad
    corrected = first_next / (1.0 - BETA_ONE**STEP)
    spread = jnp.sqrt(second_next / (1.0 - BETA_TWO**STEP)) + ADAM_EPSILON
    return (weight - rate * (corrected / spread + decay * weight), first_next, second_next)


def adam_kernel(pieces, *refs):
    weight, first, second = refs[:3]
    grads, outs = refs[3 : 3 + pieces], refs[3 + pieces :]
    start = 0
    for grad in grads:
        span = slice(start, start + grad.shape[1])
        start += grad.shape[1]
        results = adam_update(weight[:, span], first[:, span], second[:, span], grad[...], RATE_WIDE, WEIGHT_DECAY)
        for out, result in zip(outs, results):
            out[:, span] = result


def adam_rows(weight, first, second, grads, planes=1):
    rows, columns = weight.shape[0] // planes, weight.shape[1]
    block = max(rows // 8, 8) if columns > 1024 else max(rows // 2, 8)
    steps = rows // block
    state = pl.BlockSpec((block, columns), lambda plane, step: (plane * steps + step, 0))
    grad_specs = [
        pl.BlockSpec((block, grad.shape[1] // planes), lambda plane, step: (step, plane)) for grad in grads
    ]
    return pl.pallas_call(
        functools.partial(adam_kernel, len(grads)),
        out_shape=[jax.ShapeDtypeStruct(weight.shape, weight.dtype)] * 3,
        grid=(planes, steps),
        in_specs=[state] * 3 + grad_specs,
        out_specs=[state] * 3,
        cost_estimate=pl.CostEstimate(flops=20 * weight.size, bytes_accessed=28 * weight.size, transcendentals=0),
        name="adam_rows",
    )(weight, first, second, *grads)


def adam_pairs_kernel(lanes, *refs):
    weight, first, second = refs[:3]
    grads, outs, mixed = refs[3:7], refs[7:10], refs[10]
    rows = grads[0].shape[0]
    tiles = grads[0].shape[1] // lanes
    for which, grad in enumerate(grads):
        half, side = which // 2, which % 2
        for tile in range(tiles):
            place = (half * tiles + tile) * 2 + side
            mixed[pl.ds(place, rows, stride=4 * tiles), :] = grad[:, tile * lanes : (tile + 1) * lanes]
    results = adam_update(weight[...], first[...], second[...], mixed[...], RATE_WIDE, WEIGHT_DECAY)
    for out, result in zip(outs, results):
        out[...] = result


def adam_pairs(weight, first, second, grads):
    rows, _, columns = weight.shape
    lanes = 128
    deep = columns // lanes

    def seen(array):
        return array.reshape(rows, 2, deep, lanes).transpose(0, 2, 1, 3).reshape(rows * deep * 2, lanes)

    block = max(rows // 8, 8)
    state = pl.BlockSpec((block * deep * 2, lanes), lambda step: (step, 0))
    results = pl.pallas_call(
        functools.partial(adam_pairs_kernel, lanes),
        out_shape=[jax.ShapeDtypeStruct((rows * deep * 2, lanes), weight.dtype)] * 3,
        grid=(rows // block,),
        in_specs=[state] * 3 + [pl.BlockSpec((block, columns // 2), lambda step: (step, 0))] * 4,
        out_specs=[state] * 3,
        scratch_shapes=[pltpu.VMEM((block * deep * 2, lanes), jnp.float32)],
        cost_estimate=pl.CostEstimate(flops=20 * weight.size, bytes_accessed=28 * weight.size, transcendentals=0),
        name="adam_pairs",
    )(seen(weight), seen(first), seen(second), *grads)
    return [
        result.reshape(rows, deep, 2, lanes).transpose(0, 2, 1, 3).reshape(rows, 2, columns) for result in results
    ]


def adam_planes(weight, first, second, grad):
    rows, planes, columns = weight.shape

    def seen(array):
        return array.transpose(1, 0, 2).reshape(planes * rows, columns)

    results = adam_rows(seen(weight), seen(first), seen(second), [grad], planes)
    return [result.reshape(planes, rows, columns).transpose(1, 0, 2) for result in results]


def shards(
    tokens,
    bounds,
    cotangent,
    entry_weight,
    entry_first,
    entry_second,
    exit_weight,
    exit_first,
    exit_second,
    expand_weight,
    expand_first,
    expand_second,
    shrink_weight,
    shrink_first,
    shrink_second,
    conv_kernel,
    conv_first,
    conv_second,
    norm_gains,
    gain_first,
    gain_second,
):
    rows_dev = tokens.shape[0]
    channels = tokens.shape[1]
    count = lax.axis_size("seq")
    small = jnp.concatenate([conv_kernel, norm_gains], axis=0)
    small = jnp.pad(small, ((0, 64 - small.shape[0]), (0, 128 - small.shape[1]))).astype(LOW)
    entry_low = entry_weight.reshape(entry_weight.shape[0], 3 * channels).astype(LOW)
    hidden_half = shrink_weight.shape[1] // 2
    halves = (slice(0, hidden_half), slice(hidden_half, 2 * hidden_half))
    gate_low = [expand_weight[:, 0, half].astype(LOW) for half in halves]
    up_low = [expand_weight[:, 1, half].astype(LOW) for half in halves]
    shrink_low = [shrink_weight[:, half].astype(LOW) for half in halves]
    gate_full, up_full, shrink_full = [None] * 2, [None] * 2, [None] * 2
    gate_rows, up_rows, activation = [None] * 2, [None] * 2, [None] * 2
    gate_grad, up_grad = [None] * 2, [None] * 2
    shrink_part, gate_part, up_part = [None] * 2, [None] * 2, [None] * 2
    idle = NoJob()

    tokens_f = tokens.astype(jnp.float32)
    bound = jnp.broadcast_to(bounds[0], (8, 128))

    tokens_blocks = gather_blocks(tokens)
    exit_full, small_full = run_ring(GatherRing([exit_weight.astype(LOW), small]), idle, 0)
    small_full = small_full.reshape(count, 64, 128)[:, :8, : conv_kernel.shape[1]]
    small_full = small_full.swapaxes(0, 1).reshape(8, channels).astype(jnp.float32)
    taps = small_full
    gains_row = small_full[3:5]
    gain_blocks = share_small(jnp.broadcast_to(gains_row[0:1], (8, channels)))
    entry_low, small_full = tie(entry_low, small_full)
    (entry_full,) = run_ring(GatherRing([entry_low]), idle, 14)
    entry_full, exit_full = flat(entry_full), flat(exit_full)
    tokens_blocks, entry_full, gain_blocks = tie(tokens_blocks, entry_full, gain_blocks)
    cot_own, cotangent_rows, gate_low[0], entry_full = tie(turned(cotangent), cotangent, gate_low[0], entry_full)
    full, projected, conv_out, gated_rows, halo, mixer_rows, branch_term, scales, normed_one = run_ring(
        GatherRing([gate_low[0]]), EntryJob(tokens_blocks, gain_blocks, entry_full, exit_full, taps, bound), 1
    )
    scale_one = scales[:, :1]
    gate_full[0] = flat(full)
    branch_term, up_low[0] = tie(branch_term, up_low[0])
    (full,) = run_ring(GatherRing([up_low[0]]), idle, 2)
    branch, up_full[0] = tie(reduce_branch(branch_term), flat(full))
    residual = tokens_f + branch
    own_normed_two, scale_two = norm_forward(residual, gains_row[1])
    own_normed_two = with_layout_constraint(own_normed_two, Layout(major_to_minor=(0, 1)))
    own_normed_two, gate_low[1] = tie(own_normed_two, gate_low[1])
    (full,) = run_ring(GatherRing([gate_low[1]]), idle, 3)
    normed_blocks, gate_full[1] = tie(gather_blocks(own_normed_two), flat(full))
    own_normed_two, up_low[1] = tie(turned(own_normed_two), up_low[1])
    full, gate_rows[0], up_rows[0], activation[0] = run_ring(
        GatherRing([up_low[1]]), ExpandJob(normed_blocks, gate_full[0], up_full[0]), 4
    )
    normed_two, up_full[1] = tie(gather_rows(own_normed_two), flat(full))
    cotangent_rows, shrink_low[0], normed_two = tie(cotangent_rows, shrink_low[0], normed_two)
    full, gate_rows[1], up_rows[1], activation[1] = run_ring(
        GatherRing([shrink_low[0]]), ExpandJob(normed_blocks, gate_full[1], up_full[1]), 5
    )
    cot_blocks, shrink_full[0] = tie(gather_blocks(cotangent_rows), flat(full))
    cot_own, shrink_low[1], cot_blocks = tie(cot_own, shrink_low[1], cot_blocks)
    full, gate_grad[0], up_grad[0] = run_ring(
        GatherRing([shrink_low[1]]), HiddenGradJob(cot_blocks, shrink_full[0], gate_rows[0], up_rows[0]), 6
    )
    cot_full, shrink_full[1] = tie(gather_rows(cot_own), flat(full))
    shrink_part[0], gate_grad[1], up_grad[1] = run_ring(
        ScatterRing([(cot_full, activation[0])]),
        HiddenGradJob(cot_blocks, shrink_full[1], gate_rows[1], up_rows[1]),
        7,
    )
    shrink_part[1], two_term = run_ring(
        ScatterRing([(cot_full, activation[1])]), WidthJob(gate_grad + up_grad, gate_full + up_full), 8
    )
    two_term, gate_grad[0] = tie(two_term, gate_grad[0])
    gate_part[0], mixed_term = run_ring(
        ScatterRing([(normed_two, gate_grad[0])]), WidthJob(activation, shrink_full), 9
    )
    grad_normed_two, gate_part[0], mixed_term = tie(reduce_branch(two_term), gate_part[0], mixed_term)
    residual_norm_grad, gain_two_grad = norm_backward(grad_normed_two, residual, scale_two, gains_row[1])
    residual_grad = cotangent.astype(jnp.float32) + residual_norm_grad
    branch_own = with_layout_constraint(residual_grad.astype(LOW), Layout(major_to_minor=(0, 1)))
    branch_own, up_grad[0] = tie(branch_own, up_grad[0])
    (up_part[0],) = run_ring(ScatterRing([(normed_two, up_grad[0])]), idle, 10)
    branch_blocks, up_part[0] = tie(gather_blocks(branch_own), up_part[0])
    branch_own, mixed_term, gate_grad[1], branch_blocks = tie(
        turned(branch_own), mixed_term, gate_grad[1], branch_blocks
    )
    gate_part[1], projected_grad, one_term, taps_grad = run_ring(
        ScatterRing([(normed_two, gate_grad[1])]),
        MixerGradJob(branch_blocks, exit_full, entry_full, projected, conv_out, gated_rows, halo, taps, bound),
        11,
    )
    mixed_branch, gate_part[1], branch_full = tie(reduce_branch(mixed_term), gate_part[1], gather_rows(branch_own))
    mixed = (residual + mixed_branch).astype(LOW)
    one_term, up_grad[1], mixed_branch = tie(one_term, up_grad[1], mixed_branch)
    (up_part[1],) = run_ring(ScatterRing([(normed_two, up_grad[1])]), idle, 12)
    grad_normed_one, up_part[1] = tie(reduce_branch(one_term), up_part[1])
    tokens_norm_grad, gain_one_grad = norm_backward(grad_normed_one, tokens_f, scale_one, gains_row[0])
    tokens_grad = residual_grad + tokens_norm_grad
    small_grad = jnp.concatenate([taps_grad[:3], gain_one_grad[None], gain_two_grad[None]], axis=0)
    small_blocks = small_grad.reshape(5, count, conv_kernel.shape[1]).swapaxes(0, 1)
    small_blocks = jnp.pad(small_blocks, ((0, 0), (0, 3), (0, 128 - conv_kernel.shape[1])))
    entry_part, exit_part, small_part = run_ring(
        ScatterRing([(normed_one, projected_grad), (branch_full, mixer_rows)]), SmallSumJob(small_blocks), 13
    )
    kernel_part = small_part[:3, : conv_kernel.shape[1]]
    gains_part = small_part[3:5, : conv_kernel.shape[1]]
    entry_next, entry_first_next, entry_second_next = adam_planes(
        entry_weight, entry_first, entry_second, entry_part
    )
    exit_next, exit_first_next, exit_second_next = adam_rows(exit_weight, exit_first, exit_second, [exit_part])
    expand_next, expand_first_next, expand_second_next = adam_pairs(
        expand_weight, expand_first, expand_second, [gate_part[0], up_part[0], gate_part[1], up_part[1]]
    )
    shrink_next, shrink_first_next, shrink_second_next = adam_rows(
        shrink_weight, shrink_first, shrink_second, shrink_part
    )
    conv_next, conv_first_next, conv_second_next = adam_update(
        conv_kernel, conv_first, conv_second, kernel_part, RATE_CONV, 0.0
    )
    gains_next, gains_first_next, gains_second_next = adam_update(
        norm_gains, gain_first, gain_second, gains_part, RATE_GAIN, 0.0
    )
    return (
        mixed,
        tokens_grad,
        entry_next,
        entry_first_next,
        entry_second_next,
        exit_next,
        exit_first_next,
        exit_second_next,
        expand_next,
        expand_first_next,
        expand_second_next,
        shrink_next,
        shrink_first_next,
        shrink_second_next,
        conv_next,
        conv_first_next,
        conv_second_next,
        gains_next,
        gains_first_next,
        gains_second_next,
    )


def solution(mesh):
    rows = P("seq", "tp")
    stacked = P("seq", None, "tp")
    small = P(None, ("tp", "seq"))
    return jax.shard_map(
        shards,
        mesh=mesh,
        in_specs=(rows, P("seq"), rows) + (stacked,) * 3 + (rows,) * 3 + (stacked,) * 3 + (rows,) * 3 + (small,) * 6,
        out_specs=(rows, rows) + (stacked,) * 3 + (rows,) * 3 + (stacked,) * 3 + (rows,) * 3 + (small,) * 6,
        check_vma=False,
    )
```

```python
import functools

import jax
import jax.numpy as jnp
from jax import lax
from jax.experimental import pallas as pl
from jax.experimental.pallas import tpu as pltpu
from jax.sharding import PartitionSpec as P

D = 2048
STEP = 10


EPSILON = 1e-05
BETA_ONE = 0.9
BETA_TWO = 0.95
ADAM_EPSILON = 1e-08
WEIGHT_DECAY = 0.1
RATE_WIDE = 0.04
RATE_CONV = 0.5
RATE_GAIN = 0.4

MESH = pl.DeviceIdType.MESH
LOW = jnp.bfloat16
LANES = 128
VMEM_BYTES = 60 * 1024 * 1024


def ring_place(index, count):
    side = index % 2
    level = index // 2
    return level * (1 - side) + (count - 1 - level) * side


def ring_index(place, count):
    back = place // (count // 2)
    return (1 - back) * (2 * place) + back * (2 * (count - 1 - place) + 1)


def ring_ends(count):
    place = ring_place(lax.axis_index("seq"), count)
    ahead = ring_index((place + 1) % count, count)
    behind = ring_index((place + count - 1) % count, count)
    return place, ahead, behind


def greet(peers):
    barrier = pltpu.get_barrier_semaphore()
    for peer in peers:
        pl.semaphore_signal(barrier, inc=1, device_id=peer, device_id_type=MESH)
    pl.semaphore_wait(barrier, len(peers))


def split(items, sizes):
    parts, start = [], 0
    for size in sizes:
        parts.append(items[start : start + size])
        start += size
    return parts


class GatherRing:
    name = "ring_gather"

    def __init__(self, shards):
        self.count = lax.axis_size("seq")
        self.inputs = list(shards)
        self.arrays = len(shards)
        self.rows = [shard.shape[0] for shard in shards]
        self.parts = 2 if min(self.rows) % 64 == 0 else 1
        self.ticks = (self.count - 2) * self.parts
        self.out_shapes = [jax.ShapeDtypeStruct((self.count,) + shard.shape, shard.dtype) for shard in shards]
        sems = pltpu.SemaphoreType.DMA((self.arrays, 2, self.parts, self.count - 1))
        self.scratch = [sems, sems, pltpu.SemaphoreType.DMA((self.arrays,))]
        self.flops = 0
        self.bytes = 20 * sum(shard.size for shard in shards) * 2 * self.count

    def bind(self, ins, outs, scratch):
        self.shard_refs, self.full_refs = ins, outs
        self.send_sem, self.recv_sem, self.own_sem = scratch
        self.column = lax.axis_index("tp")
        self.place, self.ahead, self.behind = ring_ends(self.count)

    def pieces(self):
        return [(array, way) for array in range(self.arrays) for way in range(2)]

    def copy(self, array, way, part, step, first=False):
        move = (self.place + self.count - step) if way == 0 else (self.place + step)
        owner = ring_index(move % self.count, self.count)
        size = self.rows[array] // 2 // self.parts
        rows = pl.ds(pl.multiple_of(way * (self.rows[array] // 2) + part * size, 16), size)
        there = self.full_refs[array].at[owner, rows]
        return pltpu.make_async_remote_copy(
            src_ref=self.shard_refs[array].at[rows] if first else there,
            dst_ref=there,
            send_sem=self.send_sem.at[array, way, part, step],
            recv_sem=self.recv_sem.at[array, way, part, step],
            device_id=(self.ahead if way == 0 else self.behind, self.column),
            device_id_type=MESH,
        )

    def own(self, array):
        there = self.full_refs[array].at[lax.axis_index("seq")]
        return pltpu.make_async_copy(self.shard_refs[array], there, self.own_sem.at[array])

    def peers(self):
        return [(self.ahead, self.column), (self.behind, self.column)]

    def prepare(self):
        pass

    def start(self):
        for part in range(self.parts):
            for array, way in self.pieces():
                self.copy(array, way, part, 0, True).start()
        for array in range(self.arrays):
            self.own(array).start()

    def tick(self, index):
        step, part = 1 + index // self.parts, index % self.parts
        for array, way in self.pieces():
            self.copy(array, way, part, step - 1).wait_recv()
            self.copy(array, way, part, step).start()

    def finish(self):
        for part in range(self.parts):
            for array, way in self.pieces():
                self.copy(array, way, part, self.count - 2).wait_recv()

        def sent(step, carry):
            for part in range(self.parts):
                for array, way in self.pieces():
                    self.copy(array, way, part, step).wait_send()
            return carry

        lax.fori_loop(0, self.count - 1, sent, 0)
        for array in range(self.arrays):
            self.own(array).wait()


class ScatterRing:
    name = "ring_scatter"

    def __init__(self, pairs):
        self.count = count = lax.axis_size("seq")
        lefts = [left for left, right in pairs]
        rights = [right for left, right in pairs]
        self.inputs = lefts + rights
        self.arrays = len(pairs)
        self.rows = [left.shape[0] // count for left in lefts]
        self.columns = [right.shape[1] for right in rights]
        self.parts = 2 if min(self.columns) % 512 == 0 else 1
        self.ticks = (count - 2) * self.parts
        self.out_shapes = [
            jax.ShapeDtypeStruct((row, width), jnp.float32) for row, width in zip(self.rows, self.columns)
        ]
        sems = pltpu.SemaphoreType.DMA((self.arrays, 2, self.parts, count - 1))
        self.scratch = (
            [pltpu.VMEM(left.shape, left.dtype) for left in lefts]
            + [pltpu.VMEM(right.shape, right.dtype) for right in rights]
            + [pltpu.VMEM((2, count, row, width // 2), LOW) for row, width in zip(self.rows, self.columns)]
            + [pltpu.VMEM((row, width), jnp.float32) for row, width in zip(self.rows, self.columns)]
            + [sems, sems, pltpu.SemaphoreType.DMA((self.arrays, count + 1)), pltpu.SemaphoreType.DMA((self.arrays,))]
        )
        self.flops = sum(2 * left.size * width for left, width in zip(lefts, self.columns))
        self.bytes = 20 * sum(left.shape[0] * width * 2 for left, width in zip(lefts, self.columns))

    def bind(self, ins, outs, scratch):
        arrays = self.arrays
        self.in_refs, self.out_refs = ins, outs
        self.lefts, self.rights, self.slots, self.finals = split(scratch, [arrays] * 4)
        self.send_sem, self.recv_sem, self.load_sem, self.done_sem = scratch[4 * arrays :]
        self.column = lax.axis_index("tp")
        self.place, self.ahead, self.behind = ring_ends(self.count)

    def pieces(self):
        return [(array, way) for array in range(self.arrays) for way in range(2)]

    def span(self, array, way, part):
        half = self.columns[array] // 2
        width = half // self.parts
        inner = part * width
        return way * half + inner, inner, width

    def term(self, array, way, part, step):
        move = (self.place + 2 * self.count - 1 - step) if way == 0 else (self.place + 1 + step)
        owner = ring_index(move % self.count, self.count)
        rows = self.rows[array]
        start, _, width = self.span(array, way, part)
        left = self.lefts[array][pl.ds(pl.multiple_of(owner * rows, 16), rows), :]
        right = self.rights[array][:, pl.ds(pl.multiple_of(start, 128), width)]
        return jnp.dot(left, right, preferred_element_type=jnp.float32)

    def held(self, array, way, part, step):
        _, inner, width = self.span(array, way, part)
        return self.slots[array].at[way, step, :, pl.ds(pl.multiple_of(inner, 128), width)]

    def copy(self, array, way, part, step):
        return pltpu.make_async_remote_copy(
            src_ref=self.held(array, way, part, step),
            dst_ref=self.held(array, way, part, step + 1),
            send_sem=self.send_sem.at[array, way, part, step],
            recv_sem=self.recv_sem.at[array, way, part, step],
            device_id=(self.ahead if way == 0 else self.behind, self.column),
            device_id_type=MESH,
        )

    def right_load(self, array):
        return pltpu.make_async_copy(
            self.in_refs[array + self.arrays], self.rights[array], self.load_sem.at[array, self.count]
        )

    def left_load(self, array, step):
        owner = ring_index((self.place + 2 * self.count - 1 - step) % self.count, self.count)
        rows = pl.ds(pl.multiple_of(owner * self.rows[array], 16), self.rows[array])
        return pltpu.make_async_copy(
            self.in_refs[array].at[rows], self.lefts[array].at[rows], self.load_sem.at[array, step]
        )

    def peers(self):
        return [(self.ahead, self.column), (self.behind, self.column)]

    def prepare(self):
        for array in range(self.arrays):
            self.right_load(array).start()
            for step in (0, self.count - 2):
                self.left_load(array, step).start()

    def start(self):
        later = list(range(1, self.count - 2)) + [self.count - 1]
        for array in range(self.arrays):
            for step in later:
                self.left_load(array, step).start()
        for array in range(self.arrays):
            self.right_load(array).wait()
            for step in (0, self.count - 2):
                self.left_load(array, step).wait()
            for part in range(self.parts):
                for way in range(2):
                    self.held(array, way, part, 0)[...] = self.term(array, way, part, 0).astype(LOW)
                    self.copy(array, way, part, 0).start()
        for array in range(self.arrays):
            for step in later:
                self.left_load(array, step).wait()

    def tick(self, index):
        step, part = 1 + index // self.parts, index % self.parts
        for array, way in self.pieces():
            mine = self.term(array, way, part, step)
            self.copy(array, way, part, step - 1).wait_recv()
            held = self.held(array, way, part, step)
            held[...] = (held[...].astype(jnp.float32) + mine).astype(LOW)
            self.copy(array, way, part, step).start()

    def finish(self):
        last = self.count - 1
        for part in range(self.parts):
            for array, way in self.pieces():
                start, _, width = self.span(array, way, part)
                mine = self.term(array, way, part, last)
                self.copy(array, way, part, last - 1).wait_recv()
                self.finals[array][:, start : start + width] = (
                    self.held(array, way, part, last)[...].astype(jnp.float32) + mine
                )
        stores = [
            pltpu.make_async_copy(self.finals[array], self.out_refs[array], self.done_sem.at[array])
            for array in range(self.arrays)
        ]
        for store in stores:
            store.start()

        def sent(step, carry):
            for part in range(self.parts):
                for array, way in self.pieces():
                    self.copy(array, way, part, step).wait_send()
            return carry

        lax.fori_loop(0, last, sent, 0)
        for store in stores:
            store.wait()


class NoJob:
    inputs, out_shapes, scratch, tiles, flops = [], [], [], 0, 0

    def bind(self, ins, outs, scratch):
        pass

    def peers(self):
        return []

    def start(self):
        pass

    def finish(self):
        pass


class Job:
    wide = 256

    def __init__(self, whole, tiled, outs, tiles, flops):
        self.whole, self.tiled = whole, tiled
        self.inputs = list(whole) + [array for array, axis in tiled]
        self.axes = [axis for array, axis in tiled]
        self.out_shapes = [jax.ShapeDtypeStruct(shape, dtype) for shape, dtype in outs]
        self.tiles = tiles
        self.flops = flops
        self.scratch = (
            [pltpu.VMEM(array.shape, array.dtype) for array in self.inputs]
            + [pltpu.VMEM(shape, dtype) for shape, dtype in outs]
            + [
                pltpu.SemaphoreType.DMA((len(whole),)),
                pltpu.SemaphoreType.DMA((len(tiled), tiles)),
                pltpu.SemaphoreType.DMA((len(outs), tiles)),
            ]
        )

    def bind(self, ins, outs, scratch):
        self.in_refs, self.out_refs = ins, outs
        sizes = [len(self.whole), len(self.tiled), len(outs)]
        self.whole_v, self.tiled_v, self.outs_v = split(scratch, sizes)
        self.whole_sem, self.tiled_sem, self.out_sem = scratch[sum(sizes) :]

    def peers(self):
        return []

    def window(self, axis, index):
        span = pl.ds(pl.multiple_of(index * self.wide, 128), self.wide)
        return (span,) if axis == 0 else (slice(None), span)

    def whole_load(self, which):
        return pltpu.make_async_copy(self.in_refs[which], self.whole_v[which], self.whole_sem.at[which])

    def tiled_load(self, which, index):
        window = self.window(self.axes[which], index)
        there = self.in_refs[len(self.whole) + which].at[window]
        return pltpu.make_async_copy(there, self.tiled_v[which].at[window], self.tiled_sem.at[which, index])

    def out_window(self, index):
        return self.window(1, index)

    def store(self, which, index):
        window = self.out_window(index)
        return pltpu.make_async_copy(
            self.outs_v[which].at[window], self.out_refs[which].at[window], self.out_sem.at[which, index]
        )

    def start(self):
        for which in range(len(self.whole)):
            self.whole_load(which).start()

        def begin(index, carry):
            for which in range(len(self.tiled)):
                self.tiled_load(which, index).start()
            return carry

        lax.fori_loop(0, self.tiles, begin, 0)

    def tile(self, index):
        @pl.when(index == 0)
        def _():
            for which in range(len(self.whole)):
                self.whole_load(which).wait()

        for which in range(len(self.tiled)):
            self.tiled_load(which, index).wait()
        tiles = [ref[self.window(axis, index)] for ref, axis in zip(self.tiled_v, self.axes)]
        for which, value in enumerate(self.compute(self.whole_v, tiles)):
            self.outs_v[which][self.out_window(index)] = value
            self.store(which, index).start()

    def finish(self):
        def end(index, carry):
            for which in range(len(self.outs_v)):
                self.store(which, index).wait()
            return carry

        lax.fori_loop(0, self.tiles, end, 0)


def blocks_dot(blocks, weight):
    parts, _, depth = blocks.shape
    total = None
    for part in range(parts):
        term = jnp.dot(blocks[part], weight[part * depth : (part + 1) * depth], preferred_element_type=jnp.float32)
        total = term if total is None else total + term
    return total


class ExpandJob(Job):
    def __init__(self, normed, gate_full, up_full):
        rows, width = normed.shape[1], gate_full.shape[1]
        outs = [((rows, width), jnp.float32), ((rows, width), jnp.float32), ((rows, width), LOW)]
        super().__init__(
            [normed], [(gate_full, 1), (up_full, 1)], outs, width // self.wide, 4 * rows * gate_full.size
        )

    def compute(self, whole, tiles):
        gate_rows = blocks_dot(whole[0], tiles[0])
        up_rows = blocks_dot(whole[0], tiles[1])
        return gate_rows, up_rows, (gate_rows * jax.nn.sigmoid(gate_rows) * up_rows).astype(LOW)


class HiddenGradJob(Job):
    def __init__(self, cot, shrink_full, gate_rows, up_rows):
        rows, width = gate_rows.shape
        outs = [((rows, width), LOW), ((rows, width), LOW)]
        tiled = [(shrink_full, 1), (gate_rows, 1), (up_rows, 1)]
        super().__init__([cot], tiled, outs, width // self.wide, 2 * rows * shrink_full.size)

    def compute(self, whole, tiles):
        _, gate_rows, up_rows = tiles
        act_grad = blocks_dot(whole[0], tiles[0])
        sigmoid_gate = jax.nn.sigmoid(gate_rows)
        gate_grad = act_grad * up_rows * sigmoid_gate * (1.0 + gate_rows * (1.0 - sigmoid_gate))
        return gate_grad.astype(LOW), (act_grad * (gate_rows * sigmoid_gate)).astype(LOW)


class WidthJob(Job):
    def __init__(self, lefts, weights, before=None):
        rows, width = lefts[0].shape[0], weights[0].shape[0]
        flops = 2 * rows * sum(weight.size for weight in weights)
        self.own = width // lax.axis_size("tp")
        self.height = rows
        self.before = before
        out = ((rows * lax.axis_size("tp"), self.own), LOW)
        super().__init__(lefts, [(weight, 0) for weight in weights], [out], width // self.wide, flops)

    def out_window(self, index):
        return owner_window(index, self.wide, self.own, self.height)

    def compute(self, whole, tiles):
        total = None
        lefts = list(whole) + (list(self.before.outs_v) if self.before else [])
        for left, weight in zip(lefts, tiles):
            term = contract_cols(left[...], weight)
            total = term if total is None else total + term
        return (total.astype(LOW),)


def owner_window(index, wide, own, height):
    each = own // wide
    rows = pl.ds(pl.multiple_of(index // each * height, 16), height)
    return rows, pl.ds(pl.multiple_of(index % each * wide, 128), wide)


class MixerJob:
    def __init__(self, inputs, outs, extra, phases, flops):
        self.inputs = list(inputs)
        self.out_shapes = [jax.ShapeDtypeStruct(shape, dtype) for shape, dtype in outs]
        self.phases = phases
        self.tiles = sum(phases)
        self.flops = flops
        self.scratch = (
            [pltpu.VMEM(array.shape, array.dtype) for array in self.inputs]
            + [pltpu.VMEM(shape, dtype) for shape, dtype in outs]
            + extra
            + [
                pltpu.SemaphoreType.DMA((len(self.inputs),)),
                pltpu.SemaphoreType.DMA((len(outs),)),
                pltpu.SemaphoreType.DMA((2,)),
            ]
        )

    def bind(self, ins, outs, scratch):
        self.in_refs, self.out_refs = ins, outs
        extra = len(scratch) - len(ins) - len(outs) - 3
        self.ins_v, self.outs_v, self.extra_v = split(scratch, [len(ins), len(outs), extra])
        self.in_sem, self.out_sem, self.pass_sem = scratch[-3:]
        self.count = lax.axis_size("seq")
        self.seq = lax.axis_index("seq")
        self.column = lax.axis_index("tp")

    def peers(self):
        after = (self.seq + 1) % self.count
        before = (self.seq + self.count - 1) % self.count
        return [(after, self.column), (before, self.column)]

    def load(self, which):
        return pltpu.make_async_copy(self.in_refs[which], self.ins_v[which], self.in_sem.at[which])

    def store(self, which):
        return pltpu.make_async_copy(self.outs_v[which], self.out_refs[which], self.out_sem.at[which])

    def passing(self, source, target, forward):
        step = 1 if forward else self.count - 1
        return pltpu.make_async_remote_copy(
            src_ref=source,
            dst_ref=target,
            send_sem=self.pass_sem.at[0],
            recv_sem=self.pass_sem.at[1],
            device_id=((self.seq + step) % self.count, self.column),
            device_id_type=MESH,
        )

    def start(self):
        for which in range(len(self.inputs)):
            self.load(which).start()

    def tile(self, index):
        begin = 0
        for phase, tiles in enumerate(self.phases):
            here = index - begin

            @pl.when((here >= 0) & (here < tiles))
            def _(phase=phase, here=here, tiles=tiles):
                @pl.when(here == 0)
                def _():
                    self.before(phase)

                self.work(phase, here)

                @pl.when(here == tiles - 1)
                def _():
                    self.after(phase)

            begin += tiles

    def finish(self):
        for which in range(len(self.out_shapes)):
            self.store(which).wait()


def visible(bound_row, shape):
    position = lax.broadcasted_iota(jnp.int32, shape, 0)
    see_one = position != bound_row
    return position, see_one, see_one & (position - 1 != bound_row)


def lagged(rows, halo, position):
    last, second = halo[15:16].astype(jnp.float32), halo[14:15].astype(jnp.float32)
    one = jnp.where(position == 0, last, pltpu.roll(rows, 1, 0))
    two = jnp.where(position == 0, second, jnp.where(position == 1, last, pltpu.roll(rows, 2, 0)))
    return one, two


class EntryJob(MixerJob):
    def __init__(self, tokens, gains, entry_full, exit_full, taps, bound):
        parts, rows, own = tokens.shape
        width, columns = exit_full.shape
        self.rows, self.columns, self.own = rows, columns, own
        self.width = width
        outs = [
            ((rows, 3 * columns), jnp.float32),
            ((rows, columns), jnp.float32),
            ((rows, columns), LOW),
            ((16, columns), LOW),
            ((rows, columns), LOW),
            ((parts * rows, own), LOW),
            ((rows, 128), jnp.float32),
            ((width, rows), LOW),
        ]
        phases = [rows // 256, 3 * columns // 256, 1, columns // 128, width // 256]
        flops = 2 * rows * (entry_full.size + exit_full.size)
        super().__init__([tokens, gains, entry_full, exit_full, taps, bound], outs, [], phases, flops)

    def halo(self):
        return self.passing(self.outs_v[2].at[pl.ds(self.rows - 16, 16)], self.outs_v[3], True)

    def before(self, phase):
        if phase == 0:
            for which in (0, 1):
                self.load(which).wait()
        if phase == 1:
            self.store(6).start()
            self.store(7).start()
            self.load(2).wait()
        if phase == 3:
            for which in (4, 5):
                self.load(which).wait()
            self.halo().wait_recv()
            self.store(3).start()
        if phase == 4:
            self.load(3).wait()

    def after(self, phase):
        if phase == 1:
            self.store(0).start()
        if phase == 2:
            self.halo().start()
            self.store(2).start()
        if phase == 3:
            self.store(1).start()
            self.store(4).start()
        if phase == 4:
            self.store(5).start()

    def finish(self):
        self.halo().wait_send()
        super().finish()

    def work(self, phase, index):
        tokens, gains, entry, exits, taps, bound = self.ins_v
        projected, conv, gated, halo, mixer, term, scales, turned_rows = self.outs_v
        columns = self.columns
        if phase == 0:
            rows = pl.ds(pl.multiple_of(index * 256, 256), 256)
            values = [tokens[part, rows, :].astype(jnp.float32) for part in range(tokens.shape[0])]
            total = sum(jnp.sum(value * value, axis=1, keepdims=True) for value in values)
            scale = lax.rsqrt(total / D + EPSILON)
            scales[rows, :] = jnp.broadcast_to(scale, (256, 128))
            for part, value in enumerate(values):
                normed = (value * scale * gains[part, 0:1, :]).astype(LOW)
                tokens[part, rows, :] = normed
                turned_rows[part * self.own : (part + 1) * self.own, rows] = normed.T
        if phase == 1:
            span = pl.ds(pl.multiple_of(index * 256, 256), 256)
            projected[:, span] = blocks_dot(tokens, entry[:, span])
        if phase == 2:
            gated[...] = (projected[:, :columns] * projected[:, 2 * columns :]).astype(LOW)
        if phase == 3:
            span = pl.ds(pl.multiple_of(index * 128, 128), 128)
            middle = pl.ds(pl.multiple_of(columns + index * 128, 128), 128)
            rows = gated[:, span].astype(jnp.float32)
            position, see_one, see_two = visible(bound[0:1, :], rows.shape)
            before = halo[:, span].astype(jnp.float32) * jnp.where(self.seq > 0, 1.0, 0.0)
            one, two = lagged(rows, before, position)
            total = (
                taps[2:3, span] * rows
                + taps[1:2, span] * jnp.where(see_one, one, 0.0)
                + taps[0:1, span] * jnp.where(see_two, two, 0.0)
            )
            conv[:, span] = total
            mixer[:, span] = (projected[:, middle] * total).astype(LOW)
        if phase == 4:
            features = pl.ds(pl.multiple_of(index * 256, 256), 256)
            window = owner_window(index, 256, self.own, self.rows)
            term[window] = contract_cols(mixer[...], exits[features, :]).astype(LOW)


class MixerGradJob(MixerJob):
    def __init__(self, branch, exit_full, entry_full, projected, conv, gated, halo, taps, bound):
        parts, rows, own = branch.shape
        width, columns = exit_full.shape
        self.rows, self.columns, self.own = rows, columns, own
        outs = [((rows, 3 * columns), LOW), ((parts * rows, own), LOW), ((8, columns), jnp.float32)]
        extra = [
            pltpu.VMEM((rows, columns), jnp.float32),
            pltpu.VMEM((8, columns), jnp.float32),
            pltpu.VMEM((8, columns), jnp.float32),
        ]
        phases = [columns // 256, 1, columns // 128, width // 256]
        flops = 2 * rows * (entry_full.size + exit_full.size)
        inputs = [branch, exit_full, entry_full, projected, conv, gated, halo, taps, bound]
        super().__init__(inputs, outs, extra, phases, flops)

    def back(self):
        return self.passing(self.extra_v[1], self.extra_v[2], False)

    def before(self, phase):
        if phase == 0:
            for which in (0, 1, 3, 4):
                self.load(which).wait()
        if phase == 1:
            for which in (7, 8):
                self.load(which).wait()
        if phase == 2:
            for which in (5, 6):
                self.load(which).wait()
            self.back().wait_recv()
        if phase == 3:
            self.load(2).wait()

    def after(self, phase):
        if phase == 1:
            self.back().start()
        if phase == 2:
            self.store(0).start()
            self.store(2).start()
        if phase == 3:
            self.store(1).start()

    def finish(self):
        self.back().wait_send()
        super().finish()

    def work(self, phase, index):
        branch, exits, entry, projected, conv, gated, halo, taps, bound = self.ins_v
        grads, term, taps_grad = self.outs_v
        conv_grad, sent, returned = self.extra_v
        columns, height = self.columns, self.rows
        if phase == 0:
            span = pl.ds(pl.multiple_of(index * 256, 256), 256)
            middle = pl.ds(pl.multiple_of(columns + index * 256, 256), 256)
            mixer_grad = blocks_dot(branch, exits[:, span])
            grads[:, middle] = (mixer_grad * conv[:, span]).astype(LOW)
            conv_grad[:, span] = mixer_grad * projected[:, middle]
        if phase == 1:
            for start in range(0, columns, 128):
                span = slice(start, start + 128)
                rows = conv_grad[0:8, span]
                position, see_one, see_two = visible(bound[0:1, :], rows.shape)
                one = pltpu.roll(jnp.where(see_one, rows, 0.0) * taps[1:2, span], 1, 0)
                two = jnp.where(see_two, rows, 0.0) * taps[0:1, span]
                sent[:, span] = two + jnp.where(position == 0, 0.0, one)
            taps_grad[...] = jnp.zeros_like(taps_grad)
        if phase == 2:
            span = pl.ds(pl.multiple_of(index * 128, 128), 128)
            last = pl.ds(pl.multiple_of(2 * columns + index * 128, 128), 128)
            rows = conv_grad[:, span]
            position, see_one, see_two = visible(bound[0:1, :], rows.shape)
            seen_one, seen_two = jnp.where(see_one, rows, 0.0), jnp.where(see_two, rows, 0.0)
            one = pltpu.roll(seen_one * taps[1:2, span], height - 1, 0)
            two = pltpu.roll(seen_two * taps[0:1, span], height - 2, 0)
            after = returned[:, span] * jnp.where(self.seq < self.count - 1, 1.0, 0.0)
            gated_grad = (
                rows * taps[2:3, span]
                + jnp.where(position == height - 1, after[1:2], one)
                + jnp.where(position < height - 2, two, jnp.where(position == height - 2, after[0:1], 0.0))
            )
            grads[:, span] = (gated_grad * projected[:, last]).astype(LOW)
            grads[:, last] = (gated_grad * projected[:, span]).astype(LOW)
            own_rows = gated[:, span].astype(jnp.float32)
            before = halo[:, span].astype(jnp.float32) * jnp.where(self.seq > 0, 1.0, 0.0)
            lag_one, lag_two = lagged(own_rows, before, position)
            taps_grad[0:1, span] = jnp.sum(seen_two * lag_two, axis=0, keepdims=True)
            taps_grad[1:2, span] = jnp.sum(seen_one * lag_one, axis=0, keepdims=True)
            taps_grad[2:3, span] = jnp.sum(rows * own_rows, axis=0, keepdims=True)
        if phase == 3:
            features = pl.ds(pl.multiple_of(index * 256, 256), 256)
            window = owner_window(index, 256, self.own, height)
            term[window] = contract_cols(grads[...], entry[features, :]).astype(LOW)


class Jobs:
    def __init__(self, *jobs):
        self.jobs = jobs
        self.inputs = [item for job in jobs for item in job.inputs]
        self.out_shapes = [item for job in jobs for item in job.out_shapes]
        self.scratch = [item for job in jobs for item in job.scratch]
        self.tiles = sum(job.tiles for job in jobs)
        self.flops = sum(job.flops for job in jobs)

    def bind(self, ins, outs, scratch):
        groups = zip(
            self.jobs,
            split(ins, [len(job.inputs) for job in self.jobs]),
            split(outs, [len(job.out_shapes) for job in self.jobs]),
            split(scratch, [len(job.scratch) for job in self.jobs]),
        )
        for job, own_ins, own_outs, own_scratch in groups:
            job.bind(own_ins, own_outs, own_scratch)

    def peers(self):
        return [peer for job in self.jobs for peer in job.peers()]

    def start(self):
        for job in self.jobs:
            job.start()

    def tile(self, index):
        begin = 0
        for job in self.jobs:
            here = index - begin

            @pl.when((here >= 0) & (here < job.tiles))
            def _(job=job, here=here):
                job.tile(here)

            begin += job.tiles

    def finish(self):
        for job in self.jobs:
            job.finish()


class TurnJob(MixerJob):
    def __init__(self, blocks):
        parts, rows, own = blocks.shape
        super().__init__([blocks], [((parts * own, rows), blocks.dtype)], [], [rows // 128], 0)

    def peers(self):
        return []

    def before(self, phase):
        self.load(0).wait()

    def after(self, phase):
        self.store(0).start()

    def work(self, phase, index):
        (blocks,), (target,) = self.ins_v, self.outs_v
        parts, _, own = blocks.shape
        rows = pl.ds(pl.multiple_of(index * 128, 128), 128)
        for part in range(parts):
            target[part * own : (part + 1) * own, rows] = blocks[part, rows, :].T


class CastJob(MixerJob):
    def __init__(self, pairs, plain):
        rows, columns = plain.shape
        lanes = pairs.shape[1]
        self.rows, self.half, self.lanes = rows, columns // 2, lanes
        self.block = max(rows // 8, 16)
        outs = [((rows, columns // 2), LOW)] * 6
        super().__init__([pairs, plain], outs, [], [rows // self.block], 0)

    def peers(self):
        return []

    def before(self, phase):
        for which in range(2):
            self.load(which).wait()

    def after(self, phase):
        for which in range(6):
            self.store(which).start()

    def work(self, phase, index):
        pairs, plain = self.ins_v
        block, half, lanes = self.block, self.half, self.lanes
        tiles = half // lanes
        rows = pl.ds(pl.multiple_of(index * block, 16), block)
        start = index * (block * 4 * tiles)
        for which in range(4):
            side, plane = which // 2, which % 2
            for tile in range(tiles):
                place = (side * tiles + tile) * 2 + plane
                picked = pairs[pl.ds(start + place, block, stride=4 * tiles), :]
                self.outs_v[which][rows, tile * lanes : (tile + 1) * lanes] = picked.astype(LOW)
        for side in range(2):
            self.outs_v[4 + side][rows, :] = plain[rows, side * half : (side + 1) * half].astype(LOW)


class SmallGatherJob:
    tiles, flops = 1, 0

    def __init__(self, own):
        self.inputs = [own]
        devices, columns = lax.axis_size("seq"), lax.axis_size("tp")
        whole = (devices, columns) + own.shape
        self.out_shapes = [jax.ShapeDtypeStruct(whole, own.dtype)]
        self.scratch = [
            pltpu.VMEM(whole, own.dtype),
            pltpu.SemaphoreType.DMA((2,)),
            pltpu.SemaphoreType.DMA((columns,)),
            pltpu.SemaphoreType.DMA((columns,)),
            pltpu.SemaphoreType.DMA((devices,)),
            pltpu.SemaphoreType.DMA((devices,)),
        ]

    def bind(self, ins, outs, scratch):
        self.source, self.target = ins[0], outs[0]
        self.whole, self.local_sem, self.near_send, self.near_recv, self.far_send, self.far_recv = scratch
        self.devices, self.columns = lax.axis_size("seq"), lax.axis_size("tp")
        self.seq, self.column = lax.axis_index("seq"), lax.axis_index("tp")

    def peers(self):
        near = [(self.seq, (self.column + step) % self.columns) for step in range(1, self.columns)]
        far = [((self.seq + step) % self.devices, self.column) for step in range(1, self.devices)]
        return near + far

    def near(self, step):
        piece = self.whole.at[self.seq, self.column]
        return pltpu.make_async_remote_copy(
            src_ref=piece,
            dst_ref=piece,
            send_sem=self.near_send.at[step],
            recv_sem=self.near_recv.at[step],
            device_id=(self.seq, (self.column + step) % self.columns),
            device_id_type=MESH,
        )

    def far(self, step):
        piece = self.whole.at[self.seq]
        return pltpu.make_async_remote_copy(
            src_ref=piece,
            dst_ref=piece,
            send_sem=self.far_send.at[step],
            recv_sem=self.far_recv.at[step],
            device_id=((self.seq + step) % self.devices, self.column),
            device_id_type=MESH,
        )

    def start(self):
        load = pltpu.make_async_copy(self.source, self.whole.at[self.seq, self.column], self.local_sem.at[0])
        load.start()
        load.wait()
        for step in range(1, self.columns):
            self.near(step).start()

    def tile(self, index):
        for step in range(1, self.columns):
            self.near(step).wait()

        def begin(step, carry):
            self.far(step).start()
            return carry

        lax.fori_loop(1, self.devices, begin, 0)

    def finish(self):
        def end(step, carry):
            self.far(step).wait()
            return carry

        lax.fori_loop(1, self.devices, end, 0)
        store = pltpu.make_async_copy(self.whole, self.target, self.local_sem.at[1])
        store.start()
        store.wait()


class RowSumJob(MixerJob):
    block = 128

    def __init__(self, inputs, outs, extra, rows, flops):
        self.columns = lax.axis_size("tp")
        blocks = rows // self.block
        exchange = [
            pltpu.VMEM((self.columns, blocks, self.block), jnp.float32),
            pltpu.VMEM((blocks, self.block), jnp.float32),
            pltpu.SemaphoreType.DMA((self.columns,)),
            pltpu.SemaphoreType.DMA((self.columns,)),
        ]
        super().__init__(inputs, outs, exchange + extra, [blocks, 1, blocks], flops)

    def peers(self):
        return [(self.seq, (self.column + step) % self.columns) for step in range(1, self.columns)]

    def share(self, step):
        return pltpu.make_async_remote_copy(
            src_ref=self.extra_v[0].at[0],
            dst_ref=self.extra_v[0].at[step],
            send_sem=self.extra_v[2].at[step],
            recv_sem=self.extra_v[3].at[step],
            device_id=(self.seq, (self.column + step) % self.columns),
            device_id_type=MESH,
        )

    def before(self, phase):
        if phase == 0:
            for which in range(len(self.inputs)):
                self.load(which).wait()

    def after(self, phase):
        if phase == 0:
            for step in range(1, self.columns):
                self.share(step).start()
        if phase == 2:
            for which in range(len(self.out_shapes)):
                self.store(which).start()

    def finish(self):
        for step in range(1, self.columns):
            self.share(step).wait_send()
        super().finish()

    def work(self, phase, index):
        block = self.block
        slots, totals = self.extra_v[:2]
        rows = pl.ds(pl.multiple_of(index * block, block), block)
        if phase == 0:
            part = jnp.sum(self.values(rows), axis=1, keepdims=True)
            slots[0, pl.ds(index, 1), :] = jnp.broadcast_to(part, (block, block)).T[0:1, :]
        if phase == 1:
            for step in range(1, self.columns):
                self.share(step).wait_recv()
            totals[...] = sum(slots[step] for step in range(self.columns))
        if phase == 2:
            self.use(rows, jnp.broadcast_to(totals[pl.ds(index, 1), :], (block, block)).T)


class NormJob(RowSumJob):
    def __init__(self, rows_in, branch, gain):
        rows, own = rows_in.shape
        outs = [((rows, own), jnp.float32), ((rows, own), LOW), ((rows, 128), jnp.float32)]
        super().__init__([rows_in, branch, gain], outs, [], rows, 0)

    def values(self, rows):
        residual = self.ins_v[0][rows, :].astype(jnp.float32) + self.ins_v[1][rows, :].astype(jnp.float32)
        self.outs_v[0][rows, :] = residual
        return residual * residual

    def use(self, rows, total):
        residual, normed, scales = self.outs_v
        scale = lax.rsqrt(total / D + EPSILON)
        scales[rows, :] = scale
        normed[rows, :] = (residual[rows, :] * scale[:, 0:1] * self.ins_v[2][0:1, :]).astype(LOW)


class NormBackJob(RowSumJob):
    def __init__(self, grad, kept, scales, gain, base, rounded):
        rows, own = grad.shape
        outs = [((rows, own), jnp.float32), ((8, own), jnp.float32)]
        outs = outs + [((rows, own), LOW)] if rounded else outs
        super().__init__([grad, kept, scales, gain, base], outs, [], rows, 0)

    def parts(self, rows):
        grad, kept, scales, gain, base = self.ins_v
        return (
            grad[rows, :].astype(jnp.float32),
            kept[rows, :].astype(jnp.float32),
            scales[rows, 0:1],
            gain[0:1, :],
        )

    def before(self, phase):
        super().before(phase)
        if phase == 0:
            self.outs_v[1][...] = jnp.zeros_like(self.outs_v[1])

    def values(self, rows):
        grad, kept, scale, gain = self.parts(rows)
        product = grad * kept
        self.outs_v[1][0:1, :] += jnp.sum(product * scale, axis=0, keepdims=True)
        return product * gain

    def use(self, rows, total):
        grad, kept, scale, gain = self.parts(rows)
        rows_grad = scale * gain * grad - kept * (scale * scale * scale * total[:, 0:1] / D)
        result = self.ins_v[4][rows, :].astype(jnp.float32) + rows_grad
        self.outs_v[0][rows, :] = result
        if len(self.outs_v) > 2:
            self.outs_v[2][rows, :] = result.astype(LOW)


class SmallSumJob:
    tiles, flops = 1, 0

    def __init__(self, taps_grad, gain_grad, before):
        count = lax.axis_size("seq")
        self.inputs = [taps_grad, gain_grad]
        shape = taps_grad.shape
        self.before = before
        self.out_shapes = [jax.ShapeDtypeStruct(shape, jnp.float32)]
        self.scratch = [
            pltpu.VMEM(shape, jnp.float32),
            pltpu.VMEM(shape, jnp.float32),
            pltpu.VMEM((count,) + shape, jnp.float32),
            pltpu.VMEM(shape, jnp.float32),
            pltpu.SemaphoreType.DMA((3,)),
            pltpu.SemaphoreType.DMA((count,)),
            pltpu.SemaphoreType.DMA((count,)),
        ]

    def bind(self, ins, outs, scratch):
        self.sources, self.target = ins, outs[0]
        self.taps, self.gain, self.slots, self.total, self.local_sem, self.send_sem, self.recv_sem = scratch
        self.count = lax.axis_size("seq")
        self.seq = lax.axis_index("seq")
        self.column = lax.axis_index("tp")

    def peers(self):
        return [((self.seq + far) % self.count, self.column) for far in range(1, self.count)]

    def copy(self, far):
        return pltpu.make_async_remote_copy(
            src_ref=self.slots.at[0],
            dst_ref=self.slots.at[far],
            send_sem=self.send_sem.at[far],
            recv_sem=self.recv_sem.at[far],
            device_id=((self.seq + far) % self.count, self.column),
            device_id_type=MESH,
        )

    def loads(self):
        return [
            pltpu.make_async_copy(self.sources[which], (self.taps, self.gain)[which], self.local_sem.at[which])
            for which in range(2)
        ]

    def start(self):
        for load in self.loads():
            load.start()

    def tile(self, index):
        for load in self.loads():
            load.wait()
        self.slots[0, 0:3, :] = self.taps[0:3, :]
        self.slots[0, 3:4, :] = self.before.outs_v[1][0:1, :]
        self.slots[0, 4:5, :] = self.gain[0:1, :]
        self.slots[0, 5:8, :] = jnp.zeros_like(self.slots[0, 5:8, :])

        def begin(far, carry):
            self.copy(far).start()
            return carry

        lax.fori_loop(1, self.count, begin, 0)

    def finish(self):
        self.total[...] = self.slots[0]

        def add(far, carry):
            self.copy(far).wait_recv()
            self.total[...] += self.slots[far]
            return carry

        lax.fori_loop(1, self.count, add, 0)
        store = pltpu.make_async_copy(self.total, self.target, self.local_sem.at[2])
        store.start()

        def sent(far, carry):
            self.copy(far).wait_send()
            return carry

        lax.fori_loop(1, self.count, sent, 0)
        store.wait()


def ring_kernel(ring, job, *refs):
    sizes = [len(group) for group in (ring.inputs, job.inputs, ring.out_shapes, job.out_shapes, ring.scratch, job.scratch)]
    ring_in, job_in, ring_out, job_out, ring_scratch, job_scratch = split(refs, sizes)
    ring.bind(ring_in, ring_out, ring_scratch)
    job.bind(job_in, job_out, job_scratch)
    ring.prepare()
    greet(ring.peers() + job.peers())
    ring.start()
    job.start()
    rest = max(ring.ticks // 6, 1)
    active = ring.ticks - rest
    each = -(-job.tiles // active)

    def step(index, carry):
        late = index - rest
        first, after = late * job.tiles // active, (late + 1) * job.tiles // active
        for inner in range(each):
            tile = first + inner

            @pl.when((late >= 0) & (tile < after))
            def _(tile=tile):
                job.tile(tile)

        ring.tick(index)
        return carry

    lax.fori_loop(0, ring.ticks, step, 0)
    ring.finish()
    job.finish()


def run_ring(ring, job, collective):
    inputs = ring.inputs + job.inputs
    outs = ring.out_shapes + job.out_shapes
    return pl.pallas_call(
        functools.partial(ring_kernel, ring, job),
        out_shape=outs,
        in_specs=[pl.BlockSpec(memory_space=pl.ANY)] * len(inputs),
        out_specs=[pl.BlockSpec(memory_space=pl.ANY)] * len(outs),
        scratch_shapes=ring.scratch + job.scratch,
        compiler_params=pltpu.CompilerParams(
            collective_id=collective, has_side_effects=True, vmem_limit_bytes=VMEM_BYTES
        ),
        cost_estimate=pl.CostEstimate(flops=ring.flops + job.flops, bytes_accessed=ring.bytes, transcendentals=0),
        name=ring.name,
    )(*inputs)


def flat(full):
    return full.reshape(full.shape[0] * full.shape[1], full.shape[2])


def contract_rows(left, right):
    return lax.dot_general(
        left, right, (((0,), (0,)), ((), ())), preferred_element_type=jnp.float32
    )


def contract_cols(left, right):
    return lax.dot_general(
        left, right, (((1,), (1,)), ((), ())), preferred_element_type=jnp.float32
    )


def tie(*values):
    return lax.optimization_barrier(values)


def gather_rows(own):
    return lax.all_gather(own, "tp", axis=0, tiled=True)


def gather_blocks(own):
    return gather_rows(own).reshape(-1, *own.shape)


def reduce_branch(term):
    return lax.psum_scatter(term, "tp", scatter_dimension=0, tiled=True)


def adam_update(weight, first, second, grad, rate, decay):
    first_next = BETA_ONE * first + (1.0 - BETA_ONE) * grad
    second_next = BETA_TWO * second + (1.0 - BETA_TWO) * grad * grad
    corrected = first_next / (1.0 - BETA_ONE**STEP)
    spread = jnp.sqrt(second_next / (1.0 - BETA_TWO**STEP)) + ADAM_EPSILON
    return (weight - rate * (corrected / spread + decay * weight), first_next, second_next)


def adam_kernel(pieces, *refs):
    weight, first, second = refs[:3]
    grads, outs = refs[3 : 3 + pieces], refs[3 + pieces :]
    start = 0
    for grad in grads:
        span = slice(start, start + grad.shape[1])
        start += grad.shape[1]
        results = adam_update(weight[:, span], first[:, span], second[:, span], grad[...], RATE_WIDE, WEIGHT_DECAY)
        for out, result in zip(outs, results):
            out[:, span] = result


def adam_rows(weight, first, second, grads, planes=1):
    rows, columns = weight.shape[0] // planes, weight.shape[1]
    block = max(rows // 8, 8) if columns > 1024 else max(rows // 2, 8)
    steps = rows // block
    state = pl.BlockSpec((block, columns), lambda plane, step: (plane * steps + step, 0))
    grad_specs = [
        pl.BlockSpec((block, grad.shape[1] // planes), lambda plane, step: (step, plane)) for grad in grads
    ]
    return pl.pallas_call(
        functools.partial(adam_kernel, len(grads)),
        out_shape=[jax.ShapeDtypeStruct(weight.shape, weight.dtype)] * 3,
        grid=(planes, steps),
        in_specs=[state] * 3 + grad_specs,
        out_specs=[state] * 3,
        cost_estimate=pl.CostEstimate(flops=20 * weight.size, bytes_accessed=28 * weight.size, transcendentals=0),
        name="adam_rows",
    )(weight, first, second, *grads)


def adam_pairs_kernel(lanes, *refs):
    weight, first, second = refs[:3]
    grads, outs, mixed = refs[3:7], refs[7:10], refs[10]
    rows = grads[0].shape[0]
    tiles = grads[0].shape[1] // lanes
    for which, grad in enumerate(grads):
        half, side = which // 2, which % 2
        for tile in range(tiles):
            place = (half * tiles + tile) * 2 + side
            mixed[pl.ds(place, rows, stride=4 * tiles), :] = grad[:, tile * lanes : (tile + 1) * lanes]
    results = adam_update(weight[...], first[...], second[...], mixed[...], RATE_WIDE, WEIGHT_DECAY)
    for out, result in zip(outs, results):
        out[...] = result


def paired(array):
    rows, _, columns = array.shape
    return array.reshape(rows, 2, columns // LANES, LANES).transpose(0, 2, 1, 3).reshape(-1, LANES)


def adam_pairs(weight, first, second, grads):
    rows, _, columns = weight.shape
    deep = columns // LANES
    block = max(rows // 8, 8)
    state = pl.BlockSpec((block * deep * 2, LANES), lambda step: (step, 0))
    results = pl.pallas_call(
        functools.partial(adam_pairs_kernel, LANES),
        out_shape=[jax.ShapeDtypeStruct((rows * deep * 2, LANES), weight.dtype)] * 3,
        grid=(rows // block,),
        in_specs=[state] * 3 + [pl.BlockSpec((block, columns // 2), lambda step: (step, 0))] * 4,
        out_specs=[state] * 3,
        scratch_shapes=[pltpu.VMEM((block * deep * 2, LANES), jnp.float32)],
        cost_estimate=pl.CostEstimate(flops=20 * weight.size, bytes_accessed=28 * weight.size, transcendentals=0),
        name="adam_pairs",
    )(paired(weight), paired(first), paired(second), *grads)
    return [
        result.reshape(rows, deep, 2, LANES).transpose(0, 2, 1, 3).reshape(rows, 2, columns) for result in results
    ]


def adam_planes(weight, first, second, grad):
    rows, planes, columns = weight.shape

    def seen(array):
        return array.transpose(1, 0, 2).reshape(planes * rows, columns)

    results = adam_rows(seen(weight), seen(first), seen(second), [grad], planes)
    return [result.reshape(planes, rows, columns).transpose(1, 0, 2) for result in results]


def shards(
    tokens,
    bounds,
    cotangent,
    entry_weight,
    entry_first,
    entry_second,
    exit_weight,
    exit_first,
    exit_second,
    expand_weight,
    expand_first,
    expand_second,
    shrink_weight,
    shrink_first,
    shrink_second,
    conv_kernel,
    conv_first,
    conv_second,
    norm_gains,
    gain_first,
    gain_second,
):
    channels = tokens.shape[1]
    count = lax.axis_size("seq")
    idle = NoJob()
    seen = conv_kernel.shape[1]
    small = jnp.concatenate([conv_kernel, norm_gains], axis=0)
    small = jnp.pad(small, ((0, 16 - small.shape[0]), (0, 128 - seen))).astype(LOW)
    entry_low = entry_weight.reshape(entry_weight.shape[0], 3 * channels).astype(LOW)
    bound = jnp.broadcast_to(bounds[0], (8, 128))

    tokens_blocks = gather_blocks(tokens)
    cast = CastJob(paired(expand_weight), shrink_weight)
    entry_full, exit_full, small_full, *low = run_ring(
        GatherRing([entry_low, exit_weight.astype(LOW)]), Jobs(SmallGatherJob(small), cast), 0
    )
    entry_full, exit_full = flat(entry_full), flat(exit_full)
    gate_low, up_low, shrink_low = low[0:4:2], low[1:4:2], low[4:6]
    small_wide = small_full[:, :, :8, :seen].transpose(1, 2, 0, 3).reshape(-1, 8, channels).astype(jnp.float32)
    taps = lax.dynamic_index_in_dim(small_wide, lax.axis_index("tp"), 0, False)
    gain_blocks = small_wide[:, 3:4] + jnp.zeros((1, 8, 1), jnp.float32)
    gain_one = jnp.broadcast_to(taps[3:4], taps.shape)
    gain_two = jnp.broadcast_to(taps[4:5], taps.shape)
    gate_full, up_full, shrink_full = [None] * 2, [None] * 2, [None] * 2
    shrink_part, gate_part, up_part = [None] * 2, [None] * 2, [None] * 2

    tokens_blocks, cotangent_rows, entry_full = tie(tokens_blocks, cotangent, entry_full)
    cot_blocks = gather_blocks(cotangent_rows)
    full, projected, conv_out, gated_rows, halo, mixer_rows, branch_term, scale_one, normed_one = run_ring(
        GatherRing([gate_low[0]]), EntryJob(tokens_blocks, gain_blocks, entry_full, exit_full, taps, bound), 1
    )
    gate_full[0] = flat(full)
    cot_blocks, branch_term, up_low[0] = tie(cot_blocks, branch_term, up_low[0])
    full, cot_full = run_ring(GatherRing([up_low[0]]), TurnJob(cot_blocks), 2)
    branch, up_full[0] = tie(reduce_branch(branch_term), flat(full))
    full, residual, own_normed_two, scale_two = run_ring(
        GatherRing([gate_low[1]]), NormJob(tokens, branch, gain_two), 3
    )
    own_normed_two, gate_full[1], up_low[1] = tie(own_normed_two, flat(full), up_low[1])
    (full,) = run_ring(GatherRing([up_low[1]]), idle, 4)
    normed_blocks, up_full[1] = tie(gather_blocks(own_normed_two), flat(full))
    full, *expanded = run_ring(
        GatherRing([shrink_low[0]]),
        Jobs(*[ExpandJob(normed_blocks, gate_full[half], up_full[half]) for half in range(2)]),
        5,
    )
    gate_rows, up_rows, activation = expanded[0::3], expanded[1::3], expanded[2::3]
    shrink_full[0] = flat(full)
    full, gate_grad_one, up_grad_one, normed_two = run_ring(
        GatherRing([shrink_low[1]]),
        Jobs(HiddenGradJob(cot_blocks, shrink_full[0], gate_rows[0], up_rows[0]), TurnJob(normed_blocks)),
        6,
    )
    shrink_full[1] = flat(full)
    hidden = HiddenGradJob(cot_blocks, shrink_full[1], gate_rows[1], up_rows[1])
    width = WidthJob([gate_grad_one, up_grad_one], [gate_full[0], up_full[0], gate_full[1], up_full[1]], hidden)
    shrink_part[0], gate_grad_two, up_grad_two, two_term = run_ring(
        ScatterRing([(cot_full, activation[0])]), Jobs(hidden, width), 7
    )
    gate_grad, up_grad = [gate_grad_one, gate_grad_two], [up_grad_one, up_grad_two]
    shrink_part[1], mixed_term = run_ring(
        ScatterRing([(cot_full, activation[1])]), WidthJob(activation, shrink_full), 8
    )
    grad_normed_two, shrink_part[1], mixed_term = tie(reduce_branch(two_term), shrink_part[1], mixed_term)
    gate_part[0], residual_grad, gain_two_grad, branch_own = run_ring(
        ScatterRing([(normed_two, gate_grad[0])]),
        NormBackJob(grad_normed_two, residual, scale_two, gain_two, cotangent, True),
        9,
    )
    mixed_branch, branch_own, up_grad[0] = tie(reduce_branch(mixed_term), branch_own, up_grad[0])
    (up_part[0],) = run_ring(ScatterRing([(normed_two, up_grad[0])]), idle, 10)
    branch_blocks, up_part[0] = tie(gather_blocks(branch_own), up_part[0])
    gate_part[1], projected_grad, one_term, taps_grad = run_ring(
        ScatterRing([(normed_two, gate_grad[1])]),
        MixerGradJob(branch_blocks, exit_full, entry_full, projected, conv_out, gated_rows, halo, taps, bound),
        11,
    )
    one_term, up_grad[1], gate_part[1] = tie(one_term, up_grad[1], gate_part[1])
    up_part[1], branch_full = run_ring(ScatterRing([(normed_two, up_grad[1])]), TurnJob(branch_blocks), 12)
    grad_normed_one, up_part[1] = tie(reduce_branch(one_term), up_part[1])
    back = NormBackJob(grad_normed_one, tokens, scale_one, gain_one, residual_grad, False)
    entry_part, exit_part, tokens_grad, _, small_part = run_ring(
        ScatterRing([(normed_one, projected_grad), (branch_full, mixer_rows)]),
        Jobs(back, SmallSumJob(taps_grad, gain_two_grad, back)),
        13,
    )
    mixed = (residual + mixed_branch.astype(jnp.float32)).astype(LOW)
    small_part = lax.dynamic_slice_in_dim(small_part, lax.axis_index("seq") * seen, seen, axis=1)
    kernel_part = small_part[:3]
    gains_part = small_part[3:5]
    entry_next, entry_first_next, entry_second_next = adam_planes(
        entry_weight, entry_first, entry_second, entry_part
    )
    exit_next, exit_first_next, exit_second_next = adam_rows(exit_weight, exit_first, exit_second, [exit_part])
    expand_next, expand_first_next, expand_second_next = adam_pairs(
        expand_weight, expand_first, expand_second, [gate_part[0], up_part[0], gate_part[1], up_part[1]]
    )
    shrink_next, shrink_first_next, shrink_second_next = adam_rows(
        shrink_weight, shrink_first, shrink_second, shrink_part
    )
    conv_next, conv_first_next, conv_second_next = adam_update(
        conv_kernel, conv_first, conv_second, kernel_part, RATE_CONV, 0.0
    )
    gains_next, gains_first_next, gains_second_next = adam_update(
        norm_gains, gain_first, gain_second, gains_part, RATE_GAIN, 0.0
    )
    return (
        mixed,
        tokens_grad,
        entry_next,
        entry_first_next,
        entry_second_next,
        exit_next,
        exit_first_next,
        exit_second_next,
        expand_next,
        expand_first_next,
        expand_second_next,
        shrink_next,
        shrink_first_next,
        shrink_second_next,
        conv_next,
        conv_first_next,
        conv_second_next,
        gains_next,
        gains_first_next,
        gains_second_next,
    )


def solution(mesh):
    rows = P("seq", "tp")
    stacked = P("seq", None, "tp")
    small = P(None, ("tp", "seq"))
    return jax.shard_map(
        shards,
        mesh=mesh,
        in_specs=(rows, P("seq"), rows) + (stacked,) * 3 + (rows,) * 3 + (stacked,) * 3 + (rows,) * 3 + (small,) * 6,
        out_specs=(rows, rows) + (stacked,) * 3 + (rows,) * 3 + (stacked,) * 3 + (rows,) * 3 + (small,) * 6,
        check_vma=False,
    )
```

```python
import functools

import jax
import jax.numpy as jnp
from jax import lax
from jax.experimental import pallas as pl
from jax.experimental.pallas import tpu as pltpu
from jax.sharding import PartitionSpec as P

D = 2048
STEP = 10


EPSILON = 1e-05
BETA_ONE = 0.9
BETA_TWO = 0.95
ADAM_EPSILON = 1e-08
WEIGHT_DECAY = 0.1
RATE_WIDE = 0.04
RATE_CONV = 0.5
RATE_GAIN = 0.4

MESH = pl.DeviceIdType.MESH
LOW = jnp.bfloat16
LANES = 128
VMEM_BYTES = 60 * 1024 * 1024


def ring_place(index, count):
    side = index % 2
    level = index // 2
    return level * (1 - side) + (count - 1 - level) * side


def ring_index(place, count):
    back = place // (count // 2)
    return (1 - back) * (2 * place) + back * (2 * (count - 1 - place) + 1)


def ring_ends(count):
    place = ring_place(lax.axis_index("seq"), count)
    ahead = ring_index((place + 1) % count, count)
    behind = ring_index((place + count - 1) % count, count)
    return place, ahead, behind


def greet(peers):
    barrier = pltpu.get_barrier_semaphore()
    for peer in peers:
        pl.semaphore_signal(barrier, inc=1, device_id=peer, device_id_type=MESH)
    pl.semaphore_wait(barrier, len(peers))


def split(items, sizes):
    parts, start = [], 0
    for size in sizes:
        parts.append(items[start : start + size])
        start += size
    return parts


class GatherRing:
    def __init__(self, groups, shapes):
        self.count = lax.axis_size("seq")
        self.groups = groups
        self.rows = {full: shapes[shard].shape[0] for group in groups for shard, full in group}
        self.order = {full: place for place, full in enumerate(self.rows)}
        self.parts = 2 if min(self.rows.values()) % 64 == 0 else 1
        self.ticks = (self.count - 2) * self.parts
        arrays = len(self.rows)
        sems = pltpu.SemaphoreType.DMA((arrays, 2, self.parts, self.count - 1))
        self.scratch = [sems, sems, pltpu.SemaphoreType.DMA((arrays,))]

    def bind(self, refs, scratch):
        self.refs = refs
        self.send_sem, self.recv_sem, self.own_sem = scratch
        self.column = lax.axis_index("tp")
        self.place, self.ahead, self.behind = ring_ends(self.count)

    def copy(self, shard, full, way, part, step, first=False):
        move = (self.place + self.count - step) if way == 0 else (self.place + step)
        owner = ring_index(move % self.count, self.count)
        half = self.rows[full] // 2
        size = half // self.parts
        rows = pl.ds(pl.multiple_of(way * half + part * size, 16), size)
        there = self.refs[full].at[owner, rows]
        return pltpu.make_async_remote_copy(
            src_ref=self.refs[shard].at[rows] if first else there,
            dst_ref=there,
            send_sem=self.send_sem.at[self.order[full], way, part, step],
            recv_sem=self.recv_sem.at[self.order[full], way, part, step],
            device_id=(self.ahead if way == 0 else self.behind, self.column),
            device_id_type=MESH,
        )

    def own(self, shard, full):
        there = self.refs[full].at[lax.axis_index("seq")]
        return pltpu.make_async_copy(self.refs[shard], there, self.own_sem.at[self.order[full]])

    def pieces(self, group):
        return [(shard, full, way) for shard, full in self.groups[group] for way in range(2)]

    def begin(self, group):
        for part in range(self.parts):
            for shard, full, way in self.pieces(group):
                self.copy(shard, full, way, part, 0, True).start()
        for shard, full in self.groups[group]:
            self.own(shard, full).start()

    def tick(self, group, index):
        step, part = 1 + index // self.parts, index % self.parts
        for shard, full, way in self.pieces(group):
            self.copy(shard, full, way, part, step - 1).wait_recv()
            self.copy(shard, full, way, part, step).start()

    def settle(self, group):
        for part in range(self.parts):
            for shard, full, way in self.pieces(group):
                self.copy(shard, full, way, part, self.count - 2).wait_recv()
        for shard, full in self.groups[group]:
            self.own(shard, full).wait()

    def finish(self):
        def sent(step, carry):
            for group in range(len(self.groups)):
                for part in range(self.parts):
                    for shard, full, way in self.pieces(group):
                        self.copy(shard, full, way, part, step).wait_send()
            return carry

        lax.fori_loop(0, self.count - 1, sent, 0)


class PeerCopies:
    def __init__(self, source, target):
        self.source, self.target = source, target
        columns = lax.axis_size("tp")
        self.scratch = [pltpu.SemaphoreType.DMA((columns,)), pltpu.SemaphoreType.DMA((columns,))]

    def bind(self, refs, scratch):
        self.source_ref, self.target_ref = refs[self.source], refs[self.target]
        self.send_sem, self.recv_sem = scratch
        self.columns = lax.axis_size("tp")
        self.seq, self.column = lax.axis_index("seq"), lax.axis_index("tp")

    def block(self, peer):
        if len(self.source_ref.shape) == len(self.target_ref.shape):
            return self.source_ref.at[peer]
        return self.source_ref

    def own(self):
        return pltpu.make_async_copy(
            self.block(self.column), self.target_ref.at[self.column], self.send_sem.at[0]
        )

    def copy(self, step):
        peer = (self.column + step) % self.columns
        return pltpu.make_async_remote_copy(
            src_ref=self.block(peer),
            dst_ref=self.target_ref.at[self.column],
            send_sem=self.send_sem.at[step],
            recv_sem=self.recv_sem.at[step],
            device_id=(self.seq, peer),
            device_id_type=MESH,
        )

    def start(self):
        for step in range(1, self.columns):
            self.copy(step).start()
        self.own().start()

    def wait(self):
        self.own().wait()
        for step in range(1, self.columns):
            self.copy(step).wait_recv()

    def finish(self):
        for step in range(1, self.columns):
            self.copy(step).wait_send()


class ScatterRing:
    name = "ring_scatter"

    def __init__(self, pairs):
        self.count = count = lax.axis_size("seq")
        lefts = [left for left, right in pairs]
        rights = [right for left, right in pairs]
        self.inputs = lefts + rights
        self.arrays = len(pairs)
        self.rows = [left.shape[0] // count for left in lefts]
        self.columns = [right.shape[1] for right in rights]
        self.parts = 2 if min(self.columns) % 512 == 0 else 1
        self.ticks = (count - 2) * self.parts
        self.out_shapes = [
            jax.ShapeDtypeStruct((row, width), jnp.float32) for row, width in zip(self.rows, self.columns)
        ]
        sems = pltpu.SemaphoreType.DMA((self.arrays, 2, self.parts, count - 1))
        self.scratch = (
            [pltpu.VMEM(left.shape, left.dtype) for left in lefts]
            + [pltpu.VMEM(right.shape, right.dtype) for right in rights]
            + [pltpu.VMEM((2, count, row, width // 2), LOW) for row, width in zip(self.rows, self.columns)]
            + [pltpu.VMEM((row, width), jnp.float32) for row, width in zip(self.rows, self.columns)]
            + [sems, sems, pltpu.SemaphoreType.DMA((self.arrays, count + 1)), pltpu.SemaphoreType.DMA((self.arrays,))]
        )
        self.flops = sum(2 * left.size * width for left, width in zip(lefts, self.columns))
        self.bytes = 20 * sum(left.shape[0] * width * 2 for left, width in zip(lefts, self.columns))

    def bind(self, ins, outs, scratch):
        arrays = self.arrays
        self.in_refs, self.out_refs = ins, outs
        self.lefts, self.rights, self.slots, self.finals = split(scratch, [arrays] * 4)
        self.send_sem, self.recv_sem, self.load_sem, self.done_sem = scratch[4 * arrays :]
        self.column = lax.axis_index("tp")
        self.place, self.ahead, self.behind = ring_ends(self.count)

    def pieces(self):
        return [(array, way) for array in range(self.arrays) for way in range(2)]

    def span(self, array, way, part):
        half = self.columns[array] // 2
        width = half // self.parts
        inner = part * width
        return way * half + inner, inner, width

    def term(self, array, way, part, step):
        move = (self.place + 2 * self.count - 1 - step) if way == 0 else (self.place + 1 + step)
        owner = ring_index(move % self.count, self.count)
        rows = self.rows[array]
        start, _, width = self.span(array, way, part)
        left = self.lefts[array][pl.ds(pl.multiple_of(owner * rows, 16), rows), :]
        right = self.rights[array][:, pl.ds(pl.multiple_of(start, 128), width)]
        return jnp.dot(left, right, preferred_element_type=jnp.float32)

    def held(self, array, way, part, step):
        _, inner, width = self.span(array, way, part)
        return self.slots[array].at[way, step, :, pl.ds(pl.multiple_of(inner, 128), width)]

    def copy(self, array, way, part, step):
        return pltpu.make_async_remote_copy(
            src_ref=self.held(array, way, part, step),
            dst_ref=self.held(array, way, part, step + 1),
            send_sem=self.send_sem.at[array, way, part, step],
            recv_sem=self.recv_sem.at[array, way, part, step],
            device_id=(self.ahead if way == 0 else self.behind, self.column),
            device_id_type=MESH,
        )

    def right_load(self, array):
        return pltpu.make_async_copy(
            self.in_refs[array + self.arrays], self.rights[array], self.load_sem.at[array, self.count]
        )

    def left_load(self, array, step):
        owner = ring_index((self.place + 2 * self.count - 1 - step) % self.count, self.count)
        rows = pl.ds(pl.multiple_of(owner * self.rows[array], 16), self.rows[array])
        return pltpu.make_async_copy(
            self.in_refs[array].at[rows], self.lefts[array].at[rows], self.load_sem.at[array, step]
        )

    def peers(self):
        return [(self.ahead, self.column), (self.behind, self.column)]

    def prepare(self):
        for array in range(self.arrays):
            self.right_load(array).start()
            for step in (0, self.count - 2):
                self.left_load(array, step).start()

    def start(self):
        later = list(range(1, self.count - 2)) + [self.count - 1]
        for array in range(self.arrays):
            for step in later:
                self.left_load(array, step).start()
        for array in range(self.arrays):
            self.right_load(array).wait()
            for step in (0, self.count - 2):
                self.left_load(array, step).wait()
            for part in range(self.parts):
                for way in range(2):
                    self.held(array, way, part, 0)[...] = self.term(array, way, part, 0).astype(LOW)
                    self.copy(array, way, part, 0).start()
        for array in range(self.arrays):
            for step in later:
                self.left_load(array, step).wait()

    def tick(self, index):
        step, part = 1 + index // self.parts, index % self.parts
        for array, way in self.pieces():
            mine = self.term(array, way, part, step)
            self.copy(array, way, part, step - 1).wait_recv()
            held = self.held(array, way, part, step)
            held[...] = (held[...].astype(jnp.float32) + mine).astype(LOW)
            self.copy(array, way, part, step).start()

    def finish(self):
        last = self.count - 1
        for part in range(self.parts):
            for array, way in self.pieces():
                start, _, width = self.span(array, way, part)
                mine = self.term(array, way, part, last)
                self.copy(array, way, part, last - 1).wait_recv()
                self.finals[array][:, start : start + width] = (
                    self.held(array, way, part, last)[...].astype(jnp.float32) + mine
                )
        stores = [
            pltpu.make_async_copy(self.finals[array], self.out_refs[array], self.done_sem.at[array])
            for array in range(self.arrays)
        ]
        for store in stores:
            store.start()

        def sent(step, carry):
            for part in range(self.parts):
                for array, way in self.pieces():
                    self.copy(array, way, part, step).wait_send()
            return carry

        lax.fori_loop(0, last, sent, 0)
        for store in stores:
            store.wait()


class NoJob:
    inputs, out_shapes, scratch, kept, tiles, flops = [], [], [], [], 0, 0

    def hold(self, refs):
        pass

    def bind(self, ins, outs, scratch):
        pass

    def peers(self):
        return []

    def start(self):
        pass

    def finish(self):
        pass


class Job:
    wide = 256
    kept = []

    def hold(self, refs):
        pass

    def __init__(self, whole, tiled, outs, tiles, flops):
        self.whole, self.tiled = whole, tiled
        self.inputs = list(whole) + [array for array, axis in tiled]
        self.axes = [axis for array, axis in tiled]
        self.out_shapes = [jax.ShapeDtypeStruct(shape, dtype) for shape, dtype in outs]
        self.tiles = tiles
        self.flops = flops
        self.scratch = (
            [pltpu.VMEM(array.shape, array.dtype) for array in self.inputs]
            + [pltpu.VMEM(shape, dtype) for shape, dtype in outs]
            + [
                pltpu.SemaphoreType.DMA((len(whole),)),
                pltpu.SemaphoreType.DMA((len(tiled), tiles)),
                pltpu.SemaphoreType.DMA((len(outs), tiles)),
            ]
        )

    def bind(self, ins, outs, scratch):
        self.in_refs, self.out_refs = ins, outs
        sizes = [len(self.whole), len(self.tiled), len(outs)]
        self.whole_v, self.tiled_v, self.outs_v = split(scratch, sizes)
        self.whole_sem, self.tiled_sem, self.out_sem = scratch[sum(sizes) :]

    def peers(self):
        return []

    def window(self, axis, index):
        span = pl.ds(pl.multiple_of(index * self.wide, 128), self.wide)
        return (span,) if axis == 0 else (slice(None), span)

    def whole_load(self, which):
        return pltpu.make_async_copy(self.in_refs[which], self.whole_v[which], self.whole_sem.at[which])

    def tiled_load(self, which, index):
        window = self.window(self.axes[which], index)
        there = self.in_refs[len(self.whole) + which].at[window]
        return pltpu.make_async_copy(there, self.tiled_v[which].at[window], self.tiled_sem.at[which, index])

    def out_window(self, index):
        return self.window(1, index)

    def store(self, which, index):
        window = self.out_window(index)
        return pltpu.make_async_copy(
            self.outs_v[which].at[window], self.out_refs[which].at[window], self.out_sem.at[which, index]
        )

    def start(self):
        for which in range(len(self.whole)):
            self.whole_load(which).start()

        def begin(index, carry):
            for which in range(len(self.tiled)):
                self.tiled_load(which, index).start()
            return carry

        lax.fori_loop(0, self.tiles, begin, 0)

    def tile(self, index):
        @pl.when(index == 0)
        def _():
            for which in range(len(self.whole)):
                self.whole_load(which).wait()

        for which in range(len(self.tiled)):
            self.tiled_load(which, index).wait()
        tiles = [ref[self.window(axis, index)] for ref, axis in zip(self.tiled_v, self.axes)]
        for which, value in enumerate(self.compute(self.whole_v, tiles)):
            self.outs_v[which][self.out_window(index)] = value
            self.store(which, index).start()

    def finish(self):
        def end(index, carry):
            for which in range(len(self.outs_v)):
                self.store(which, index).wait()
            return carry

        lax.fori_loop(0, self.tiles, end, 0)


def blocks_dot(blocks, weight):
    parts, _, depth = blocks.shape
    total = None
    for part in range(parts):
        term = jnp.dot(blocks[part], weight[part * depth : (part + 1) * depth], preferred_element_type=jnp.float32)
        total = term if total is None else total + term
    return total


class ExpandJob(Job):
    def __init__(self, normed, gate_full, up_full):
        rows, width = normed.shape[1], gate_full.shape[1]
        outs = [((rows, width), jnp.float32), ((rows, width), jnp.float32), ((rows, width), LOW)]
        super().__init__(
            [normed], [(gate_full, 1), (up_full, 1)], outs, width // self.wide, 4 * rows * gate_full.size
        )

    def compute(self, whole, tiles):
        gate_rows = blocks_dot(whole[0], tiles[0])
        up_rows = blocks_dot(whole[0], tiles[1])
        return gate_rows, up_rows, (gate_rows * jax.nn.sigmoid(gate_rows) * up_rows).astype(LOW)


class HiddenGradJob(Job):
    def __init__(self, cot, shrink_full, gate_rows, up_rows):
        rows, width = gate_rows.shape
        outs = [((rows, width), LOW), ((rows, width), LOW)]
        tiled = [(shrink_full, 1), (gate_rows, 1), (up_rows, 1)]
        super().__init__([cot], tiled, outs, width // self.wide, 2 * rows * shrink_full.size)

    def compute(self, whole, tiles):
        _, gate_rows, up_rows = tiles
        act_grad = blocks_dot(whole[0], tiles[0])
        sigmoid_gate = jax.nn.sigmoid(gate_rows)
        gate_grad = act_grad * up_rows * sigmoid_gate * (1.0 + gate_rows * (1.0 - sigmoid_gate))
        return gate_grad.astype(LOW), (act_grad * (gate_rows * sigmoid_gate)).astype(LOW)


class WidthJob(Job):
    def __init__(self, lefts, weights, before=None):
        rows, width = lefts[0].shape[0], weights[0].shape[0]
        flops = 2 * rows * sum(weight.size for weight in weights)
        self.own = width // lax.axis_size("tp")
        self.height = rows
        self.before = before
        out = ((rows * lax.axis_size("tp"), self.own), LOW)
        super().__init__(lefts, [(weight, 0) for weight in weights], [out], width // self.wide, flops)

    def out_window(self, index):
        return owner_window(index, self.wide, self.own, self.height)

    def compute(self, whole, tiles):
        total = None
        lefts = list(whole) + (list(self.before.outs_v) if self.before else [])
        for left, weight in zip(lefts, tiles):
            term = contract_cols(left[...], weight)
            total = term if total is None else total + term
        return (total.astype(LOW),)


def owner_window(index, wide, own, height):
    each = own // wide
    rows = pl.ds(pl.multiple_of(index // each * height, 16), height)
    return rows, pl.ds(pl.multiple_of(index % each * wide, 128), wide)


class MixerJob:
    kept = []

    def hold(self, refs):
        self.kept_refs = refs

    def __init__(self, inputs, outs, extra, phases, flops):
        self.inputs = list(inputs)
        self.out_shapes = [jax.ShapeDtypeStruct(shape, dtype) for shape, dtype in outs]
        self.phases = phases
        self.tiles = sum(phases)
        self.flops = flops
        self.scratch = (
            [pltpu.VMEM(array.shape, array.dtype) for array in self.inputs]
            + [pltpu.VMEM(shape, dtype) for shape, dtype in outs]
            + extra
            + [
                pltpu.SemaphoreType.DMA((len(self.inputs),)),
                pltpu.SemaphoreType.DMA((len(outs),)),
            ]
        )

    def bind(self, ins, outs, scratch):
        self.in_refs, self.out_refs = ins, outs
        extra = len(scratch) - len(ins) - len(outs) - 2
        self.ins_v, self.outs_v, self.extra_v = split(scratch, [len(ins), len(outs), extra])
        self.in_sem, self.out_sem = scratch[-2:]
        self.count = lax.axis_size("seq")
        self.seq = lax.axis_index("seq")
        self.column = lax.axis_index("tp")

    def peers(self):
        after = (self.seq + 1) % self.count
        before = (self.seq + self.count - 1) % self.count
        return [(after, self.column), (before, self.column)]

    def load(self, which):
        return pltpu.make_async_copy(self.in_refs[which], self.ins_v[which], self.in_sem.at[which])

    def store(self, which):
        return pltpu.make_async_copy(self.outs_v[which], self.out_refs[which], self.out_sem.at[which])

    def passing(self, source, target, forward):
        step = 1 if forward else self.count - 1
        return pltpu.make_async_remote_copy(
            src_ref=source,
            dst_ref=target,
            send_sem=self.kept_refs[1].at[0],
            recv_sem=self.kept_refs[1].at[1],
            device_id=((self.seq + step) % self.count, self.column),
            device_id_type=MESH,
        )

    def start(self):
        for which in range(len(self.inputs)):
            self.load(which).start()

    def tile(self, index):
        begin = 0
        for phase, tiles in enumerate(self.phases):
            here = index - begin

            @pl.when((here >= 0) & (here < tiles))
            def _(phase=phase, here=here, tiles=tiles):
                @pl.when(here == 0)
                def _():
                    self.before(phase)

                self.work(phase, here)

                @pl.when(here == tiles - 1)
                def _():
                    self.after(phase)

            begin += tiles

    def finish(self):
        for which in range(len(self.out_shapes)):
            self.store(which).wait()


def visible(bound_row, shape):
    position = lax.broadcasted_iota(jnp.int32, shape, 0)
    see_one = position != bound_row
    return position, see_one, see_one & (position - 1 != bound_row)


def lagged(rows, halo, position):
    last, second = halo[15:16].astype(jnp.float32), halo[14:15].astype(jnp.float32)
    one = jnp.where(position == 0, last, pltpu.roll(rows, 1, 0))
    two = jnp.where(position == 0, second, jnp.where(position == 1, last, pltpu.roll(rows, 2, 0)))
    return one, two


class EntryJob(MixerJob):
    then = None

    def __init__(self, tokens, wide, entry_full, exit_full, bound):
        parts, rows, own = tokens.shape
        width, columns = exit_full.shape
        self.rows, self.columns, self.own = rows, columns, own
        self.width = width
        outs = [
            ((rows, 3 * columns), jnp.float32),
            ((rows, columns), jnp.float32),
            ((rows, columns), LOW),
            ((16, columns), LOW),
            ((rows, columns), LOW),
            ((parts, rows, own), LOW),
            ((rows, 128), jnp.float32),
            ((width, rows), LOW),
        ]
        phases = [rows // 256, 3 * columns // 256, 1, columns // 128, width // 256]
        flops = 2 * rows * (entry_full.size + exit_full.size)
        super().__init__([tokens, wide, entry_full, exit_full, bound], outs, [], phases, flops)
        self.kept = [pltpu.VMEM((16, columns), LOW), pltpu.SemaphoreType.DMA((2,))]

    def halo(self):
        return self.passing(self.outs_v[2].at[pl.ds(self.rows - 16, 16)], self.kept_refs[0], True)

    def before(self, phase):
        if phase == 0:
            for which in (0, 1):
                self.load(which).wait()
        if phase == 1:
            self.store(6).start()
            self.store(7).start()
            self.load(2).wait()
        if phase == 3:
            self.load(4).wait()
            self.halo().wait_recv()
            self.outs_v[3][...] = self.kept_refs[0][...]
            self.store(3).start()
        if phase == 4:
            self.load(3).wait()

    def after(self, phase):
        if phase == 1:
            self.store(0).start()
        if phase == 2:
            self.halo().start()
            self.store(2).start()
        if phase == 3:
            self.store(1).start()
            self.store(4).start()
        if phase == 4:
            self.store(5).start()

    def finish(self):
        self.store(5).wait()
        if self.then:
            self.then.start()
        self.halo().wait_send()
        for which in (0, 1, 2, 3, 4, 6, 7):
            self.store(which).wait()

    def work(self, phase, index):
        tokens, wide, entry, exits, bound = self.ins_v
        taps = wide.at[self.column]
        projected, conv, gated, halo, mixer, term, scales, turned_rows = self.outs_v
        columns = self.columns
        if phase == 0:
            rows = pl.ds(pl.multiple_of(index * 256, 256), 256)
            values = [tokens[part, rows, :].astype(jnp.float32) for part in range(tokens.shape[0])]
            total = sum(jnp.sum(value * value, axis=1, keepdims=True) for value in values)
            scale = lax.rsqrt(total / D + EPSILON)
            scales[rows, :] = jnp.broadcast_to(scale, (256, 128))
            for part, value in enumerate(values):
                normed = (value * scale * wide[part, 3:4, :]).astype(LOW)
                tokens[part, rows, :] = normed
                turned_rows[part * self.own : (part + 1) * self.own, rows] = normed.T
        if phase == 1:
            span = pl.ds(pl.multiple_of(index * 256, 256), 256)
            projected[:, span] = blocks_dot(tokens, entry[:, span])
        if phase == 2:
            gated[...] = (projected[:, :columns] * projected[:, 2 * columns :]).astype(LOW)
        if phase == 3:
            span = pl.ds(pl.multiple_of(index * 128, 128), 128)
            middle = pl.ds(pl.multiple_of(columns + index * 128, 128), 128)
            rows = gated[:, span].astype(jnp.float32)
            position, see_one, see_two = visible(bound[0:1, :], rows.shape)
            before = halo[:, span].astype(jnp.float32) * jnp.where(self.seq > 0, 1.0, 0.0)
            one, two = lagged(rows, before, position)
            total = (
                taps[2:3, span] * rows
                + taps[1:2, span] * jnp.where(see_one, one, 0.0)
                + taps[0:1, span] * jnp.where(see_two, two, 0.0)
            )
            conv[:, span] = total
            mixer[:, span] = (projected[:, middle] * total).astype(LOW)
        if phase == 4:
            features = pl.ds(pl.multiple_of(index * 256, 256), 256)
            owner, inner = index // (self.own // 256), index % (self.own // 256)
            span = pl.ds(pl.multiple_of(inner * 256, 256), 256)
            term[owner, :, span] = contract_cols(mixer[...], exits[features, :]).astype(LOW)


class MixerGradJob(MixerJob):
    def __init__(self, branch, exit_full, entry_full, projected, conv, gated, halo, wide, bound):
        parts, rows, own = branch.shape
        width, columns = exit_full.shape
        self.rows, self.columns, self.own = rows, columns, own
        outs = [((rows, 3 * columns), LOW), ((parts * rows, own), LOW), ((8, columns), jnp.float32)]
        extra = [
            pltpu.VMEM((rows, columns), jnp.float32),
            pltpu.VMEM((8, columns), jnp.float32),
        ]
        self.kept = [pltpu.VMEM((8, columns), jnp.float32), pltpu.SemaphoreType.DMA((2,))]
        phases = [columns // 256, 1, columns // 128, width // 256]
        flops = 2 * rows * (entry_full.size + exit_full.size)
        inputs = [branch, exit_full, entry_full, projected, conv, gated, halo, wide, bound]
        super().__init__(inputs, outs, extra, phases, flops)

    def back(self):
        return self.passing(self.extra_v[1], self.kept_refs[0], False)

    def before(self, phase):
        if phase == 0:
            for which in (0, 1, 3, 4):
                self.load(which).wait()
        if phase == 1:
            for which in (7, 8):
                self.load(which).wait()
        if phase == 2:
            for which in (5, 6):
                self.load(which).wait()
            self.back().wait_recv()
        if phase == 3:
            self.load(2).wait()

    def after(self, phase):
        if phase == 1:
            self.back().start()
        if phase == 2:
            self.store(0).start()
            self.store(2).start()
        if phase == 3:
            self.store(1).start()

    def finish(self):
        self.back().wait_send()
        super().finish()

    def work(self, phase, index):
        branch, exits, entry, projected, conv, gated, halo, wide, bound = self.ins_v
        taps = wide.at[self.column]
        grads, term, taps_grad = self.outs_v
        conv_grad, sent = self.extra_v
        returned = self.kept_refs[0]
        columns, height = self.columns, self.rows
        if phase == 0:
            span = pl.ds(pl.multiple_of(index * 256, 256), 256)
            middle = pl.ds(pl.multiple_of(columns + index * 256, 256), 256)
            mixer_grad = blocks_dot(branch, exits[:, span])
            grads[:, middle] = (mixer_grad * conv[:, span]).astype(LOW)
            conv_grad[:, span] = mixer_grad * projected[:, middle]
        if phase == 1:
            for start in range(0, columns, 128):
                span = slice(start, start + 128)
                rows = conv_grad[0:8, span]
                position, see_one, see_two = visible(bound[0:1, :], rows.shape)
                one = pltpu.roll(jnp.where(see_one, rows, 0.0) * taps[1:2, span], 1, 0)
                two = jnp.where(see_two, rows, 0.0) * taps[0:1, span]
                sent[:, span] = two + jnp.where(position == 0, 0.0, one)
            taps_grad[...] = jnp.zeros_like(taps_grad)
        if phase == 2:
            span = pl.ds(pl.multiple_of(index * 128, 128), 128)
            last = pl.ds(pl.multiple_of(2 * columns + index * 128, 128), 128)
            rows = conv_grad[:, span]
            position, see_one, see_two = visible(bound[0:1, :], rows.shape)
            seen_one, seen_two = jnp.where(see_one, rows, 0.0), jnp.where(see_two, rows, 0.0)
            one = pltpu.roll(seen_one * taps[1:2, span], height - 1, 0)
            two = pltpu.roll(seen_two * taps[0:1, span], height - 2, 0)
            after = returned[:, span] * jnp.where(self.seq < self.count - 1, 1.0, 0.0)
            gated_grad = (
                rows * taps[2:3, span]
                + jnp.where(position == height - 1, after[1:2], one)
                + jnp.where(position < height - 2, two, jnp.where(position == height - 2, after[0:1], 0.0))
            )
            grads[:, span] = (gated_grad * projected[:, last]).astype(LOW)
            grads[:, last] = (gated_grad * projected[:, span]).astype(LOW)
            own_rows = gated[:, span].astype(jnp.float32)
            before = halo[:, span].astype(jnp.float32) * jnp.where(self.seq > 0, 1.0, 0.0)
            lag_one, lag_two = lagged(own_rows, before, position)
            taps_grad[0:1, span] = jnp.sum(seen_two * lag_two, axis=0, keepdims=True)
            taps_grad[1:2, span] = jnp.sum(seen_one * lag_one, axis=0, keepdims=True)
            taps_grad[2:3, span] = jnp.sum(rows * own_rows, axis=0, keepdims=True)
        if phase == 3:
            features = pl.ds(pl.multiple_of(index * 256, 256), 256)
            window = owner_window(index, 256, self.own, height)
            term[window] = contract_cols(grads[...], entry[features, :]).astype(LOW)


class Jobs:
    def __init__(self, *jobs):
        self.jobs = jobs
        self.inputs = [item for job in jobs for item in job.inputs]
        self.out_shapes = [item for job in jobs for item in job.out_shapes]
        self.scratch = [item for job in jobs for item in job.scratch]
        self.kept = [item for job in jobs for item in job.kept]
        self.tiles = sum(job.tiles for job in jobs)
        self.flops = sum(job.flops for job in jobs)

    def hold(self, refs):
        for job, own in zip(self.jobs, split(refs, [len(job.kept) for job in self.jobs])):
            job.hold(own)

    def bind(self, ins, outs, scratch):
        groups = zip(
            self.jobs,
            split(ins, [len(job.inputs) for job in self.jobs]),
            split(outs, [len(job.out_shapes) for job in self.jobs]),
            split(scratch, [len(job.scratch) for job in self.jobs]),
        )
        for job, own_ins, own_outs, own_scratch in groups:
            job.bind(own_ins, own_outs, own_scratch)

    def peers(self):
        return [peer for job in self.jobs for peer in job.peers()]

    def start(self):
        for job in self.jobs:
            job.start()

    def tile(self, index):
        begin = 0
        for job in self.jobs:
            here = index - begin

            @pl.when((here >= 0) & (here < job.tiles))
            def _(job=job, here=here):
                job.tile(here)

            begin += job.tiles

    def finish(self):
        for job in self.jobs:
            job.finish()


class TurnJob(MixerJob):
    def __init__(self, blocks):
        parts, rows, own = blocks.shape
        super().__init__([blocks], [((parts * own, rows), blocks.dtype)], [], [rows // 128], 0)

    def peers(self):
        return []

    def before(self, phase):
        self.load(0).wait()

    def after(self, phase):
        self.store(0).start()

    def work(self, phase, index):
        (blocks,), (target,) = self.ins_v, self.outs_v
        parts, _, own = blocks.shape
        rows = pl.ds(pl.multiple_of(index * 128, 128), 128)
        for part in range(parts):
            target[part * own : (part + 1) * own, rows] = blocks[part, rows, :].T


class CastJob(MixerJob):
    def __init__(self, pairs, plain):
        rows, columns = plain.shape
        lanes = pairs.shape[1]
        self.rows, self.half, self.lanes = rows, columns // 2, lanes
        self.block = max(rows // 8, 16)
        outs = [((rows, columns // 2), LOW)] * 6
        super().__init__([pairs, plain], outs, [], [rows // self.block], 0)

    def peers(self):
        return []

    def before(self, phase):
        for which in range(2):
            self.load(which).wait()

    def after(self, phase):
        for which in range(6):
            self.store(which).start()

    def work(self, phase, index):
        pairs, plain = self.ins_v
        block, half, lanes = self.block, self.half, self.lanes
        tiles = half // lanes
        rows = pl.ds(pl.multiple_of(index * block, 16), block)
        start = index * (block * 4 * tiles)
        for which in range(4):
            side, plane = which // 2, which % 2
            for tile in range(tiles):
                place = (side * tiles + tile) * 2 + plane
                picked = pairs[pl.ds(start + place, block, stride=4 * tiles), :]
                self.outs_v[which][rows, tile * lanes : (tile + 1) * lanes] = picked.astype(LOW)
        for side in range(2):
            self.outs_v[4 + side][rows, :] = plain[rows, side * half : (side + 1) * half].astype(LOW)


class SmallGatherJob:
    tiles, flops = 1, 0

    def __init__(self, own, seen):
        self.inputs = [own]
        self.seen = seen
        devices, columns = lax.axis_size("seq"), lax.axis_size("tp")
        wide = (columns, 8, devices * seen)
        self.out_shapes = [jax.ShapeDtypeStruct(wide, jnp.float32)]
        self.scratch = [pltpu.VMEM(wide, jnp.float32), pltpu.SemaphoreType.DMA((2,))]
        self.kept = [
            pltpu.VMEM((devices, columns) + own.shape, own.dtype),
            pltpu.SemaphoreType.DMA((columns,)),
            pltpu.SemaphoreType.DMA((columns,)),
            pltpu.SemaphoreType.DMA((devices,)),
            pltpu.SemaphoreType.DMA((devices,)),
        ]

    def hold(self, refs):
        self.whole, self.near_send, self.near_recv, self.far_send, self.far_recv = refs
        self.devices, self.columns = lax.axis_size("seq"), lax.axis_size("tp")
        self.seq, self.column = lax.axis_index("seq"), lax.axis_index("tp")

    def bind(self, ins, outs, scratch):
        self.source, self.target = ins[0], outs[0]
        self.wide, self.local_sem = scratch

    def peers(self):
        near = [(self.seq, (self.column + step) % self.columns) for step in range(1, self.columns)]
        far = [((self.seq + step) % self.devices, self.column) for step in range(1, self.devices)]
        return near + far

    def near(self, step):
        piece = self.whole.at[self.seq, self.column]
        return pltpu.make_async_remote_copy(
            src_ref=piece,
            dst_ref=piece,
            send_sem=self.near_send.at[step],
            recv_sem=self.near_recv.at[step],
            device_id=(self.seq, (self.column + step) % self.columns),
            device_id_type=MESH,
        )

    def far(self, step):
        piece = self.whole.at[self.seq]
        return pltpu.make_async_remote_copy(
            src_ref=piece,
            dst_ref=piece,
            send_sem=self.far_send.at[step],
            recv_sem=self.far_recv.at[step],
            device_id=((self.seq + step) % self.devices, self.column),
            device_id_type=MESH,
        )

    def start(self):
        load = pltpu.make_async_copy(self.source, self.whole.at[self.seq, self.column], self.local_sem.at[0])
        load.start()
        load.wait()
        for step in range(1, self.columns):
            self.near(step).start()

    def tile(self, index):
        for step in range(1, self.columns):
            self.near(step).wait()

        def begin(step, carry):
            self.far(step).start()
            return carry

        lax.fori_loop(1, self.devices, begin, 0)

    def finish(self):
        def end(step, carry):
            self.far(step).wait()
            return carry

        lax.fori_loop(1, self.devices, end, 0)
        each = LANES // self.seen
        for column in range(self.columns):
            for start in range(0, self.devices, each):
                total = None
                for inner in range(each):
                    piece = self.whole[start + inner, column, :, :].astype(jnp.float32)[:8]
                    piece = pltpu.roll(piece, inner * self.seen, 1) if inner else piece
                    total = piece if total is None else total + piece
                self.wide[column, :, start * self.seen : start * self.seen + LANES] = total
        store = pltpu.make_async_copy(self.wide, self.target, self.local_sem.at[1])
        store.start()
        store.wait()


class RowSumJob(MixerJob):
    block = 128

    def __init__(self, inputs, outs, extra, rows, flops):
        self.columns = lax.axis_size("tp")
        blocks = rows // self.block
        self.kept = [
            pltpu.VMEM((self.columns, blocks, self.block), jnp.float32),
            pltpu.SemaphoreType.DMA((self.columns,)),
            pltpu.SemaphoreType.DMA((self.columns,)),
        ]
        totals = pltpu.VMEM((blocks, self.block), jnp.float32)
        super().__init__(inputs, outs, [totals] + extra, [blocks, 1, blocks], flops)

    def peers(self):
        return [(self.seq, (self.column + step) % self.columns) for step in range(1, self.columns)]

    def share(self, step):
        return pltpu.make_async_remote_copy(
            src_ref=self.kept_refs[0].at[0],
            dst_ref=self.kept_refs[0].at[step],
            send_sem=self.kept_refs[1].at[step],
            recv_sem=self.kept_refs[2].at[step],
            device_id=(self.seq, (self.column + step) % self.columns),
            device_id_type=MESH,
        )

    def before(self, phase):
        if phase == 0:
            for which in range(len(self.inputs)):
                self.load(which).wait()

    def after(self, phase):
        if phase == 0:
            for step in range(1, self.columns):
                self.share(step).start()
        if phase == 2:
            for which in range(len(self.out_shapes)):
                self.store(which).start()

    def finish(self):
        for step in range(1, self.columns):
            self.share(step).wait_send()
        super().finish()

    def work(self, phase, index):
        block = self.block
        slots, totals = self.kept_refs[0], self.extra_v[0]
        rows = pl.ds(pl.multiple_of(index * block, block), block)
        if phase == 0:
            part = jnp.sum(self.values(rows), axis=1, keepdims=True)
            slots[0, pl.ds(index, 1), :] = jnp.broadcast_to(part, (block, block)).T[0:1, :]
        if phase == 1:
            for step in range(1, self.columns):
                self.share(step).wait_recv()
            totals[...] = sum(slots[step] for step in range(self.columns))
        if phase == 2:
            self.use(rows, jnp.broadcast_to(totals[pl.ds(index, 1), :], (block, block)).T)


class NormJob(RowSumJob):
    then = None

    def __init__(self, rows_in, terms, wide):
        rows, own = rows_in.shape
        outs = [((rows, own), jnp.float32), ((rows, own), LOW), ((rows, 128), jnp.float32)]
        super().__init__([rows_in, terms, wide], outs, [], rows, 0)

    def values(self, rows):
        rows_in, terms, _ = self.ins_v
        residual = sum(terms[part, rows, :].astype(jnp.float32) for part in range(self.columns))
        residual = rows_in[rows, :].astype(jnp.float32) + residual
        self.outs_v[0][rows, :] = residual
        return residual * residual

    def use(self, rows, total):
        residual, normed, scales = self.outs_v
        scale = lax.rsqrt(total / D + EPSILON)
        scales[rows, :] = scale
        gain = self.ins_v[2].at[self.column]
        normed[rows, :] = (residual[rows, :] * scale[:, 0:1] * gain[4:5, :]).astype(LOW)

    def finish(self):
        self.store(1).wait()
        if self.then:
            self.then.start()
        for step in range(1, self.columns):
            self.share(step).wait_send()
        for which in (0, 2):
            self.store(which).wait()


class NormBackJob(RowSumJob):
    def __init__(self, grad, kept, scales, wide, row, base, rounded):
        rows, own = grad.shape
        outs = [((rows, own), jnp.float32), ((8, own), jnp.float32)]
        outs = outs + [((rows, own), LOW)] if rounded else outs
        self.row = row
        super().__init__([grad, kept, scales, wide, base], outs, [], rows, 0)

    def parts(self, rows):
        grad, kept, scales, wide, base = self.ins_v
        gain = wide.at[self.column]
        return (
            grad[rows, :].astype(jnp.float32),
            kept[rows, :].astype(jnp.float32),
            scales[rows, 0:1],
            gain[self.row : self.row + 1, :],
        )

    def before(self, phase):
        super().before(phase)
        if phase == 0:
            self.outs_v[1][...] = jnp.zeros_like(self.outs_v[1])

    def values(self, rows):
        grad, kept, scale, gain = self.parts(rows)
        product = grad * kept
        self.outs_v[1][0:1, :] += jnp.sum(product * scale, axis=0, keepdims=True)
        return product * gain

    def use(self, rows, total):
        grad, kept, scale, gain = self.parts(rows)
        rows_grad = scale * gain * grad - kept * (scale * scale * scale * total[:, 0:1] / D)
        result = self.ins_v[4][rows, :].astype(jnp.float32) + rows_grad
        self.outs_v[0][rows, :] = result
        if len(self.outs_v) > 2:
            self.outs_v[2][rows, :] = result.astype(LOW)


class SmallSumJob:
    tiles, flops = 1, 0

    def __init__(self, taps_grad, gain_grad, before):
        count = lax.axis_size("seq")
        self.inputs = [taps_grad, gain_grad]
        shape = taps_grad.shape
        self.before = before
        self.out_shapes = [jax.ShapeDtypeStruct(shape, jnp.float32)]
        self.scratch = [pltpu.VMEM(shape, jnp.float32)] * 3 + [pltpu.SemaphoreType.DMA((3,))]
        self.kept = [
            pltpu.VMEM((count,) + shape, jnp.float32),
            pltpu.SemaphoreType.DMA((count,)),
            pltpu.SemaphoreType.DMA((count,)),
        ]

    def hold(self, refs):
        self.slots, self.send_sem, self.recv_sem = refs

    def bind(self, ins, outs, scratch):
        self.sources, self.target = ins, outs[0]
        self.taps, self.gain, self.total, self.local_sem = scratch
        self.count = lax.axis_size("seq")
        self.seq = lax.axis_index("seq")
        self.column = lax.axis_index("tp")

    def peers(self):
        return [((self.seq + far) % self.count, self.column) for far in range(1, self.count)]

    def copy(self, far):
        return pltpu.make_async_remote_copy(
            src_ref=self.slots.at[0],
            dst_ref=self.slots.at[far],
            send_sem=self.send_sem.at[far],
            recv_sem=self.recv_sem.at[far],
            device_id=((self.seq + far) % self.count, self.column),
            device_id_type=MESH,
        )

    def loads(self):
        return [
            pltpu.make_async_copy(self.sources[which], (self.taps, self.gain)[which], self.local_sem.at[which])
            for which in range(2)
        ]

    def start(self):
        for load in self.loads():
            load.start()

    def tile(self, index):
        for load in self.loads():
            load.wait()
        self.slots[0, 0:3, :] = self.taps[0:3, :]
        self.slots[0, 3:4, :] = self.before.outs_v[1][0:1, :]
        self.slots[0, 4:5, :] = self.gain[0:1, :]
        self.slots[0, 5:8, :] = jnp.zeros_like(self.slots[0, 5:8, :])

        def begin(far, carry):
            self.copy(far).start()
            return carry

        lax.fori_loop(1, self.count, begin, 0)

    def finish(self):
        self.total[...] = self.slots[0]

        def add(far, carry):
            self.copy(far).wait_recv()
            self.total[...] += self.slots[far]
            return carry

        lax.fori_loop(1, self.count, add, 0)
        store = pltpu.make_async_copy(self.total, self.target, self.local_sem.at[2])
        store.start()

        def sent(far, carry):
            self.copy(far).wait_send()
            return carry

        lax.fori_loop(1, self.count, sent, 0)
        store.wait()


def with_ticks(job, ticks, tick, rest=None, ready=None):
    rest = max(ticks // 6, 1) if rest is None else ticks * rest // 12
    active = ticks - rest
    each = -(-job.tiles // active)

    def step(index, carry):
        late = index - rest
        if ready:
            pl.when(late == -1)(ready)

        first, after = late * job.tiles // active, (late + 1) * job.tiles // active
        for inner in range(each):
            tile = first + inner

            @pl.when((late >= 0) & (tile < after))
            def _(tile=tile):
                job.tile(tile)

        tick(index)
        return carry

    lax.fori_loop(0, ticks, step, 0)


def ring_kernel(ring, job, *refs):
    parts = (ring.inputs, job.inputs, ring.out_shapes, job.out_shapes, ring.scratch, job.scratch, job.kept)
    ring_in, job_in, ring_out, job_out, ring_scratch, job_scratch, job_kept = split(refs, [len(part) for part in parts])
    ring.bind(ring_in, ring_out, ring_scratch)
    job.hold(job_kept)
    job.bind(job_in, job_out, job_scratch)
    ring.prepare()
    greet(ring.peers() + job.peers())
    ring.start()
    job.start()
    with_ticks(job, ring.ticks, ring.tick)
    ring.finish()
    job.finish()


def run_forward(arrays, seen):
    count, columns = lax.axis_size("seq"), lax.axis_size("tp")
    shapes = {name: jax.ShapeDtypeStruct(array.shape, array.dtype) for name, array in arrays.items()}
    inputs = list(shapes)
    sections = []

    def define(name, shape, dtype):
        shapes[name] = jax.ShapeDtypeStruct(shape, dtype)

    def add(job, ins, outs):
        for name, shape in zip(outs, job.out_shapes):
            shapes[name] = shape
        return job, ins, outs

    def flat_of(full):
        shape = shapes[full].shape
        return jax.ShapeDtypeStruct((shape[0] * shape[1], shape[2]), LOW)

    rows, own = arrays["tokens"].shape
    for name in ("tokens_blocks", "cot_blocks", "branch_terms", "normed_blocks"):
        define(name, (columns, rows, own), LOW)
    low = ["gate_low0", "up_low0", "gate_low1", "up_low1", "shrink_low0", "shrink_low1"]
    small_job = SmallGatherJob(shapes["small"], seen)
    cast_job = CastJob(shapes["pairs"], shapes["shrink"])
    first = [add(small_job, ["small"], ["wide"]), add(cast_job, ["pairs", "shrink"], low)]
    groups = [[("entry_low", "entry_full"), ("exit_low", "exit_full")]]
    groups += [[(name, name.replace("low", "full"))] for name in low]
    for group in groups:
        for shard, full in group:
            define(full, (count,) + shapes[shard].shape, LOW)
    ring = GatherRing(groups, shapes)
    tokens_sent = PeerCopies("tokens", "tokens_blocks")
    cot_sent = PeerCopies("cotangent", "cot_blocks")
    branch_sent = PeerCopies("term", "branch_terms")
    normed_sent = PeerCopies("normed_own", "normed_blocks")
    exchanges = [tokens_sent, cot_sent, branch_sent, normed_sent]

    entry_job = EntryJob(
        shapes["tokens_blocks"], shapes["wide"], flat_of("entry_full"), flat_of("exit_full"), shapes["bound"]
    )
    entry_job.then = branch_sent
    entry_outs = ["projected", "conv_out", "gated", "halo", "mixer", "term", "scale_one", "normed_one"]
    norm_job = NormJob(shapes["tokens"], shapes["branch_terms"], shapes["wide"])
    norm_job.then = normed_sent
    turn_cot = add(TurnJob(shapes["cot_blocks"]), ["cot_blocks"], ["cot_full"])
    expands = []
    for half in "01":
        job = ExpandJob(shapes["normed_blocks"], flat_of("gate_full" + half), flat_of("up_full" + half))
        names = ["normed_blocks", "gate_full" + half, "up_full" + half]
        expands.append(add(job, names, ["gate_rows" + half, "up_rows" + half, "activation" + half]))
    hidden_job = HiddenGradJob(shapes["cot_blocks"], flat_of("shrink_full0"), shapes["gate_rows0"], shapes["up_rows0"])
    hidden = add(hidden_job, ["cot_blocks", "shrink_full0", "gate_rows0", "up_rows0"], ["gate_grad0", "up_grad0"])
    turn_normed = add(TurnJob(shapes["normed_blocks"]), ["normed_blocks"], ["normed_two"])
    entry = add(entry_job, ["tokens_blocks", "wide", "entry_full", "exit_full", "bound"], entry_outs)
    norm = add(norm_job, ["tokens", "branch_terms", "wide"], ["residual", "normed_own", "scale_two"])
    rests = [2, 1, 2, 4, 2, 4, 2]
    sections = [
        (first, []),
        ([entry], [tokens_sent]),
        ([turn_cot], [cot_sent]),
        ([norm], [branch_sent]),
        ([], []),
        (expands, [normed_sent]),
        ([hidden, turn_normed], []),
    ]
    outputs = [name for name in shapes if name not in inputs]
    together = [Jobs(*[job for job, _, _ in jobs]) for jobs, _ in sections]
    kept = [item for jobs in together for item in jobs.kept]
    exchange_scratch = [item for exchange in exchanges for item in exchange.scratch]
    weights_full = {full for group in groups for _, full in group}

    def kernel(*all_refs):
        in_refs, out_refs, ring_scratch, sems, kept_refs = split(
            all_refs, [len(inputs), len(outputs), len(ring.scratch), len(exchange_scratch), len(kept)]
        )
        refs = dict(zip(inputs + outputs, in_refs + out_refs))
        ring.bind(refs, ring_scratch)
        for place, exchange in enumerate(exchanges):
            exchange.bind(refs, sems[2 * place : 2 * place + 2])
        for jobs, own in zip(together, split(kept_refs, [len(jobs.kept) for jobs in together])):
            jobs.hold(own)
        greet(small_job.peers())
        ring.begin(0)
        tokens_sent.start()
        for group, (jobs, waits) in enumerate(sections):
            job_ins = [rows_of(refs[name], name in weights_full) for _, ins, _ in jobs for name in ins]
            job_outs = [refs[name] for _, _, outs in jobs for name in outs]

            work = together[group]

            def ready():
                for exchange in waits:
                    exchange.wait()
                work.start()

            def section(*scratch):
                work.bind(job_ins, job_outs, list(scratch))
                if not waits:
                    work.start()
                tick = functools.partial(ring.tick, group)
                with_ticks(work, ring.ticks, tick, rests[group], ready if waits else None)
                if group == 0:
                    work.finish()
                    cot_sent.start()
                if group + 1 < len(sections):
                    ring.begin(group + 1)
                if group > 0:
                    work.finish()

            pl.run_scoped(section, *work.scratch)
            ring.settle(group)
        ring.finish()
        for exchange in exchanges:
            exchange.finish()

    flops = sum(job.flops for jobs, _ in sections for job, _, _ in jobs)
    results = pl.pallas_call(
        kernel,
        out_shape=[shapes[name] for name in outputs],
        in_specs=[pl.BlockSpec(memory_space=pl.ANY)] * len(inputs),
        out_specs=[pl.BlockSpec(memory_space=pl.ANY)] * len(outputs),
        scratch_shapes=ring.scratch + exchange_scratch + kept,
        compiler_params=pltpu.CompilerParams(
            collective_id=0, has_side_effects=True, vmem_limit_bytes=VMEM_BYTES
        ),
        cost_estimate=pl.CostEstimate(flops=flops, bytes_accessed=10**9, transcendentals=0),
        name="forward",
    )(*arrays.values())
    named = dict(zip(outputs, results))
    return {name: flat(array) if name in weights_full else array for name, array in named.items()}


def rows_of(ref, gathered):
    if not gathered:
        return ref
    count, rows, columns = ref.shape
    return ref.reshape(count * rows, columns)


def run_ring(ring, job, collective):
    inputs = ring.inputs + job.inputs
    outs = ring.out_shapes + job.out_shapes
    return pl.pallas_call(
        functools.partial(ring_kernel, ring, job),
        out_shape=outs,
        in_specs=[pl.BlockSpec(memory_space=pl.ANY)] * len(inputs),
        out_specs=[pl.BlockSpec(memory_space=pl.ANY)] * len(outs),
        scratch_shapes=ring.scratch + job.scratch + job.kept,
        compiler_params=pltpu.CompilerParams(
            collective_id=collective, has_side_effects=True, vmem_limit_bytes=VMEM_BYTES
        ),
        cost_estimate=pl.CostEstimate(flops=ring.flops + job.flops, bytes_accessed=ring.bytes, transcendentals=0),
        name=ring.name,
    )(*inputs)


def flat(full):
    return full.reshape(full.shape[0] * full.shape[1], full.shape[2])


def contract_rows(left, right):
    return lax.dot_general(
        left, right, (((0,), (0,)), ((), ())), preferred_element_type=jnp.float32
    )


def contract_cols(left, right):
    return lax.dot_general(
        left, right, (((1,), (1,)), ((), ())), preferred_element_type=jnp.float32
    )


def tie(*values):
    return lax.optimization_barrier(values)


def gather_rows(own):
    return lax.all_gather(own, "tp", axis=0, tiled=True)


def gather_blocks(own):
    return gather_rows(own).reshape(-1, *own.shape)


def reduce_branch(term):
    return lax.psum_scatter(term, "tp", scatter_dimension=0, tiled=True)


def adam_update(weight, first, second, grad, rate, decay):
    first_next = BETA_ONE * first + (1.0 - BETA_ONE) * grad
    second_next = BETA_TWO * second + (1.0 - BETA_TWO) * grad * grad
    corrected = first_next / (1.0 - BETA_ONE**STEP)
    spread = jnp.sqrt(second_next / (1.0 - BETA_TWO**STEP)) + ADAM_EPSILON
    return (weight - rate * (corrected / spread + decay * weight), first_next, second_next)


def adam_kernel(pieces, *refs):
    weight, first, second = refs[:3]
    grads, outs = refs[3 : 3 + pieces], refs[3 + pieces :]
    start = 0
    for grad in grads:
        span = slice(start, start + grad.shape[1])
        start += grad.shape[1]
        results = adam_update(weight[:, span], first[:, span], second[:, span], grad[...], RATE_WIDE, WEIGHT_DECAY)
        for out, result in zip(outs, results):
            out[:, span] = result


def adam_rows(weight, first, second, grads, planes=1):
    rows, columns = weight.shape[0] // planes, weight.shape[1]
    block = max(rows // 8, 8) if columns > 1024 else max(rows // 2, 8)
    steps = rows // block
    state = pl.BlockSpec((block, columns), lambda plane, step: (plane * steps + step, 0))
    grad_specs = [
        pl.BlockSpec((block, grad.shape[1] // planes), lambda plane, step: (step, plane)) for grad in grads
    ]
    return pl.pallas_call(
        functools.partial(adam_kernel, len(grads)),
        out_shape=[jax.ShapeDtypeStruct(weight.shape, weight.dtype)] * 3,
        grid=(planes, steps),
        in_specs=[state] * 3 + grad_specs,
        out_specs=[state] * 3,
        cost_estimate=pl.CostEstimate(flops=20 * weight.size, bytes_accessed=28 * weight.size, transcendentals=0),
        name="adam_rows",
    )(weight, first, second, *grads)


def adam_pairs_kernel(lanes, *refs):
    weight, first, second = refs[:3]
    grads, outs, mixed = refs[3:7], refs[7:10], refs[10]
    rows = grads[0].shape[0]
    tiles = grads[0].shape[1] // lanes
    for which, grad in enumerate(grads):
        half, side = which // 2, which % 2
        for tile in range(tiles):
            place = (half * tiles + tile) * 2 + side
            mixed[pl.ds(place, rows, stride=4 * tiles), :] = grad[:, tile * lanes : (tile + 1) * lanes]
    results = adam_update(weight[...], first[...], second[...], mixed[...], RATE_WIDE, WEIGHT_DECAY)
    for out, result in zip(outs, results):
        out[...] = result


def paired(array):
    rows, _, columns = array.shape
    return array.reshape(rows, 2, columns // LANES, LANES).transpose(0, 2, 1, 3).reshape(-1, LANES)


def adam_pairs(weight, first, second, grads):
    rows, _, columns = weight.shape
    deep = columns // LANES
    block = max(rows // 8, 8)
    state = pl.BlockSpec((block * deep * 2, LANES), lambda step: (step, 0))
    results = pl.pallas_call(
        functools.partial(adam_pairs_kernel, LANES),
        out_shape=[jax.ShapeDtypeStruct((rows * deep * 2, LANES), weight.dtype)] * 3,
        grid=(rows // block,),
        in_specs=[state] * 3 + [pl.BlockSpec((block, columns // 2), lambda step: (step, 0))] * 4,
        out_specs=[state] * 3,
        scratch_shapes=[pltpu.VMEM((block * deep * 2, LANES), jnp.float32)],
        cost_estimate=pl.CostEstimate(flops=20 * weight.size, bytes_accessed=28 * weight.size, transcendentals=0),
        name="adam_pairs",
    )(paired(weight), paired(first), paired(second), *grads)
    return [
        result.reshape(rows, deep, 2, LANES).transpose(0, 2, 1, 3).reshape(rows, 2, columns) for result in results
    ]


def adam_planes(weight, first, second, grad):
    rows, planes, columns = weight.shape

    def seen(array):
        return array.transpose(1, 0, 2).reshape(planes * rows, columns)

    results = adam_rows(seen(weight), seen(first), seen(second), [grad], planes)
    return [result.reshape(planes, rows, columns).transpose(1, 0, 2) for result in results]


def shards(
    tokens,
    bounds,
    cotangent,
    entry_weight,
    entry_first,
    entry_second,
    exit_weight,
    exit_first,
    exit_second,
    expand_weight,
    expand_first,
    expand_second,
    shrink_weight,
    shrink_first,
    shrink_second,
    conv_kernel,
    conv_first,
    conv_second,
    norm_gains,
    gain_first,
    gain_second,
):
    channels = tokens.shape[1]
    idle = NoJob()
    seen = conv_kernel.shape[1]
    small = jnp.concatenate([conv_kernel, norm_gains], axis=0)
    small = jnp.pad(small, ((0, 16 - small.shape[0]), (0, LANES - seen))).astype(LOW)
    entry_low = entry_weight.reshape(entry_weight.shape[0], 3 * channels).astype(LOW)
    bound = jnp.broadcast_to(bounds[0], (8, 128))
    made = run_forward(
        {
            "entry_low": entry_low,
            "exit_low": exit_weight.astype(LOW),
            "small": small,
            "tokens": tokens,
            "cotangent": cotangent,
            "bound": bound,
            "pairs": paired(expand_weight),
            "shrink": shrink_weight,
        },
        seen,
    )
    entry_full, exit_full, wide = made["entry_full"], made["exit_full"], made["wide"]
    gate_full, up_full, shrink_full, activation, gate_rows, up_rows = (
        [made[name + half] for half in "01"]
        for name in ("gate_full", "up_full", "shrink_full", "activation", "gate_rows", "up_rows")
    )
    cot_blocks, cot_full, normed_one, normed_two = (
        made[name] for name in ("cot_blocks", "cot_full", "normed_one", "normed_two")
    )
    residual, scale_one, scale_two = made["residual"], made["scale_one"], made["scale_two"]
    gate_grad_one, up_grad_one = made["gate_grad0"], made["up_grad0"]
    shrink_part, gate_part, up_part = [None] * 2, [None] * 2, [None] * 2
    hidden = HiddenGradJob(cot_blocks, shrink_full[1], gate_rows[1], up_rows[1])
    width = WidthJob([gate_grad_one, up_grad_one], [gate_full[0], up_full[0], gate_full[1], up_full[1]], hidden)
    shrink_part[0], gate_grad_two, up_grad_two, two_term = run_ring(
        ScatterRing([(cot_full, activation[0])]), Jobs(hidden, width), 7
    )
    gate_grad, up_grad = [gate_grad_one, gate_grad_two], [up_grad_one, up_grad_two]
    shrink_part[1], mixed_term = run_ring(
        ScatterRing([(cot_full, activation[1])]), WidthJob(activation, shrink_full), 8
    )
    grad_normed_two, shrink_part[1], mixed_term = tie(reduce_branch(two_term), shrink_part[1], mixed_term)
    gate_part[0], residual_grad, gain_two_grad, branch_own = run_ring(
        ScatterRing([(normed_two, gate_grad[0])]),
        NormBackJob(grad_normed_two, residual, scale_two, wide, 4, cotangent, True),
        9,
    )
    mixed_branch, branch_own, up_grad[0] = tie(reduce_branch(mixed_term), branch_own, up_grad[0])
    (up_part[0],) = run_ring(ScatterRing([(normed_two, up_grad[0])]), idle, 10)
    branch_blocks, up_part[0] = tie(gather_blocks(branch_own), up_part[0])
    gate_part[1], projected_grad, one_term, taps_grad = run_ring(
        ScatterRing([(normed_two, gate_grad[1])]),
        MixerGradJob(
            branch_blocks,
            exit_full,
            entry_full,
            made["projected"],
            made["conv_out"],
            made["gated"],
            made["halo"],
            wide,
            bound,
        ),
        11,
    )
    one_term, up_grad[1], gate_part[1] = tie(one_term, up_grad[1], gate_part[1])
    up_part[1], branch_full = run_ring(ScatterRing([(normed_two, up_grad[1])]), TurnJob(branch_blocks), 12)
    grad_normed_one, up_part[1] = tie(reduce_branch(one_term), up_part[1])
    back = NormBackJob(grad_normed_one, tokens, scale_one, wide, 3, residual_grad, False)
    entry_part, exit_part, tokens_grad, _, small_part = run_ring(
        ScatterRing([(normed_one, projected_grad), (branch_full, made["mixer"])]),
        Jobs(back, SmallSumJob(taps_grad, gain_two_grad, back)),
        13,
    )
    mixed = (residual + mixed_branch.astype(jnp.float32)).astype(LOW)
    small_part = lax.dynamic_slice_in_dim(small_part, lax.axis_index("seq") * seen, seen, axis=1)
    kernel_part = small_part[:3]
    gains_part = small_part[3:5]
    entry_next, entry_first_next, entry_second_next = adam_planes(
        entry_weight, entry_first, entry_second, entry_part
    )
    exit_next, exit_first_next, exit_second_next = adam_rows(exit_weight, exit_first, exit_second, [exit_part])
    expand_next, expand_first_next, expand_second_next = adam_pairs(
        expand_weight, expand_first, expand_second, [gate_part[0], up_part[0], gate_part[1], up_part[1]]
    )
    shrink_next, shrink_first_next, shrink_second_next = adam_rows(
        shrink_weight, shrink_first, shrink_second, shrink_part
    )
    conv_next, conv_first_next, conv_second_next = adam_update(
        conv_kernel, conv_first, conv_second, kernel_part, RATE_CONV, 0.0
    )
    gains_next, gains_first_next, gains_second_next = adam_update(
        norm_gains, gain_first, gain_second, gains_part, RATE_GAIN, 0.0
    )
    return (
        mixed,
        tokens_grad,
        entry_next,
        entry_first_next,
        entry_second_next,
        exit_next,
        exit_first_next,
        exit_second_next,
        expand_next,
        expand_first_next,
        expand_second_next,
        shrink_next,
        shrink_first_next,
        shrink_second_next,
        conv_next,
        conv_first_next,
        conv_second_next,
        gains_next,
        gains_first_next,
        gains_second_next,
    )


def solution(mesh):
    rows = P("seq", "tp")
    stacked = P("seq", None, "tp")
    small = P(None, ("tp", "seq"))
    return jax.shard_map(
        shards,
        mesh=mesh,
        in_specs=(rows, P("seq"), rows) + (stacked,) * 3 + (rows,) * 3 + (stacked,) * 3 + (rows,) * 3 + (small,) * 6,
        out_specs=(rows, rows) + (stacked,) * 3 + (rows,) * 3 + (stacked,) * 3 + (rows,) * 3 + (small,) * 6,
        check_vma=False,
    )
```

```python
import functools

import jax
import jax.numpy as jnp
from jax import lax
from jax.experimental import pallas as pl
from jax.experimental.pallas import tpu as pltpu
from jax.sharding import PartitionSpec as P

D = 2048
STEP = 10


EPSILON = 1e-05
BETA_ONE = 0.9
BETA_TWO = 0.95
ADAM_EPSILON = 1e-08
WEIGHT_DECAY = 0.1
RATE_WIDE = 0.04
RATE_CONV = 0.5
RATE_GAIN = 0.4

MESH = pl.DeviceIdType.MESH
LOW = jnp.bfloat16
LANES = 128
VMEM_BYTES = 60 * 1024 * 1024


def ring_place(index, count):
    side = index % 2
    level = index // 2
    return level * (1 - side) + (count - 1 - level) * side


def ring_index(place, count):
    back = place // (count // 2)
    return (1 - back) * (2 * place) + back * (2 * (count - 1 - place) + 1)


def ring_ends(count):
    place = ring_place(lax.axis_index("seq"), count)
    ahead = ring_index((place + 1) % count, count)
    behind = ring_index((place + count - 1) % count, count)
    return place, ahead, behind


def greet(peers):
    barrier = pltpu.get_barrier_semaphore()
    for peer in peers:
        pl.semaphore_signal(barrier, inc=1, device_id=peer, device_id_type=MESH)
    pl.semaphore_wait(barrier, len(peers))


def split(items, sizes):
    parts, start = [], 0
    for size in sizes:
        parts.append(items[start : start + size])
        start += size
    return parts


class GatherRing:
    def __init__(self, groups, shapes):
        self.count = lax.axis_size("seq")
        self.groups = groups
        self.rows = {full: shapes[shard].shape[0] for group in groups for shard, full in group}
        self.order = {full: place for place, full in enumerate(self.rows)}
        self.parts = 2 if min(self.rows.values()) % 64 == 0 else 1
        self.ticks = (self.count - 2) * self.parts
        arrays = len(self.rows)
        sems = pltpu.SemaphoreType.DMA((arrays, 2, self.parts, self.count - 1))
        self.scratch = [sems, sems, pltpu.SemaphoreType.DMA((arrays,))]
        self.flops = 0

    def bind(self, refs, scratch):
        self.refs = refs
        self.send_sem, self.recv_sem, self.own_sem = scratch
        self.column = lax.axis_index("tp")
        self.place, self.ahead, self.behind = ring_ends(self.count)

    def copy(self, shard, full, way, part, step, first=False):
        move = (self.place + self.count - step) if way == 0 else (self.place + step)
        owner = ring_index(move % self.count, self.count)
        half = self.rows[full] // 2
        size = half // self.parts
        rows = pl.ds(pl.multiple_of(way * half + part * size, 16), size)
        there = self.refs[full].at[owner, rows]
        return pltpu.make_async_remote_copy(
            src_ref=self.refs[shard].at[rows] if first else there,
            dst_ref=there,
            send_sem=self.send_sem.at[self.order[full], way, part, step],
            recv_sem=self.recv_sem.at[self.order[full], way, part, step],
            device_id=(self.ahead if way == 0 else self.behind, self.column),
            device_id_type=MESH,
        )

    def own(self, shard, full):
        there = self.refs[full].at[lax.axis_index("seq")]
        return pltpu.make_async_copy(self.refs[shard], there, self.own_sem.at[self.order[full]])

    def pieces(self, group):
        return [(shard, full, way) for shard, full in self.groups[group] for way in range(2)]

    def begin(self, group):
        for part in range(self.parts):
            for shard, full, way in self.pieces(group):
                self.copy(shard, full, way, part, 0, True).start()
        for shard, full in self.groups[group]:
            self.own(shard, full).start()

    def tick(self, group, index):
        step, part = 1 + index // self.parts, index % self.parts
        for shard, full, way in self.pieces(group):
            self.copy(shard, full, way, part, step - 1).wait_recv()
            self.copy(shard, full, way, part, step).start()

    def prepare(self):
        pass

    def turn(self, group):
        self.begin(group)
        self.settle(group - 1)

    def settled(self, group):
        pass

    def settle(self, group):
        for part in range(self.parts):
            for shard, full, way in self.pieces(group):
                self.copy(shard, full, way, part, self.count - 2).wait_recv()
        for shard, full in self.groups[group]:
            self.own(shard, full).wait()

    def finish(self):
        def sent(step, carry):
            for group in range(len(self.groups)):
                for part in range(self.parts):
                    for shard, full, way in self.pieces(group):
                        self.copy(shard, full, way, part, step).wait_send()
            return carry

        lax.fori_loop(0, self.count - 1, sent, 0)


class PeerCopies:
    def __init__(self, source, target):
        self.source, self.target = source, target
        columns = lax.axis_size("tp")
        self.scratch = [pltpu.SemaphoreType.DMA((columns,)), pltpu.SemaphoreType.DMA((columns,))]

    def bind(self, refs, scratch):
        self.source_ref, self.target_ref = refs[self.source], refs[self.target]
        self.send_sem, self.recv_sem = scratch
        self.columns = lax.axis_size("tp")
        self.seq, self.column = lax.axis_index("seq"), lax.axis_index("tp")

    def block(self, peer):
        if len(self.source_ref.shape) == len(self.target_ref.shape):
            return self.source_ref.at[peer]
        return self.source_ref

    def own(self):
        return pltpu.make_async_copy(
            self.block(self.column), self.target_ref.at[self.column], self.send_sem.at[0]
        )

    def copy(self, step):
        peer = (self.column + step) % self.columns
        return pltpu.make_async_remote_copy(
            src_ref=self.block(peer),
            dst_ref=self.target_ref.at[self.column],
            send_sem=self.send_sem.at[step],
            recv_sem=self.recv_sem.at[step],
            device_id=(self.seq, peer),
            device_id_type=MESH,
        )

    def start(self):
        for step in range(1, self.columns):
            self.copy(step).start()
        self.own().start()

    def wait(self):
        self.own().wait()
        for step in range(1, self.columns):
            self.copy(step).wait_recv()

    def finish(self):
        for step in range(1, self.columns):
            self.copy(step).wait_send()


class ScatterRing:
    def __init__(self, groups, places, shapes, wide):
        self.count = lax.axis_size("seq")
        self.groups, self.places, self.wide = groups, places, wide
        self.names = list(places)
        left = shapes[self.names[0]]
        features, tokens = left.shape
        self.rows = features // self.count
        self.parts = 2
        self.ticks = (self.count - 2) * self.parts
        sems = pltpu.SemaphoreType.DMA((len(groups), 2, self.parts, self.count - 1))
        buffers = max(places.values()) + 1
        self.scratch = [
            pltpu.VMEM((buffers, features, tokens), LOW),
            pltpu.VMEM((2, 2, tokens, wide), LOW),
            pltpu.VMEM((2, 2, self.count, self.rows, wide), LOW),
            pltpu.VMEM((2, self.rows, 2 * wide), jnp.float32),
            sems,
            sems,
            pltpu.SemaphoreType.DMA((len(self.names),)),
            pltpu.SemaphoreType.DMA((2, 2)),
            pltpu.SemaphoreType.DMA((2,)),
        ]
        self.flops = 4 * len(groups) * features * tokens * wide
        self.out_shapes = [jax.ShapeDtypeStruct((self.rows, 2 * wide), jnp.float32)] * len(groups)

    def bind(self, refs, scratch):
        self.refs, self.out_refs = refs, [refs[name] for name in self.outs]
        self.lefts, self.rights, self.slots, self.finals = scratch[:4]
        self.send_sem, self.recv_sem, self.left_sem, self.right_sem, self.done_sem = scratch[4:]
        self.column = lax.axis_index("tp")
        self.place, self.ahead, self.behind = ring_ends(self.count)

    def left_load(self, name):
        return pltpu.make_async_copy(
            self.refs[name], self.lefts.at[self.places[name]], self.left_sem.at[self.names.index(name)]
        )

    def right_load(self, group, way):
        _, name, start = self.groups[group][way]
        source = self.refs[name].at[:, pl.ds(start, self.wide)]
        return pltpu.make_async_copy(source, self.rights.at[group % 2, way], self.right_sem.at[group % 2, way])

    def fetch(self, group):
        for way in range(2):
            self.right_load(group, way).start()

    def span(self, part):
        width = self.wide // self.parts
        return pl.ds(pl.multiple_of(part * width, 128), width)

    def term(self, group, way, part, step):
        move = (self.place + 2 * self.count - 1 - step) if way == 0 else (self.place + 1 + step)
        owner = ring_index(move % self.count, self.count)
        rows = pl.ds(pl.multiple_of(owner * self.rows, 16), self.rows)
        left = self.lefts[self.places[self.groups[group][way][0]], rows, :]
        right = self.rights[group % 2, way, :, self.span(part)]
        return jnp.dot(left, right, preferred_element_type=jnp.float32)

    def held(self, group, way, part, step):
        return self.slots.at[group % 2, way, step, :, self.span(part)]

    def copy(self, group, way, part, step):
        return pltpu.make_async_remote_copy(
            src_ref=self.held(group, way, part, step),
            dst_ref=self.held(group, way, part, step + 1),
            send_sem=self.send_sem.at[group, way, part, step],
            recv_sem=self.recv_sem.at[group, way, part, step],
            device_id=(self.ahead if way == 0 else self.behind, self.column),
            device_id_type=MESH,
        )

    def store(self, group):
        return pltpu.make_async_copy(self.finals.at[group % 2], self.out_refs[group], self.done_sem.at[group % 2])

    def prepare(self):
        self.left_load("cot_full").start()
        self.fetch(0)
        self.left_load("normed_two").start()

    def turn(self, group):
        self.begin(group)
        self.settle(group - 1)
        self.settled(group - 1)

    def settled(self, group):
        if group + 2 < len(self.groups):
            self.fetch(group + 2)
        if group == 1:
            self.left_load("normed_one").start()
        if group == 5:
            self.left_load("branch_full").start()

    def begin(self, group):
        for name, first in (("cot_full", 0), ("normed_two", 2), ("normed_one", 6), ("branch_full", 7)):
            if group == first:
                self.left_load(name).wait()
        for way in range(2):
            self.right_load(group, way).wait()
        for part in range(self.parts):
            for way in range(2):
                self.held(group, way, part, 0)[...] = self.term(group, way, part, 0).astype(LOW)
                self.copy(group, way, part, 0).start()

    def tick(self, group, index):
        step, part = 1 + index // self.parts, index % self.parts
        for way in range(2):
            mine = self.term(group, way, part, step)
            self.copy(group, way, part, step - 1).wait_recv()
            held = self.held(group, way, part, step)
            held[...] = (held[...].astype(jnp.float32) + mine).astype(LOW)
            self.copy(group, way, part, step).start()

    def settle(self, group):
        last = self.count - 1
        if group >= 2:
            self.store(group - 2).wait()
        for part in range(self.parts):
            for way in range(2):
                mine = self.term(group, way, part, last)
                self.copy(group, way, part, last - 1).wait_recv()
                width = self.wide // self.parts
                start = way * self.wide + part * width
                self.finals[group % 2, :, start : start + width] = (
                    self.held(group, way, part, last)[...].astype(jnp.float32) + mine
                )
        self.store(group).start()

        def sent(step, carry):
            for part in range(self.parts):
                for way in range(2):
                    self.copy(group, way, part, step).wait_send()
            return carry

        lax.fori_loop(0, last, sent, 0)

    def finish(self):
        for group in range(max(len(self.groups) - 2, 0), len(self.groups)):
            self.store(group).wait()


class Job:
    wide = 256
    kept = []

    def hold(self, refs):
        pass

    def __init__(self, whole, tiled, outs, tiles, flops):
        self.whole, self.tiled = whole, tiled
        self.inputs = list(whole) + [array for array, axis in tiled]
        self.axes = [axis for array, axis in tiled]
        self.out_shapes = [jax.ShapeDtypeStruct(shape, dtype) for shape, dtype in outs]
        self.tiles = tiles
        self.flops = flops
        self.scratch = (
            [pltpu.VMEM(array.shape, array.dtype) for array in self.inputs]
            + [pltpu.VMEM(shape, dtype) for shape, dtype in outs]
            + [
                pltpu.SemaphoreType.DMA((len(whole),)),
                pltpu.SemaphoreType.DMA((len(tiled), tiles)),
                pltpu.SemaphoreType.DMA((len(outs), tiles)),
            ]
        )

    def bind(self, ins, outs, scratch):
        self.in_refs, self.out_refs = ins, outs
        sizes = [len(self.whole), len(self.tiled), len(outs)]
        self.whole_v, self.tiled_v, self.outs_v = split(scratch, sizes)
        self.whole_sem, self.tiled_sem, self.out_sem = scratch[sum(sizes) :]

    def peers(self):
        return []

    def window(self, axis, index):
        span = pl.ds(pl.multiple_of(index * self.wide, 128), self.wide)
        return (span,) if axis == 0 else (slice(None), span)

    def whole_load(self, which):
        return pltpu.make_async_copy(self.in_refs[which], self.whole_v[which], self.whole_sem.at[which])

    def tiled_load(self, which, index):
        window = self.window(self.axes[which], index)
        there = self.in_refs[len(self.whole) + which].at[window]
        return pltpu.make_async_copy(there, self.tiled_v[which].at[window], self.tiled_sem.at[which, index])

    def out_window(self, index):
        return self.window(1, index)

    def store(self, which, index):
        window = self.out_window(index)
        return pltpu.make_async_copy(
            self.outs_v[which].at[window], self.out_refs[which].at[window], self.out_sem.at[which, index]
        )

    def start(self):
        for which in range(len(self.whole)):
            self.whole_load(which).start()

        def begin(index, carry):
            for which in range(len(self.tiled)):
                self.tiled_load(which, index).start()
            return carry

        lax.fori_loop(0, self.tiles, begin, 0)

    def tile(self, index):
        @pl.when(index == 0)
        def _():
            for which in range(len(self.whole)):
                self.whole_load(which).wait()

        for which in range(len(self.tiled)):
            self.tiled_load(which, index).wait()
        tiles = [ref[self.window(axis, index)] for ref, axis in zip(self.tiled_v, self.axes)]
        for which, value in enumerate(self.compute(self.whole_v, tiles)):
            self.outs_v[which][self.out_window(index)] = value
            self.store(which, index).start()

    def finish(self):
        def end(index, carry):
            for which in range(len(self.outs_v)):
                self.store(which, index).wait()
            return carry

        lax.fori_loop(0, self.tiles, end, 0)


def blocks_dot(blocks, weight):
    parts, _, depth = blocks.shape
    total = None
    for part in range(parts):
        term = jnp.dot(blocks[part], weight[part * depth : (part + 1) * depth], preferred_element_type=jnp.float32)
        total = term if total is None else total + term
    return total


class ExpandJob(Job):
    def __init__(self, normed, gate_full, up_full):
        rows, width = normed.shape[1], gate_full.shape[1]
        outs = [((rows, width), jnp.float32), ((rows, width), jnp.float32), ((rows, width), LOW)]
        super().__init__(
            [normed], [(gate_full, 1), (up_full, 1)], outs, width // self.wide, 4 * rows * gate_full.size
        )

    def compute(self, whole, tiles):
        gate_rows = blocks_dot(whole[0], tiles[0])
        up_rows = blocks_dot(whole[0], tiles[1])
        return gate_rows, up_rows, (gate_rows * jax.nn.sigmoid(gate_rows) * up_rows).astype(LOW)


class HiddenGradJob(Job):
    def __init__(self, cot, shrink_full, gate_rows, up_rows):
        rows, width = gate_rows.shape
        outs = [((rows, width), LOW), ((rows, width), LOW)]
        tiled = [(shrink_full, 1), (gate_rows, 1), (up_rows, 1)]
        super().__init__([cot], tiled, outs, width // self.wide, 2 * rows * shrink_full.size)

    def compute(self, whole, tiles):
        _, gate_rows, up_rows = tiles
        act_grad = blocks_dot(whole[0], tiles[0])
        sigmoid_gate = jax.nn.sigmoid(gate_rows)
        gate_grad = act_grad * up_rows * sigmoid_gate * (1.0 + gate_rows * (1.0 - sigmoid_gate))
        return gate_grad.astype(LOW), (act_grad * (gate_rows * sigmoid_gate)).astype(LOW)


class WidthJob(Job):
    then = None

    def __init__(self, lefts, weights):
        rows, width = lefts[0].shape[0], weights[0].shape[0]
        flops = 2 * rows * sum(weight.size for weight in weights)
        parts = lax.axis_size("tp")
        self.own = width // parts
        out = ((parts, rows, self.own), LOW)
        super().__init__(lefts, [(weight, 0) for weight in weights], [out], width // self.wide, flops)

    def out_window(self, index):
        each = self.own // self.wide
        return index // each, slice(None), pl.ds(pl.multiple_of(index % each * self.wide, 128), self.wide)

    def compute(self, whole, tiles):
        total = None
        for left, weight in zip(whole, tiles):
            term = contract_cols(left[...], weight)
            total = term if total is None else total + term
        return (total.astype(LOW),)

    def finish(self):
        super().finish()
        if self.then:
            self.then.start()


class MixerJob:
    kept = []

    def hold(self, refs):
        self.kept_refs = refs

    def __init__(self, inputs, outs, extra, phases, flops):
        self.inputs = list(inputs)
        self.out_shapes = [jax.ShapeDtypeStruct(shape, dtype) for shape, dtype in outs]
        self.phases = phases
        self.tiles = sum(phases)
        self.flops = flops
        self.scratch = (
            [pltpu.VMEM(array.shape, array.dtype) for array in self.inputs]
            + [pltpu.VMEM(shape, dtype) for shape, dtype in outs]
            + extra
            + [
                pltpu.SemaphoreType.DMA((len(self.inputs),)),
                pltpu.SemaphoreType.DMA((len(outs),)),
            ]
        )

    def bind(self, ins, outs, scratch):
        self.in_refs, self.out_refs = ins, outs
        extra = len(scratch) - len(ins) - len(outs) - 2
        self.ins_v, self.outs_v, self.extra_v = split(scratch, [len(ins), len(outs), extra])
        self.in_sem, self.out_sem = scratch[-2:]
        self.count = lax.axis_size("seq")
        self.seq = lax.axis_index("seq")
        self.column = lax.axis_index("tp")

    def peers(self):
        after = (self.seq + 1) % self.count
        before = (self.seq + self.count - 1) % self.count
        return [(after, self.column), (before, self.column)]

    def load(self, which):
        return pltpu.make_async_copy(self.in_refs[which], self.ins_v[which], self.in_sem.at[which])

    def store(self, which):
        return pltpu.make_async_copy(self.outs_v[which], self.out_refs[which], self.out_sem.at[which])

    def passing(self, source, target, forward):
        step = 1 if forward else self.count - 1
        return pltpu.make_async_remote_copy(
            src_ref=source,
            dst_ref=target,
            send_sem=self.kept_refs[1].at[0],
            recv_sem=self.kept_refs[1].at[1],
            device_id=((self.seq + step) % self.count, self.column),
            device_id_type=MESH,
        )

    def start(self):
        for which in range(len(self.inputs)):
            self.load(which).start()

    def tile(self, index):
        begin = 0
        for phase, tiles in enumerate(self.phases):
            here = index - begin

            @pl.when((here >= 0) & (here < tiles))
            def _(phase=phase, here=here, tiles=tiles):
                @pl.when(here == 0)
                def _():
                    self.before(phase)

                self.work(phase, here)

                @pl.when(here == tiles - 1)
                def _():
                    self.after(phase)

            begin += tiles

    def finish(self):
        for which in range(len(self.out_shapes)):
            self.store(which).wait()


def visible(bound_row, shape):
    position = lax.broadcasted_iota(jnp.int32, shape, 0)
    see_one = position != bound_row
    return position, see_one, see_one & (position - 1 != bound_row)


def lagged(rows, halo, position):
    last, second = halo[15:16].astype(jnp.float32), halo[14:15].astype(jnp.float32)
    one = jnp.where(position == 0, last, pltpu.roll(rows, 1, 0))
    two = jnp.where(position == 0, second, jnp.where(position == 1, last, pltpu.roll(rows, 2, 0)))
    return one, two


class EntryJob(MixerJob):
    then = None

    def __init__(self, tokens, wide, entry_full, exit_full, bound):
        parts, rows, own = tokens.shape
        width, columns = exit_full.shape
        self.rows, self.columns, self.own = rows, columns, own
        self.width = width
        outs = [
            ((rows, 3 * columns), jnp.float32),
            ((rows, columns), jnp.float32),
            ((rows, columns), LOW),
            ((16, columns), LOW),
            ((rows, columns), LOW),
            ((parts, rows, own), LOW),
            ((rows, 128), jnp.float32),
            ((width, rows), LOW),
        ]
        phases = [rows // 256, 3 * columns // 256, 1, columns // 128, width // 256]
        flops = 2 * rows * (entry_full.size + exit_full.size)
        super().__init__([tokens, wide, entry_full, exit_full, bound], outs, [], phases, flops)
        self.kept = [pltpu.VMEM((16, columns), LOW), pltpu.SemaphoreType.DMA((2,))]

    def halo(self):
        return self.passing(self.outs_v[2].at[pl.ds(self.rows - 16, 16)], self.kept_refs[0], True)

    def before(self, phase):
        if phase == 0:
            for which in (0, 1):
                self.load(which).wait()
        if phase == 1:
            self.store(6).start()
            self.store(7).start()
            self.load(2).wait()
        if phase == 3:
            self.load(4).wait()
            self.halo().wait_recv()
            self.outs_v[3][...] = self.kept_refs[0][...]
            self.store(3).start()
        if phase == 4:
            self.load(3).wait()

    def after(self, phase):
        if phase == 1:
            self.store(0).start()
        if phase == 2:
            self.halo().start()
            self.store(2).start()
        if phase == 3:
            self.store(1).start()
            self.store(4).start()
        if phase == 4:
            self.store(5).start()

    def finish(self):
        self.store(5).wait()
        if self.then:
            self.then.start()
        self.halo().wait_send()
        for which in (0, 1, 2, 3, 4, 6, 7):
            self.store(which).wait()

    def work(self, phase, index):
        tokens, wide, entry, exits, bound = self.ins_v
        taps = wide.at[self.column]
        projected, conv, gated, halo, mixer, term, scales, turned_rows = self.outs_v
        columns = self.columns
        if phase == 0:
            rows = pl.ds(pl.multiple_of(index * 256, 256), 256)
            values = [tokens[part, rows, :].astype(jnp.float32) for part in range(tokens.shape[0])]
            total = sum(jnp.sum(value * value, axis=1, keepdims=True) for value in values)
            scale = lax.rsqrt(total / D + EPSILON)
            scales[rows, :] = jnp.broadcast_to(scale, (256, 128))
            for part, value in enumerate(values):
                normed = (value * scale * wide[part, 3:4, :]).astype(LOW)
                tokens[part, rows, :] = normed
                turned_rows[part * self.own : (part + 1) * self.own, rows] = normed.T
        if phase == 1:
            span = pl.ds(pl.multiple_of(index * 256, 256), 256)
            projected[:, span] = blocks_dot(tokens, entry[:, span])
        if phase == 2:
            gated[...] = (projected[:, :columns] * projected[:, 2 * columns :]).astype(LOW)
        if phase == 3:
            span = pl.ds(pl.multiple_of(index * 128, 128), 128)
            middle = pl.ds(pl.multiple_of(columns + index * 128, 128), 128)
            rows = gated[:, span].astype(jnp.float32)
            position, see_one, see_two = visible(bound[0:1, :], rows.shape)
            before = halo[:, span].astype(jnp.float32) * jnp.where(self.seq > 0, 1.0, 0.0)
            one, two = lagged(rows, before, position)
            total = (
                taps[2:3, span] * rows
                + taps[1:2, span] * jnp.where(see_one, one, 0.0)
                + taps[0:1, span] * jnp.where(see_two, two, 0.0)
            )
            conv[:, span] = total
            mixer[:, span] = (projected[:, middle] * total).astype(LOW)
        if phase == 4:
            features = pl.ds(pl.multiple_of(index * 256, 256), 256)
            owner, inner = index // (self.own // 256), index % (self.own // 256)
            span = pl.ds(pl.multiple_of(inner * 256, 256), 256)
            term[owner, :, span] = contract_cols(mixer[...], exits[features, :]).astype(LOW)


class MixerGradJob(MixerJob):
    then = None

    def __init__(self, branch, exit_full, entry_full, projected, conv, gated, halo, wide, bound):
        parts, rows, own = branch.shape
        width, columns = exit_full.shape
        self.rows, self.columns, self.own = rows, columns, own
        outs = [((rows, 3 * columns), LOW), ((parts, rows, own), LOW), ((8, columns), jnp.float32)]
        extra = [
            pltpu.VMEM((rows, columns), jnp.float32),
            pltpu.VMEM((8, columns), jnp.float32),
        ]
        self.kept = [pltpu.VMEM((8, columns), jnp.float32), pltpu.SemaphoreType.DMA((2,))]
        phases = [columns // 256, 1, columns // 128, width // 256]
        flops = 2 * rows * (entry_full.size + exit_full.size)
        inputs = [branch, exit_full, entry_full, projected, conv, gated, halo, wide, bound]
        super().__init__(inputs, outs, extra, phases, flops)

    def back(self):
        return self.passing(self.extra_v[1], self.kept_refs[0], False)

    def before(self, phase):
        if phase == 0:
            for which in (0, 1, 3, 4):
                self.load(which).wait()
        if phase == 1:
            for which in (7, 8):
                self.load(which).wait()
        if phase == 2:
            for which in (5, 6):
                self.load(which).wait()
            self.back().wait_recv()
        if phase == 3:
            self.load(2).wait()

    def after(self, phase):
        if phase == 1:
            self.back().start()
        if phase == 2:
            self.store(0).start()
            self.store(2).start()
        if phase == 3:
            self.store(1).start()

    def finish(self):
        self.store(1).wait()
        if self.then:
            self.then.start()
        self.back().wait_send()
        for which in (0, 2):
            self.store(which).wait()

    def work(self, phase, index):
        branch, exits, entry, projected, conv, gated, halo, wide, bound = self.ins_v
        taps = wide.at[self.column]
        grads, term, taps_grad = self.outs_v
        conv_grad, sent = self.extra_v
        returned = self.kept_refs[0]
        columns, height = self.columns, self.rows
        if phase == 0:
            span = pl.ds(pl.multiple_of(index * 256, 256), 256)
            middle = pl.ds(pl.multiple_of(columns + index * 256, 256), 256)
            mixer_grad = blocks_dot(branch, exits[:, span])
            grads[:, middle] = (mixer_grad * conv[:, span]).astype(LOW)
            conv_grad[:, span] = mixer_grad * projected[:, middle]
        if phase == 1:
            for start in range(0, columns, 128):
                span = slice(start, start + 128)
                rows = conv_grad[0:8, span]
                position, see_one, see_two = visible(bound[0:1, :], rows.shape)
                one = pltpu.roll(jnp.where(see_one, rows, 0.0) * taps[1:2, span], 1, 0)
                two = jnp.where(see_two, rows, 0.0) * taps[0:1, span]
                sent[:, span] = two + jnp.where(position == 0, 0.0, one)
            taps_grad[...] = jnp.zeros_like(taps_grad)
        if phase == 2:
            span = pl.ds(pl.multiple_of(index * 128, 128), 128)
            last = pl.ds(pl.multiple_of(2 * columns + index * 128, 128), 128)
            rows = conv_grad[:, span]
            position, see_one, see_two = visible(bound[0:1, :], rows.shape)
            seen_one, seen_two = jnp.where(see_one, rows, 0.0), jnp.where(see_two, rows, 0.0)
            one = pltpu.roll(seen_one * taps[1:2, span], height - 1, 0)
            two = pltpu.roll(seen_two * taps[0:1, span], height - 2, 0)
            after = returned[:, span] * jnp.where(self.seq < self.count - 1, 1.0, 0.0)
            gated_grad = (
                rows * taps[2:3, span]
                + jnp.where(position == height - 1, after[1:2], one)
                + jnp.where(position < height - 2, two, jnp.where(position == height - 2, after[0:1], 0.0))
            )
            grads[:, span] = (gated_grad * projected[:, last]).astype(LOW)
            grads[:, last] = (gated_grad * projected[:, span]).astype(LOW)
            own_rows = gated[:, span].astype(jnp.float32)
            before = halo[:, span].astype(jnp.float32) * jnp.where(self.seq > 0, 1.0, 0.0)
            lag_one, lag_two = lagged(own_rows, before, position)
            taps_grad[0:1, span] = jnp.sum(seen_two * lag_two, axis=0, keepdims=True)
            taps_grad[1:2, span] = jnp.sum(seen_one * lag_one, axis=0, keepdims=True)
            taps_grad[2:3, span] = jnp.sum(rows * own_rows, axis=0, keepdims=True)
        if phase == 3:
            features = pl.ds(pl.multiple_of(index * 256, 256), 256)
            owner, inner = index // (self.own // 256), index % (self.own // 256)
            span = pl.ds(pl.multiple_of(inner * 256, 256), 256)
            term[owner, :, span] = contract_cols(grads[...], entry[features, :]).astype(LOW)


class Jobs:
    def __init__(self, *jobs):
        self.jobs = jobs
        self.inputs = [item for job in jobs for item in job.inputs]
        self.out_shapes = [item for job in jobs for item in job.out_shapes]
        self.scratch = [item for job in jobs for item in job.scratch]
        self.kept = [item for job in jobs for item in job.kept]
        self.tiles = sum(job.tiles for job in jobs)
        self.flops = sum(job.flops for job in jobs)

    def hold(self, refs):
        for job, own in zip(self.jobs, split(refs, [len(job.kept) for job in self.jobs])):
            job.hold(own)

    def bind(self, ins, outs, scratch):
        groups = zip(
            self.jobs,
            split(ins, [len(job.inputs) for job in self.jobs]),
            split(outs, [len(job.out_shapes) for job in self.jobs]),
            split(scratch, [len(job.scratch) for job in self.jobs]),
        )
        for job, own_ins, own_outs, own_scratch in groups:
            job.bind(own_ins, own_outs, own_scratch)

    def peers(self):
        return [peer for job in self.jobs for peer in job.peers()]

    def start(self):
        for job in self.jobs:
            job.start()

    def tile(self, index):
        begin = 0
        for job in self.jobs:
            here = index - begin

            @pl.when((here >= 0) & (here < job.tiles))
            def _(job=job, here=here):
                job.tile(here)

            begin += job.tiles

    def finish(self):
        for job in self.jobs:
            job.finish()


class TurnJob(MixerJob):
    def __init__(self, blocks):
        parts, rows, own = blocks.shape
        super().__init__([blocks], [((parts * own, rows), blocks.dtype)], [], [rows // 128], 0)

    def peers(self):
        return []

    def before(self, phase):
        self.load(0).wait()

    def after(self, phase):
        self.store(0).start()

    def work(self, phase, index):
        (blocks,), (target,) = self.ins_v, self.outs_v
        parts, _, own = blocks.shape
        rows = pl.ds(pl.multiple_of(index * 128, 128), 128)
        for part in range(parts):
            target[part * own : (part + 1) * own, rows] = blocks[part, rows, :].T


class CastJob(MixerJob):
    def __init__(self, pairs, plain):
        rows, columns = plain.shape
        lanes = pairs.shape[1]
        self.rows, self.half, self.lanes = rows, columns // 2, lanes
        self.block = max(rows // 8, 16)
        outs = [((rows, columns // 2), LOW)] * 6
        super().__init__([pairs, plain], outs, [], [rows // self.block], 0)

    def peers(self):
        return []

    def before(self, phase):
        for which in range(2):
            self.load(which).wait()

    def after(self, phase):
        for which in range(6):
            self.store(which).start()

    def work(self, phase, index):
        pairs, plain = self.ins_v
        block, half, lanes = self.block, self.half, self.lanes
        tiles = half // lanes
        rows = pl.ds(pl.multiple_of(index * block, 16), block)
        start = index * (block * 4 * tiles)
        for which in range(4):
            side, plane = which // 2, which % 2
            for tile in range(tiles):
                place = (side * tiles + tile) * 2 + plane
                picked = pairs[pl.ds(start + place, block, stride=4 * tiles), :]
                self.outs_v[which][rows, tile * lanes : (tile + 1) * lanes] = picked.astype(LOW)
        for side in range(2):
            self.outs_v[4 + side][rows, :] = plain[rows, side * half : (side + 1) * half].astype(LOW)


class SmallGatherJob:
    tiles, flops = 1, 0

    def __init__(self, own, seen):
        self.inputs = [own]
        self.seen = seen
        devices, columns = lax.axis_size("seq"), lax.axis_size("tp")
        wide = (columns, 8, devices * seen)
        self.out_shapes = [jax.ShapeDtypeStruct(wide, jnp.float32)]
        self.scratch = [pltpu.VMEM(wide, jnp.float32), pltpu.SemaphoreType.DMA((2,))]
        self.kept = [
            pltpu.VMEM((devices, columns) + own.shape, own.dtype),
            pltpu.SemaphoreType.DMA((columns,)),
            pltpu.SemaphoreType.DMA((columns,)),
            pltpu.SemaphoreType.DMA((devices,)),
            pltpu.SemaphoreType.DMA((devices,)),
        ]

    def hold(self, refs):
        self.whole, self.near_send, self.near_recv, self.far_send, self.far_recv = refs
        self.devices, self.columns = lax.axis_size("seq"), lax.axis_size("tp")
        self.seq, self.column = lax.axis_index("seq"), lax.axis_index("tp")

    def bind(self, ins, outs, scratch):
        self.source, self.target = ins[0], outs[0]
        self.wide, self.local_sem = scratch

    def peers(self):
        near = [(self.seq, (self.column + step) % self.columns) for step in range(1, self.columns)]
        far = [((self.seq + step) % self.devices, self.column) for step in range(1, self.devices)]
        return near + far

    def near(self, step):
        piece = self.whole.at[self.seq, self.column]
        return pltpu.make_async_remote_copy(
            src_ref=piece,
            dst_ref=piece,
            send_sem=self.near_send.at[step],
            recv_sem=self.near_recv.at[step],
            device_id=(self.seq, (self.column + step) % self.columns),
            device_id_type=MESH,
        )

    def far(self, step):
        piece = self.whole.at[self.seq]
        return pltpu.make_async_remote_copy(
            src_ref=piece,
            dst_ref=piece,
            send_sem=self.far_send.at[step],
            recv_sem=self.far_recv.at[step],
            device_id=((self.seq + step) % self.devices, self.column),
            device_id_type=MESH,
        )

    def start(self):
        load = pltpu.make_async_copy(self.source, self.whole.at[self.seq, self.column], self.local_sem.at[0])
        load.start()
        load.wait()
        for step in range(1, self.columns):
            self.near(step).start()

    def tile(self, index):
        for step in range(1, self.columns):
            self.near(step).wait()

        def begin(step, carry):
            self.far(step).start()
            return carry

        lax.fori_loop(1, self.devices, begin, 0)

    def finish(self):
        def end(step, carry):
            self.far(step).wait()
            return carry

        lax.fori_loop(1, self.devices, end, 0)
        each = LANES // self.seen
        for column in range(self.columns):
            for start in range(0, self.devices, each):
                total = None
                for inner in range(each):
                    piece = self.whole[start + inner, column, :, :].astype(jnp.float32)[:8]
                    piece = pltpu.roll(piece, inner * self.seen, 1) if inner else piece
                    total = piece if total is None else total + piece
                self.wide[column, :, start * self.seen : start * self.seen + LANES] = total
        store = pltpu.make_async_copy(self.wide, self.target, self.local_sem.at[1])
        store.start()
        store.wait()


class RowSumJob(MixerJob):
    block = 128

    def __init__(self, inputs, outs, extra, rows, flops):
        self.columns = lax.axis_size("tp")
        blocks = rows // self.block
        self.kept = [
            pltpu.VMEM((self.columns, blocks, self.block), jnp.float32),
            pltpu.SemaphoreType.DMA((self.columns,)),
            pltpu.SemaphoreType.DMA((self.columns,)),
        ]
        totals = pltpu.VMEM((blocks, self.block), jnp.float32)
        super().__init__(inputs, outs, [totals] + extra, [blocks, 1, blocks], flops)

    def peers(self):
        return [(self.seq, (self.column + step) % self.columns) for step in range(1, self.columns)]

    def share(self, step):
        return pltpu.make_async_remote_copy(
            src_ref=self.kept_refs[0].at[0],
            dst_ref=self.kept_refs[0].at[step],
            send_sem=self.kept_refs[1].at[step],
            recv_sem=self.kept_refs[2].at[step],
            device_id=(self.seq, (self.column + step) % self.columns),
            device_id_type=MESH,
        )

    def before(self, phase):
        if phase == 0:
            for which in range(len(self.inputs)):
                self.load(which).wait()

    def after(self, phase):
        if phase == 0:
            for step in range(1, self.columns):
                self.share(step).start()
        if phase == 2:
            for which in range(len(self.out_shapes)):
                self.store(which).start()

    def finish(self):
        for step in range(1, self.columns):
            self.share(step).wait_send()
        super().finish()

    def work(self, phase, index):
        block = self.block
        slots, totals = self.kept_refs[0], self.extra_v[0]
        rows = pl.ds(pl.multiple_of(index * block, block), block)
        if phase == 0:
            part = jnp.sum(self.values(rows), axis=1, keepdims=True)
            slots[0, pl.ds(index, 1), :] = jnp.broadcast_to(part, (block, block)).T[0:1, :]
        if phase == 1:
            for step in range(1, self.columns):
                self.share(step).wait_recv()
            totals[...] = sum(slots[step] for step in range(self.columns))
        if phase == 2:
            self.use(rows, jnp.broadcast_to(totals[pl.ds(index, 1), :], (block, block)).T)


class NormJob(RowSumJob):
    then = None

    def __init__(self, rows_in, terms, wide):
        rows, own = rows_in.shape
        outs = [((rows, own), jnp.float32), ((rows, own), LOW), ((rows, 128), jnp.float32)]
        super().__init__([rows_in, terms, wide], outs, [], rows, 0)

    def values(self, rows):
        rows_in, terms, _ = self.ins_v
        residual = sum(terms[part, rows, :].astype(jnp.float32) for part in range(self.columns))
        residual = rows_in[rows, :].astype(jnp.float32) + residual
        self.outs_v[0][rows, :] = residual
        return residual * residual

    def use(self, rows, total):
        residual, normed, scales = self.outs_v
        scale = lax.rsqrt(total / D + EPSILON)
        scales[rows, :] = scale
        gain = self.ins_v[2].at[self.column]
        normed[rows, :] = (residual[rows, :] * scale[:, 0:1] * gain[4:5, :]).astype(LOW)

    def finish(self):
        self.store(1).wait()
        if self.then:
            self.then.start()
        for step in range(1, self.columns):
            self.share(step).wait_send()
        for which in (0, 2):
            self.store(which).wait()


class NormBackJob(RowSumJob):
    then = None

    def __init__(self, terms, kept, scales, wide, row, base, rounded):
        _, rows, own = terms.shape
        outs = [((rows, own), jnp.float32), ((8, own), jnp.float32)]
        outs = outs + [((rows, own), LOW)] if rounded else outs
        self.row = row
        super().__init__([terms, kept, scales, wide, base], outs, [], rows, 0)

    def parts(self, rows):
        terms, kept, scales, wide, base = self.ins_v
        gain = wide.at[self.column]
        return (
            sum(terms[part, rows, :].astype(jnp.float32) for part in range(self.columns)),
            kept[rows, :].astype(jnp.float32),
            scales[rows, 0:1],
            gain[self.row : self.row + 1, :],
        )

    def before(self, phase):
        super().before(phase)
        if phase == 0:
            self.outs_v[1][...] = jnp.zeros_like(self.outs_v[1])

    def values(self, rows):
        grad, kept, scale, gain = self.parts(rows)
        product = grad * kept
        self.outs_v[1][0:1, :] += jnp.sum(product * scale, axis=0, keepdims=True)
        return product * gain

    def use(self, rows, total):
        grad, kept, scale, gain = self.parts(rows)
        rows_grad = scale * gain * grad - kept * (scale * scale * scale * total[:, 0:1] / D)
        result = self.ins_v[4][rows, :].astype(jnp.float32) + rows_grad
        self.outs_v[0][rows, :] = result
        if len(self.outs_v) > 2:
            self.outs_v[2][rows, :] = result.astype(LOW)

    def finish(self):
        if self.then:
            self.store(2).wait()
            self.then.start()
        for step in range(1, self.columns):
            self.share(step).wait_send()
        for which in range(len(self.out_shapes)):
            if which != 2 or not self.then:
                self.store(which).wait()


class SumJob(MixerJob):
    def __init__(self, base, terms):
        rows, own = base.shape
        super().__init__([base, terms], [((rows, own), LOW)], [], [rows // 128], 0)

    def before(self, phase):
        for which in range(2):
            self.load(which).wait()

    def after(self, phase):
        self.store(0).start()

    def work(self, phase, index):
        base, terms = self.ins_v
        rows = pl.ds(pl.multiple_of(index * 128, 128), 128)
        total = sum(terms[part, rows, :].astype(jnp.float32) for part in range(terms.shape[0]))
        self.outs_v[0][rows, :] = (base[rows, :] + total).astype(LOW)


class SmallSumJob:
    tiles, flops = 1, 0

    def __init__(self, taps_grad, gain_grad, before):
        count = lax.axis_size("seq")
        self.inputs = [taps_grad, gain_grad]
        shape = taps_grad.shape
        self.before = before
        self.out_shapes = [jax.ShapeDtypeStruct(shape, jnp.float32)]
        self.scratch = [pltpu.VMEM(shape, jnp.float32)] * 3 + [pltpu.SemaphoreType.DMA((3,))]
        self.kept = [
            pltpu.VMEM((count,) + shape, jnp.float32),
            pltpu.SemaphoreType.DMA((count,)),
            pltpu.SemaphoreType.DMA((count,)),
        ]

    def hold(self, refs):
        self.slots, self.send_sem, self.recv_sem = refs

    def bind(self, ins, outs, scratch):
        self.sources, self.target = ins, outs[0]
        self.taps, self.gain, self.total, self.local_sem = scratch
        self.count = lax.axis_size("seq")
        self.seq = lax.axis_index("seq")
        self.column = lax.axis_index("tp")

    def peers(self):
        return [((self.seq + far) % self.count, self.column) for far in range(1, self.count)]

    def copy(self, far):
        return pltpu.make_async_remote_copy(
            src_ref=self.slots.at[0],
            dst_ref=self.slots.at[far],
            send_sem=self.send_sem.at[far],
            recv_sem=self.recv_sem.at[far],
            device_id=((self.seq + far) % self.count, self.column),
            device_id_type=MESH,
        )

    def loads(self):
        return [
            pltpu.make_async_copy(self.sources[which], (self.taps, self.gain)[which], self.local_sem.at[which])
            for which in range(2)
        ]

    def start(self):
        for load in self.loads():
            load.start()

    def tile(self, index):
        for load in self.loads():
            load.wait()
        self.slots[0, 0:3, :] = self.taps[0:3, :]
        self.slots[0, 3:4, :] = self.before.outs_v[1][0:1, :]
        self.slots[0, 4:5, :] = self.gain[0:1, :]
        self.slots[0, 5:8, :] = jnp.zeros_like(self.slots[0, 5:8, :])

        def begin(far, carry):
            self.copy(far).start()
            return carry

        lax.fori_loop(1, self.count, begin, 0)

    def finish(self):
        self.total[...] = self.slots[0]

        def add(far, carry):
            self.copy(far).wait_recv()
            self.total[...] += self.slots[far]
            return carry

        lax.fori_loop(1, self.count, add, 0)
        store = pltpu.make_async_copy(self.total, self.target, self.local_sem.at[2])
        store.start()

        def sent(far, carry):
            self.copy(far).wait_send()
            return carry

        lax.fori_loop(1, self.count, sent, 0)
        store.wait()


class Section:
    def __init__(self, ranges, jobs=(), waits=(), rest=1, calls=(), early=True):
        self.ranges, self.jobs, self.waits, self.rest, self.calls, self.early = ranges, jobs, waits, rest, calls, early
        self.job = Jobs(*[job for job, _, _ in jobs])

    def run(self, ring, ins, outs):
        job = self.job
        ranges = [(group, low * ring.ticks // 12, high * ring.ticks // 12) for group, low, high in self.ranges]
        total = sum(high - low for _, low, high in ranges)
        rest = self.rest * ring.ticks // 12
        active = total - rest
        each = -(-job.tiles // active)

        def ready():
            for exchange in self.waits:
                exchange.wait()
            job.start()

        def body(*scratch):
            job.bind(ins, outs, list(scratch))
            if not self.waits:
                job.start()
            done = 0
            for place, (group, low, high) in enumerate(ranges):
                if low == 0 and group > 0 and place > 0:
                    ring.turn(group)
                if place == 0:
                    for call in self.calls:
                        call.start()

                def step(index, carry, group=group, shift=done - low):
                    late = index + shift - rest
                    first, after = late * job.tiles // active, (late + 1) * job.tiles // active
                    if self.waits:
                        pl.when(late == -1)(ready)
                    for inner in range(each):
                        tile = first + inner

                        @pl.when((late >= 0) & (tile < after))
                        def _(tile=tile):
                            job.tile(tile)

                    ring.tick(group, index)
                    return carry

                lax.fori_loop(low, high, step, 0)
                done += high - low
            group, _, high = ranges[-1]
            ends = high == ring.ticks and group + 1 < len(ring.groups)
            if ends and self.early:
                ring.begin(group + 1)
            job.finish()
            if ends and not self.early:
                ring.begin(group + 1)

        pl.run_scoped(body, *job.scratch)
        group, _, high = ranges[-1]
        if high == ring.ticks:
            ring.settle(group)
            ring.settled(group)


class Plan:
    def __init__(self, arrays):
        self.arrays = arrays
        self.shapes = {name: jax.ShapeDtypeStruct(array.shape, array.dtype) for name, array in arrays.items()}
        self.inputs = list(self.shapes)
        self.weights = set()

    def define(self, name, shape, dtype):
        self.shapes[name] = jax.ShapeDtypeStruct(shape, dtype)

    def add(self, job, ins, outs):
        for name, shape in zip(outs, job.out_shapes):
            self.shapes[name] = shape
        return job, ins, outs

    def flat(self, full):
        shape = self.shapes[full].shape
        return jax.ShapeDtypeStruct((shape[0] * shape[1], shape[2]), LOW)

    def run(self, ring, sections, exchanges, peers, start, name, collective):
        inputs = self.inputs
        outputs = [made for made in self.shapes if made not in inputs]
        kept = [item for section in sections for item in section.job.kept]
        sems = [item for exchange in exchanges for item in exchange.scratch]

        def kernel(*all_refs):
            in_refs, out_refs, ring_scratch, sem_refs, kept_refs = split(
                all_refs, [len(inputs), len(outputs), len(ring.scratch), len(sems), len(kept)]
            )
            refs = dict(zip(inputs + outputs, in_refs + out_refs))
            ring.bind(refs, ring_scratch)
            for place, exchange in enumerate(exchanges):
                exchange.bind(refs, sem_refs[2 * place : 2 * place + 2])
            for section, own in zip(sections, split(kept_refs, [len(section.job.kept) for section in sections])):
                section.job.hold(own)
            ring.prepare()
            greet(peers())
            ring.begin(0)
            ring.settled(-1)
            for exchange in start:
                exchange.start()
            for section in sections:
                ins = [rows_of(refs[made], made in self.weights) for _, names, _ in section.jobs for made in names]
                outs = [refs[made] for _, _, names in section.jobs for made in names]
                section.run(ring, ins, outs)
            ring.finish()
            for exchange in exchanges:
                exchange.finish()

        flops = ring.flops + sum(section.job.flops for section in sections)
        results = pl.pallas_call(
            kernel,
            out_shape=[self.shapes[made] for made in outputs],
            in_specs=[pl.BlockSpec(memory_space=pl.ANY)] * len(inputs),
            out_specs=[pl.BlockSpec(memory_space=pl.ANY)] * len(outputs),
            scratch_shapes=ring.scratch + sems + kept,
            compiler_params=pltpu.CompilerParams(
                collective_id=collective, has_side_effects=True, vmem_limit_bytes=VMEM_BYTES
            ),
            cost_estimate=pl.CostEstimate(flops=flops, bytes_accessed=10**9, transcendentals=0),
            name=name,
        )(*self.arrays.values())
        named = dict(zip(outputs, results))
        return {made: flat(array) if made in self.weights else array for made, array in named.items()}


def row_and_column_peers():
    seq, column = lax.axis_index("seq"), lax.axis_index("tp")
    devices, columns = lax.axis_size("seq"), lax.axis_size("tp")
    near = [(seq, (column + step) % columns) for step in range(1, columns)]
    return near + [((seq + step) % devices, column) for step in range(1, devices)]


def run_forward(arrays, seen):
    count, columns = lax.axis_size("seq"), lax.axis_size("tp")
    plan = Plan(arrays)
    shapes, add = plan.shapes, plan.add
    rows, own = arrays["tokens"].shape
    for name in ("tokens_blocks", "cot_blocks", "branch_terms", "normed_blocks"):
        plan.define(name, (columns, rows, own), LOW)
    low = ["gate_low0", "up_low0", "gate_low1", "up_low1", "shrink_low0", "shrink_low1"]
    small = add(SmallGatherJob(shapes["small"], seen), ["small"], ["wide"])
    cast = add(CastJob(shapes["pairs"], shapes["shrink"]), ["pairs", "shrink"], low)
    groups = [[("entry_low", "entry_full"), ("exit_low", "exit_full")]]
    groups += [[(name, name.replace("low", "full"))] for name in low]
    for group in groups:
        for shard, full in group:
            plan.define(full, (count,) + shapes[shard].shape, LOW)
            plan.weights.add(full)
    ring = GatherRing(groups, shapes)
    tokens_sent = PeerCopies("tokens", "tokens_blocks")
    cot_sent = PeerCopies("cotangent", "cot_blocks")
    branch_sent = PeerCopies("term", "branch_terms")
    normed_sent = PeerCopies("normed_own", "normed_blocks")

    entry_job = EntryJob(
        shapes["tokens_blocks"], shapes["wide"], plan.flat("entry_full"), plan.flat("exit_full"), shapes["bound"]
    )
    entry_job.then = branch_sent
    entry = add(
        entry_job,
        ["tokens_blocks", "wide", "entry_full", "exit_full", "bound"],
        ["projected", "conv_out", "gated", "halo", "mixer", "term", "scale_one", "normed_one"],
    )
    turn_cot = add(TurnJob(shapes["cot_blocks"]), ["cot_blocks"], ["cot_full"])
    norm_job = NormJob(shapes["tokens"], shapes["branch_terms"], shapes["wide"])
    norm_job.then = normed_sent
    norm = add(norm_job, ["tokens", "branch_terms", "wide"], ["residual", "normed_own", "scale_two"])
    expands = []
    for half in "01":
        job = ExpandJob(shapes["normed_blocks"], plan.flat("gate_full" + half), plan.flat("up_full" + half))
        names = ["normed_blocks", "gate_full" + half, "up_full" + half]
        expands.append(add(job, names, ["gate_rows" + half, "up_rows" + half, "activation" + half]))
    hidden_job = HiddenGradJob(shapes["cot_blocks"], plan.flat("shrink_full0"), shapes["gate_rows0"], shapes["up_rows0"])
    hidden = add(hidden_job, ["cot_blocks", "shrink_full0", "gate_rows0", "up_rows0"], ["gate_grad0", "up_grad0"])
    turn_normed = add(TurnJob(shapes["normed_blocks"]), ["normed_blocks"], ["normed_two"])
    sections = [
        Section([(0, 0, 12)], [small, cast], early=False),
        Section([(1, 0, 12)], [entry], [tokens_sent], calls=[cot_sent]),
        Section([(2, 0, 12)], [turn_cot], [cot_sent], rest=3),
        Section([(3, 0, 12)], [norm], [branch_sent], rest=4),
        Section([(4, 0, 12)]),
        Section([(5, 0, 12)], expands, [normed_sent], rest=4),
        Section([(6, 0, 12)], [hidden, turn_normed]),
    ]
    exchanges = [tokens_sent, cot_sent, branch_sent, normed_sent]
    return plan.run(ring, sections, exchanges, row_and_column_peers, [tokens_sent], "forward", 0)


def run_backward(arrays):
    columns = lax.axis_size("tp")
    plan = Plan(arrays)
    shapes, add = plan.shapes, plan.add
    rows, own = arrays["tokens"].shape
    for name in ("two_terms", "mixed_terms", "branch_blocks", "one_terms"):
        plan.define(name, (columns, rows, own), LOW)
    two_sent = PeerCopies("two_term", "two_terms")
    mixed_sent = PeerCopies("mixed_term", "mixed_terms")
    branch_sent = PeerCopies("branch_own", "branch_blocks")
    one_sent = PeerCopies("one_term", "one_terms")

    hidden = add(
        HiddenGradJob(shapes["cot_blocks"], shapes["shrink_full1"], shapes["gate_rows1"], shapes["up_rows1"]),
        ["cot_blocks", "shrink_full1", "gate_rows1", "up_rows1"],
        ["gate_grad1", "up_grad1"],
    )
    names = [["gate_grad0", "up_grad0", "gate_grad1", "up_grad1"], ["gate_full0", "up_full0", "gate_full1", "up_full1"]]
    two_job = WidthJob(*[[shapes[name] for name in side] for side in names])
    two_job.then = two_sent
    two = add(two_job, names[0] + names[1], ["two_term"])
    names = [["activation0", "activation1"], ["shrink_full0", "shrink_full1"]]
    mixed = add(WidthJob(*[[shapes[name] for name in side] for side in names]), names[0] + names[1], ["mixed_term"])
    back_two = NormBackJob(
        shapes["two_terms"], shapes["residual"], shapes["scale_two"], shapes["wide"], 4, shapes["cotangent"], True
    )
    back_two.then = branch_sent
    names = ["two_terms", "residual", "scale_two", "wide", "cotangent"]
    norm_two = add(back_two, names, ["residual_grad", "gain_two_grad", "branch_own"])
    names = ["branch_blocks", "exit_full", "entry_full", "projected", "conv_out", "gated", "halo", "wide", "bound"]
    mixer_job = MixerGradJob(*[shapes[name] for name in names])
    mixer_job.then = one_sent
    mixer = add(mixer_job, names, ["projected_grad", "one_term", "taps_grad"])
    turn = add(TurnJob(shapes["branch_blocks"]), ["branch_blocks"], ["branch_full"])
    back_one = NormBackJob(
        shapes["one_terms"], shapes["tokens"], shapes["scale_one"], shapes["wide"], 3, shapes["residual_grad"], False
    )
    names = ["one_terms", "tokens", "scale_one", "wide", "residual_grad"]
    norm_one = add(back_one, names, ["tokens_grad", "gain_one_grad"])
    small_job = SmallSumJob(shapes["taps_grad"], shapes["gain_two_grad"], back_one)
    small = add(small_job, ["taps_grad", "gain_two_grad"], ["small_part"])
    total = add(SumJob(shapes["residual"], shapes["mixed_terms"]), ["residual", "mixed_terms"], ["mixed"])

    wide = own
    halves = [("cot_full", "activation0"), ("cot_full", "activation1")]
    halves += [("normed_two", name) for name in ("gate_grad0", "up_grad0", "gate_grad1", "up_grad1")]
    halves += [("normed_one", "projected_grad")]
    groups = [[(left, right, 0), (left, right, wide)] for left, right in halves]
    groups += [[("normed_one", "projected_grad", 2 * wide), ("branch_full", "mixer", 0)]]
    places = {"cot_full": 0, "normed_two": 1, "normed_one": 0, "branch_full": 2}
    ring = ScatterRing(groups, places, shapes, wide)
    sums = ["shrink0", "shrink1", "gate0", "up0", "gate1", "up1", "entry", "entry_exit"]
    for name, shape in zip(sums, ring.out_shapes):
        plan.shapes[name] = shape
    ring.outs = sums
    sections = [
        Section([(0, 0, 5)], [hidden]),
        Section([(0, 5, 12), (1, 0, 4)], [two]),
        Section([(1, 4, 12), (2, 0, 5)], [mixed]),
        Section([(2, 5, 12)], [norm_two], [two_sent]),
        Section([(3, 0, 12)]),
        Section([(4, 0, 12)], [mixer], [branch_sent], rest=2),
        Section([(5, 0, 12)], [turn], calls=[mixed_sent]),
        Section([(6, 0, 12)], [norm_one, small], [one_sent], rest=3),
        Section([(7, 0, 12)], [total], [mixed_sent]),
    ]
    exchanges = [two_sent, mixed_sent, branch_sent, one_sent]
    return plan.run(ring, sections, exchanges, row_and_column_peers, [], "backward", 1)


def rows_of(ref, gathered):
    if not gathered:
        return ref
    count, rows, columns = ref.shape
    return ref.reshape(count * rows, columns)


def flat(full):
    return full.reshape(full.shape[0] * full.shape[1], full.shape[2])


def contract_cols(left, right):
    return lax.dot_general(
        left, right, (((1,), (1,)), ((), ())), preferred_element_type=jnp.float32
    )


def adam_update(weight, first, second, grad, rate, decay):
    first_next = BETA_ONE * first + (1.0 - BETA_ONE) * grad
    second_next = BETA_TWO * second + (1.0 - BETA_TWO) * grad * grad
    corrected = first_next / (1.0 - BETA_ONE**STEP)
    spread = jnp.sqrt(second_next / (1.0 - BETA_TWO**STEP)) + ADAM_EPSILON
    return (weight - rate * (corrected / spread + decay * weight), first_next, second_next)


def adam_kernel(pieces, *refs):
    weight, first, second = refs[:3]
    grads, outs = refs[3 : 3 + pieces], refs[3 + pieces :]
    start = 0
    for grad in grads:
        span = slice(start, start + grad.shape[1])
        start += grad.shape[1]
        results = adam_update(weight[:, span], first[:, span], second[:, span], grad[...], RATE_WIDE, WEIGHT_DECAY)
        for out, result in zip(outs, results):
            out[:, span] = result


def adam_rows(weight, first, second, grads):
    rows, columns = weight.shape
    block = max(rows // 4, 8)
    state = pl.BlockSpec((block, columns), lambda step: (step, 0))
    grad_specs = [pl.BlockSpec((block, grad.shape[1]), lambda step: (step, 0)) for grad in grads]
    return pl.pallas_call(
        functools.partial(adam_kernel, len(grads)),
        out_shape=[jax.ShapeDtypeStruct(weight.shape, weight.dtype)] * 3,
        grid=(rows // block,),
        in_specs=[state] * 3 + grad_specs,
        out_specs=[state] * 3,
        compiler_params=pltpu.CompilerParams(vmem_limit_bytes=VMEM_BYTES),
        cost_estimate=pl.CostEstimate(flops=20 * weight.size, bytes_accessed=28 * weight.size, transcendentals=0),
        name="adam_rows",
    )(weight, first, second, *grads)


def adam_mixer_kernel(*refs):
    entries, exits, grads, outs = refs[:3], refs[3:6], refs[6:8], refs[8:]
    planes, _, columns = entries[0].shape
    for plane in range(planes + 1):
        grad = grads[plane // 2][:, plane % 2 * columns : (plane % 2 + 1) * columns]
        state = [ref[plane] for ref in entries] if plane < planes else [ref[...] for ref in exits]
        results = adam_update(*state, grad, RATE_WIDE, WEIGHT_DECAY)
        for place, result in enumerate(results):
            if plane < planes:
                outs[place][plane] = result
            else:
                outs[3 + place][...] = result


def adam_mixer(entries, exits, grad, last):
    rows, planes, columns = entries[0].shape
    block = max(rows // 4, 8)
    entry_spec = pl.BlockSpec((planes, block, columns), lambda step: (0, step, 0))
    exit_spec = pl.BlockSpec((block, columns), lambda step: (step, 0))
    grad_spec = pl.BlockSpec((block, 2 * columns), lambda step: (step, 0))
    size = entries[0].size + exits[0].size
    results = pl.pallas_call(
        adam_mixer_kernel,
        out_shape=[jax.ShapeDtypeStruct((planes, rows, columns), jnp.float32)] * 3
        + [jax.ShapeDtypeStruct((rows, columns), jnp.float32)] * 3,
        grid=(rows // block,),
        in_specs=[entry_spec] * 3 + [exit_spec] * 3 + [grad_spec] * 2,
        out_specs=[entry_spec] * 3 + [exit_spec] * 3,
        compiler_params=pltpu.CompilerParams(vmem_limit_bytes=VMEM_BYTES),
        cost_estimate=pl.CostEstimate(flops=20 * size, bytes_accessed=28 * size, transcendentals=0),
        name="adam_mixer",
    )(*[array.transpose(1, 0, 2) for array in entries], *exits, grad, last)
    return [result.transpose(1, 0, 2) for result in results[:3]] + list(results[3:])


def adam_pairs_kernel(lanes, *refs):
    weight, first, second = refs[:3]
    grads, outs, mixed = refs[3:7], refs[7:10], refs[10]
    rows = grads[0].shape[0]
    tiles = grads[0].shape[1] // lanes
    for which, grad in enumerate(grads):
        half, side = which // 2, which % 2
        for tile in range(tiles):
            place = (half * tiles + tile) * 2 + side
            mixed[pl.ds(place, rows, stride=4 * tiles), :] = grad[:, tile * lanes : (tile + 1) * lanes]
    results = adam_update(weight[...], first[...], second[...], mixed[...], RATE_WIDE, WEIGHT_DECAY)
    for out, result in zip(outs, results):
        out[...] = result


def paired(array):
    rows, _, columns = array.shape
    return array.reshape(rows, 2, columns // LANES, LANES).transpose(0, 2, 1, 3).reshape(-1, LANES)


def adam_pairs(weight, first, second, grads):
    rows, _, columns = weight.shape
    deep = columns // LANES
    block = max(rows // 8, 8)
    state = pl.BlockSpec((block * deep * 2, LANES), lambda step: (step, 0))
    results = pl.pallas_call(
        functools.partial(adam_pairs_kernel, LANES),
        out_shape=[jax.ShapeDtypeStruct((rows * deep * 2, LANES), weight.dtype)] * 3,
        grid=(rows // block,),
        in_specs=[state] * 3 + [pl.BlockSpec((block, columns // 2), lambda step: (step, 0))] * 4,
        out_specs=[state] * 3,
        scratch_shapes=[pltpu.VMEM((block * deep * 2, LANES), jnp.float32)],
        cost_estimate=pl.CostEstimate(flops=20 * weight.size, bytes_accessed=28 * weight.size, transcendentals=0),
        name="adam_pairs",
    )(paired(weight), paired(first), paired(second), *grads)
    return [
        result.reshape(rows, deep, 2, LANES).transpose(0, 2, 1, 3).reshape(rows, 2, columns) for result in results
    ]


def shards(
    tokens,
    bounds,
    cotangent,
    entry_weight,
    entry_first,
    entry_second,
    exit_weight,
    exit_first,
    exit_second,
    expand_weight,
    expand_first,
    expand_second,
    shrink_weight,
    shrink_first,
    shrink_second,
    conv_kernel,
    conv_first,
    conv_second,
    norm_gains,
    gain_first,
    gain_second,
):
    channels = tokens.shape[1]
    seen = conv_kernel.shape[1]
    small = jnp.concatenate([conv_kernel, norm_gains], axis=0)
    small = jnp.pad(small, ((0, 16 - small.shape[0]), (0, LANES - seen))).astype(LOW)
    entry_low = entry_weight.reshape(entry_weight.shape[0], 3 * channels).astype(LOW)
    bound = jnp.broadcast_to(bounds[0], (8, 128))
    made = run_forward(
        {
            "entry_low": entry_low,
            "exit_low": exit_weight.astype(LOW),
            "small": small,
            "tokens": tokens,
            "cotangent": cotangent,
            "bound": bound,
            "pairs": paired(expand_weight),
            "shrink": shrink_weight,
        },
        seen,
    )
    names = ["wide", "exit_full", "entry_full", "projected", "conv_out", "gated", "halo", "mixer", "residual"]
    names += ["scale_one", "scale_two", "cot_blocks", "cot_full", "normed_one", "normed_two", "gate_grad0", "up_grad0"]
    names += ["gate_rows1", "up_rows1", "activation0", "activation1"]
    names += [name + half for name in ("gate_full", "up_full", "shrink_full") for half in "01"]
    given = {"tokens": tokens, "cotangent": cotangent, "bound": bound}
    grads = run_backward(given | {name: made[name] for name in names})
    mixed, tokens_grad = grads["mixed"], grads["tokens_grad"]
    small_part = lax.dynamic_slice_in_dim(grads["small_part"], lax.axis_index("seq") * seen, seen, axis=1)
    kernel_part = small_part[:3]
    gains_part = small_part[3:5]
    (
        entry_next,
        entry_first_next,
        entry_second_next,
        exit_next,
        exit_first_next,
        exit_second_next,
    ) = adam_mixer(
        (entry_weight, entry_first, entry_second),
        (exit_weight, exit_first, exit_second),
        grads["entry"],
        grads["entry_exit"],
    )
    expand_next, expand_first_next, expand_second_next = adam_pairs(
        expand_weight, expand_first, expand_second, [grads[name] for name in ("gate0", "up0", "gate1", "up1")]
    )
    shrink_next, shrink_first_next, shrink_second_next = adam_rows(
        shrink_weight, shrink_first, shrink_second, [grads["shrink0"], grads["shrink1"]]
    )
    conv_next, conv_first_next, conv_second_next = adam_update(
        conv_kernel, conv_first, conv_second, kernel_part, RATE_CONV, 0.0
    )
    gains_next, gains_first_next, gains_second_next = adam_update(
        norm_gains, gain_first, gain_second, gains_part, RATE_GAIN, 0.0
    )
    return (
        mixed,
        tokens_grad,
        entry_next,
        entry_first_next,
        entry_second_next,
        exit_next,
        exit_first_next,
        exit_second_next,
        expand_next,
        expand_first_next,
        expand_second_next,
        shrink_next,
        shrink_first_next,
        shrink_second_next,
        conv_next,
        conv_first_next,
        conv_second_next,
        gains_next,
        gains_first_next,
        gains_second_next,
    )


def solution(mesh):
    rows = P("seq", "tp")
    stacked = P("seq", None, "tp")
    small = P(None, ("tp", "seq"))
    return jax.shard_map(
        shards,
        mesh=mesh,
        in_specs=(rows, P("seq"), rows) + (stacked,) * 3 + (rows,) * 3 + (stacked,) * 3 + (rows,) * 3 + (small,) * 6,
        out_specs=(rows, rows) + (stacked,) * 3 + (rows,) * 3 + (stacked,) * 3 + (rows,) * 3 + (small,) * 6,
        check_vma=False,
    )
```

```python
import functools

import jax
import jax.numpy as jnp
from jax import lax
from jax.experimental import pallas as pl
from jax.experimental.pallas import tpu as pltpu
from jax.sharding import PartitionSpec as P

D = 2048
STEP = 10


EPSILON = 1e-05
BETA_ONE = 0.9
BETA_TWO = 0.95
ADAM_EPSILON = 1e-08
WEIGHT_DECAY = 0.1
RATE_WIDE = 0.04
RATE_CONV = 0.5
RATE_GAIN = 0.4

MESH = pl.DeviceIdType.MESH
LOW = jnp.bfloat16
LANES = 128
VMEM_BYTES = 60 * 1024 * 1024


def ring_place(index, count):
    side = index % 2
    level = index // 2
    return level * (1 - side) + (count - 1 - level) * side


def ring_index(place, count):
    back = place // (count // 2)
    return (1 - back) * (2 * place) + back * (2 * (count - 1 - place) + 1)


def ring_ends(count):
    place = ring_place(lax.axis_index("seq"), count)
    ahead = ring_index((place + 1) % count, count)
    behind = ring_index((place + count - 1) % count, count)
    return place, ahead, behind


def greet(peers):
    barrier = pltpu.get_barrier_semaphore()
    for peer in peers:
        pl.semaphore_signal(barrier, inc=1, device_id=peer, device_id_type=MESH)
    pl.semaphore_wait(barrier, len(peers))


def split(items, sizes):
    parts, start = [], 0
    for size in sizes:
        parts.append(items[start : start + size])
        start += size
    return parts


class GatherRing:
    def __init__(self, groups, shapes):
        self.count = lax.axis_size("seq")
        self.groups = groups
        self.rows = {full: shapes[shard].shape[0] for group in groups for shard, full in group}
        self.order = {full: place for place, full in enumerate(self.rows)}
        self.parts = 2 if min(self.rows.values()) % 64 == 0 else 1
        self.ticks = (self.count - 2) * self.parts
        arrays = len(self.rows)
        sems = pltpu.SemaphoreType.DMA((arrays, 2, self.parts, self.count - 1))
        self.scratch = [sems, sems, pltpu.SemaphoreType.DMA((arrays,))]
        self.flops = 0

    def bind(self, refs, scratch):
        self.refs = refs
        self.send_sem, self.recv_sem, self.own_sem = scratch
        self.column = lax.axis_index("tp")
        self.place, self.ahead, self.behind = ring_ends(self.count)

    def copy(self, shard, full, way, part, step, first=False):
        move = (self.place + self.count - step) if way == 0 else (self.place + step)
        owner = ring_index(move % self.count, self.count)
        half = self.rows[full] // 2
        size = half // self.parts
        rows = pl.ds(pl.multiple_of(way * half + part * size, 16), size)
        there = self.refs[full].at[owner, rows]
        return pltpu.make_async_remote_copy(
            src_ref=self.refs[shard].at[rows] if first else there,
            dst_ref=there,
            send_sem=self.send_sem.at[self.order[full], way, part, step],
            recv_sem=self.recv_sem.at[self.order[full], way, part, step],
            device_id=(self.ahead if way == 0 else self.behind, self.column),
            device_id_type=MESH,
        )

    def own(self, shard, full):
        there = self.refs[full].at[lax.axis_index("seq")]
        return pltpu.make_async_copy(self.refs[shard], there, self.own_sem.at[self.order[full]])

    def pieces(self, group):
        return [(shard, full, way) for shard, full in self.groups[group] for way in range(2)]

    def begin(self, group):
        for part in range(self.parts):
            for shard, full, way in self.pieces(group):
                self.copy(shard, full, way, part, 0, True).start()
        for shard, full in self.groups[group]:
            self.own(shard, full).start()

    def tick(self, group, index):
        step, part = 1 + index // self.parts, index % self.parts
        for shard, full, way in self.pieces(group):
            self.copy(shard, full, way, part, step - 1).wait_recv()
            self.copy(shard, full, way, part, step).start()

    def prepare(self):
        pass

    def turn(self, group):
        self.begin(group)
        self.settle(group - 1)

    def settled(self, group):
        pass

    def settle(self, group):
        for part in range(self.parts):
            for shard, full, way in self.pieces(group):
                self.copy(shard, full, way, part, self.count - 2).wait_recv()
        for shard, full in self.groups[group]:
            self.own(shard, full).wait()

    def finish(self):
        def sent(step, carry):
            for group in range(len(self.groups)):
                for part in range(self.parts):
                    for shard, full, way in self.pieces(group):
                        self.copy(shard, full, way, part, step).wait_send()
            return carry

        lax.fori_loop(0, self.count - 1, sent, 0)


class PeerCopies:
    def __init__(self, source, target):
        self.source, self.target = source, target
        columns = lax.axis_size("tp")
        self.scratch = [pltpu.SemaphoreType.DMA((columns,)), pltpu.SemaphoreType.DMA((columns,))]

    def bind(self, refs, scratch):
        self.source_ref, self.target_ref = refs[self.source], refs[self.target]
        self.send_sem, self.recv_sem = scratch
        self.columns = lax.axis_size("tp")
        self.seq, self.column = lax.axis_index("seq"), lax.axis_index("tp")

    def block(self, peer):
        if len(self.source_ref.shape) == len(self.target_ref.shape):
            return self.source_ref.at[peer]
        return self.source_ref

    def own(self):
        return pltpu.make_async_copy(
            self.block(self.column), self.target_ref.at[self.column], self.send_sem.at[0]
        )

    def copy(self, step):
        peer = (self.column + step) % self.columns
        return pltpu.make_async_remote_copy(
            src_ref=self.block(peer),
            dst_ref=self.target_ref.at[self.column],
            send_sem=self.send_sem.at[step],
            recv_sem=self.recv_sem.at[step],
            device_id=(self.seq, peer),
            device_id_type=MESH,
        )

    def start(self):
        for step in range(1, self.columns):
            self.copy(step).start()
        self.own().start()

    def wait(self):
        self.own().wait()
        for step in range(1, self.columns):
            self.copy(step).wait_recv()

    def finish(self):
        for step in range(1, self.columns):
            self.copy(step).wait_send()


class ScatterRing:
    def __init__(self, groups, places, shapes, wide):
        self.count = lax.axis_size("seq")
        self.groups, self.places, self.wide = groups, places, wide
        self.names = list(places)
        left = shapes[self.names[0]]
        features, tokens = left.shape
        self.rows = features // self.count
        self.parts = 2
        self.ticks = (self.count - 2) * self.parts
        sems = pltpu.SemaphoreType.DMA((len(groups), 2, self.parts, self.count - 1))
        buffers = max(places.values()) + 1
        self.scratch = [
            pltpu.VMEM((buffers, features, tokens), LOW),
            pltpu.VMEM((2, 2, tokens, wide), LOW),
            pltpu.VMEM((2, 2, self.count, self.rows, wide), LOW),
            pltpu.VMEM((2, self.rows, 2 * wide), jnp.float32),
            sems,
            sems,
            pltpu.SemaphoreType.DMA((len(self.names),)),
            pltpu.SemaphoreType.DMA((2, 2)),
            pltpu.SemaphoreType.DMA((2,)),
        ]
        self.flops = 4 * len(groups) * features * tokens * wide
        self.out_shapes = [jax.ShapeDtypeStruct((self.rows, 2 * wide), jnp.float32)] * len(groups)

    def bind(self, refs, scratch):
        self.refs, self.out_refs = refs, [refs[name] for name in self.outs]
        self.lefts, self.rights, self.slots, self.finals = scratch[:4]
        self.send_sem, self.recv_sem, self.left_sem, self.right_sem, self.done_sem = scratch[4:]
        self.column = lax.axis_index("tp")
        self.place, self.ahead, self.behind = ring_ends(self.count)

    def left_load(self, name):
        return pltpu.make_async_copy(
            self.refs[name], self.lefts.at[self.places[name]], self.left_sem.at[self.names.index(name)]
        )

    def right_load(self, group, way):
        _, name, start = self.groups[group][way]
        source = self.refs[name].at[:, pl.ds(start, self.wide)]
        return pltpu.make_async_copy(source, self.rights.at[group % 2, way], self.right_sem.at[group % 2, way])

    def fetch(self, group):
        for way in range(2):
            self.right_load(group, way).start()

    def span(self, part):
        width = self.wide // self.parts
        return pl.ds(pl.multiple_of(part * width, 128), width)

    def term(self, group, way, part, step):
        move = (self.place + 2 * self.count - 1 - step) if way == 0 else (self.place + 1 + step)
        owner = ring_index(move % self.count, self.count)
        rows = pl.ds(pl.multiple_of(owner * self.rows, 16), self.rows)
        left = self.lefts[self.places[self.groups[group][way][0]], rows, :]
        right = self.rights[group % 2, way, :, self.span(part)]
        return jnp.dot(left, right, preferred_element_type=jnp.float32)

    def held(self, group, way, part, step):
        return self.slots.at[group % 2, way, step, :, self.span(part)]

    def copy(self, group, way, part, step):
        return pltpu.make_async_remote_copy(
            src_ref=self.held(group, way, part, step),
            dst_ref=self.held(group, way, part, step + 1),
            send_sem=self.send_sem.at[group, way, part, step],
            recv_sem=self.recv_sem.at[group, way, part, step],
            device_id=(self.ahead if way == 0 else self.behind, self.column),
            device_id_type=MESH,
        )

    def store(self, group):
        return pltpu.make_async_copy(self.finals.at[group % 2], self.out_refs[group], self.done_sem.at[group % 2])

    def prepare(self):
        self.left_load("cot_full").start()
        self.fetch(0)
        self.left_load("normed_two").start()

    def turn(self, group):
        self.begin(group)
        self.settle(group - 1)
        self.settled(group - 1)

    def settled(self, group):
        if group + 2 < len(self.groups):
            self.fetch(group + 2)
        if group == 1:
            self.left_load("normed_one").start()
        if group == 5:
            self.left_load("branch_full").start()

    def begin(self, group):
        for name, first in (("cot_full", 0), ("normed_two", 2), ("normed_one", 6), ("branch_full", 7)):
            if group == first:
                self.left_load(name).wait()
        for way in range(2):
            self.right_load(group, way).wait()
        for part in range(self.parts):
            for way in range(2):
                self.held(group, way, part, 0)[...] = self.term(group, way, part, 0).astype(LOW)
                self.copy(group, way, part, 0).start()

    def tick(self, group, index):
        step, part = 1 + index // self.parts, index % self.parts
        for way in range(2):
            mine = self.term(group, way, part, step)
            self.copy(group, way, part, step - 1).wait_recv()
            held = self.held(group, way, part, step)
            held[...] = (held[...].astype(jnp.float32) + mine).astype(LOW)
            self.copy(group, way, part, step).start()

    def settle(self, group):
        last = self.count - 1
        if group >= 1:
            self.store(group - 1).wait()
        for part in range(self.parts):
            for way in range(2):
                mine = self.term(group, way, part, last)
                self.copy(group, way, part, last - 1).wait_recv()
                width = self.wide // self.parts
                start = way * self.wide + part * width
                self.finals[group % 2, :, start : start + width] = (
                    self.held(group, way, part, last)[...].astype(jnp.float32) + mine
                )
        self.store(group).start()

        def sent(step, carry):
            for part in range(self.parts):
                for way in range(2):
                    self.copy(group, way, part, step).wait_send()
            return carry

        lax.fori_loop(0, last, sent, 0)

    def finish(self):
        self.store(len(self.groups) - 1).wait()


class Job:
    wide = 256
    kept = []
    late = ()

    def hold(self, refs):
        pass

    def __init__(self, whole, tiled, outs, tiles, flops):
        self.whole, self.tiled = whole, tiled
        self.inputs = list(whole) + [array for array, axis in tiled]
        self.axes = [axis for array, axis in tiled]
        self.out_shapes = [jax.ShapeDtypeStruct(shape, dtype) for shape, dtype in outs]
        self.tiles = tiles
        self.flops = flops
        self.scratch = (
            [pltpu.VMEM(array.shape, array.dtype) for array in self.inputs]
            + [pltpu.VMEM(shape, dtype) for shape, dtype in outs]
            + [
                pltpu.SemaphoreType.DMA((len(whole),)),
                pltpu.SemaphoreType.DMA((len(tiled), tiles)),
                pltpu.SemaphoreType.DMA((len(outs), tiles)),
            ]
        )

    def bind(self, ins, outs, scratch):
        self.in_refs, self.out_refs = ins, outs
        sizes = [len(self.whole), len(self.tiled), len(outs)]
        self.whole_v, self.tiled_v, self.outs_v = split(scratch, sizes)
        self.whole_sem, self.tiled_sem, self.out_sem = scratch[sum(sizes) :]

    def peers(self):
        return []

    def window(self, axis, index):
        span = pl.ds(pl.multiple_of(index * self.wide, 128), self.wide)
        return (span,) if axis == 0 else (slice(None), span)

    def whole_load(self, which):
        return pltpu.make_async_copy(self.in_refs[which], self.whole_v[which], self.whole_sem.at[which])

    def tiled_load(self, which, index):
        window = self.window(self.axes[which], index)
        there = self.in_refs[len(self.whole) + which].at[window]
        return pltpu.make_async_copy(there, self.tiled_v[which].at[window], self.tiled_sem.at[which, index])

    def out_window(self, index):
        return self.window(1, index)

    def store(self, which, index):
        window = self.out_window(index)
        return pltpu.make_async_copy(
            self.outs_v[which].at[window], self.out_refs[which].at[window], self.out_sem.at[which, index]
        )

    def start(self, late):
        for which in range(len(self.whole)):
            if late == (which in self.late):
                self.whole_load(which).start()

        def begin(index, carry):
            for which in range(len(self.tiled)):
                self.tiled_load(which, index).start()
            return carry

        if not late:
            lax.fori_loop(0, self.tiles, begin, 0)

    def tile(self, index):
        @pl.when(index == 0)
        def _():
            for which in range(len(self.whole)):
                self.whole_load(which).wait()

        for which in range(len(self.tiled)):
            self.tiled_load(which, index).wait()
        tiles = [ref[self.window(axis, index)] for ref, axis in zip(self.tiled_v, self.axes)]
        for which, value in enumerate(self.compute(self.whole_v, tiles)):
            self.outs_v[which][self.out_window(index)] = value
            self.store(which, index).start()

    def finish(self):
        def end(index, carry):
            for which in range(len(self.outs_v)):
                self.store(which, index).wait()
            return carry

        lax.fori_loop(0, self.tiles, end, 0)


def blocks_dot(blocks, weight):
    parts, _, depth = blocks.shape
    total = None
    for part in range(parts):
        term = jnp.dot(blocks[part], weight[part * depth : (part + 1) * depth], preferred_element_type=jnp.float32)
        total = term if total is None else total + term
    return total


class ExpandJob(Job):

    late = (0,)

    def __init__(self, normed, gate_full, up_full):
        rows, width = normed.shape[1], gate_full.shape[1]
        outs = [((rows, width), jnp.float32), ((rows, width), jnp.float32), ((rows, width), LOW)]
        super().__init__(
            [normed], [(gate_full, 1), (up_full, 1)], outs, width // self.wide, 4 * rows * gate_full.size
        )

    def compute(self, whole, tiles):
        gate_rows = blocks_dot(whole[0], tiles[0])
        up_rows = blocks_dot(whole[0], tiles[1])
        return gate_rows, up_rows, (gate_rows * jax.nn.sigmoid(gate_rows) * up_rows).astype(LOW)


class HiddenGradJob(Job):
    def __init__(self, cot, shrink_full, gate_rows, up_rows):
        rows, width = gate_rows.shape
        outs = [((rows, width), LOW), ((rows, width), LOW)]
        tiled = [(shrink_full, 1), (gate_rows, 1), (up_rows, 1)]
        super().__init__([cot], tiled, outs, width // self.wide, 2 * rows * shrink_full.size)

    def compute(self, whole, tiles):
        _, gate_rows, up_rows = tiles
        act_grad = blocks_dot(whole[0], tiles[0])
        sigmoid_gate = jax.nn.sigmoid(gate_rows)
        gate_grad = act_grad * up_rows * sigmoid_gate * (1.0 + gate_rows * (1.0 - sigmoid_gate))
        return gate_grad.astype(LOW), (act_grad * (gate_rows * sigmoid_gate)).astype(LOW)


class WidthJob(Job):
    then = None

    def __init__(self, lefts, weights):
        rows, width = lefts[0].shape[0], weights[0].shape[0]
        flops = 2 * rows * sum(weight.size for weight in weights)
        parts = lax.axis_size("tp")
        self.own = width // parts
        out = ((parts, rows, self.own), LOW)
        super().__init__(lefts, [(weight, 0) for weight in weights], [out], width // self.wide, flops)

    def out_window(self, index):
        each = self.own // self.wide
        return index // each, slice(None), pl.ds(pl.multiple_of(index % each * self.wide, 128), self.wide)

    def compute(self, whole, tiles):
        total = None
        for left, weight in zip(whole, tiles):
            term = contract_cols(left[...], weight)
            total = term if total is None else total + term
        return (total.astype(LOW),)

    def finish(self):
        super().finish()
        if self.then:
            self.then.start()


class MixerJob:
    kept = []
    late = ()

    def hold(self, refs):
        self.kept_refs = refs

    def __init__(self, inputs, outs, extra, phases, flops):
        self.inputs = list(inputs)
        self.out_shapes = [jax.ShapeDtypeStruct(shape, dtype) for shape, dtype in outs]
        self.phases = phases
        self.tiles = sum(phases)
        self.flops = flops
        self.scratch = (
            [pltpu.VMEM(array.shape, array.dtype) for array in self.inputs]
            + [pltpu.VMEM(shape, dtype) for shape, dtype in outs]
            + extra
            + [
                pltpu.SemaphoreType.DMA((len(self.inputs),)),
                pltpu.SemaphoreType.DMA((len(outs),)),
            ]
        )

    def bind(self, ins, outs, scratch):
        self.in_refs, self.out_refs = ins, outs
        extra = len(scratch) - len(ins) - len(outs) - 2
        self.ins_v, self.outs_v, self.extra_v = split(scratch, [len(ins), len(outs), extra])
        self.in_sem, self.out_sem = scratch[-2:]
        self.count = lax.axis_size("seq")
        self.seq = lax.axis_index("seq")
        self.column = lax.axis_index("tp")

    def peers(self):
        after = (self.seq + 1) % self.count
        before = (self.seq + self.count - 1) % self.count
        return [(after, self.column), (before, self.column)]

    def load(self, which):
        return pltpu.make_async_copy(self.in_refs[which], self.ins_v[which], self.in_sem.at[which])

    def store(self, which):
        return pltpu.make_async_copy(self.outs_v[which], self.out_refs[which], self.out_sem.at[which])

    def passing(self, source, target, forward):
        step = 1 if forward else self.count - 1
        return pltpu.make_async_remote_copy(
            src_ref=source,
            dst_ref=target,
            send_sem=self.kept_refs[1].at[0],
            recv_sem=self.kept_refs[1].at[1],
            device_id=((self.seq + step) % self.count, self.column),
            device_id_type=MESH,
        )

    def start(self, late):
        for which in range(len(self.inputs)):
            if late == (which in self.late):
                self.load(which).start()

    def tile(self, index):
        begin = 0
        for phase, tiles in enumerate(self.phases):
            here = index - begin

            @pl.when((here >= 0) & (here < tiles))
            def _(phase=phase, here=here, tiles=tiles):
                @pl.when(here == 0)
                def _():
                    self.before(phase)

                self.work(phase, here)

                @pl.when(here == tiles - 1)
                def _():
                    self.after(phase)

            begin += tiles

    def finish(self):
        for which in range(len(self.out_shapes)):
            self.store(which).wait()


def visible(bound_row, shape):
    position = lax.broadcasted_iota(jnp.int32, shape, 0)
    see_one = position != bound_row
    return position, see_one, see_one & (position - 1 != bound_row)


def lagged(rows, halo, position):
    last, second = halo[15:16].astype(jnp.float32), halo[14:15].astype(jnp.float32)
    one = jnp.where(position == 0, last, pltpu.roll(rows, 1, 0))
    two = jnp.where(position == 0, second, jnp.where(position == 1, last, pltpu.roll(rows, 2, 0)))
    return one, two


class EntryJob(MixerJob):
    then = None
    late = (0,)

    def __init__(self, tokens, wide, entry_full, exit_full, bound):
        parts, rows, own = tokens.shape
        width, columns = exit_full.shape
        self.rows, self.columns, self.own = rows, columns, own
        self.width = width
        outs = [
            ((rows, 3 * columns), jnp.float32),
            ((rows, columns), jnp.float32),
            ((rows, columns), LOW),
            ((16, columns), LOW),
            ((rows, columns), LOW),
            ((parts, rows, own), LOW),
            ((rows, 128), jnp.float32),
            ((width, rows), LOW),
        ]
        phases = [rows // 256, 3 * columns // 256, 1, columns // 128, width // 256]
        flops = 2 * rows * (entry_full.size + exit_full.size)
        super().__init__([tokens, wide, entry_full, exit_full, bound], outs, [], phases, flops)
        self.kept = [pltpu.VMEM((16, columns), LOW), pltpu.SemaphoreType.DMA((2,))]

    def halo(self):
        return self.passing(self.outs_v[2].at[pl.ds(self.rows - 16, 16)], self.kept_refs[0], True)

    def before(self, phase):
        if phase == 0:
            for which in (0, 1):
                self.load(which).wait()
        if phase == 1:
            self.store(6).start()
            self.store(7).start()
            self.load(2).wait()
        if phase == 3:
            self.load(4).wait()
            self.halo().wait_recv()
            self.outs_v[3][...] = self.kept_refs[0][...]
            self.store(3).start()
        if phase == 4:
            self.load(3).wait()

    def after(self, phase):
        if phase == 1:
            self.store(0).start()
        if phase == 2:
            self.halo().start()
            self.store(2).start()
        if phase == 3:
            self.store(1).start()
            self.store(4).start()
        if phase == 4:
            self.store(5).start()

    def finish(self):
        self.store(5).wait()
        if self.then:
            self.then.start()
        self.halo().wait_send()
        for which in (0, 1, 2, 3, 4, 6, 7):
            self.store(which).wait()

    def work(self, phase, index):
        tokens, wide, entry, exits, bound = self.ins_v
        taps = wide.at[self.column]
        projected, conv, gated, halo, mixer, term, scales, turned_rows = self.outs_v
        columns = self.columns
        if phase == 0:
            rows = pl.ds(pl.multiple_of(index * 256, 256), 256)
            values = [tokens[part, rows, :].astype(jnp.float32) for part in range(tokens.shape[0])]
            total = sum(jnp.sum(value * value, axis=1, keepdims=True) for value in values)
            scale = lax.rsqrt(total / D + EPSILON)
            scales[rows, :] = jnp.broadcast_to(scale, (256, 128))
            for part, value in enumerate(values):
                normed = (value * scale * wide[part, 3:4, :]).astype(LOW)
                tokens[part, rows, :] = normed
                turned_rows[part * self.own : (part + 1) * self.own, rows] = normed.T
        if phase == 1:
            span = pl.ds(pl.multiple_of(index * 256, 256), 256)
            projected[:, span] = blocks_dot(tokens, entry[:, span])
        if phase == 2:
            gated[...] = (projected[:, :columns] * projected[:, 2 * columns :]).astype(LOW)
        if phase == 3:
            span = pl.ds(pl.multiple_of(index * 128, 128), 128)
            middle = pl.ds(pl.multiple_of(columns + index * 128, 128), 128)
            rows = gated[:, span].astype(jnp.float32)
            position, see_one, see_two = visible(bound[0:1, :], rows.shape)
            before = halo[:, span].astype(jnp.float32) * jnp.where(self.seq > 0, 1.0, 0.0)
            one, two = lagged(rows, before, position)
            total = (
                taps[2:3, span] * rows
                + taps[1:2, span] * jnp.where(see_one, one, 0.0)
                + taps[0:1, span] * jnp.where(see_two, two, 0.0)
            )
            conv[:, span] = total
            mixer[:, span] = (projected[:, middle] * total).astype(LOW)
        if phase == 4:
            features = pl.ds(pl.multiple_of(index * 256, 256), 256)
            owner, inner = index // (self.own // 256), index % (self.own // 256)
            span = pl.ds(pl.multiple_of(inner * 256, 256), 256)
            term[owner, :, span] = contract_cols(mixer[...], exits[features, :]).astype(LOW)


class MixerGradJob(MixerJob):
    then = None
    late = (0,)

    def __init__(self, branch, exit_full, entry_full, projected, conv, gated, halo, wide, bound):
        parts, rows, own = branch.shape
        width, columns = exit_full.shape
        self.rows, self.columns, self.own = rows, columns, own
        outs = [((rows, 3 * columns), LOW), ((parts, rows, own), LOW), ((8, columns), jnp.float32)]
        extra = [
            pltpu.VMEM((rows, columns), jnp.float32),
            pltpu.VMEM((8, columns), jnp.float32),
        ]
        self.kept = [pltpu.VMEM((8, columns), jnp.float32), pltpu.SemaphoreType.DMA((2,))]
        phases = [columns // 256, 1, columns // 128, width // 256]
        flops = 2 * rows * (entry_full.size + exit_full.size)
        inputs = [branch, exit_full, entry_full, projected, conv, gated, halo, wide, bound]
        super().__init__(inputs, outs, extra, phases, flops)

    def back(self):
        return self.passing(self.extra_v[1], self.kept_refs[0], False)

    def before(self, phase):
        if phase == 0:
            for which in (0, 1, 3, 4):
                self.load(which).wait()
        if phase == 1:
            for which in (7, 8):
                self.load(which).wait()
        if phase == 2:
            for which in (5, 6):
                self.load(which).wait()
            self.back().wait_recv()
        if phase == 3:
            self.load(2).wait()

    def after(self, phase):
        if phase == 1:
            self.back().start()
        if phase == 2:
            self.store(0).start()
            self.store(2).start()
        if phase == 3:
            self.store(1).start()

    def finish(self):
        self.store(1).wait()
        if self.then:
            self.then.start()
        self.back().wait_send()
        for which in (0, 2):
            self.store(which).wait()

    def work(self, phase, index):
        branch, exits, entry, projected, conv, gated, halo, wide, bound = self.ins_v
        taps = wide.at[self.column]
        grads, term, taps_grad = self.outs_v
        conv_grad, sent = self.extra_v
        returned = self.kept_refs[0]
        columns, height = self.columns, self.rows
        if phase == 0:
            span = pl.ds(pl.multiple_of(index * 256, 256), 256)
            middle = pl.ds(pl.multiple_of(columns + index * 256, 256), 256)
            mixer_grad = blocks_dot(branch, exits[:, span])
            grads[:, middle] = (mixer_grad * conv[:, span]).astype(LOW)
            conv_grad[:, span] = mixer_grad * projected[:, middle]
        if phase == 1:
            for start in range(0, columns, 128):
                span = slice(start, start + 128)
                rows = conv_grad[0:8, span]
                position, see_one, see_two = visible(bound[0:1, :], rows.shape)
                one = pltpu.roll(jnp.where(see_one, rows, 0.0) * taps[1:2, span], 1, 0)
                two = jnp.where(see_two, rows, 0.0) * taps[0:1, span]
                sent[:, span] = two + jnp.where(position == 0, 0.0, one)
            taps_grad[...] = jnp.zeros_like(taps_grad)
        if phase == 2:
            span = pl.ds(pl.multiple_of(index * 128, 128), 128)
            last = pl.ds(pl.multiple_of(2 * columns + index * 128, 128), 128)
            rows = conv_grad[:, span]
            position, see_one, see_two = visible(bound[0:1, :], rows.shape)
            seen_one, seen_two = jnp.where(see_one, rows, 0.0), jnp.where(see_two, rows, 0.0)
            one = pltpu.roll(seen_one * taps[1:2, span], height - 1, 0)
            two = pltpu.roll(seen_two * taps[0:1, span], height - 2, 0)
            after = returned[:, span] * jnp.where(self.seq < self.count - 1, 1.0, 0.0)
            gated_grad = (
                rows * taps[2:3, span]
                + jnp.where(position == height - 1, after[1:2], one)
                + jnp.where(position < height - 2, two, jnp.where(position == height - 2, after[0:1], 0.0))
            )
            grads[:, span] = (gated_grad * projected[:, last]).astype(LOW)
            grads[:, last] = (gated_grad * projected[:, span]).astype(LOW)
            own_rows = gated[:, span].astype(jnp.float32)
            before = halo[:, span].astype(jnp.float32) * jnp.where(self.seq > 0, 1.0, 0.0)
            lag_one, lag_two = lagged(own_rows, before, position)
            taps_grad[0:1, span] = jnp.sum(seen_two * lag_two, axis=0, keepdims=True)
            taps_grad[1:2, span] = jnp.sum(seen_one * lag_one, axis=0, keepdims=True)
            taps_grad[2:3, span] = jnp.sum(rows * own_rows, axis=0, keepdims=True)
        if phase == 3:
            features = pl.ds(pl.multiple_of(index * 256, 256), 256)
            owner, inner = index // (self.own // 256), index % (self.own // 256)
            span = pl.ds(pl.multiple_of(inner * 256, 256), 256)
            term[owner, :, span] = contract_cols(grads[...], entry[features, :]).astype(LOW)


class Jobs:
    def __init__(self, *jobs):
        self.jobs = jobs
        self.inputs = [item for job in jobs for item in job.inputs]
        self.out_shapes = [item for job in jobs for item in job.out_shapes]
        self.scratch = [item for job in jobs for item in job.scratch]
        self.kept = [item for job in jobs for item in job.kept]
        self.tiles = sum(job.tiles for job in jobs)
        self.flops = sum(job.flops for job in jobs)

    def hold(self, refs):
        for job, own in zip(self.jobs, split(refs, [len(job.kept) for job in self.jobs])):
            job.hold(own)

    def bind(self, ins, outs, scratch):
        groups = zip(
            self.jobs,
            split(ins, [len(job.inputs) for job in self.jobs]),
            split(outs, [len(job.out_shapes) for job in self.jobs]),
            split(scratch, [len(job.scratch) for job in self.jobs]),
        )
        for job, own_ins, own_outs, own_scratch in groups:
            job.bind(own_ins, own_outs, own_scratch)

    def peers(self):
        return [peer for job in self.jobs for peer in job.peers()]

    def start(self, late):
        for job in self.jobs:
            job.start(late)

    def tile(self, index):
        begin = 0
        for job in self.jobs:
            here = index - begin

            @pl.when((here >= 0) & (here < job.tiles))
            def _(job=job, here=here):
                job.tile(here)

            begin += job.tiles

    def finish(self):
        for job in self.jobs:
            job.finish()


class TurnJob(MixerJob):
    late = (0,)

    def __init__(self, blocks):
        parts, rows, own = blocks.shape
        super().__init__([blocks], [((parts * own, rows), blocks.dtype)], [], [rows // 128], 0)

    def peers(self):
        return []

    def before(self, phase):
        self.load(0).wait()

    def after(self, phase):
        self.store(0).start()

    def work(self, phase, index):
        (blocks,), (target,) = self.ins_v, self.outs_v
        parts, _, own = blocks.shape
        rows = pl.ds(pl.multiple_of(index * 128, 128), 128)
        for part in range(parts):
            target[part * own : (part + 1) * own, rows] = blocks[part, rows, :].T


class CastJob(MixerJob):
    def __init__(self, pairs, plain):
        rows, columns = plain.shape
        lanes = pairs.shape[1]
        self.rows, self.half, self.lanes = rows, columns // 2, lanes
        self.block = max(rows // 8, 16)
        outs = [((rows, columns // 2), LOW)] * 6
        super().__init__([pairs, plain], outs, [], [rows // self.block], 0)

    def peers(self):
        return []

    def before(self, phase):
        for which in range(2):
            self.load(which).wait()

    def after(self, phase):
        for which in range(6):
            self.store(which).start()

    def work(self, phase, index):
        pairs, plain = self.ins_v
        block, half, lanes = self.block, self.half, self.lanes
        tiles = half // lanes
        rows = pl.ds(pl.multiple_of(index * block, 16), block)
        start = index * (block * 4 * tiles)
        for which in range(4):
            side, plane = which // 2, which % 2
            for tile in range(tiles):
                place = (side * tiles + tile) * 2 + plane
                picked = pairs[pl.ds(start + place, block, stride=4 * tiles), :]
                self.outs_v[which][rows, tile * lanes : (tile + 1) * lanes] = picked.astype(LOW)
        for side in range(2):
            self.outs_v[4 + side][rows, :] = plain[rows, side * half : (side + 1) * half].astype(LOW)


class SmallGatherJob:
    tiles, flops = 1, 0

    def __init__(self, own, seen):
        self.inputs = [own]
        self.seen = seen
        devices, columns = lax.axis_size("seq"), lax.axis_size("tp")
        wide = (columns, 8, devices * seen)
        self.out_shapes = [jax.ShapeDtypeStruct(wide, jnp.float32)]
        self.scratch = [pltpu.VMEM(wide, jnp.float32), pltpu.SemaphoreType.DMA((2,))]
        self.kept = [
            pltpu.VMEM((devices, columns) + own.shape, own.dtype),
            pltpu.SemaphoreType.DMA((columns,)),
            pltpu.SemaphoreType.DMA((columns,)),
            pltpu.SemaphoreType.DMA((devices,)),
            pltpu.SemaphoreType.DMA((devices,)),
        ]

    def hold(self, refs):
        self.whole, self.near_send, self.near_recv, self.far_send, self.far_recv = refs
        self.devices, self.columns = lax.axis_size("seq"), lax.axis_size("tp")
        self.seq, self.column = lax.axis_index("seq"), lax.axis_index("tp")

    def bind(self, ins, outs, scratch):
        self.source, self.target = ins[0], outs[0]
        self.wide, self.local_sem = scratch

    def peers(self):
        near = [(self.seq, (self.column + step) % self.columns) for step in range(1, self.columns)]
        far = [((self.seq + step) % self.devices, self.column) for step in range(1, self.devices)]
        return near + far

    def near(self, step):
        piece = self.whole.at[self.seq, self.column]
        return pltpu.make_async_remote_copy(
            src_ref=piece,
            dst_ref=piece,
            send_sem=self.near_send.at[step],
            recv_sem=self.near_recv.at[step],
            device_id=(self.seq, (self.column + step) % self.columns),
            device_id_type=MESH,
        )

    def far(self, step):
        piece = self.whole.at[self.seq]
        return pltpu.make_async_remote_copy(
            src_ref=piece,
            dst_ref=piece,
            send_sem=self.far_send.at[step],
            recv_sem=self.far_recv.at[step],
            device_id=((self.seq + step) % self.devices, self.column),
            device_id_type=MESH,
        )

    def start(self, late):
        if late:
            return
        load = pltpu.make_async_copy(self.source, self.whole.at[self.seq, self.column], self.local_sem.at[0])
        load.start()
        load.wait()
        for step in range(1, self.columns):
            self.near(step).start()

    def tile(self, index):
        for step in range(1, self.columns):
            self.near(step).wait()

        def begin(step, carry):
            self.far(step).start()
            return carry

        lax.fori_loop(1, self.devices, begin, 0)

    def finish(self):
        def end(step, carry):
            self.far(step).wait()
            return carry

        lax.fori_loop(1, self.devices, end, 0)
        each = LANES // self.seen
        for column in range(self.columns):
            for start in range(0, self.devices, each):
                total = None
                for inner in range(each):
                    piece = self.whole[start + inner, column, :, :].astype(jnp.float32)[:8]
                    piece = pltpu.roll(piece, inner * self.seen, 1) if inner else piece
                    total = piece if total is None else total + piece
                self.wide[column, :, start * self.seen : start * self.seen + LANES] = total
        store = pltpu.make_async_copy(self.wide, self.target, self.local_sem.at[1])
        store.start()
        store.wait()


class RowSumJob(MixerJob):
    block = 128

    def __init__(self, inputs, outs, extra, rows, flops):
        self.columns = lax.axis_size("tp")
        blocks = rows // self.block
        self.kept = [
            pltpu.VMEM((self.columns, blocks, self.block), jnp.float32),
            pltpu.SemaphoreType.DMA((self.columns,)),
            pltpu.SemaphoreType.DMA((self.columns,)),
        ]
        totals = pltpu.VMEM((blocks, self.block), jnp.float32)
        super().__init__(inputs, outs, [totals] + extra, [blocks, 1, blocks], flops)

    def peers(self):
        return [(self.seq, (self.column + step) % self.columns) for step in range(1, self.columns)]

    def share(self, step):
        return pltpu.make_async_remote_copy(
            src_ref=self.kept_refs[0].at[0],
            dst_ref=self.kept_refs[0].at[step],
            send_sem=self.kept_refs[1].at[step],
            recv_sem=self.kept_refs[2].at[step],
            device_id=(self.seq, (self.column + step) % self.columns),
            device_id_type=MESH,
        )

    def before(self, phase):
        if phase == 0:
            for which in range(len(self.inputs)):
                self.load(which).wait()

    def after(self, phase):
        if phase == 0:
            for step in range(1, self.columns):
                self.share(step).start()
        if phase == 2:
            for which in range(len(self.out_shapes)):
                self.store(which).start()

    def finish(self):
        for step in range(1, self.columns):
            self.share(step).wait_send()
        super().finish()

    def work(self, phase, index):
        block = self.block
        slots, totals = self.kept_refs[0], self.extra_v[0]
        rows = pl.ds(pl.multiple_of(index * block, block), block)
        if phase == 0:
            part = jnp.sum(self.values(rows), axis=1, keepdims=True)
            slots[0, pl.ds(index, 1), :] = jnp.broadcast_to(part, (block, block)).T[0:1, :]
        if phase == 1:
            for step in range(1, self.columns):
                self.share(step).wait_recv()
            totals[...] = sum(slots[step] for step in range(self.columns))
        if phase == 2:
            self.use(rows, jnp.broadcast_to(totals[pl.ds(index, 1), :], (block, block)).T)


class NormJob(RowSumJob):
    then = None
    late = (1,)

    def __init__(self, rows_in, terms, wide):
        rows, own = rows_in.shape
        outs = [((rows, own), jnp.float32), ((rows, own), LOW), ((rows, 128), jnp.float32)]
        super().__init__([rows_in, terms, wide], outs, [], rows, 0)

    def values(self, rows):
        rows_in, terms, _ = self.ins_v
        residual = sum(terms[part, rows, :].astype(jnp.float32) for part in range(self.columns))
        residual = rows_in[rows, :].astype(jnp.float32) + residual
        self.outs_v[0][rows, :] = residual
        return residual * residual

    def use(self, rows, total):
        residual, normed, scales = self.outs_v
        scale = lax.rsqrt(total / D + EPSILON)
        scales[rows, :] = scale
        gain = self.ins_v[2].at[self.column]
        normed[rows, :] = (residual[rows, :] * scale[:, 0:1] * gain[4:5, :]).astype(LOW)

    def finish(self):
        self.store(1).wait()
        if self.then:
            self.then.start()
        for step in range(1, self.columns):
            self.share(step).wait_send()
        for which in (0, 2):
            self.store(which).wait()


class NormBackJob(RowSumJob):
    then = None
    late = (0,)

    def __init__(self, terms, kept, scales, wide, row, base, rounded):
        _, rows, own = terms.shape
        outs = [((rows, own), jnp.float32), ((8, own), jnp.float32)]
        outs = outs + [((rows, own), LOW)] if rounded else outs
        self.row = row
        super().__init__([terms, kept, scales, wide, base], outs, [], rows, 0)

    def parts(self, rows):
        terms, kept, scales, wide, base = self.ins_v
        gain = wide.at[self.column]
        return (
            sum(terms[part, rows, :].astype(jnp.float32) for part in range(self.columns)),
            kept[rows, :].astype(jnp.float32),
            scales[rows, 0:1],
            gain[self.row : self.row + 1, :],
        )

    def before(self, phase):
        super().before(phase)
        if phase == 0:
            self.outs_v[1][...] = jnp.zeros_like(self.outs_v[1])

    def values(self, rows):
        grad, kept, scale, gain = self.parts(rows)
        product = grad * kept
        self.outs_v[1][0:1, :] += jnp.sum(product * scale, axis=0, keepdims=True)
        return product * gain

    def use(self, rows, total):
        grad, kept, scale, gain = self.parts(rows)
        rows_grad = scale * gain * grad - kept * (scale * scale * scale * total[:, 0:1] / D)
        result = self.ins_v[4][rows, :].astype(jnp.float32) + rows_grad
        self.outs_v[0][rows, :] = result
        if len(self.outs_v) > 2:
            self.outs_v[2][rows, :] = result.astype(LOW)

    def finish(self):
        if self.then:
            self.store(2).wait()
            self.then.start()
        for step in range(1, self.columns):
            self.share(step).wait_send()
        for which in range(len(self.out_shapes)):
            if which != 2 or not self.then:
                self.store(which).wait()


class SumJob(MixerJob):
    late = (1,)

    def __init__(self, base, terms):
        rows, own = base.shape
        super().__init__([base, terms], [((rows, own), LOW)], [], [rows // 128], 0)

    def before(self, phase):
        for which in range(2):
            self.load(which).wait()

    def after(self, phase):
        self.store(0).start()

    def work(self, phase, index):
        base, terms = self.ins_v
        rows = pl.ds(pl.multiple_of(index * 128, 128), 128)
        total = sum(terms[part, rows, :].astype(jnp.float32) for part in range(terms.shape[0]))
        self.outs_v[0][rows, :] = (base[rows, :] + total).astype(LOW)


class SmallSumJob:
    tiles, flops = 1, 0

    def __init__(self, taps_grad, gain_grad, before):
        count = lax.axis_size("seq")
        self.inputs = [taps_grad, gain_grad]
        shape = taps_grad.shape
        self.before = before
        self.out_shapes = [jax.ShapeDtypeStruct(shape, jnp.float32)]
        self.scratch = [pltpu.VMEM(shape, jnp.float32)] * 3 + [pltpu.SemaphoreType.DMA((3,))]
        self.kept = [
            pltpu.VMEM((count,) + shape, jnp.float32),
            pltpu.SemaphoreType.DMA((count,)),
            pltpu.SemaphoreType.DMA((count,)),
        ]

    def hold(self, refs):
        self.slots, self.send_sem, self.recv_sem = refs

    def bind(self, ins, outs, scratch):
        self.sources, self.target = ins, outs[0]
        self.taps, self.gain, self.total, self.local_sem = scratch
        self.count = lax.axis_size("seq")
        self.seq = lax.axis_index("seq")
        self.column = lax.axis_index("tp")

    def peers(self):
        return [((self.seq + far) % self.count, self.column) for far in range(1, self.count)]

    def copy(self, far):
        return pltpu.make_async_remote_copy(
            src_ref=self.slots.at[0],
            dst_ref=self.slots.at[far],
            send_sem=self.send_sem.at[far],
            recv_sem=self.recv_sem.at[far],
            device_id=((self.seq + far) % self.count, self.column),
            device_id_type=MESH,
        )

    def loads(self):
        return [
            pltpu.make_async_copy(self.sources[which], (self.taps, self.gain)[which], self.local_sem.at[which])
            for which in range(2)
        ]

    def start(self, late):
        if late:
            return
        for load in self.loads():
            load.start()

    def tile(self, index):
        for load in self.loads():
            load.wait()
        self.slots[0, 0:3, :] = self.taps[0:3, :]
        self.slots[0, 3:4, :] = self.before.outs_v[1][0:1, :]
        self.slots[0, 4:5, :] = self.gain[0:1, :]
        self.slots[0, 5:8, :] = jnp.zeros_like(self.slots[0, 5:8, :])

        def begin(far, carry):
            self.copy(far).start()
            return carry

        lax.fori_loop(1, self.count, begin, 0)

    def finish(self):
        self.total[...] = self.slots[0]

        def add(far, carry):
            self.copy(far).wait_recv()
            self.total[...] += self.slots[far]
            return carry

        lax.fori_loop(1, self.count, add, 0)
        store = pltpu.make_async_copy(self.total, self.target, self.local_sem.at[2])
        store.start()

        def sent(far, carry):
            self.copy(far).wait_send()
            return carry

        lax.fori_loop(1, self.count, sent, 0)
        store.wait()


class Section:
    def __init__(self, ranges, jobs=(), waits=(), rest=1, calls=(), early=True):
        self.ranges, self.jobs, self.waits, self.rest, self.calls, self.early = ranges, jobs, waits, rest, calls, early
        self.job = Jobs(*[job for job, _, _ in jobs])

    def run(self, ring, ins, outs):
        job = self.job
        ranges = [(group, low * ring.ticks // 12, high * ring.ticks // 12) for group, low, high in self.ranges]
        total = sum(high - low for _, low, high in ranges)
        rest = self.rest * ring.ticks // 12
        active = total - rest
        each = -(-job.tiles // active)

        def ready():
            for exchange in self.waits:
                exchange.wait()
            job.start(True)

        def body(*scratch):
            job.bind(ins, outs, list(scratch))
            job.start(False)
            if not self.waits:
                job.start(True)
            done = 0
            for place, (group, low, high) in enumerate(ranges):
                if low == 0 and group > 0 and place > 0:
                    ring.turn(group)
                if place == 0:
                    for call in self.calls:
                        call.start()

                def step(index, carry, group=group, shift=done - low):
                    late = index + shift - rest
                    first, after = late * job.tiles // active, (late + 1) * job.tiles // active
                    if self.waits:
                        pl.when(late == -1)(ready)
                    for inner in range(each):
                        tile = first + inner

                        @pl.when((late >= 0) & (tile < after))
                        def _(tile=tile):
                            job.tile(tile)

                    ring.tick(group, index)
                    return carry

                lax.fori_loop(low, high, step, 0)
                done += high - low
            group, _, high = ranges[-1]
            ends = high == ring.ticks and group + 1 < len(ring.groups)
            if ends and self.early:
                ring.begin(group + 1)
            job.finish()
            if ends and not self.early:
                ring.begin(group + 1)

        pl.run_scoped(body, *job.scratch)
        group, _, high = ranges[-1]
        if high == ring.ticks:
            ring.settle(group)
            ring.settled(group)


class Plan:
    def __init__(self, arrays):
        self.arrays = arrays
        self.shapes = {name: jax.ShapeDtypeStruct(array.shape, array.dtype) for name, array in arrays.items()}
        self.inputs = list(self.shapes)
        self.weights = set()

    def define(self, name, shape, dtype):
        self.shapes[name] = jax.ShapeDtypeStruct(shape, dtype)

    def add(self, job, ins, outs):
        for name, shape in zip(outs, job.out_shapes):
            self.shapes[name] = shape
        return job, ins, outs

    def flat(self, full):
        shape = self.shapes[full].shape
        return jax.ShapeDtypeStruct((shape[0] * shape[1], shape[2]), LOW)

    def run(self, ring, sections, exchanges, peers, name, collective):
        inputs = self.inputs
        outputs = [made for made in self.shapes if made not in inputs]
        kept = [item for section in sections for item in section.job.kept]
        sems = [item for exchange in exchanges for item in exchange.scratch]

        def kernel(*all_refs):
            in_refs, out_refs, ring_scratch, sem_refs, kept_refs = split(
                all_refs, [len(inputs), len(outputs), len(ring.scratch), len(sems), len(kept)]
            )
            refs = dict(zip(inputs + outputs, in_refs + out_refs))
            ring.bind(refs, ring_scratch)
            for place, exchange in enumerate(exchanges):
                exchange.bind(refs, sem_refs[2 * place : 2 * place + 2])
            for section, own in zip(sections, split(kept_refs, [len(section.job.kept) for section in sections])):
                section.job.hold(own)
            ring.prepare()
            greet(peers())
            ring.begin(0)
            ring.settled(-1)
            for section in sections:
                ins = [rows_of(refs[made], made in self.weights) for _, names, _ in section.jobs for made in names]
                outs = [refs[made] for _, _, names in section.jobs for made in names]
                section.run(ring, ins, outs)
            ring.finish()
            for exchange in exchanges:
                exchange.finish()

        flops = ring.flops + sum(section.job.flops for section in sections)
        results = pl.pallas_call(
            kernel,
            out_shape=[self.shapes[made] for made in outputs],
            in_specs=[pl.BlockSpec(memory_space=pl.ANY)] * len(inputs),
            out_specs=[pl.BlockSpec(memory_space=pl.ANY)] * len(outputs),
            scratch_shapes=ring.scratch + sems + kept,
            compiler_params=pltpu.CompilerParams(
                collective_id=collective, has_side_effects=True, vmem_limit_bytes=VMEM_BYTES
            ),
            cost_estimate=pl.CostEstimate(flops=flops, bytes_accessed=10**9, transcendentals=0),
            name=name,
        )(*self.arrays.values())
        named = dict(zip(outputs, results))
        return {made: flat(array) if made in self.weights else array for made, array in named.items()}


def row_and_column_peers():
    seq, column = lax.axis_index("seq"), lax.axis_index("tp")
    devices, columns = lax.axis_size("seq"), lax.axis_size("tp")
    near = [(seq, (column + step) % columns) for step in range(1, columns)]
    return near + [((seq + step) % devices, column) for step in range(1, devices)]


def run_forward(arrays, seen):
    count, columns = lax.axis_size("seq"), lax.axis_size("tp")
    plan = Plan(arrays)
    shapes, add = plan.shapes, plan.add
    rows, own = arrays["tokens"].shape
    for name in ("tokens_blocks", "cot_blocks", "branch_terms", "normed_blocks"):
        plan.define(name, (columns, rows, own), LOW)
    low = ["gate_low0", "up_low0", "gate_low1", "up_low1", "shrink_low0", "shrink_low1"]
    small = add(SmallGatherJob(shapes["small"], seen), ["small"], ["wide"])
    cast = add(CastJob(shapes["pairs"], shapes["shrink"]), ["pairs", "shrink"], low)
    groups = [[("entry_low", "entry_full"), ("exit_low", "exit_full")]]
    groups += [[(name, name.replace("low", "full"))] for name in low]
    for group in groups:
        for shard, full in group:
            plan.define(full, (count,) + shapes[shard].shape, LOW)
            plan.weights.add(full)
    ring = GatherRing(groups, shapes)
    tokens_sent = PeerCopies("tokens", "tokens_blocks")
    cot_sent = PeerCopies("cotangent", "cot_blocks")
    branch_sent = PeerCopies("term", "branch_terms")
    normed_sent = PeerCopies("normed_own", "normed_blocks")

    entry_job = EntryJob(
        shapes["tokens_blocks"], shapes["wide"], plan.flat("entry_full"), plan.flat("exit_full"), shapes["bound"]
    )
    entry_job.then = branch_sent
    entry = add(
        entry_job,
        ["tokens_blocks", "wide", "entry_full", "exit_full", "bound"],
        ["projected", "conv_out", "gated", "halo", "mixer", "term", "scale_one", "normed_one"],
    )
    turn_cot = add(TurnJob(shapes["cot_blocks"]), ["cot_blocks"], ["cot_full"])
    norm_job = NormJob(shapes["tokens"], shapes["branch_terms"], shapes["wide"])
    norm_job.then = normed_sent
    norm = add(norm_job, ["tokens", "branch_terms", "wide"], ["residual", "normed_own", "scale_two"])
    expands = []
    for half in "01":
        job = ExpandJob(shapes["normed_blocks"], plan.flat("gate_full" + half), plan.flat("up_full" + half))
        names = ["normed_blocks", "gate_full" + half, "up_full" + half]
        expands.append(add(job, names, ["gate_rows" + half, "up_rows" + half, "activation" + half]))
    hidden_job = HiddenGradJob(shapes["cot_blocks"], plan.flat("shrink_full0"), shapes["gate_rows0"], shapes["up_rows0"])
    hidden = add(hidden_job, ["cot_blocks", "shrink_full0", "gate_rows0", "up_rows0"], ["gate_grad0", "up_grad0"])
    turn_normed = add(TurnJob(shapes["normed_blocks"]), ["normed_blocks"], ["normed_two"])
    sections = [
        Section([(0, 0, 12)], [small, cast], calls=[tokens_sent], early=False),
        Section([(1, 0, 12)], [entry], [tokens_sent], calls=[cot_sent]),
        Section([(2, 0, 12)], [turn_cot], [cot_sent], rest=3),
        Section([(3, 0, 12)], [norm], [branch_sent], rest=4),
        Section([(4, 0, 12)]),
        Section([(5, 0, 12)], expands, [normed_sent], rest=4),
        Section([(6, 0, 12)], [hidden, turn_normed]),
    ]
    exchanges = [tokens_sent, cot_sent, branch_sent, normed_sent]
    return plan.run(ring, sections, exchanges, row_and_column_peers, "forward", 0)


def run_backward(arrays):
    columns = lax.axis_size("tp")
    plan = Plan(arrays)
    shapes, add = plan.shapes, plan.add
    rows, own = arrays["tokens"].shape
    for name in ("two_terms", "mixed_terms", "branch_blocks", "one_terms"):
        plan.define(name, (columns, rows, own), LOW)
    two_sent = PeerCopies("two_term", "two_terms")
    mixed_sent = PeerCopies("mixed_term", "mixed_terms")
    branch_sent = PeerCopies("branch_own", "branch_blocks")
    one_sent = PeerCopies("one_term", "one_terms")

    hidden = add(
        HiddenGradJob(shapes["cot_blocks"], shapes["shrink_full1"], shapes["gate_rows1"], shapes["up_rows1"]),
        ["cot_blocks", "shrink_full1", "gate_rows1", "up_rows1"],
        ["gate_grad1", "up_grad1"],
    )
    names = [["gate_grad0", "up_grad0", "gate_grad1", "up_grad1"], ["gate_full0", "up_full0", "gate_full1", "up_full1"]]
    two_job = WidthJob(*[[shapes[name] for name in side] for side in names])
    two_job.then = two_sent
    two = add(two_job, names[0] + names[1], ["two_term"])
    names = [["activation0", "activation1"], ["shrink_full0", "shrink_full1"]]
    mixed = add(WidthJob(*[[shapes[name] for name in side] for side in names]), names[0] + names[1], ["mixed_term"])
    back_two = NormBackJob(
        shapes["two_terms"], shapes["residual"], shapes["scale_two"], shapes["wide"], 4, shapes["cotangent"], True
    )
    back_two.then = branch_sent
    names = ["two_terms", "residual", "scale_two", "wide", "cotangent"]
    norm_two = add(back_two, names, ["residual_grad", "gain_two_grad", "branch_own"])
    names = ["branch_blocks", "exit_full", "entry_full", "projected", "conv_out", "gated", "halo", "wide", "bound"]
    mixer_job = MixerGradJob(*[shapes[name] for name in names])
    mixer_job.then = one_sent
    mixer = add(mixer_job, names, ["projected_grad", "one_term", "taps_grad"])
    turn = add(TurnJob(shapes["branch_blocks"]), ["branch_blocks"], ["branch_full"])
    back_one = NormBackJob(
        shapes["one_terms"], shapes["tokens"], shapes["scale_one"], shapes["wide"], 3, shapes["residual_grad"], False
    )
    names = ["one_terms", "tokens", "scale_one", "wide", "residual_grad"]
    norm_one = add(back_one, names, ["tokens_grad", "gain_one_grad"])
    small_job = SmallSumJob(shapes["taps_grad"], shapes["gain_two_grad"], back_one)
    small = add(small_job, ["taps_grad", "gain_two_grad"], ["small_part"])
    total = add(SumJob(shapes["residual"], shapes["mixed_terms"]), ["residual", "mixed_terms"], ["mixed"])

    wide = own
    halves = [("cot_full", "activation0"), ("cot_full", "activation1")]
    halves += [("normed_two", name) for name in ("gate_grad0", "up_grad0", "gate_grad1", "up_grad1")]
    halves += [("normed_one", "projected_grad")]
    groups = [[(left, right, 0), (left, right, wide)] for left, right in halves]
    groups += [[("normed_one", "projected_grad", 2 * wide), ("branch_full", "mixer", 0)]]
    places = {"cot_full": 0, "normed_two": 1, "normed_one": 0, "branch_full": 2}
    ring = ScatterRing(groups, places, shapes, wide)
    sums = ["shrink0", "shrink1", "gate0", "up0", "gate1", "up1", "entry", "entry_exit"]
    for name, shape in zip(sums, ring.out_shapes):
        plan.shapes[name] = shape
    ring.outs = sums
    sections = [
        Section([(0, 0, 5)], [hidden]),
        Section([(0, 5, 12), (1, 0, 4)], [two], rest=2),
        Section([(1, 4, 12), (2, 0, 5)], [mixed]),
        Section([(2, 5, 12)], [norm_two], [two_sent], rest=3),
        Section([(3, 0, 12)]),
        Section([(4, 0, 12)], [mixer], [branch_sent], rest=3),
        Section([(5, 0, 12)], [turn], calls=[mixed_sent]),
        Section([(6, 0, 12)], [norm_one, small], [one_sent], rest=3),
        Section([(7, 0, 12)], [total], [mixed_sent]),
    ]
    exchanges = [two_sent, mixed_sent, branch_sent, one_sent]
    return plan.run(ring, sections, exchanges, row_and_column_peers, "backward", 1)


def rows_of(ref, gathered):
    if not gathered:
        return ref
    count, rows, columns = ref.shape
    return ref.reshape(count * rows, columns)


def flat(full):
    return full.reshape(full.shape[0] * full.shape[1], full.shape[2])


def contract_cols(left, right):
    return lax.dot_general(
        left, right, (((1,), (1,)), ((), ())), preferred_element_type=jnp.float32
    )


def adam_update(weight, first, second, grad, rate, decay):
    first_next = BETA_ONE * first + (1.0 - BETA_ONE) * grad
    second_next = BETA_TWO * second + (1.0 - BETA_TWO) * grad * grad
    corrected = first_next / (1.0 - BETA_ONE**STEP)
    spread = jnp.sqrt(second_next / (1.0 - BETA_TWO**STEP)) + ADAM_EPSILON
    return (weight - rate * (corrected / spread + decay * weight), first_next, second_next)


def adam_kernel(pieces, *refs):
    weight, first, second = refs[:3]
    grads, outs = refs[3 : 3 + pieces], refs[3 + pieces :]
    start = 0
    for grad in grads:
        span = slice(start, start + grad.shape[1])
        start += grad.shape[1]
        results = adam_update(weight[:, span], first[:, span], second[:, span], grad[...], RATE_WIDE, WEIGHT_DECAY)
        for out, result in zip(outs, results):
            out[:, span] = result


def adam_rows(weight, first, second, grads):
    rows, columns = weight.shape
    block = max(rows // 4, 8)
    state = pl.BlockSpec((block, columns), lambda step: (step, 0))
    grad_specs = [pl.BlockSpec((block, grad.shape[1]), lambda step: (step, 0)) for grad in grads]
    return pl.pallas_call(
        functools.partial(adam_kernel, len(grads)),
        out_shape=[jax.ShapeDtypeStruct(weight.shape, weight.dtype)] * 3,
        grid=(rows // block,),
        in_specs=[state] * 3 + grad_specs,
        out_specs=[state] * 3,
        compiler_params=pltpu.CompilerParams(vmem_limit_bytes=VMEM_BYTES),
        cost_estimate=pl.CostEstimate(flops=20 * weight.size, bytes_accessed=28 * weight.size, transcendentals=0),
        name="adam_rows",
    )(weight, first, second, *grads)


def adam_mixer_kernel(*refs):
    entries, exits, grads, outs = refs[:3], refs[3:6], refs[6:8], refs[8:]
    planes, _, columns = entries[0].shape
    for plane in range(planes + 1):
        grad = grads[plane // 2][:, plane % 2 * columns : (plane % 2 + 1) * columns]
        state = [ref[plane] for ref in entries] if plane < planes else [ref[...] for ref in exits]
        results = adam_update(*state, grad, RATE_WIDE, WEIGHT_DECAY)
        for place, result in enumerate(results):
            if plane < planes:
                outs[place][plane] = result
            else:
                outs[3 + place][...] = result


def adam_mixer(entries, exits, grad, last):
    rows, planes, columns = entries[0].shape
    block = max(rows // 4, 8)
    entry_spec = pl.BlockSpec((planes, block, columns), lambda step: (0, step, 0))
    exit_spec = pl.BlockSpec((block, columns), lambda step: (step, 0))
    grad_spec = pl.BlockSpec((block, 2 * columns), lambda step: (step, 0))
    size = entries[0].size + exits[0].size
    results = pl.pallas_call(
        adam_mixer_kernel,
        out_shape=[jax.ShapeDtypeStruct((planes, rows, columns), jnp.float32)] * 3
        + [jax.ShapeDtypeStruct((rows, columns), jnp.float32)] * 3,
        grid=(rows // block,),
        in_specs=[entry_spec] * 3 + [exit_spec] * 3 + [grad_spec] * 2,
        out_specs=[entry_spec] * 3 + [exit_spec] * 3,
        compiler_params=pltpu.CompilerParams(vmem_limit_bytes=VMEM_BYTES),
        cost_estimate=pl.CostEstimate(flops=20 * size, bytes_accessed=28 * size, transcendentals=0),
        name="adam_mixer",
    )(*[array.transpose(1, 0, 2) for array in entries], *exits, grad, last)
    return [result.transpose(1, 0, 2) for result in results[:3]] + list(results[3:])


def adam_pairs_kernel(lanes, *refs):
    weight, first, second = refs[:3]
    grads, outs, mixed = refs[3:7], refs[7:10], refs[10]
    rows = grads[0].shape[0]
    tiles = grads[0].shape[1] // lanes
    for which, grad in enumerate(grads):
        half, side = which // 2, which % 2
        for tile in range(tiles):
            place = (half * tiles + tile) * 2 + side
            mixed[pl.ds(place, rows, stride=4 * tiles), :] = grad[:, tile * lanes : (tile + 1) * lanes]
    results = adam_update(weight[...], first[...], second[...], mixed[...], RATE_WIDE, WEIGHT_DECAY)
    for out, result in zip(outs, results):
        out[...] = result


def paired(array):
    rows, _, columns = array.shape
    return array.reshape(rows, 2, columns // LANES, LANES).transpose(0, 2, 1, 3).reshape(-1, LANES)


def adam_pairs(weight, first, second, grads):
    rows, _, columns = weight.shape
    deep = columns // LANES
    block = max(rows // 8, 8)
    state = pl.BlockSpec((block * deep * 2, LANES), lambda step: (step, 0))
    results = pl.pallas_call(
        functools.partial(adam_pairs_kernel, LANES),
        out_shape=[jax.ShapeDtypeStruct((rows * deep * 2, LANES), weight.dtype)] * 3,
        grid=(rows // block,),
        in_specs=[state] * 3 + [pl.BlockSpec((block, columns // 2), lambda step: (step, 0))] * 4,
        out_specs=[state] * 3,
        scratch_shapes=[pltpu.VMEM((block * deep * 2, LANES), jnp.float32)],
        cost_estimate=pl.CostEstimate(flops=20 * weight.size, bytes_accessed=28 * weight.size, transcendentals=0),
        name="adam_pairs",
    )(paired(weight), paired(first), paired(second), *grads)
    return [
        result.reshape(rows, deep, 2, LANES).transpose(0, 2, 1, 3).reshape(rows, 2, columns) for result in results
    ]


def shards(
    tokens,
    bounds,
    cotangent,
    entry_weight,
    entry_first,
    entry_second,
    exit_weight,
    exit_first,
    exit_second,
    expand_weight,
    expand_first,
    expand_second,
    shrink_weight,
    shrink_first,
    shrink_second,
    conv_kernel,
    conv_first,
    conv_second,
    norm_gains,
    gain_first,
    gain_second,
):
    channels = tokens.shape[1]
    seen = conv_kernel.shape[1]
    small = jnp.concatenate([conv_kernel, norm_gains], axis=0)
    small = jnp.pad(small, ((0, 16 - small.shape[0]), (0, LANES - seen))).astype(LOW)
    entry_low = entry_weight.reshape(entry_weight.shape[0], 3 * channels).astype(LOW)
    bound = jnp.broadcast_to(bounds[0], (8, 128))
    made = run_forward(
        {
            "entry_low": entry_low,
            "exit_low": exit_weight.astype(LOW),
            "small": small,
            "tokens": tokens,
            "cotangent": cotangent,
            "bound": bound,
            "pairs": paired(expand_weight),
            "shrink": shrink_weight,
        },
        seen,
    )
    names = ["wide", "exit_full", "entry_full", "projected", "conv_out", "gated", "halo", "mixer", "residual"]
    names += ["scale_one", "scale_two", "cot_blocks", "cot_full", "normed_one", "normed_two", "gate_grad0", "up_grad0"]
    names += ["gate_rows1", "up_rows1", "activation0", "activation1"]
    names += [name + half for name in ("gate_full", "up_full", "shrink_full") for half in "01"]
    given = {"tokens": tokens, "cotangent": cotangent, "bound": bound}
    grads = run_backward(given | {name: made[name] for name in names})
    mixed, tokens_grad = grads["mixed"], grads["tokens_grad"]
    small_part = lax.dynamic_slice_in_dim(grads["small_part"], lax.axis_index("seq") * seen, seen, axis=1)
    kernel_part = small_part[:3]
    gains_part = small_part[3:5]
    (
        entry_next,
        entry_first_next,
        entry_second_next,
        exit_next,
        exit_first_next,
        exit_second_next,
    ) = adam_mixer(
        (entry_weight, entry_first, entry_second),
        (exit_weight, exit_first, exit_second),
        grads["entry"],
        grads["entry_exit"],
    )
    expand_next, expand_first_next, expand_second_next = adam_pairs(
        expand_weight, expand_first, expand_second, [grads[name] for name in ("gate0", "up0", "gate1", "up1")]
    )
    shrink_next, shrink_first_next, shrink_second_next = adam_rows(
        shrink_weight, shrink_first, shrink_second, [grads["shrink0"], grads["shrink1"]]
    )
    conv_next, conv_first_next, conv_second_next = adam_update(
        conv_kernel, conv_first, conv_second, kernel_part, RATE_CONV, 0.0
    )
    gains_next, gains_first_next, gains_second_next = adam_update(
        norm_gains, gain_first, gain_second, gains_part, RATE_GAIN, 0.0
    )
    return (
        mixed,
        tokens_grad,
        entry_next,
        entry_first_next,
        entry_second_next,
        exit_next,
        exit_first_next,
        exit_second_next,
        expand_next,
        expand_first_next,
        expand_second_next,
        shrink_next,
        shrink_first_next,
        shrink_second_next,
        conv_next,
        conv_first_next,
        conv_second_next,
        gains_next,
        gains_first_next,
        gains_second_next,
    )


def solution(mesh):
    rows = P("seq", "tp")
    stacked = P("seq", None, "tp")
    small = P(None, ("tp", "seq"))
    return jax.shard_map(
        shards,
        mesh=mesh,
        in_specs=(rows, P("seq"), rows) + (stacked,) * 3 + (rows,) * 3 + (stacked,) * 3 + (rows,) * 3 + (small,) * 6,
        out_specs=(rows, rows) + (stacked,) * 3 + (rows,) * 3 + (stacked,) * 3 + (rows,) * 3 + (small,) * 6,
        check_vma=False,
    )
```

```python
import functools

import jax
import jax.numpy as jnp
from jax import lax
from jax.experimental import pallas as pl
from jax.experimental.pallas import tpu as pltpu
from jax.sharding import PartitionSpec as P

D = 2048
STEP = 10


EPSILON = 1e-05
BETA_ONE = 0.9
BETA_TWO = 0.95
ADAM_EPSILON = 1e-08
WEIGHT_DECAY = 0.1
RATE_WIDE = 0.04
RATE_CONV = 0.5
RATE_GAIN = 0.4

MESH = pl.DeviceIdType.MESH
LOW = jnp.bfloat16
LANES = 128
VMEM_BYTES = 60 * 1024 * 1024


def ring_place(index, count):
    side = index % 2
    level = index // 2
    return level * (1 - side) + (count - 1 - level) * side


def ring_index(place, count):
    back = place // (count // 2)
    return (1 - back) * (2 * place) + back * (2 * (count - 1 - place) + 1)


def ring_ends(count):
    place = ring_place(lax.axis_index("seq"), count)
    ahead = ring_index((place + 1) % count, count)
    behind = ring_index((place + count - 1) % count, count)
    return place, ahead, behind


def greet(peers):
    barrier = pltpu.get_barrier_semaphore()
    for peer in peers:
        pl.semaphore_signal(barrier, inc=1, device_id=peer, device_id_type=MESH)
    pl.semaphore_wait(barrier, len(peers))


def split(items, sizes):
    parts, start = [], 0
    for size in sizes:
        parts.append(items[start : start + size])
        start += size
    return parts


class GatherRing:
    def __init__(self, groups, shapes):
        self.count = lax.axis_size("seq")
        self.groups = groups
        self.rows = {full: shapes[shard].shape[0] for group in groups for shard, full in group}
        self.order = {full: place for place, full in enumerate(self.rows)}
        self.parts = 2 if min(self.rows.values()) % 64 == 0 else 1
        self.ticks = (self.count - 2) * self.parts
        arrays = len(self.rows)
        sems = pltpu.SemaphoreType.DMA((arrays, 2, self.parts, self.count - 1))
        self.scratch = [sems, sems, pltpu.SemaphoreType.DMA((arrays,))]
        self.flops = 0

    def bind(self, refs, scratch):
        self.refs = refs
        self.send_sem, self.recv_sem, self.own_sem = scratch
        self.column = lax.axis_index("tp")
        self.place, self.ahead, self.behind = ring_ends(self.count)

    def copy(self, shard, full, way, part, step, first=False):
        move = (self.place + self.count - step) if way == 0 else (self.place + step)
        owner = ring_index(move % self.count, self.count)
        half = self.rows[full] // 2
        size = half // self.parts
        rows = pl.ds(pl.multiple_of(way * half + part * size, 16), size)
        there = self.refs[full].at[owner, rows]
        return pltpu.make_async_remote_copy(
            src_ref=self.refs[shard].at[rows] if first else there,
            dst_ref=there,
            send_sem=self.send_sem.at[self.order[full], way, part, step],
            recv_sem=self.recv_sem.at[self.order[full], way, part, step],
            device_id=(self.ahead if way == 0 else self.behind, self.column),
            device_id_type=MESH,
        )

    def own(self, shard, full):
        there = self.refs[full].at[lax.axis_index("seq")]
        return pltpu.make_async_copy(self.refs[shard], there, self.own_sem.at[self.order[full]])

    def pieces(self, group):
        return [(shard, full, way) for shard, full in self.groups[group] for way in range(2)]

    def begin(self, group):
        for part in range(self.parts):
            for shard, full, way in self.pieces(group):
                self.copy(shard, full, way, part, 0, True).start()
        for shard, full in self.groups[group]:
            self.own(shard, full).start()

    def tick(self, group, index):
        step, part = 1 + index // self.parts, index % self.parts
        for shard, full, way in self.pieces(group):
            self.copy(shard, full, way, part, step - 1).wait_recv()
            self.copy(shard, full, way, part, step).start()

    def prepare(self):
        pass

    def turn(self, group):
        self.begin(group)
        self.settle(group - 1)

    def settled(self, group):
        pass

    def settle(self, group):
        for part in range(self.parts):
            for shard, full, way in self.pieces(group):
                self.copy(shard, full, way, part, self.count - 2).wait_recv()
        for shard, full in self.groups[group]:
            self.own(shard, full).wait()

    def finish(self):
        def sent(step, carry):
            for group in range(len(self.groups)):
                for part in range(self.parts):
                    for shard, full, way in self.pieces(group):
                        self.copy(shard, full, way, part, step).wait_send()
            return carry

        lax.fori_loop(0, self.count - 1, sent, 0)


class PeerCopies:
    def __init__(self, source, target):
        self.source, self.target = source, target
        columns = lax.axis_size("tp")
        self.scratch = [pltpu.SemaphoreType.DMA((columns,)), pltpu.SemaphoreType.DMA((columns,))]

    def bind(self, refs, scratch):
        self.source_ref, self.target_ref = refs[self.source], refs[self.target]
        self.send_sem, self.recv_sem = scratch
        self.columns = lax.axis_size("tp")
        self.seq, self.column = lax.axis_index("seq"), lax.axis_index("tp")

    def block(self, peer):
        if len(self.source_ref.shape) == len(self.target_ref.shape):
            return self.source_ref.at[peer]
        return self.source_ref

    def own(self):
        return pltpu.make_async_copy(
            self.block(self.column), self.target_ref.at[self.column], self.send_sem.at[0]
        )

    def copy(self, step):
        peer = (self.column + step) % self.columns
        return pltpu.make_async_remote_copy(
            src_ref=self.block(peer),
            dst_ref=self.target_ref.at[self.column],
            send_sem=self.send_sem.at[step],
            recv_sem=self.recv_sem.at[step],
            device_id=(self.seq, peer),
            device_id_type=MESH,
        )

    def start(self):
        for step in range(1, self.columns):
            self.copy(step).start()
        self.own().start()

    def wait(self):
        self.own().wait()
        for step in range(1, self.columns):
            self.copy(step).wait_recv()

    def finish(self):
        for step in range(1, self.columns):
            self.copy(step).wait_send()


class ScatterRing:
    def __init__(self, groups, places, shapes, wide):
        self.count = lax.axis_size("seq")
        self.groups, self.places, self.wide = groups, places, wide
        self.names = list(places)
        left = shapes[self.names[0]]
        features, tokens = left.shape
        self.rows = features // self.count
        self.parts = 2
        self.ticks = (self.count - 2) * self.parts
        sems = pltpu.SemaphoreType.DMA((len(groups), 2, self.parts, self.count - 1))
        buffers = max(places.values()) + 1
        self.scratch = [
            pltpu.VMEM((buffers, features, tokens), LOW),
            pltpu.VMEM((2, 2, tokens, wide), LOW),
            pltpu.VMEM((2, 2, self.count, self.rows, wide), LOW),
            pltpu.VMEM((2, self.rows, 2 * wide), jnp.float32),
            sems,
            sems,
            pltpu.SemaphoreType.DMA((len(self.names),)),
            pltpu.SemaphoreType.DMA((2, 2)),
            pltpu.SemaphoreType.DMA((2,)),
        ]
        self.flops = 4 * len(groups) * features * tokens * wide
        self.out_shapes = [jax.ShapeDtypeStruct((self.rows, 2 * wide), jnp.float32)] * len(groups)

    def bind(self, refs, scratch):
        self.refs, self.out_refs = refs, [refs[name] for name in self.outs]
        self.lefts, self.rights, self.slots, self.finals = scratch[:4]
        self.send_sem, self.recv_sem, self.left_sem, self.right_sem, self.done_sem = scratch[4:]
        self.column = lax.axis_index("tp")
        self.place, self.ahead, self.behind = ring_ends(self.count)

    def left_load(self, name):
        return pltpu.make_async_copy(
            self.refs[name], self.lefts.at[self.places[name]], self.left_sem.at[self.names.index(name)]
        )

    def right_load(self, group, way):
        _, name, start = self.groups[group][way]
        source = self.refs[name].at[:, pl.ds(start, self.wide)]
        return pltpu.make_async_copy(source, self.rights.at[group % 2, way], self.right_sem.at[group % 2, way])

    def fetch(self, group):
        for way in range(2):
            self.right_load(group, way).start()

    def span(self, part):
        width = self.wide // self.parts
        return pl.ds(pl.multiple_of(part * width, 128), width)

    def term(self, group, way, part, step):
        move = (self.place + 2 * self.count - 1 - step) if way == 0 else (self.place + 1 + step)
        owner = ring_index(move % self.count, self.count)
        rows = pl.ds(pl.multiple_of(owner * self.rows, 16), self.rows)
        left = self.lefts[self.places[self.groups[group][way][0]], rows, :]
        right = self.rights[group % 2, way, :, self.span(part)]
        return jnp.dot(left, right, preferred_element_type=jnp.float32)

    def held(self, group, way, part, step):
        return self.slots.at[group % 2, way, step, :, self.span(part)]

    def copy(self, group, way, part, step):
        return pltpu.make_async_remote_copy(
            src_ref=self.held(group, way, part, step),
            dst_ref=self.held(group, way, part, step + 1),
            send_sem=self.send_sem.at[group, way, part, step],
            recv_sem=self.recv_sem.at[group, way, part, step],
            device_id=(self.ahead if way == 0 else self.behind, self.column),
            device_id_type=MESH,
        )

    def store(self, group):
        return pltpu.make_async_copy(self.finals.at[group % 2], self.out_refs[group], self.done_sem.at[group % 2])

    def prepare(self):
        self.left_load("cot_full").start()
        self.fetch(0)
        self.left_load("normed_two").start()

    def turn(self, group):
        self.begin(group)
        self.settle(group - 1)
        self.settled(group - 1)

    def settled(self, group):
        if group + 2 < len(self.groups):
            self.fetch(group + 2)
        if group == 1:
            self.left_load("normed_one").start()
        if group == 5:
            self.left_load("branch_full").start()

    def begin(self, group):
        for name, first in (("cot_full", 0), ("normed_two", 2), ("normed_one", 6), ("branch_full", 7)):
            if group == first:
                self.left_load(name).wait()
        for way in range(2):
            self.right_load(group, way).wait()
        for part in range(self.parts):
            for way in range(2):
                self.held(group, way, part, 0)[...] = self.term(group, way, part, 0).astype(LOW)
                self.copy(group, way, part, 0).start()

    def tick(self, group, index):
        step, part = 1 + index // self.parts, index % self.parts
        for way in range(2):
            mine = self.term(group, way, part, step)
            self.copy(group, way, part, step - 1).wait_recv()
            held = self.held(group, way, part, step)
            held[...] = (held[...].astype(jnp.float32) + mine).astype(LOW)
            self.copy(group, way, part, step).start()

    def settle(self, group):
        last = self.count - 1
        if group >= 1:
            self.store(group - 1).wait()
        for part in range(self.parts):
            for way in range(2):
                mine = self.term(group, way, part, last)
                self.copy(group, way, part, last - 1).wait_recv()
                width = self.wide // self.parts
                start = way * self.wide + part * width
                self.finals[group % 2, :, start : start + width] = (
                    self.held(group, way, part, last)[...].astype(jnp.float32) + mine
                )
        self.store(group).start()

        def sent(step, carry):
            for part in range(self.parts):
                for way in range(2):
                    self.copy(group, way, part, step).wait_send()
            return carry

        lax.fori_loop(0, last, sent, 0)

    def finish(self):
        self.store(len(self.groups) - 1).wait()


class Job:
    wide = 256
    kept = []
    late = ()

    def hold(self, refs):
        pass

    def __init__(self, whole, tiled, outs, tiles, flops):
        self.whole, self.tiled = whole, tiled
        self.inputs = list(whole) + [array for array, axis in tiled]
        self.axes = [axis for array, axis in tiled]
        self.out_shapes = [jax.ShapeDtypeStruct(shape, dtype) for shape, dtype in outs]
        self.tiles = tiles
        self.flops = flops
        self.scratch = (
            [pltpu.VMEM(array.shape, array.dtype) for array in self.inputs]
            + [pltpu.VMEM(shape, dtype) for shape, dtype in outs]
            + [
                pltpu.SemaphoreType.DMA((len(whole),)),
                pltpu.SemaphoreType.DMA((len(tiled), tiles)),
                pltpu.SemaphoreType.DMA((len(outs), tiles)),
            ]
        )

    def bind(self, ins, outs, scratch):
        self.in_refs, self.out_refs = ins, outs
        sizes = [len(self.whole), len(self.tiled), len(outs)]
        self.whole_v, self.tiled_v, self.outs_v = split(scratch, sizes)
        self.whole_sem, self.tiled_sem, self.out_sem = scratch[sum(sizes) :]

    def peers(self):
        return []

    def window(self, axis, index):
        span = pl.ds(pl.multiple_of(index * self.wide, 128), self.wide)
        return (span,) if axis == 0 else (slice(None), span)

    def whole_load(self, which):
        return pltpu.make_async_copy(self.in_refs[which], self.whole_v[which], self.whole_sem.at[which])

    def tiled_load(self, which, index):
        window = self.window(self.axes[which], index)
        there = self.in_refs[len(self.whole) + which].at[window]
        return pltpu.make_async_copy(there, self.tiled_v[which].at[window], self.tiled_sem.at[which, index])

    def out_window(self, index):
        return self.window(1, index)

    def store(self, which, index):
        window = self.out_window(index)
        return pltpu.make_async_copy(
            self.outs_v[which].at[window], self.out_refs[which].at[window], self.out_sem.at[which, index]
        )

    def start(self, late):
        for which in range(len(self.whole)):
            if late == (which in self.late):
                self.whole_load(which).start()

        def begin(index, carry):
            for which in range(len(self.tiled)):
                self.tiled_load(which, index).start()
            return carry

        if not late:
            lax.fori_loop(0, self.tiles, begin, 0)

    def tile(self, index):
        @pl.when(index == 0)
        def _():
            for which in range(len(self.whole)):
                self.whole_load(which).wait()

        for which in range(len(self.tiled)):
            self.tiled_load(which, index).wait()
        tiles = [ref[self.window(axis, index)] for ref, axis in zip(self.tiled_v, self.axes)]
        for which, value in enumerate(self.compute(self.whole_v, tiles)):
            self.outs_v[which][self.out_window(index)] = value
            self.store(which, index).start()

    def finish(self):
        def end(index, carry):
            for which in range(len(self.outs_v)):
                self.store(which, index).wait()
            return carry

        lax.fori_loop(0, self.tiles, end, 0)


def blocks_dot(blocks, weight):
    parts, _, depth = blocks.shape
    total = None
    for part in range(parts):
        term = jnp.dot(blocks[part], weight[part * depth : (part + 1) * depth], preferred_element_type=jnp.float32)
        total = term if total is None else total + term
    return total


class ExpandJob(Job):

    late = (0,)

    def __init__(self, normed, gate_full, up_full):
        rows, width = normed.shape[1], gate_full.shape[1]
        outs = [((rows, width), jnp.float32), ((rows, width), jnp.float32), ((rows, width), LOW)]
        super().__init__(
            [normed], [(gate_full, 1), (up_full, 1)], outs, width // self.wide, 4 * rows * gate_full.size
        )

    def compute(self, whole, tiles):
        gate_rows = blocks_dot(whole[0], tiles[0])
        up_rows = blocks_dot(whole[0], tiles[1])
        return gate_rows, up_rows, (gate_rows * jax.nn.sigmoid(gate_rows) * up_rows).astype(LOW)


class HiddenGradJob(Job):
    def __init__(self, cot, shrink_full, gate_rows, up_rows):
        rows, width = gate_rows.shape
        outs = [((rows, width), LOW), ((rows, width), LOW)]
        tiled = [(shrink_full, 1), (gate_rows, 1), (up_rows, 1)]
        super().__init__([cot], tiled, outs, width // self.wide, 2 * rows * shrink_full.size)

    def compute(self, whole, tiles):
        _, gate_rows, up_rows = tiles
        act_grad = blocks_dot(whole[0], tiles[0])
        sigmoid_gate = jax.nn.sigmoid(gate_rows)
        gate_grad = act_grad * up_rows * sigmoid_gate * (1.0 + gate_rows * (1.0 - sigmoid_gate))
        return gate_grad.astype(LOW), (act_grad * (gate_rows * sigmoid_gate)).astype(LOW)


class WidthJob(Job):
    then = None

    def __init__(self, lefts, weights):
        rows, width = lefts[0].shape[0], weights[0].shape[0]
        flops = 2 * rows * sum(weight.size for weight in weights)
        parts = lax.axis_size("tp")
        self.own = width // parts
        out = ((parts, rows, self.own), LOW)
        super().__init__(lefts, [(weight, 0) for weight in weights], [out], width // self.wide, flops)

    def out_window(self, index):
        each = self.own // self.wide
        return index // each, slice(None), pl.ds(pl.multiple_of(index % each * self.wide, 128), self.wide)

    def compute(self, whole, tiles):
        total = None
        for left, weight in zip(whole, tiles):
            term = contract_cols(left[...], weight)
            total = term if total is None else total + term
        return (total.astype(LOW),)

    def finish(self):
        super().finish()
        if self.then:
            self.then.start()


class MixerJob:
    kept = []
    late = ()

    def hold(self, refs):
        self.kept_refs = refs

    def __init__(self, inputs, outs, extra, phases, flops):
        self.inputs = list(inputs)
        self.out_shapes = [jax.ShapeDtypeStruct(shape, dtype) for shape, dtype in outs]
        self.phases = phases
        self.tiles = sum(phases)
        self.flops = flops
        self.scratch = (
            [pltpu.VMEM(array.shape, array.dtype) for array in self.inputs]
            + [pltpu.VMEM(shape, dtype) for shape, dtype in outs]
            + extra
            + [
                pltpu.SemaphoreType.DMA((len(self.inputs),)),
                pltpu.SemaphoreType.DMA((len(outs),)),
            ]
        )

    def bind(self, ins, outs, scratch):
        self.in_refs, self.out_refs = ins, outs
        extra = len(scratch) - len(ins) - len(outs) - 2
        self.ins_v, self.outs_v, self.extra_v = split(scratch, [len(ins), len(outs), extra])
        self.in_sem, self.out_sem = scratch[-2:]
        self.count = lax.axis_size("seq")
        self.seq = lax.axis_index("seq")
        self.column = lax.axis_index("tp")

    def peers(self):
        after = (self.seq + 1) % self.count
        before = (self.seq + self.count - 1) % self.count
        return [(after, self.column), (before, self.column)]

    def load(self, which):
        return pltpu.make_async_copy(self.in_refs[which], self.ins_v[which], self.in_sem.at[which])

    def store(self, which):
        return pltpu.make_async_copy(self.outs_v[which], self.out_refs[which], self.out_sem.at[which])

    def passing(self, source, target, forward):
        step = 1 if forward else self.count - 1
        return pltpu.make_async_remote_copy(
            src_ref=source,
            dst_ref=target,
            send_sem=self.kept_refs[1].at[0],
            recv_sem=self.kept_refs[1].at[1],
            device_id=((self.seq + step) % self.count, self.column),
            device_id_type=MESH,
        )

    def start(self, late):
        for which in range(len(self.inputs)):
            if late == (which in self.late):
                self.load(which).start()

    def tile(self, index):
        begin = 0
        for phase, tiles in enumerate(self.phases):
            here = index - begin

            @pl.when((here >= 0) & (here < tiles))
            def _(phase=phase, here=here, tiles=tiles):
                @pl.when(here == 0)
                def _():
                    self.before(phase)

                self.work(phase, here)

                @pl.when(here == tiles - 1)
                def _():
                    self.after(phase)

            begin += tiles

    def finish(self):
        for which in range(len(self.out_shapes)):
            self.store(which).wait()


def visible(bound_row, shape):
    position = lax.broadcasted_iota(jnp.int32, shape, 0)
    see_one = position != bound_row
    return position, see_one, see_one & (position - 1 != bound_row)


def lagged(rows, halo, position):
    last, second = halo[15:16].astype(jnp.float32), halo[14:15].astype(jnp.float32)
    one = jnp.where(position == 0, last, pltpu.roll(rows, 1, 0))
    two = jnp.where(position == 0, second, jnp.where(position == 1, last, pltpu.roll(rows, 2, 0)))
    return one, two


class EntryJob(MixerJob):
    then = None
    late = (0,)

    def __init__(self, tokens, wide, entry_full, exit_full, bound):
        parts, rows, own = tokens.shape
        width, columns = exit_full.shape
        self.rows, self.columns, self.own = rows, columns, own
        self.width = width
        outs = [
            ((rows, 3 * columns), jnp.float32),
            ((rows, columns), jnp.float32),
            ((rows, columns), LOW),
            ((16, columns), LOW),
            ((rows, columns), LOW),
            ((parts, rows, own), LOW),
            ((rows, 128), jnp.float32),
            ((width, rows), LOW),
        ]
        phases = [rows // 256, 3 * columns // 256, 1, columns // 128, width // 256]
        flops = 2 * rows * (entry_full.size + exit_full.size)
        super().__init__([tokens, wide, entry_full, exit_full, bound], outs, [], phases, flops)
        self.kept = [pltpu.VMEM((16, columns), LOW), pltpu.SemaphoreType.DMA((2,))]

    def halo(self):
        return self.passing(self.outs_v[2].at[pl.ds(self.rows - 16, 16)], self.kept_refs[0], True)

    def before(self, phase):
        if phase == 0:
            for which in (0, 1):
                self.load(which).wait()
        if phase == 1:
            self.store(6).start()
            self.store(7).start()
            self.load(2).wait()
        if phase == 3:
            self.load(4).wait()
            self.halo().wait_recv()
            self.outs_v[3][...] = self.kept_refs[0][...]
            self.store(3).start()
        if phase == 4:
            self.load(3).wait()

    def after(self, phase):
        if phase == 1:
            self.store(0).start()
        if phase == 2:
            self.halo().start()
            self.store(2).start()
        if phase == 3:
            self.store(1).start()
            self.store(4).start()
        if phase == 4:
            self.store(5).start()

    def finish(self):
        self.store(5).wait()
        if self.then:
            self.then.start()
        self.halo().wait_send()
        for which in (0, 1, 2, 3, 4, 6, 7):
            self.store(which).wait()

    def work(self, phase, index):
        tokens, wide, entry, exits, bound = self.ins_v
        taps = wide.at[self.column]
        projected, conv, gated, halo, mixer, term, scales, turned_rows = self.outs_v
        columns = self.columns
        if phase == 0:
            rows = pl.ds(pl.multiple_of(index * 256, 256), 256)
            values = [tokens[part, rows, :].astype(jnp.float32) for part in range(tokens.shape[0])]
            total = sum(jnp.sum(value * value, axis=1, keepdims=True) for value in values)
            scale = lax.rsqrt(total / D + EPSILON)
            scales[rows, :] = jnp.broadcast_to(scale, (256, 128))
            for part, value in enumerate(values):
                normed = (value * scale * wide[part, 3:4, :]).astype(LOW)
                tokens[part, rows, :] = normed
                turned_rows[part * self.own : (part + 1) * self.own, rows] = normed.T
        if phase == 1:
            span = pl.ds(pl.multiple_of(index * 256, 256), 256)
            projected[:, span] = blocks_dot(tokens, entry[:, span])
        if phase == 2:
            gated[...] = (projected[:, :columns] * projected[:, 2 * columns :]).astype(LOW)
        if phase == 3:
            span = pl.ds(pl.multiple_of(index * 128, 128), 128)
            middle = pl.ds(pl.multiple_of(columns + index * 128, 128), 128)
            rows = gated[:, span].astype(jnp.float32)
            position, see_one, see_two = visible(bound[0:1, :], rows.shape)
            before = halo[:, span].astype(jnp.float32) * jnp.where(self.seq > 0, 1.0, 0.0)
            one, two = lagged(rows, before, position)
            total = (
                taps[2:3, span] * rows
                + taps[1:2, span] * jnp.where(see_one, one, 0.0)
                + taps[0:1, span] * jnp.where(see_two, two, 0.0)
            )
            conv[:, span] = total
            mixer[:, span] = (projected[:, middle] * total).astype(LOW)
        if phase == 4:
            features = pl.ds(pl.multiple_of(index * 256, 256), 256)
            owner, inner = index // (self.own // 256), index % (self.own // 256)
            span = pl.ds(pl.multiple_of(inner * 256, 256), 256)
            term[owner, :, span] = contract_cols(mixer[...], exits[features, :]).astype(LOW)


class MixerGradJob(MixerJob):
    then = None
    late = (0,)

    def __init__(self, branch, exit_full, entry_full, projected, conv, gated, halo, wide, bound):
        parts, rows, own = branch.shape
        width, columns = exit_full.shape
        self.rows, self.columns, self.own = rows, columns, own
        outs = [((rows, 3 * columns), LOW), ((parts, rows, own), LOW), ((8, columns), jnp.float32)]
        extra = [
            pltpu.VMEM((rows, columns), jnp.float32),
            pltpu.VMEM((8, columns), jnp.float32),
        ]
        self.kept = [pltpu.VMEM((8, columns), jnp.float32), pltpu.SemaphoreType.DMA((2,))]
        phases = [columns // 256, 1, columns // 128, width // 256]
        flops = 2 * rows * (entry_full.size + exit_full.size)
        inputs = [branch, exit_full, entry_full, projected, conv, gated, halo, wide, bound]
        super().__init__(inputs, outs, extra, phases, flops)

    def back(self):
        return self.passing(self.extra_v[1], self.kept_refs[0], False)

    def before(self, phase):
        if phase == 0:
            for which in (0, 1, 3, 4):
                self.load(which).wait()
        if phase == 1:
            for which in (7, 8):
                self.load(which).wait()
        if phase == 2:
            for which in (5, 6):
                self.load(which).wait()
            self.back().wait_recv()
        if phase == 3:
            self.load(2).wait()

    def after(self, phase):
        if phase == 1:
            self.back().start()
        if phase == 2:
            self.store(0).start()
            self.store(2).start()
        if phase == 3:
            self.store(1).start()

    def finish(self):
        self.store(1).wait()
        if self.then:
            self.then.start()
        self.back().wait_send()
        for which in (0, 2):
            self.store(which).wait()

    def work(self, phase, index):
        branch, exits, entry, projected, conv, gated, halo, wide, bound = self.ins_v
        taps = wide.at[self.column]
        grads, term, taps_grad = self.outs_v
        conv_grad, sent = self.extra_v
        returned = self.kept_refs[0]
        columns, height = self.columns, self.rows
        if phase == 0:
            span = pl.ds(pl.multiple_of(index * 256, 256), 256)
            middle = pl.ds(pl.multiple_of(columns + index * 256, 256), 256)
            mixer_grad = blocks_dot(branch, exits[:, span])
            grads[:, middle] = (mixer_grad * conv[:, span]).astype(LOW)
            conv_grad[:, span] = mixer_grad * projected[:, middle]
        if phase == 1:
            for start in range(0, columns, 128):
                span = slice(start, start + 128)
                rows = conv_grad[0:8, span]
                position, see_one, see_two = visible(bound[0:1, :], rows.shape)
                one = pltpu.roll(jnp.where(see_one, rows, 0.0) * taps[1:2, span], 1, 0)
                two = jnp.where(see_two, rows, 0.0) * taps[0:1, span]
                sent[:, span] = two + jnp.where(position == 0, 0.0, one)
            taps_grad[...] = jnp.zeros_like(taps_grad)
        if phase == 2:
            span = pl.ds(pl.multiple_of(index * 128, 128), 128)
            last = pl.ds(pl.multiple_of(2 * columns + index * 128, 128), 128)
            rows = conv_grad[:, span]
            position, see_one, see_two = visible(bound[0:1, :], rows.shape)
            seen_one, seen_two = jnp.where(see_one, rows, 0.0), jnp.where(see_two, rows, 0.0)
            one = pltpu.roll(seen_one * taps[1:2, span], height - 1, 0)
            two = pltpu.roll(seen_two * taps[0:1, span], height - 2, 0)
            after = returned[:, span] * jnp.where(self.seq < self.count - 1, 1.0, 0.0)
            gated_grad = (
                rows * taps[2:3, span]
                + jnp.where(position == height - 1, after[1:2], one)
                + jnp.where(position < height - 2, two, jnp.where(position == height - 2, after[0:1], 0.0))
            )
            grads[:, span] = (gated_grad * projected[:, last]).astype(LOW)
            grads[:, last] = (gated_grad * projected[:, span]).astype(LOW)
            own_rows = gated[:, span].astype(jnp.float32)
            before = halo[:, span].astype(jnp.float32) * jnp.where(self.seq > 0, 1.0, 0.0)
            lag_one, lag_two = lagged(own_rows, before, position)
            taps_grad[0:1, span] = jnp.sum(seen_two * lag_two, axis=0, keepdims=True)
            taps_grad[1:2, span] = jnp.sum(seen_one * lag_one, axis=0, keepdims=True)
            taps_grad[2:3, span] = jnp.sum(rows * own_rows, axis=0, keepdims=True)
        if phase == 3:
            features = pl.ds(pl.multiple_of(index * 256, 256), 256)
            owner, inner = index // (self.own // 256), index % (self.own // 256)
            span = pl.ds(pl.multiple_of(inner * 256, 256), 256)
            term[owner, :, span] = contract_cols(grads[...], entry[features, :]).astype(LOW)


class Jobs:
    def __init__(self, *jobs):
        self.jobs = jobs
        self.inputs = [item for job in jobs for item in job.inputs]
        self.out_shapes = [item for job in jobs for item in job.out_shapes]
        self.scratch = [item for job in jobs for item in job.scratch]
        self.kept = [item for job in jobs for item in job.kept]
        self.tiles = sum(job.tiles for job in jobs)
        self.flops = sum(job.flops for job in jobs)

    def hold(self, refs):
        for job, own in zip(self.jobs, split(refs, [len(job.kept) for job in self.jobs])):
            job.hold(own)

    def bind(self, ins, outs, scratch):
        groups = zip(
            self.jobs,
            split(ins, [len(job.inputs) for job in self.jobs]),
            split(outs, [len(job.out_shapes) for job in self.jobs]),
            split(scratch, [len(job.scratch) for job in self.jobs]),
        )
        for job, own_ins, own_outs, own_scratch in groups:
            job.bind(own_ins, own_outs, own_scratch)

    def peers(self):
        return [peer for job in self.jobs for peer in job.peers()]

    def start(self, late):
        for job in self.jobs:
            job.start(late)

    def tile(self, index):
        begin = 0
        for job in self.jobs:
            here = index - begin

            @pl.when((here >= 0) & (here < job.tiles))
            def _(job=job, here=here):
                job.tile(here)

            begin += job.tiles

    def finish(self):
        for job in self.jobs:
            job.finish()


class TurnJob(MixerJob):
    late = (0,)

    def __init__(self, blocks):
        parts, rows, own = blocks.shape
        super().__init__([blocks], [((parts * own, rows), blocks.dtype)], [], [rows // 128], 0)

    def peers(self):
        return []

    def before(self, phase):
        self.load(0).wait()

    def after(self, phase):
        self.store(0).start()

    def work(self, phase, index):
        (blocks,), (target,) = self.ins_v, self.outs_v
        parts, _, own = blocks.shape
        rows = pl.ds(pl.multiple_of(index * 128, 128), 128)
        for part in range(parts):
            target[part * own : (part + 1) * own, rows] = blocks[part, rows, :].T


class CastJob(MixerJob):
    def __init__(self, pairs, plain):
        rows, columns = plain.shape
        lanes = pairs.shape[1]
        self.rows, self.half, self.lanes = rows, columns // 2, lanes
        self.block = max(rows // 8, 16)
        outs = [((rows, columns // 2), LOW)] * 6
        super().__init__([pairs, plain], outs, [], [rows // self.block], 0)

    def peers(self):
        return []

    def before(self, phase):
        for which in range(2):
            self.load(which).wait()

    def after(self, phase):
        for which in range(6):
            self.store(which).start()

    def work(self, phase, index):
        pairs, plain = self.ins_v
        block, half, lanes = self.block, self.half, self.lanes
        tiles = half // lanes
        rows = pl.ds(pl.multiple_of(index * block, 16), block)
        start = index * (block * 4 * tiles)
        for which in range(4):
            side, plane = which // 2, which % 2
            for tile in range(tiles):
                place = (side * tiles + tile) * 2 + plane
                picked = pairs[pl.ds(start + place, block, stride=4 * tiles), :]
                self.outs_v[which][rows, tile * lanes : (tile + 1) * lanes] = picked.astype(LOW)
        for side in range(2):
            self.outs_v[4 + side][rows, :] = plain[rows, side * half : (side + 1) * half].astype(LOW)


class SmallGatherJob:
    tiles, flops = 1, 0

    def __init__(self, own, seen):
        self.inputs = [own]
        self.seen = seen
        devices, columns = lax.axis_size("seq"), lax.axis_size("tp")
        wide = (columns, 8, devices * seen)
        self.out_shapes = [jax.ShapeDtypeStruct(wide, jnp.float32)]
        self.scratch = [pltpu.VMEM(wide, jnp.float32), pltpu.SemaphoreType.DMA((2,))]
        self.kept = [
            pltpu.VMEM((devices, columns) + own.shape, own.dtype),
            pltpu.SemaphoreType.DMA((columns,)),
            pltpu.SemaphoreType.DMA((columns,)),
            pltpu.SemaphoreType.DMA((devices,)),
            pltpu.SemaphoreType.DMA((devices,)),
        ]

    def hold(self, refs):
        self.whole, self.near_send, self.near_recv, self.far_send, self.far_recv = refs
        self.devices, self.columns = lax.axis_size("seq"), lax.axis_size("tp")
        self.seq, self.column = lax.axis_index("seq"), lax.axis_index("tp")

    def bind(self, ins, outs, scratch):
        self.source, self.target = ins[0], outs[0]
        self.wide, self.local_sem = scratch

    def peers(self):
        near = [(self.seq, (self.column + step) % self.columns) for step in range(1, self.columns)]
        far = [((self.seq + step) % self.devices, self.column) for step in range(1, self.devices)]
        return near + far

    def near(self, step):
        piece = self.whole.at[self.seq, self.column]
        return pltpu.make_async_remote_copy(
            src_ref=piece,
            dst_ref=piece,
            send_sem=self.near_send.at[step],
            recv_sem=self.near_recv.at[step],
            device_id=(self.seq, (self.column + step) % self.columns),
            device_id_type=MESH,
        )

    def far(self, step):
        piece = self.whole.at[self.seq]
        return pltpu.make_async_remote_copy(
            src_ref=piece,
            dst_ref=piece,
            send_sem=self.far_send.at[step],
            recv_sem=self.far_recv.at[step],
            device_id=((self.seq + step) % self.devices, self.column),
            device_id_type=MESH,
        )

    def start(self, late):
        if late:
            return
        load = pltpu.make_async_copy(self.source, self.whole.at[self.seq, self.column], self.local_sem.at[0])
        load.start()
        load.wait()
        for step in range(1, self.columns):
            self.near(step).start()

    def tile(self, index):
        for step in range(1, self.columns):
            self.near(step).wait()

        def begin(step, carry):
            self.far(step).start()
            return carry

        lax.fori_loop(1, self.devices, begin, 0)

    def finish(self):
        def end(step, carry):
            self.far(step).wait()
            return carry

        lax.fori_loop(1, self.devices, end, 0)
        each = LANES // self.seen
        for column in range(self.columns):
            for start in range(0, self.devices, each):
                total = None
                for inner in range(each):
                    piece = self.whole[start + inner, column, :, :].astype(jnp.float32)[:8]
                    piece = pltpu.roll(piece, inner * self.seen, 1) if inner else piece
                    total = piece if total is None else total + piece
                self.wide[column, :, start * self.seen : start * self.seen + LANES] = total
        store = pltpu.make_async_copy(self.wide, self.target, self.local_sem.at[1])
        store.start()
        store.wait()


class RowSumJob(MixerJob):
    block = 128

    def __init__(self, inputs, outs, extra, rows, flops):
        self.columns = lax.axis_size("tp")
        blocks = rows // self.block
        self.kept = [
            pltpu.VMEM((self.columns, blocks, self.block), jnp.float32),
            pltpu.SemaphoreType.DMA((self.columns,)),
            pltpu.SemaphoreType.DMA((self.columns,)),
        ]
        totals = pltpu.VMEM((blocks, self.block), jnp.float32)
        super().__init__(inputs, outs, [totals] + extra, [blocks, 1, blocks], flops)

    def peers(self):
        return [(self.seq, (self.column + step) % self.columns) for step in range(1, self.columns)]

    def share(self, step):
        return pltpu.make_async_remote_copy(
            src_ref=self.kept_refs[0].at[0],
            dst_ref=self.kept_refs[0].at[step],
            send_sem=self.kept_refs[1].at[step],
            recv_sem=self.kept_refs[2].at[step],
            device_id=(self.seq, (self.column + step) % self.columns),
            device_id_type=MESH,
        )

    def before(self, phase):
        if phase == 0:
            for which in range(len(self.inputs)):
                self.load(which).wait()

    def after(self, phase):
        if phase == 0:
            for step in range(1, self.columns):
                self.share(step).start()
        if phase == 2:
            for which in range(len(self.out_shapes)):
                self.store(which).start()

    def finish(self):
        for step in range(1, self.columns):
            self.share(step).wait_send()
        super().finish()

    def work(self, phase, index):
        block = self.block
        slots, totals = self.kept_refs[0], self.extra_v[0]
        rows = pl.ds(pl.multiple_of(index * block, block), block)
        if phase == 0:
            part = jnp.sum(self.values(rows), axis=1, keepdims=True)
            slots[0, pl.ds(index, 1), :] = jnp.broadcast_to(part, (block, block)).T[0:1, :]
        if phase == 1:
            for step in range(1, self.columns):
                self.share(step).wait_recv()
            totals[...] = sum(slots[step] for step in range(self.columns))
        if phase == 2:
            self.use(rows, jnp.broadcast_to(totals[pl.ds(index, 1), :], (block, block)).T)


class NormJob(RowSumJob):
    then = None
    late = (1,)

    def __init__(self, rows_in, terms, wide):
        rows, own = rows_in.shape
        outs = [((rows, own), jnp.float32), ((rows, own), LOW), ((rows, 128), jnp.float32)]
        super().__init__([rows_in, terms, wide], outs, [], rows, 0)

    def values(self, rows):
        rows_in, terms, _ = self.ins_v
        residual = sum(terms[part, rows, :].astype(jnp.float32) for part in range(self.columns))
        residual = rows_in[rows, :].astype(jnp.float32) + residual
        self.outs_v[0][rows, :] = residual
        return residual * residual

    def use(self, rows, total):
        residual, normed, scales = self.outs_v
        scale = lax.rsqrt(total / D + EPSILON)
        scales[rows, :] = scale
        gain = self.ins_v[2].at[self.column]
        normed[rows, :] = (residual[rows, :] * scale[:, 0:1] * gain[4:5, :]).astype(LOW)

    def finish(self):
        self.store(1).wait()
        if self.then:
            self.then.start()
        for step in range(1, self.columns):
            self.share(step).wait_send()
        for which in (0, 2):
            self.store(which).wait()


class NormBackJob(RowSumJob):
    then = None
    late = (0,)

    def __init__(self, terms, kept, scales, wide, row, base, rounded):
        _, rows, own = terms.shape
        outs = [((rows, own), jnp.float32), ((8, own), jnp.float32)]
        outs = outs + [((rows, own), LOW)] if rounded else outs
        self.row = row
        super().__init__([terms, kept, scales, wide, base], outs, [], rows, 0)

    def parts(self, rows):
        terms, kept, scales, wide, base = self.ins_v
        gain = wide.at[self.column]
        return (
            sum(terms[part, rows, :].astype(jnp.float32) for part in range(self.columns)),
            kept[rows, :].astype(jnp.float32),
            scales[rows, 0:1],
            gain[self.row : self.row + 1, :],
        )

    def before(self, phase):
        super().before(phase)
        if phase == 0:
            self.outs_v[1][...] = jnp.zeros_like(self.outs_v[1])

    def values(self, rows):
        grad, kept, scale, gain = self.parts(rows)
        product = grad * kept
        self.outs_v[1][0:1, :] += jnp.sum(product * scale, axis=0, keepdims=True)
        return product * gain

    def use(self, rows, total):
        grad, kept, scale, gain = self.parts(rows)
        rows_grad = scale * gain * grad - kept * (scale * scale * scale * total[:, 0:1] / D)
        result = self.ins_v[4][rows, :].astype(jnp.float32) + rows_grad
        self.outs_v[0][rows, :] = result
        if len(self.outs_v) > 2:
            self.outs_v[2][rows, :] = result.astype(LOW)

    def finish(self):
        if self.then:
            self.store(2).wait()
            self.then.start()
        for step in range(1, self.columns):
            self.share(step).wait_send()
        for which in range(len(self.out_shapes)):
            if which != 2 or not self.then:
                self.store(which).wait()


class SumJob(MixerJob):
    late = (1,)

    def __init__(self, base, terms):
        rows, own = base.shape
        super().__init__([base, terms], [((rows, own), LOW)], [], [rows // 128], 0)

    def before(self, phase):
        for which in range(2):
            self.load(which).wait()

    def after(self, phase):
        self.store(0).start()

    def work(self, phase, index):
        base, terms = self.ins_v
        rows = pl.ds(pl.multiple_of(index * 128, 128), 128)
        total = sum(terms[part, rows, :].astype(jnp.float32) for part in range(terms.shape[0]))
        self.outs_v[0][rows, :] = (base[rows, :] + total).astype(LOW)


class SmallSumJob:
    tiles, flops = 1, 0

    def __init__(self, taps_grad, gain_grad, before):
        count = lax.axis_size("seq")
        self.inputs = [taps_grad, gain_grad]
        shape = taps_grad.shape
        self.before = before
        self.out_shapes = [jax.ShapeDtypeStruct(shape, jnp.float32)]
        self.scratch = [pltpu.VMEM(shape, jnp.float32)] * 3 + [pltpu.SemaphoreType.DMA((3,))]
        self.kept = [
            pltpu.VMEM((count,) + shape, jnp.float32),
            pltpu.SemaphoreType.DMA((count,)),
            pltpu.SemaphoreType.DMA((count,)),
        ]

    def hold(self, refs):
        self.slots, self.send_sem, self.recv_sem = refs

    def bind(self, ins, outs, scratch):
        self.sources, self.target = ins, outs[0]
        self.taps, self.gain, self.total, self.local_sem = scratch
        self.count = lax.axis_size("seq")
        self.seq = lax.axis_index("seq")
        self.column = lax.axis_index("tp")

    def peers(self):
        return [((self.seq + far) % self.count, self.column) for far in range(1, self.count)]

    def copy(self, far):
        return pltpu.make_async_remote_copy(
            src_ref=self.slots.at[0],
            dst_ref=self.slots.at[far],
            send_sem=self.send_sem.at[far],
            recv_sem=self.recv_sem.at[far],
            device_id=((self.seq + far) % self.count, self.column),
            device_id_type=MESH,
        )

    def loads(self):
        return [
            pltpu.make_async_copy(self.sources[which], (self.taps, self.gain)[which], self.local_sem.at[which])
            for which in range(2)
        ]

    def start(self, late):
        if late:
            return
        for load in self.loads():
            load.start()

    def tile(self, index):
        for load in self.loads():
            load.wait()
        self.slots[0, 0:3, :] = self.taps[0:3, :]
        self.slots[0, 3:4, :] = self.before.outs_v[1][0:1, :]
        self.slots[0, 4:5, :] = self.gain[0:1, :]
        self.slots[0, 5:8, :] = jnp.zeros_like(self.slots[0, 5:8, :])

        def begin(far, carry):
            self.copy(far).start()
            return carry

        lax.fori_loop(1, self.count, begin, 0)

    def finish(self):
        self.total[...] = self.slots[0]

        def add(far, carry):
            self.copy(far).wait_recv()
            self.total[...] += self.slots[far]
            return carry

        lax.fori_loop(1, self.count, add, 0)
        store = pltpu.make_async_copy(self.total, self.target, self.local_sem.at[2])
        store.start()

        def sent(far, carry):
            self.copy(far).wait_send()
            return carry

        lax.fori_loop(1, self.count, sent, 0)
        store.wait()


class Section:
    def __init__(self, ranges, jobs=(), waits=(), rest=1, calls=(), early=True, then=()):
        self.ranges, self.jobs, self.waits, self.rest, self.calls, self.early = ranges, jobs, waits, rest, calls, early
        self.then = then
        self.job = Jobs(*[job for job, _, _ in jobs])

    def run(self, ring, ins, outs):
        job = self.job
        ranges = [(group, low * ring.ticks // 12, high * ring.ticks // 12) for group, low, high in self.ranges]
        total = sum(high - low for _, low, high in ranges)
        rest = self.rest * ring.ticks // 12
        active = total - rest
        each = -(-job.tiles // active)

        def ready():
            for exchange in self.waits:
                exchange.wait()
            for exchange in self.then:
                exchange.start()
            job.start(True)

        def body(*scratch):
            job.bind(ins, outs, list(scratch))
            job.start(False)
            if not self.waits:
                job.start(True)
            done = 0
            for place, (group, low, high) in enumerate(ranges):
                if low == 0 and group > 0 and place > 0:
                    ring.turn(group)
                if place == 0:
                    for call in self.calls:
                        call.start()

                def step(index, carry, group=group, shift=done - low):
                    late = index + shift - rest
                    first, after = late * job.tiles // active, (late + 1) * job.tiles // active
                    if self.waits:
                        pl.when(late == -1)(ready)
                    for inner in range(each):
                        tile = first + inner

                        @pl.when((late >= 0) & (tile < after))
                        def _(tile=tile):
                            job.tile(tile)

                    ring.tick(group, index)
                    return carry

                lax.fori_loop(low, high, step, 0)
                done += high - low
            group, _, high = ranges[-1]
            ends = high == ring.ticks and group + 1 < len(ring.groups)
            if ends and self.early:
                ring.begin(group + 1)
            job.finish()
            if ends and not self.early:
                ring.begin(group + 1)

        pl.run_scoped(body, *job.scratch)
        group, _, high = ranges[-1]
        if high == ring.ticks:
            ring.settle(group)
            ring.settled(group)


class Plan:
    def __init__(self, arrays):
        self.arrays = arrays
        self.shapes = {name: jax.ShapeDtypeStruct(array.shape, array.dtype) for name, array in arrays.items()}
        self.inputs = list(self.shapes)
        self.weights = set()

    def define(self, name, shape, dtype):
        self.shapes[name] = jax.ShapeDtypeStruct(shape, dtype)

    def add(self, job, ins, outs):
        for name, shape in zip(outs, job.out_shapes):
            self.shapes[name] = shape
        return job, ins, outs

    def flat(self, full):
        shape = self.shapes[full].shape
        return jax.ShapeDtypeStruct((shape[0] * shape[1], shape[2]), LOW)

    def run(self, ring, sections, exchanges, peers, name, collective):
        inputs = self.inputs
        outputs = [made for made in self.shapes if made not in inputs]
        kept = [item for section in sections for item in section.job.kept]
        sems = [item for exchange in exchanges for item in exchange.scratch]

        def kernel(*all_refs):
            in_refs, out_refs, ring_scratch, sem_refs, kept_refs = split(
                all_refs, [len(inputs), len(outputs), len(ring.scratch), len(sems), len(kept)]
            )
            refs = dict(zip(inputs + outputs, in_refs + out_refs))
            ring.bind(refs, ring_scratch)
            for place, exchange in enumerate(exchanges):
                exchange.bind(refs, sem_refs[2 * place : 2 * place + 2])
            for section, own in zip(sections, split(kept_refs, [len(section.job.kept) for section in sections])):
                section.job.hold(own)
            ring.prepare()
            greet(peers())
            ring.begin(0)
            ring.settled(-1)
            for section in sections:
                ins = [rows_of(refs[made], made in self.weights) for _, names, _ in section.jobs for made in names]
                outs = [refs[made] for _, _, names in section.jobs for made in names]
                section.run(ring, ins, outs)
            ring.finish()
            for exchange in exchanges:
                exchange.finish()

        flops = ring.flops + sum(section.job.flops for section in sections)
        results = pl.pallas_call(
            kernel,
            out_shape=[self.shapes[made] for made in outputs],
            in_specs=[pl.BlockSpec(memory_space=pl.ANY)] * len(inputs),
            out_specs=[pl.BlockSpec(memory_space=pl.ANY)] * len(outputs),
            scratch_shapes=ring.scratch + sems + kept,
            compiler_params=pltpu.CompilerParams(
                collective_id=collective, has_side_effects=True, vmem_limit_bytes=VMEM_BYTES
            ),
            cost_estimate=pl.CostEstimate(flops=flops, bytes_accessed=10**9, transcendentals=0),
            name=name,
        )(*self.arrays.values())
        named = dict(zip(outputs, results))
        return {made: flat(array) if made in self.weights else array for made, array in named.items()}


def row_and_column_peers():
    seq, column = lax.axis_index("seq"), lax.axis_index("tp")
    devices, columns = lax.axis_size("seq"), lax.axis_size("tp")
    near = [(seq, (column + step) % columns) for step in range(1, columns)]
    return near + [((seq + step) % devices, column) for step in range(1, devices)]


def run_forward(arrays, seen):
    count, columns = lax.axis_size("seq"), lax.axis_size("tp")
    plan = Plan(arrays)
    shapes, add = plan.shapes, plan.add
    rows, own = arrays["tokens"].shape
    for name in ("tokens_blocks", "cot_blocks", "branch_terms", "normed_blocks"):
        plan.define(name, (columns, rows, own), LOW)
    low = ["gate_low0", "up_low0", "gate_low1", "up_low1", "shrink_low0", "shrink_low1"]
    small = add(SmallGatherJob(shapes["small"], seen), ["small"], ["wide"])
    cast = add(CastJob(shapes["pairs"], shapes["shrink"]), ["pairs", "shrink"], low)
    groups = [[("entry_low", "entry_full"), ("exit_low", "exit_full")]]
    groups += [[(name, name.replace("low", "full"))] for name in low]
    for group in groups:
        for shard, full in group:
            plan.define(full, (count,) + shapes[shard].shape, LOW)
            plan.weights.add(full)
    ring = GatherRing(groups, shapes)
    tokens_sent = PeerCopies("tokens", "tokens_blocks")
    cot_sent = PeerCopies("cotangent", "cot_blocks")
    branch_sent = PeerCopies("term", "branch_terms")
    normed_sent = PeerCopies("normed_own", "normed_blocks")

    entry_job = EntryJob(
        shapes["tokens_blocks"], shapes["wide"], plan.flat("entry_full"), plan.flat("exit_full"), shapes["bound"]
    )
    entry_job.then = branch_sent
    entry = add(
        entry_job,
        ["tokens_blocks", "wide", "entry_full", "exit_full", "bound"],
        ["projected", "conv_out", "gated", "halo", "mixer", "term", "scale_one", "normed_one"],
    )
    turn_cot = add(TurnJob(shapes["cot_blocks"]), ["cot_blocks"], ["cot_full"])
    norm_job = NormJob(shapes["tokens"], shapes["branch_terms"], shapes["wide"])
    norm_job.then = normed_sent
    norm = add(norm_job, ["tokens", "branch_terms", "wide"], ["residual", "normed_own", "scale_two"])
    expands = []
    for half in "01":
        job = ExpandJob(shapes["normed_blocks"], plan.flat("gate_full" + half), plan.flat("up_full" + half))
        names = ["normed_blocks", "gate_full" + half, "up_full" + half]
        expands.append(add(job, names, ["gate_rows" + half, "up_rows" + half, "activation" + half]))
    hidden_job = HiddenGradJob(shapes["cot_blocks"], plan.flat("shrink_full0"), shapes["gate_rows0"], shapes["up_rows0"])
    hidden = add(hidden_job, ["cot_blocks", "shrink_full0", "gate_rows0", "up_rows0"], ["gate_grad0", "up_grad0"])
    turn_normed = add(TurnJob(shapes["normed_blocks"]), ["normed_blocks"], ["normed_two"])
    sections = [
        Section([(0, 0, 12)], [small, cast], calls=[tokens_sent], early=False),
        Section([(1, 0, 12)], [entry], [tokens_sent], calls=[cot_sent]),
        Section([(2, 0, 12)], [turn_cot], [cot_sent], rest=3),
        Section([(3, 0, 12)], [norm], [branch_sent], rest=4),
        Section([(4, 0, 12)]),
        Section([(5, 0, 12)], expands, [normed_sent], rest=4),
        Section([(6, 0, 12)], [hidden, turn_normed]),
    ]
    exchanges = [tokens_sent, cot_sent, branch_sent, normed_sent]
    return plan.run(ring, sections, exchanges, row_and_column_peers, "forward", 0)


def run_backward(arrays):
    columns = lax.axis_size("tp")
    plan = Plan(arrays)
    shapes, add = plan.shapes, plan.add
    rows, own = arrays["tokens"].shape
    for name in ("two_terms", "mixed_terms", "branch_blocks", "one_terms"):
        plan.define(name, (columns, rows, own), LOW)
    two_sent = PeerCopies("two_term", "two_terms")
    mixed_sent = PeerCopies("mixed_term", "mixed_terms")
    branch_sent = PeerCopies("branch_own", "branch_blocks")
    one_sent = PeerCopies("one_term", "one_terms")

    hidden = add(
        HiddenGradJob(shapes["cot_blocks"], shapes["shrink_full1"], shapes["gate_rows1"], shapes["up_rows1"]),
        ["cot_blocks", "shrink_full1", "gate_rows1", "up_rows1"],
        ["gate_grad1", "up_grad1"],
    )
    names = [["gate_grad0", "up_grad0", "gate_grad1", "up_grad1"], ["gate_full0", "up_full0", "gate_full1", "up_full1"]]
    two_job = WidthJob(*[[shapes[name] for name in side] for side in names])
    two_job.then = two_sent
    two = add(two_job, names[0] + names[1], ["two_term"])
    names = [["activation0", "activation1"], ["shrink_full0", "shrink_full1"]]
    mixed = add(WidthJob(*[[shapes[name] for name in side] for side in names]), names[0] + names[1], ["mixed_term"])
    back_two = NormBackJob(
        shapes["two_terms"], shapes["residual"], shapes["scale_two"], shapes["wide"], 4, shapes["cotangent"], True
    )
    back_two.then = branch_sent
    names = ["two_terms", "residual", "scale_two", "wide", "cotangent"]
    norm_two = add(back_two, names, ["residual_grad", "gain_two_grad", "branch_own"])
    names = ["branch_blocks", "exit_full", "entry_full", "projected", "conv_out", "gated", "halo", "wide", "bound"]
    mixer_job = MixerGradJob(*[shapes[name] for name in names])
    mixer_job.then = one_sent
    mixer = add(mixer_job, names, ["projected_grad", "one_term", "taps_grad"])
    turn = add(TurnJob(shapes["branch_blocks"]), ["branch_blocks"], ["branch_full"])
    back_one = NormBackJob(
        shapes["one_terms"], shapes["tokens"], shapes["scale_one"], shapes["wide"], 3, shapes["residual_grad"], False
    )
    names = ["one_terms", "tokens", "scale_one", "wide", "residual_grad"]
    norm_one = add(back_one, names, ["tokens_grad", "gain_one_grad"])
    small_job = SmallSumJob(shapes["taps_grad"], shapes["gain_two_grad"], back_one)
    small = add(small_job, ["taps_grad", "gain_two_grad"], ["small_part"])
    total = add(SumJob(shapes["residual"], shapes["mixed_terms"]), ["residual", "mixed_terms"], ["mixed"])

    wide = own
    halves = [("cot_full", "activation0"), ("cot_full", "activation1")]
    halves += [("normed_two", name) for name in ("gate_grad0", "up_grad0", "gate_grad1", "up_grad1")]
    halves += [("normed_one", "projected_grad")]
    groups = [[(left, right, 0), (left, right, wide)] for left, right in halves]
    groups += [[("normed_one", "projected_grad", 2 * wide), ("branch_full", "mixer", 0)]]
    places = {"cot_full": 0, "normed_two": 1, "normed_one": 0, "branch_full": 2}
    ring = ScatterRing(groups, places, shapes, wide)
    sums = ["shrink0", "shrink1", "gate0", "up0", "gate1", "up1", "entry", "entry_exit"]
    for name, shape in zip(sums, ring.out_shapes):
        plan.shapes[name] = shape
    ring.outs = sums
    sections = [
        Section([(0, 0, 5)], [hidden]),
        Section([(0, 5, 12), (1, 0, 4)], [two], rest=2),
        Section([(1, 4, 12), (2, 0, 5)], [mixed]),
        Section([(2, 5, 12)], [norm_two], [two_sent], rest=3),
        Section([(3, 0, 12)]),
        Section([(4, 0, 12)], [mixer], [branch_sent], rest=3, then=[mixed_sent]),
        Section([(5, 0, 12)], [turn]),
        Section([(6, 0, 12)], [norm_one, small], [one_sent], rest=5),
        Section([(7, 0, 12)], [total], [mixed_sent]),
    ]
    exchanges = [two_sent, mixed_sent, branch_sent, one_sent]
    return plan.run(ring, sections, exchanges, row_and_column_peers, "backward", 1)


def rows_of(ref, gathered):
    if not gathered:
        return ref
    count, rows, columns = ref.shape
    return ref.reshape(count * rows, columns)


def flat(full):
    return full.reshape(full.shape[0] * full.shape[1], full.shape[2])


def contract_cols(left, right):
    return lax.dot_general(
        left, right, (((1,), (1,)), ((), ())), preferred_element_type=jnp.float32
    )


def adam_update(weight, first, second, grad, rate, decay):
    first_next = BETA_ONE * first + (1.0 - BETA_ONE) * grad
    second_next = BETA_TWO * second + (1.0 - BETA_TWO) * grad * grad
    corrected = first_next / (1.0 - BETA_ONE**STEP)
    spread = jnp.sqrt(second_next / (1.0 - BETA_TWO**STEP)) + ADAM_EPSILON
    return (weight - rate * (corrected / spread + decay * weight), first_next, second_next)


def adam_kernel(pieces, *refs):
    weight, first, second = refs[:3]
    grads, outs = refs[3 : 3 + pieces], refs[3 + pieces :]
    start = 0
    for grad in grads:
        span = slice(start, start + grad.shape[1])
        start += grad.shape[1]
        results = adam_update(weight[:, span], first[:, span], second[:, span], grad[...], RATE_WIDE, WEIGHT_DECAY)
        for out, result in zip(outs, results):
            out[:, span] = result


def adam_rows(weight, first, second, grads):
    rows, columns = weight.shape
    block = max(rows // 4, 8)
    state = pl.BlockSpec((block, columns), lambda step: (step, 0))
    grad_specs = [pl.BlockSpec((block, grad.shape[1]), lambda step: (step, 0)) for grad in grads]
    return pl.pallas_call(
        functools.partial(adam_kernel, len(grads)),
        out_shape=[jax.ShapeDtypeStruct(weight.shape, weight.dtype)] * 3,
        grid=(rows // block,),
        in_specs=[state] * 3 + grad_specs,
        out_specs=[state] * 3,
        compiler_params=pltpu.CompilerParams(vmem_limit_bytes=VMEM_BYTES),
        cost_estimate=pl.CostEstimate(flops=20 * weight.size, bytes_accessed=28 * weight.size, transcendentals=0),
        name="adam_rows",
    )(weight, first, second, *grads)


def adam_mixer_kernel(*refs):
    entries, exits, grads, outs = refs[:3], refs[3:6], refs[6:8], refs[8:]
    planes, _, columns = entries[0].shape
    for plane in range(planes + 1):
        grad = grads[plane // 2][:, plane % 2 * columns : (plane % 2 + 1) * columns]
        state = [ref[plane] for ref in entries] if plane < planes else [ref[...] for ref in exits]
        results = adam_update(*state, grad, RATE_WIDE, WEIGHT_DECAY)
        for place, result in enumerate(results):
            if plane < planes:
                outs[place][plane] = result
            else:
                outs[3 + place][...] = result


def adam_mixer(entries, exits, grad, last):
    rows, planes, columns = entries[0].shape
    block = max(rows // 4, 8)
    entry_spec = pl.BlockSpec((planes, block, columns), lambda step: (0, step, 0))
    exit_spec = pl.BlockSpec((block, columns), lambda step: (step, 0))
    grad_spec = pl.BlockSpec((block, 2 * columns), lambda step: (step, 0))
    size = entries[0].size + exits[0].size
    results = pl.pallas_call(
        adam_mixer_kernel,
        out_shape=[jax.ShapeDtypeStruct((planes, rows, columns), jnp.float32)] * 3
        + [jax.ShapeDtypeStruct((rows, columns), jnp.float32)] * 3,
        grid=(rows // block,),
        in_specs=[entry_spec] * 3 + [exit_spec] * 3 + [grad_spec] * 2,
        out_specs=[entry_spec] * 3 + [exit_spec] * 3,
        compiler_params=pltpu.CompilerParams(vmem_limit_bytes=VMEM_BYTES),
        cost_estimate=pl.CostEstimate(flops=20 * size, bytes_accessed=28 * size, transcendentals=0),
        name="adam_mixer",
    )(*[array.transpose(1, 0, 2) for array in entries], *exits, grad, last)
    return [result.transpose(1, 0, 2) for result in results[:3]] + list(results[3:])


def adam_pairs_kernel(lanes, *refs):
    weight, first, second = refs[:3]
    grads, outs, mixed = refs[3:7], refs[7:10], refs[10]
    rows = grads[0].shape[0]
    tiles = grads[0].shape[1] // lanes
    for which, grad in enumerate(grads):
        half, side = which // 2, which % 2
        for tile in range(tiles):
            place = (half * tiles + tile) * 2 + side
            mixed[pl.ds(place, rows, stride=4 * tiles), :] = grad[:, tile * lanes : (tile + 1) * lanes]
    results = adam_update(weight[...], first[...], second[...], mixed[...], RATE_WIDE, WEIGHT_DECAY)
    for out, result in zip(outs, results):
        out[...] = result


def paired(array):
    rows, _, columns = array.shape
    return array.reshape(rows, 2, columns // LANES, LANES).transpose(0, 2, 1, 3).reshape(-1, LANES)


def adam_pairs(weight, first, second, grads):
    rows, _, columns = weight.shape
    deep = columns // LANES
    block = max(rows // 8, 8)
    state = pl.BlockSpec((block * deep * 2, LANES), lambda step: (step, 0))
    results = pl.pallas_call(
        functools.partial(adam_pairs_kernel, LANES),
        out_shape=[jax.ShapeDtypeStruct((rows * deep * 2, LANES), weight.dtype)] * 3,
        grid=(rows // block,),
        in_specs=[state] * 3 + [pl.BlockSpec((block, columns // 2), lambda step: (step, 0))] * 4,
        out_specs=[state] * 3,
        scratch_shapes=[pltpu.VMEM((block * deep * 2, LANES), jnp.float32)],
        cost_estimate=pl.CostEstimate(flops=20 * weight.size, bytes_accessed=28 * weight.size, transcendentals=0),
        name="adam_pairs",
    )(paired(weight), paired(first), paired(second), *grads)
    return [
        result.reshape(rows, deep, 2, LANES).transpose(0, 2, 1, 3).reshape(rows, 2, columns) for result in results
    ]


def shards(
    tokens,
    bounds,
    cotangent,
    entry_weight,
    entry_first,
    entry_second,
    exit_weight,
    exit_first,
    exit_second,
    expand_weight,
    expand_first,
    expand_second,
    shrink_weight,
    shrink_first,
    shrink_second,
    conv_kernel,
    conv_first,
    conv_second,
    norm_gains,
    gain_first,
    gain_second,
):
    channels = tokens.shape[1]
    seen = conv_kernel.shape[1]
    small = jnp.concatenate([conv_kernel, norm_gains], axis=0)
    small = jnp.pad(small, ((0, 16 - small.shape[0]), (0, LANES - seen))).astype(LOW)
    entry_low = entry_weight.reshape(entry_weight.shape[0], 3 * channels).astype(LOW)
    bound = jnp.broadcast_to(bounds[0], (8, 128))
    made = run_forward(
        {
            "entry_low": entry_low,
            "exit_low": exit_weight.astype(LOW),
            "small": small,
            "tokens": tokens,
            "cotangent": cotangent,
            "bound": bound,
            "pairs": paired(expand_weight),
            "shrink": shrink_weight,
        },
        seen,
    )
    names = ["wide", "exit_full", "entry_full", "projected", "conv_out", "gated", "halo", "mixer", "residual"]
    names += ["scale_one", "scale_two", "cot_blocks", "cot_full", "normed_one", "normed_two", "gate_grad0", "up_grad0"]
    names += ["gate_rows1", "up_rows1", "activation0", "activation1"]
    names += [name + half for name in ("gate_full", "up_full", "shrink_full") for half in "01"]
    given = {"tokens": tokens, "cotangent": cotangent, "bound": bound}
    grads = run_backward(given | {name: made[name] for name in names})
    mixed, tokens_grad = grads["mixed"], grads["tokens_grad"]
    small_part = lax.dynamic_slice_in_dim(grads["small_part"], lax.axis_index("seq") * seen, seen, axis=1)
    kernel_part = small_part[:3]
    gains_part = small_part[3:5]
    (
        entry_next,
        entry_first_next,
        entry_second_next,
        exit_next,
        exit_first_next,
        exit_second_next,
    ) = adam_mixer(
        (entry_weight, entry_first, entry_second),
        (exit_weight, exit_first, exit_second),
        grads["entry"],
        grads["entry_exit"],
    )
    expand_next, expand_first_next, expand_second_next = adam_pairs(
        expand_weight, expand_first, expand_second, [grads[name] for name in ("gate0", "up0", "gate1", "up1")]
    )
    shrink_next, shrink_first_next, shrink_second_next = adam_rows(
        shrink_weight, shrink_first, shrink_second, [grads["shrink0"], grads["shrink1"]]
    )
    conv_next, conv_first_next, conv_second_next = adam_update(
        conv_kernel, conv_first, conv_second, kernel_part, RATE_CONV, 0.0
    )
    gains_next, gains_first_next, gains_second_next = adam_update(
        norm_gains, gain_first, gain_second, gains_part, RATE_GAIN, 0.0
    )
    return (
        mixed,
        tokens_grad,
        entry_next,
        entry_first_next,
        entry_second_next,
        exit_next,
        exit_first_next,
        exit_second_next,
        expand_next,
        expand_first_next,
        expand_second_next,
        shrink_next,
        shrink_first_next,
        shrink_second_next,
        conv_next,
        conv_first_next,
        conv_second_next,
        gains_next,
        gains_first_next,
        gains_second_next,
    )


def solution(mesh):
    rows = P("seq", "tp")
    stacked = P("seq", None, "tp")
    small = P(None, ("tp", "seq"))
    return jax.shard_map(
        shards,
        mesh=mesh,
        in_specs=(rows, P("seq"), rows) + (stacked,) * 3 + (rows,) * 3 + (stacked,) * 3 + (rows,) * 3 + (small,) * 6,
        out_specs=(rows, rows) + (stacked,) * 3 + (rows,) * 3 + (stacked,) * 3 + (rows,) * 3 + (small,) * 6,
        check_vma=False,
    )
```

```python
import functools

import jax
import jax.numpy as jnp
from jax import lax
from jax.experimental import pallas as pl
from jax.experimental.pallas import tpu as pltpu
from jax.sharding import PartitionSpec as P

D = 2048
STEP = 10


EPSILON = 1e-05
BETA_ONE = 0.9
BETA_TWO = 0.95
ADAM_EPSILON = 1e-08
WEIGHT_DECAY = 0.1
RATE_WIDE = 0.04
RATE_CONV = 0.5
RATE_GAIN = 0.4

MESH = pl.DeviceIdType.MESH
LOW = jnp.bfloat16
LANES = 128
VMEM_BYTES = 60 * 1024 * 1024


def ring_place(index, count):
    side = index % 2
    level = index // 2
    return level * (1 - side) + (count - 1 - level) * side


def ring_index(place, count):
    back = place // (count // 2)
    return (1 - back) * (2 * place) + back * (2 * (count - 1 - place) + 1)


def ring_ends(count):
    place = ring_place(lax.axis_index("seq"), count)
    ahead = ring_index((place + 1) % count, count)
    behind = ring_index((place + count - 1) % count, count)
    return place, ahead, behind


def greet(peers):
    barrier = pltpu.get_barrier_semaphore()
    for peer in peers:
        pl.semaphore_signal(barrier, inc=1, device_id=peer, device_id_type=MESH)
    pl.semaphore_wait(barrier, len(peers))


def split(items, sizes):
    parts, start = [], 0
    for size in sizes:
        parts.append(items[start : start + size])
        start += size
    return parts


class GatherRing:
    def __init__(self, groups, shapes):
        self.count = lax.axis_size("seq")
        self.groups = groups
        self.rows = {full: shapes[shard].shape[0] for group in groups for shard, full in group}
        self.order = {full: place for place, full in enumerate(self.rows)}
        self.parts = 2 if min(self.rows.values()) % 64 == 0 else 1
        self.ticks = (self.count - 2) * self.parts
        arrays = len(self.rows)
        sems = pltpu.SemaphoreType.DMA((arrays, 2, self.parts, self.count - 1))
        self.scratch = [sems, sems, pltpu.SemaphoreType.DMA((arrays,))]
        self.flops = 0

    def bind(self, refs, scratch):
        self.refs = refs
        self.send_sem, self.recv_sem, self.own_sem = scratch
        self.column = lax.axis_index("tp")
        self.place, self.ahead, self.behind = ring_ends(self.count)

    def copy(self, shard, full, way, part, step, first=False):
        move = (self.place + self.count - step) if way == 0 else (self.place + step)
        owner = ring_index(move % self.count, self.count)
        half = self.rows[full] // 2
        size = half // self.parts
        rows = pl.ds(pl.multiple_of(way * half + part * size, 16), size)
        there = self.refs[full].at[owner, rows]
        return pltpu.make_async_remote_copy(
            src_ref=self.refs[shard].at[rows] if first else there,
            dst_ref=there,
            send_sem=self.send_sem.at[self.order[full], way, part, step],
            recv_sem=self.recv_sem.at[self.order[full], way, part, step],
            device_id=(self.ahead if way == 0 else self.behind, self.column),
            device_id_type=MESH,
        )

    def own(self, shard, full):
        there = self.refs[full].at[lax.axis_index("seq")]
        return pltpu.make_async_copy(self.refs[shard], there, self.own_sem.at[self.order[full]])

    def pieces(self, group):
        return [(shard, full, way) for shard, full in self.groups[group] for way in range(2)]

    def begin(self, group):
        for part in range(self.parts):
            for shard, full, way in self.pieces(group):
                self.copy(shard, full, way, part, 0, True).start()
        for shard, full in self.groups[group]:
            self.own(shard, full).start()

    def tick(self, group, index):
        step, part = 1 + index // self.parts, index % self.parts
        for shard, full, way in self.pieces(group):
            self.copy(shard, full, way, part, step - 1).wait_recv()
            self.copy(shard, full, way, part, step).start()

    def prepare(self):
        pass

    def turn(self, group):
        self.begin(group)
        self.settle(group - 1)

    def settled(self, group):
        pass

    def settle(self, group):
        for part in range(self.parts):
            for shard, full, way in self.pieces(group):
                self.copy(shard, full, way, part, self.count - 2).wait_recv()
        for shard, full in self.groups[group]:
            self.own(shard, full).wait()

    def finish(self):
        def sent(step, carry):
            for group in range(len(self.groups)):
                for part in range(self.parts):
                    for shard, full, way in self.pieces(group):
                        self.copy(shard, full, way, part, step).wait_send()
            return carry

        lax.fori_loop(0, self.count - 1, sent, 0)


class PeerCopies:
    def __init__(self, source, target):
        self.source, self.target = source, target
        columns = lax.axis_size("tp")
        self.scratch = [pltpu.SemaphoreType.DMA((columns,)), pltpu.SemaphoreType.DMA((columns,))]

    def bind(self, refs, scratch):
        self.source_ref, self.target_ref = refs[self.source], refs[self.target]
        self.send_sem, self.recv_sem = scratch
        self.columns = lax.axis_size("tp")
        self.seq, self.column = lax.axis_index("seq"), lax.axis_index("tp")

    def block(self, peer):
        if len(self.source_ref.shape) == len(self.target_ref.shape):
            return self.source_ref.at[peer]
        return self.source_ref

    def own(self):
        return pltpu.make_async_copy(
            self.block(self.column), self.target_ref.at[self.column], self.send_sem.at[0]
        )

    def copy(self, step):
        peer = (self.column + step) % self.columns
        return pltpu.make_async_remote_copy(
            src_ref=self.block(peer),
            dst_ref=self.target_ref.at[self.column],
            send_sem=self.send_sem.at[step],
            recv_sem=self.recv_sem.at[step],
            device_id=(self.seq, peer),
            device_id_type=MESH,
        )

    def start(self):
        for step in range(1, self.columns):
            self.copy(step).start()
        self.own().start()

    def wait(self):
        self.own().wait()
        for step in range(1, self.columns):
            self.copy(step).wait_recv()

    def finish(self):
        for step in range(1, self.columns):
            self.copy(step).wait_send()


class ScatterRing:
    def __init__(self, groups, places, shapes, wide):
        self.count = lax.axis_size("seq")
        self.groups, self.places, self.wide = groups, places, wide
        self.names = list(places)
        left = shapes[self.names[0]]
        features, tokens = left.shape
        self.rows = features // self.count
        self.parts = 2
        self.ticks = (self.count - 2) * self.parts
        sems = pltpu.SemaphoreType.DMA((len(groups), 2, self.parts, self.count - 1))
        buffers = max(places.values()) + 1
        self.scratch = [
            pltpu.VMEM((buffers, features, tokens), LOW),
            pltpu.VMEM((2, 2, tokens, wide), LOW),
            pltpu.VMEM((2, 2, self.count, self.rows, wide), LOW),
            pltpu.VMEM((2, self.rows, 2 * wide), jnp.float32),
            sems,
            sems,
            pltpu.SemaphoreType.DMA((len(self.names),)),
            pltpu.SemaphoreType.DMA((2, 2)),
            pltpu.SemaphoreType.DMA((2,)),
        ]
        self.flops = 4 * len(groups) * features * tokens * wide
        self.out_shapes = [jax.ShapeDtypeStruct((self.rows, 2 * wide), jnp.float32)] * len(groups)

    def bind(self, refs, scratch):
        self.refs, self.out_refs = refs, [refs[name] for name in self.outs]
        self.lefts, self.rights, self.slots, self.finals = scratch[:4]
        self.send_sem, self.recv_sem, self.left_sem, self.right_sem, self.done_sem = scratch[4:]
        self.column = lax.axis_index("tp")
        self.place, self.ahead, self.behind = ring_ends(self.count)

    def left_load(self, name):
        return pltpu.make_async_copy(
            self.refs[name], self.lefts.at[self.places[name]], self.left_sem.at[self.names.index(name)]
        )

    def right_load(self, group, way):
        _, name, start = self.groups[group][way]
        source = self.refs[name].at[:, pl.ds(start, self.wide)]
        return pltpu.make_async_copy(source, self.rights.at[group % 2, way], self.right_sem.at[group % 2, way])

    def fetch(self, group):
        for way in range(2):
            self.right_load(group, way).start()

    def span(self, part):
        width = self.wide // self.parts
        return pl.ds(pl.multiple_of(part * width, 128), width)

    def term(self, group, way, part, step):
        move = (self.place + 2 * self.count - 1 - step) if way == 0 else (self.place + 1 + step)
        owner = ring_index(move % self.count, self.count)
        rows = pl.ds(pl.multiple_of(owner * self.rows, 16), self.rows)
        left = self.lefts[self.places[self.groups[group][way][0]], rows, :]
        right = self.rights[group % 2, way, :, self.span(part)]
        return jnp.dot(left, right, preferred_element_type=jnp.float32)

    def held(self, group, way, part, step):
        return self.slots.at[group % 2, way, step, :, self.span(part)]

    def copy(self, group, way, part, step):
        return pltpu.make_async_remote_copy(
            src_ref=self.held(group, way, part, step),
            dst_ref=self.held(group, way, part, step + 1),
            send_sem=self.send_sem.at[group, way, part, step],
            recv_sem=self.recv_sem.at[group, way, part, step],
            device_id=(self.ahead if way == 0 else self.behind, self.column),
            device_id_type=MESH,
        )

    def store(self, group):
        return pltpu.make_async_copy(self.finals.at[group % 2], self.out_refs[group], self.done_sem.at[group % 2])

    def prepare(self):
        self.left_load("cot_full").start()
        self.fetch(0)
        self.left_load("normed_two").start()

    def turn(self, group):
        self.begin(group)
        self.settle(group - 1)
        self.settled(group - 1)

    def settled(self, group):
        if group + 2 < len(self.groups):
            self.fetch(group + 2)
        if group == 1:
            self.left_load("normed_one").start()
        if group == 5:
            self.left_load("branch_full").start()

    def begin(self, group):
        for name, first in (("cot_full", 0), ("normed_two", 2), ("normed_one", 6), ("branch_full", 7)):
            if group == first:
                self.left_load(name).wait()
        for way in range(2):
            self.right_load(group, way).wait()
        for part in range(self.parts):
            for way in range(2):
                self.held(group, way, part, 0)[...] = self.term(group, way, part, 0).astype(LOW)
                self.copy(group, way, part, 0).start()

    def tick(self, group, index):
        step, part = 1 + index // self.parts, index % self.parts
        for way in range(2):
            mine = self.term(group, way, part, step)
            self.copy(group, way, part, step - 1).wait_recv()
            held = self.held(group, way, part, step)
            held[...] = (held[...].astype(jnp.float32) + mine).astype(LOW)
            self.copy(group, way, part, step).start()

    def settle(self, group):
        last = self.count - 1
        if group >= 1:
            self.store(group - 1).wait()
        for part in range(self.parts):
            for way in range(2):
                mine = self.term(group, way, part, last)
                self.copy(group, way, part, last - 1).wait_recv()
                width = self.wide // self.parts
                start = way * self.wide + part * width
                self.finals[group % 2, :, start : start + width] = (
                    self.held(group, way, part, last)[...].astype(jnp.float32) + mine
                )
        self.store(group).start()

        def sent(step, carry):
            for part in range(self.parts):
                for way in range(2):
                    self.copy(group, way, part, step).wait_send()
            return carry

        lax.fori_loop(0, last, sent, 0)

    def finish(self):
        self.store(len(self.groups) - 1).wait()


class Job:
    wide = 256
    kept = []
    late = ()

    def hold(self, refs):
        pass

    def __init__(self, whole, tiled, outs, tiles, flops):
        self.whole, self.tiled = whole, tiled
        self.inputs = list(whole) + [array for array, axis in tiled]
        self.axes = [axis for array, axis in tiled]
        self.out_shapes = [jax.ShapeDtypeStruct(shape, dtype) for shape, dtype in outs]
        self.tiles = tiles
        self.flops = flops
        self.scratch = (
            [pltpu.VMEM(array.shape, array.dtype) for array in self.inputs]
            + [pltpu.VMEM(shape, dtype) for shape, dtype in outs]
            + [
                pltpu.SemaphoreType.DMA((len(whole),)),
                pltpu.SemaphoreType.DMA((len(tiled), tiles)),
                pltpu.SemaphoreType.DMA((len(outs), tiles)),
            ]
        )

    def bind(self, ins, outs, scratch):
        self.in_refs, self.out_refs = ins, outs
        sizes = [len(self.whole), len(self.tiled), len(outs)]
        self.whole_v, self.tiled_v, self.outs_v = split(scratch, sizes)
        self.whole_sem, self.tiled_sem, self.out_sem = scratch[sum(sizes) :]

    def peers(self):
        return []

    def window(self, axis, index):
        span = pl.ds(pl.multiple_of(index * self.wide, 128), self.wide)
        return (span,) if axis == 0 else (slice(None), span)

    def whole_load(self, which):
        return pltpu.make_async_copy(self.in_refs[which], self.whole_v[which], self.whole_sem.at[which])

    def tiled_load(self, which, index):
        window = self.window(self.axes[which], index)
        there = self.in_refs[len(self.whole) + which].at[window]
        return pltpu.make_async_copy(there, self.tiled_v[which].at[window], self.tiled_sem.at[which, index])

    def out_window(self, index):
        return self.window(1, index)

    def store(self, which, index):
        window = self.out_window(index)
        return pltpu.make_async_copy(
            self.outs_v[which].at[window], self.out_refs[which].at[window], self.out_sem.at[which, index]
        )

    def start(self, late):
        for which in range(len(self.whole)):
            if late == (which in self.late):
                self.whole_load(which).start()

        def begin(index, carry):
            for which in range(len(self.tiled)):
                self.tiled_load(which, index).start()
            return carry

        if not late:
            lax.fori_loop(0, self.tiles, begin, 0)

    def tile(self, index):
        @pl.when(index == 0)
        def _():
            for which in range(len(self.whole)):
                self.whole_load(which).wait()

        for which in range(len(self.tiled)):
            self.tiled_load(which, index).wait()
        tiles = [ref[self.window(axis, index)] for ref, axis in zip(self.tiled_v, self.axes)]
        for which, value in enumerate(self.compute(self.whole_v, tiles)):
            self.outs_v[which][self.out_window(index)] = value
            self.store(which, index).start()

    def finish(self):
        def end(index, carry):
            for which in range(len(self.outs_v)):
                self.store(which, index).wait()
            return carry

        lax.fori_loop(0, self.tiles, end, 0)


def blocks_dot(blocks, weight):
    parts, _, depth = blocks.shape
    total = None
    for part in range(parts):
        term = jnp.dot(blocks[part], weight[part * depth : (part + 1) * depth], preferred_element_type=jnp.float32)
        total = term if total is None else total + term
    return total


class ExpandJob(Job):

    late = (0,)

    def __init__(self, normed, gate_full, up_full):
        rows, width = normed.shape[1], gate_full.shape[1]
        outs = [((rows, width), jnp.float32), ((rows, width), jnp.float32), ((rows, width), LOW)]
        super().__init__(
            [normed], [(gate_full, 1), (up_full, 1)], outs, width // self.wide, 4 * rows * gate_full.size
        )

    def compute(self, whole, tiles):
        gate_rows = blocks_dot(whole[0], tiles[0])
        up_rows = blocks_dot(whole[0], tiles[1])
        return gate_rows, up_rows, (gate_rows * jax.nn.sigmoid(gate_rows) * up_rows).astype(LOW)


class HiddenGradJob(Job):
    def __init__(self, cot, shrink_full, gate_rows, up_rows):
        rows, width = gate_rows.shape
        outs = [((rows, width), LOW), ((rows, width), LOW)]
        tiled = [(shrink_full, 1), (gate_rows, 1), (up_rows, 1)]
        super().__init__([cot], tiled, outs, width // self.wide, 2 * rows * shrink_full.size)

    def compute(self, whole, tiles):
        _, gate_rows, up_rows = tiles
        act_grad = blocks_dot(whole[0], tiles[0])
        sigmoid_gate = jax.nn.sigmoid(gate_rows)
        gate_grad = act_grad * up_rows * sigmoid_gate * (1.0 + gate_rows * (1.0 - sigmoid_gate))
        return gate_grad.astype(LOW), (act_grad * (gate_rows * sigmoid_gate)).astype(LOW)


class WidthJob(Job):
    then = None

    def __init__(self, lefts, weights):
        rows, width = lefts[0].shape[0], weights[0].shape[0]
        flops = 2 * rows * sum(weight.size for weight in weights)
        parts = lax.axis_size("tp")
        self.own = width // parts
        out = ((parts, rows, self.own), LOW)
        super().__init__(lefts, [(weight, 0) for weight in weights], [out], width // self.wide, flops)

    def out_window(self, index):
        each = self.own // self.wide
        return index // each, slice(None), pl.ds(pl.multiple_of(index % each * self.wide, 128), self.wide)

    def compute(self, whole, tiles):
        total = None
        for left, weight in zip(whole, tiles):
            term = contract_cols(left[...], weight)
            total = term if total is None else total + term
        return (total.astype(LOW),)

    def finish(self):
        super().finish()
        if self.then:
            self.then.start()


class MixerJob:
    kept = []
    late = ()

    def hold(self, refs):
        self.kept_refs = refs

    def __init__(self, inputs, outs, extra, phases, flops):
        self.inputs = list(inputs)
        self.out_shapes = [jax.ShapeDtypeStruct(shape, dtype) for shape, dtype in outs]
        self.phases = phases
        self.tiles = sum(phases)
        self.flops = flops
        self.scratch = (
            [pltpu.VMEM(array.shape, array.dtype) for array in self.inputs]
            + [pltpu.VMEM(shape, dtype) for shape, dtype in outs]
            + extra
            + [
                pltpu.SemaphoreType.DMA((len(self.inputs),)),
                pltpu.SemaphoreType.DMA((len(outs),)),
            ]
        )

    def bind(self, ins, outs, scratch):
        self.in_refs, self.out_refs = ins, outs
        extra = len(scratch) - len(ins) - len(outs) - 2
        self.ins_v, self.outs_v, self.extra_v = split(scratch, [len(ins), len(outs), extra])
        self.in_sem, self.out_sem = scratch[-2:]
        self.count = lax.axis_size("seq")
        self.seq = lax.axis_index("seq")
        self.column = lax.axis_index("tp")

    def peers(self):
        after = (self.seq + 1) % self.count
        before = (self.seq + self.count - 1) % self.count
        return [(after, self.column), (before, self.column)]

    def load(self, which):
        return pltpu.make_async_copy(self.in_refs[which], self.ins_v[which], self.in_sem.at[which])

    def store(self, which):
        return pltpu.make_async_copy(self.outs_v[which], self.out_refs[which], self.out_sem.at[which])

    def passing(self, source, target, forward):
        step = 1 if forward else self.count - 1
        return pltpu.make_async_remote_copy(
            src_ref=source,
            dst_ref=target,
            send_sem=self.kept_refs[1].at[0],
            recv_sem=self.kept_refs[1].at[1],
            device_id=((self.seq + step) % self.count, self.column),
            device_id_type=MESH,
        )

    def start(self, late):
        for which in range(len(self.inputs)):
            if late == (which in self.late):
                self.load(which).start()

    def tile(self, index):
        begin = 0
        for phase, tiles in enumerate(self.phases):
            here = index - begin

            @pl.when((here >= 0) & (here < tiles))
            def _(phase=phase, here=here, tiles=tiles):
                @pl.when(here == 0)
                def _():
                    self.before(phase)

                self.work(phase, here)

                @pl.when(here == tiles - 1)
                def _():
                    self.after(phase)

            begin += tiles

    def finish(self):
        for which in range(len(self.out_shapes)):
            self.store(which).wait()


def visible(bound_row, shape):
    position = lax.broadcasted_iota(jnp.int32, shape, 0)
    see_one = position != bound_row
    return position, see_one, see_one & (position - 1 != bound_row)


def lagged(rows, halo, position):
    last, second = halo[15:16].astype(jnp.float32), halo[14:15].astype(jnp.float32)
    one = jnp.where(position == 0, last, pltpu.roll(rows, 1, 0))
    two = jnp.where(position == 0, second, jnp.where(position == 1, last, pltpu.roll(rows, 2, 0)))
    return one, two


class EntryJob(MixerJob):
    then = None
    late = (0,)

    def __init__(self, tokens, wide, entry_full, exit_full, bound):
        parts, rows, own = tokens.shape
        width, columns = exit_full.shape
        self.rows, self.columns, self.own = rows, columns, own
        self.width = width
        outs = [
            ((rows, 3 * columns), jnp.float32),
            ((rows, columns), jnp.float32),
            ((rows, columns), LOW),
            ((16, columns), LOW),
            ((rows, columns), LOW),
            ((parts, rows, own), LOW),
            ((rows, 128), jnp.float32),
            ((width, rows), LOW),
        ]
        phases = [rows // 256, 3 * columns // 256, 1, columns // 128, width // 256]
        flops = 2 * rows * (entry_full.size + exit_full.size)
        super().__init__([tokens, wide, entry_full, exit_full, bound], outs, [], phases, flops)
        self.kept = [pltpu.VMEM((16, columns), LOW), pltpu.SemaphoreType.DMA((2,))]

    def halo(self):
        return self.passing(self.outs_v[2].at[pl.ds(self.rows - 16, 16)], self.kept_refs[0], True)

    def before(self, phase):
        if phase == 0:
            for which in (0, 1):
                self.load(which).wait()
        if phase == 1:
            self.store(6).start()
            self.store(7).start()
            self.load(2).wait()
        if phase == 3:
            self.load(4).wait()
            self.halo().wait_recv()
            self.outs_v[3][...] = self.kept_refs[0][...]
            self.store(3).start()
        if phase == 4:
            self.load(3).wait()

    def after(self, phase):
        if phase == 1:
            self.store(0).start()
        if phase == 2:
            self.halo().start()
            self.store(2).start()
        if phase == 3:
            self.store(1).start()
            self.store(4).start()
        if phase == 4:
            self.store(5).start()

    def finish(self):
        self.store(5).wait()
        if self.then:
            self.then.start()
        self.halo().wait_send()
        for which in (0, 1, 2, 3, 4, 6, 7):
            self.store(which).wait()

    def work(self, phase, index):
        tokens, wide, entry, exits, bound = self.ins_v
        taps = wide.at[self.column]
        projected, conv, gated, halo, mixer, term, scales, turned_rows = self.outs_v
        columns = self.columns
        if phase == 0:
            rows = pl.ds(pl.multiple_of(index * 256, 256), 256)
            values = [tokens[part, rows, :].astype(jnp.float32) for part in range(tokens.shape[0])]
            total = sum(jnp.sum(value * value, axis=1, keepdims=True) for value in values)
            scale = lax.rsqrt(total / D + EPSILON)
            scales[rows, :] = jnp.broadcast_to(scale, (256, 128))
            for part, value in enumerate(values):
                normed = (value * scale * wide[part, 3:4, :]).astype(LOW)
                tokens[part, rows, :] = normed
                turned_rows[part * self.own : (part + 1) * self.own, rows] = normed.T
        if phase == 1:
            span = pl.ds(pl.multiple_of(index * 256, 256), 256)
            projected[:, span] = blocks_dot(tokens, entry[:, span])
        if phase == 2:
            gated[...] = (projected[:, :columns] * projected[:, 2 * columns :]).astype(LOW)
        if phase == 3:
            span = pl.ds(pl.multiple_of(index * 128, 128), 128)
            middle = pl.ds(pl.multiple_of(columns + index * 128, 128), 128)
            rows = gated[:, span].astype(jnp.float32)
            position, see_one, see_two = visible(bound[0:1, :], rows.shape)
            before = halo[:, span].astype(jnp.float32) * jnp.where(self.seq > 0, 1.0, 0.0)
            one, two = lagged(rows, before, position)
            total = (
                taps[2:3, span] * rows
                + taps[1:2, span] * jnp.where(see_one, one, 0.0)
                + taps[0:1, span] * jnp.where(see_two, two, 0.0)
            )
            conv[:, span] = total
            mixer[:, span] = (projected[:, middle] * total).astype(LOW)
        if phase == 4:
            features = pl.ds(pl.multiple_of(index * 256, 256), 256)
            owner, inner = index // (self.own // 256), index % (self.own // 256)
            span = pl.ds(pl.multiple_of(inner * 256, 256), 256)
            term[owner, :, span] = contract_cols(mixer[...], exits[features, :]).astype(LOW)


class MixerGradJob(MixerJob):
    then = None
    late = (0,)

    def __init__(self, branch, exit_full, entry_full, projected, conv, gated, halo, wide, bound):
        parts, rows, own = branch.shape
        width, columns = exit_full.shape
        self.rows, self.columns, self.own = rows, columns, own
        outs = [((rows, 3 * columns), LOW), ((parts, rows, own), LOW), ((8, columns), jnp.float32)]
        extra = [
            pltpu.VMEM((rows, columns), jnp.float32),
            pltpu.VMEM((8, columns), jnp.float32),
        ]
        self.kept = [pltpu.VMEM((8, columns), jnp.float32), pltpu.SemaphoreType.DMA((2,))]
        phases = [columns // 256, 1, columns // 128, width // 256]
        flops = 2 * rows * (entry_full.size + exit_full.size)
        inputs = [branch, exit_full, entry_full, projected, conv, gated, halo, wide, bound]
        super().__init__(inputs, outs, extra, phases, flops)

    def back(self):
        return self.passing(self.extra_v[1], self.kept_refs[0], False)

    def before(self, phase):
        if phase == 0:
            for which in (0, 1, 3, 4):
                self.load(which).wait()
        if phase == 1:
            for which in (7, 8):
                self.load(which).wait()
        if phase == 2:
            for which in (5, 6):
                self.load(which).wait()
            self.back().wait_recv()
        if phase == 3:
            self.load(2).wait()

    def after(self, phase):
        if phase == 1:
            self.back().start()
        if phase == 2:
            self.store(0).start()
            self.store(2).start()
        if phase == 3:
            self.store(1).start()

    def finish(self):
        self.store(1).wait()
        if self.then:
            self.then.start()
        self.back().wait_send()
        for which in (0, 2):
            self.store(which).wait()

    def work(self, phase, index):
        branch, exits, entry, projected, conv, gated, halo, wide, bound = self.ins_v
        taps = wide.at[self.column]
        grads, term, taps_grad = self.outs_v
        conv_grad, sent = self.extra_v
        returned = self.kept_refs[0]
        columns, height = self.columns, self.rows
        if phase == 0:
            span = pl.ds(pl.multiple_of(index * 256, 256), 256)
            middle = pl.ds(pl.multiple_of(columns + index * 256, 256), 256)
            mixer_grad = blocks_dot(branch, exits[:, span])
            grads[:, middle] = (mixer_grad * conv[:, span]).astype(LOW)
            conv_grad[:, span] = mixer_grad * projected[:, middle]
        if phase == 1:
            for start in range(0, columns, 128):
                span = slice(start, start + 128)
                rows = conv_grad[0:8, span]
                position, see_one, see_two = visible(bound[0:1, :], rows.shape)
                one = pltpu.roll(jnp.where(see_one, rows, 0.0) * taps[1:2, span], 1, 0)
                two = jnp.where(see_two, rows, 0.0) * taps[0:1, span]
                sent[:, span] = two + jnp.where(position == 0, 0.0, one)
            taps_grad[...] = jnp.zeros_like(taps_grad)
        if phase == 2:
            span = pl.ds(pl.multiple_of(index * 128, 128), 128)
            last = pl.ds(pl.multiple_of(2 * columns + index * 128, 128), 128)
            rows = conv_grad[:, span]
            position, see_one, see_two = visible(bound[0:1, :], rows.shape)
            seen_one, seen_two = jnp.where(see_one, rows, 0.0), jnp.where(see_two, rows, 0.0)
            one = pltpu.roll(seen_one * taps[1:2, span], height - 1, 0)
            two = pltpu.roll(seen_two * taps[0:1, span], height - 2, 0)
            after = returned[:, span] * jnp.where(self.seq < self.count - 1, 1.0, 0.0)
            gated_grad = (
                rows * taps[2:3, span]
                + jnp.where(position == height - 1, after[1:2], one)
                + jnp.where(position < height - 2, two, jnp.where(position == height - 2, after[0:1], 0.0))
            )
            grads[:, span] = (gated_grad * projected[:, last]).astype(LOW)
            grads[:, last] = (gated_grad * projected[:, span]).astype(LOW)
            own_rows = gated[:, span].astype(jnp.float32)
            before = halo[:, span].astype(jnp.float32) * jnp.where(self.seq > 0, 1.0, 0.0)
            lag_one, lag_two = lagged(own_rows, before, position)
            taps_grad[0:1, span] = jnp.sum(seen_two * lag_two, axis=0, keepdims=True)
            taps_grad[1:2, span] = jnp.sum(seen_one * lag_one, axis=0, keepdims=True)
            taps_grad[2:3, span] = jnp.sum(rows * own_rows, axis=0, keepdims=True)
        if phase == 3:
            features = pl.ds(pl.multiple_of(index * 256, 256), 256)
            owner, inner = index // (self.own // 256), index % (self.own // 256)
            span = pl.ds(pl.multiple_of(inner * 256, 256), 256)
            term[owner, :, span] = contract_cols(grads[...], entry[features, :]).astype(LOW)


class Jobs:
    def __init__(self, *jobs):
        self.jobs = jobs
        self.inputs = [item for job in jobs for item in job.inputs]
        self.out_shapes = [item for job in jobs for item in job.out_shapes]
        self.scratch = [item for job in jobs for item in job.scratch]
        self.kept = [item for job in jobs for item in job.kept]
        self.tiles = sum(job.tiles for job in jobs)
        self.flops = sum(job.flops for job in jobs)

    def hold(self, refs):
        for job, own in zip(self.jobs, split(refs, [len(job.kept) for job in self.jobs])):
            job.hold(own)

    def bind(self, ins, outs, scratch):
        groups = zip(
            self.jobs,
            split(ins, [len(job.inputs) for job in self.jobs]),
            split(outs, [len(job.out_shapes) for job in self.jobs]),
            split(scratch, [len(job.scratch) for job in self.jobs]),
        )
        for job, own_ins, own_outs, own_scratch in groups:
            job.bind(own_ins, own_outs, own_scratch)

    def peers(self):
        return [peer for job in self.jobs for peer in job.peers()]

    def start(self, late):
        for job in self.jobs:
            job.start(late)

    def tile(self, index):
        begin = 0
        for job in self.jobs:
            here = index - begin

            @pl.when((here >= 0) & (here < job.tiles))
            def _(job=job, here=here):
                job.tile(here)

            begin += job.tiles

    def finish(self):
        for job in self.jobs:
            job.finish()


class TurnJob(MixerJob):
    late = (0,)

    def __init__(self, blocks):
        parts, rows, own = blocks.shape
        super().__init__([blocks], [((parts * own, rows), blocks.dtype)], [], [rows // 128], 0)

    def peers(self):
        return []

    def before(self, phase):
        self.load(0).wait()

    def after(self, phase):
        self.store(0).start()

    def work(self, phase, index):
        (blocks,), (target,) = self.ins_v, self.outs_v
        parts, _, own = blocks.shape
        rows = pl.ds(pl.multiple_of(index * 128, 128), 128)
        for part in range(parts):
            target[part * own : (part + 1) * own, rows] = blocks[part, rows, :].T


class CastJob(MixerJob):
    def __init__(self, pairs, plain):
        rows, columns = plain.shape
        lanes = pairs.shape[1]
        self.rows, self.half, self.lanes = rows, columns // 2, lanes
        self.block = max(rows // 8, 16)
        outs = [((rows, columns // 2), LOW)] * 6
        super().__init__([pairs, plain], outs, [], [rows // self.block], 0)

    def peers(self):
        return []

    def before(self, phase):
        for which in range(2):
            self.load(which).wait()

    def after(self, phase):
        for which in range(6):
            self.store(which).start()

    def work(self, phase, index):
        pairs, plain = self.ins_v
        block, half, lanes = self.block, self.half, self.lanes
        tiles = half // lanes
        rows = pl.ds(pl.multiple_of(index * block, 16), block)
        start = index * (block * 4 * tiles)
        for which in range(4):
            side, plane = which // 2, which % 2
            for tile in range(tiles):
                place = (side * tiles + tile) * 2 + plane
                picked = pairs[pl.ds(start + place, block, stride=4 * tiles), :]
                self.outs_v[which][rows, tile * lanes : (tile + 1) * lanes] = picked.astype(LOW)
        for side in range(2):
            self.outs_v[4 + side][rows, :] = plain[rows, side * half : (side + 1) * half].astype(LOW)


class SmallGatherJob:
    tiles, flops = 1, 0

    def __init__(self, own, seen):
        self.inputs = [own]
        self.seen = seen
        devices, columns = lax.axis_size("seq"), lax.axis_size("tp")
        wide = (columns, 8, devices * seen)
        self.out_shapes = [jax.ShapeDtypeStruct(wide, jnp.float32)]
        self.scratch = [pltpu.VMEM(wide, jnp.float32), pltpu.SemaphoreType.DMA((2,))]
        self.kept = [
            pltpu.VMEM((devices, columns) + own.shape, own.dtype),
            pltpu.SemaphoreType.DMA((columns,)),
            pltpu.SemaphoreType.DMA((columns,)),
            pltpu.SemaphoreType.DMA((devices,)),
            pltpu.SemaphoreType.DMA((devices,)),
        ]

    def hold(self, refs):
        self.whole, self.near_send, self.near_recv, self.far_send, self.far_recv = refs
        self.devices, self.columns = lax.axis_size("seq"), lax.axis_size("tp")
        self.seq, self.column = lax.axis_index("seq"), lax.axis_index("tp")

    def bind(self, ins, outs, scratch):
        self.source, self.target = ins[0], outs[0]
        self.wide, self.local_sem = scratch

    def peers(self):
        near = [(self.seq, (self.column + step) % self.columns) for step in range(1, self.columns)]
        far = [((self.seq + step) % self.devices, self.column) for step in range(1, self.devices)]
        return near + far

    def near(self, step):
        piece = self.whole.at[self.seq, self.column]
        return pltpu.make_async_remote_copy(
            src_ref=piece,
            dst_ref=piece,
            send_sem=self.near_send.at[step],
            recv_sem=self.near_recv.at[step],
            device_id=(self.seq, (self.column + step) % self.columns),
            device_id_type=MESH,
        )

    def far(self, step):
        piece = self.whole.at[self.seq]
        return pltpu.make_async_remote_copy(
            src_ref=piece,
            dst_ref=piece,
            send_sem=self.far_send.at[step],
            recv_sem=self.far_recv.at[step],
            device_id=((self.seq + step) % self.devices, self.column),
            device_id_type=MESH,
        )

    def start(self, late):
        if late:
            return
        load = pltpu.make_async_copy(self.source, self.whole.at[self.seq, self.column], self.local_sem.at[0])
        load.start()
        load.wait()
        for step in range(1, self.columns):
            self.near(step).start()

    def tile(self, index):
        for step in range(1, self.columns):
            self.near(step).wait()

        def begin(step, carry):
            self.far(step).start()
            return carry

        lax.fori_loop(1, self.devices, begin, 0)

    def finish(self):
        def end(step, carry):
            self.far(step).wait()
            return carry

        lax.fori_loop(1, self.devices, end, 0)
        each = LANES // self.seen
        for column in range(self.columns):
            for start in range(0, self.devices, each):
                total = None
                for inner in range(each):
                    piece = self.whole[start + inner, column, :, :].astype(jnp.float32)[:8]
                    piece = pltpu.roll(piece, inner * self.seen, 1) if inner else piece
                    total = piece if total is None else total + piece
                self.wide[column, :, start * self.seen : start * self.seen + LANES] = total
        store = pltpu.make_async_copy(self.wide, self.target, self.local_sem.at[1])
        store.start()
        store.wait()


class RowSumJob(MixerJob):
    block = 128

    def __init__(self, inputs, outs, extra, rows, flops):
        self.columns = lax.axis_size("tp")
        blocks = rows // self.block
        self.kept = [
            pltpu.VMEM((self.columns, blocks, self.block), jnp.float32),
            pltpu.SemaphoreType.DMA((self.columns,)),
            pltpu.SemaphoreType.DMA((self.columns,)),
        ]
        totals = pltpu.VMEM((blocks, self.block), jnp.float32)
        super().__init__(inputs, outs, [totals] + extra, [blocks, 1, blocks], flops)

    def peers(self):
        return [(self.seq, (self.column + step) % self.columns) for step in range(1, self.columns)]

    def share(self, step):
        return pltpu.make_async_remote_copy(
            src_ref=self.kept_refs[0].at[0],
            dst_ref=self.kept_refs[0].at[step],
            send_sem=self.kept_refs[1].at[step],
            recv_sem=self.kept_refs[2].at[step],
            device_id=(self.seq, (self.column + step) % self.columns),
            device_id_type=MESH,
        )

    def before(self, phase):
        if phase == 0:
            for which in range(len(self.inputs)):
                self.load(which).wait()

    def after(self, phase):
        if phase == 0:
            for step in range(1, self.columns):
                self.share(step).start()
        if phase == 2:
            for which in range(len(self.out_shapes)):
                self.store(which).start()

    def finish(self):
        for step in range(1, self.columns):
            self.share(step).wait_send()
        super().finish()

    def work(self, phase, index):
        block = self.block
        slots, totals = self.kept_refs[0], self.extra_v[0]
        rows = pl.ds(pl.multiple_of(index * block, block), block)
        if phase == 0:
            part = jnp.sum(self.values(rows), axis=1, keepdims=True)
            slots[0, pl.ds(index, 1), :] = jnp.broadcast_to(part, (block, block)).T[0:1, :]
        if phase == 1:
            for step in range(1, self.columns):
                self.share(step).wait_recv()
            totals[...] = sum(slots[step] for step in range(self.columns))
        if phase == 2:
            self.use(rows, jnp.broadcast_to(totals[pl.ds(index, 1), :], (block, block)).T)


class NormJob(RowSumJob):
    then = None
    late = (1,)

    def __init__(self, rows_in, terms, wide):
        rows, own = rows_in.shape
        outs = [((rows, own), jnp.float32), ((rows, own), LOW), ((rows, 128), jnp.float32)]
        super().__init__([rows_in, terms, wide], outs, [], rows, 0)

    def values(self, rows):
        rows_in, terms, _ = self.ins_v
        residual = sum(terms[part, rows, :].astype(jnp.float32) for part in range(self.columns))
        residual = rows_in[rows, :].astype(jnp.float32) + residual
        self.outs_v[0][rows, :] = residual
        return residual * residual

    def use(self, rows, total):
        residual, normed, scales = self.outs_v
        scale = lax.rsqrt(total / D + EPSILON)
        scales[rows, :] = scale
        gain = self.ins_v[2].at[self.column]
        normed[rows, :] = (residual[rows, :] * scale[:, 0:1] * gain[4:5, :]).astype(LOW)

    def finish(self):
        self.store(1).wait()
        if self.then:
            self.then.start()
        for step in range(1, self.columns):
            self.share(step).wait_send()
        for which in (0, 2):
            self.store(which).wait()


class NormBackJob(RowSumJob):
    then = None
    late = (0,)

    def __init__(self, terms, kept, scales, wide, row, base, rounded):
        _, rows, own = terms.shape
        outs = [((rows, own), jnp.float32), ((8, own), jnp.float32)]
        outs = outs + [((rows, own), LOW)] if rounded else outs
        self.row = row
        super().__init__([terms, kept, scales, wide, base], outs, [], rows, 0)

    def parts(self, rows):
        terms, kept, scales, wide, base = self.ins_v
        gain = wide.at[self.column]
        return (
            sum(terms[part, rows, :].astype(jnp.float32) for part in range(self.columns)),
            kept[rows, :].astype(jnp.float32),
            scales[rows, 0:1],
            gain[self.row : self.row + 1, :],
        )

    def before(self, phase):
        super().before(phase)
        if phase == 0:
            self.outs_v[1][...] = jnp.zeros_like(self.outs_v[1])

    def values(self, rows):
        grad, kept, scale, gain = self.parts(rows)
        product = grad * kept
        self.outs_v[1][0:1, :] += jnp.sum(product * scale, axis=0, keepdims=True)
        return product * gain

    def use(self, rows, total):
        grad, kept, scale, gain = self.parts(rows)
        rows_grad = scale * gain * grad - kept * (scale * scale * scale * total[:, 0:1] / D)
        result = self.ins_v[4][rows, :].astype(jnp.float32) + rows_grad
        self.outs_v[0][rows, :] = result
        if len(self.outs_v) > 2:
            self.outs_v[2][rows, :] = result.astype(LOW)

    def finish(self):
        if self.then:
            self.store(2).wait()
            self.then.start()
        for step in range(1, self.columns):
            self.share(step).wait_send()
        for which in range(len(self.out_shapes)):
            if which != 2 or not self.then:
                self.store(which).wait()


class SumJob(MixerJob):
    late = (1,)

    def __init__(self, base, terms):
        rows, own = base.shape
        super().__init__([base, terms], [((rows, own), LOW)], [], [rows // 128], 0)

    def before(self, phase):
        for which in range(2):
            self.load(which).wait()

    def after(self, phase):
        self.store(0).start()

    def work(self, phase, index):
        base, terms = self.ins_v
        rows = pl.ds(pl.multiple_of(index * 128, 128), 128)
        total = sum(terms[part, rows, :].astype(jnp.float32) for part in range(terms.shape[0]))
        self.outs_v[0][rows, :] = (base[rows, :] + total).astype(LOW)


class AdamJob(MixerJob):
    deep = 1

    def __init__(self, weight, grads, extra=()):
        rows = grads[0].shape[0]
        self.block = max(rows // 8, 8)
        tiles = rows // self.block
        outs = [(weight.shape, jnp.float32)] * 3
        super().__init__([weight] * 3 + list(grads), outs, list(extra), [tiles], 0)
        self.scratch[-1] = pltpu.SemaphoreType.DMA((3, tiles))

    def peers(self):
        return []

    def before(self, phase):
        for which in range(len(self.inputs)):
            self.load(which).wait()

    def after(self, phase):
        pass

    def piece(self, which, index):
        size = self.block * self.deep
        rows = pl.ds(pl.multiple_of(index * size, 8), size)
        return pltpu.make_async_copy(
            self.outs_v[which].at[rows], self.out_refs[which].at[rows], self.out_sem.at[which, index]
        )

    def work(self, phase, index):
        rows = pl.ds(pl.multiple_of(index * self.block, 8), self.block)
        start = 0
        for grad in self.ins_v[3:]:
            span = slice(start, start + grad.shape[1])
            start += grad.shape[1]
            state = [ref[rows, span] for ref in self.ins_v[:3]]
            for out, result in zip(self.outs_v, adam_update(*state, grad[rows, :], RATE_WIDE, WEIGHT_DECAY)):
                out[rows, span] = result
        for which in range(3):
            self.piece(which, index).start()

    def finish(self):
        def end(index, carry):
            for which in range(3):
                self.piece(which, index).wait()
            return carry

        lax.fori_loop(0, self.tiles, end, 0)


class AdamPairsJob(AdamJob):
    def __init__(self, weight, grads):
        rows = grads[0].shape[0]
        self.deep = weight.shape[0] // rows
        size = max(rows // 8, 8) * self.deep
        super().__init__(weight, grads, [pltpu.VMEM((size, LANES), jnp.float32)])

    def work(self, phase, index):
        size = self.block * self.deep
        rows = pl.ds(pl.multiple_of(index * self.block, 8), self.block)
        seen = pl.ds(pl.multiple_of(index * size, 8), size)
        mixed = self.extra_v[0]
        for which, grad in enumerate(self.ins_v[3:]):
            half, side = which // 2, which % 2
            tiles = grad.shape[1] // LANES
            for tile in range(tiles):
                place = (half * tiles + tile) * 2 + side
                picked = grad[rows, tile * LANES : (tile + 1) * LANES]
                mixed[pl.ds(place, self.block, stride=self.deep), :] = picked
        state = [ref[seen, :] for ref in self.ins_v[:3]]
        for out, result in zip(self.outs_v, adam_update(*state, mixed[...], RATE_WIDE, WEIGHT_DECAY)):
            out[seen, :] = result
        for which in range(3):
            self.piece(which, index).start()


class SmallSumJob:
    tiles, flops = 1, 0

    def __init__(self, taps_grad, gain_grad, before):
        count = lax.axis_size("seq")
        self.inputs = [taps_grad, gain_grad]
        shape = taps_grad.shape
        self.before = before
        self.out_shapes = [jax.ShapeDtypeStruct(shape, jnp.float32)]
        self.scratch = [pltpu.VMEM(shape, jnp.float32)] * 3 + [pltpu.SemaphoreType.DMA((3,))]
        self.kept = [
            pltpu.VMEM((count,) + shape, jnp.float32),
            pltpu.SemaphoreType.DMA((count,)),
            pltpu.SemaphoreType.DMA((count,)),
        ]

    def hold(self, refs):
        self.slots, self.send_sem, self.recv_sem = refs

    def bind(self, ins, outs, scratch):
        self.sources, self.target = ins, outs[0]
        self.taps, self.gain, self.total, self.local_sem = scratch
        self.count = lax.axis_size("seq")
        self.seq = lax.axis_index("seq")
        self.column = lax.axis_index("tp")

    def peers(self):
        return [((self.seq + far) % self.count, self.column) for far in range(1, self.count)]

    def copy(self, far):
        return pltpu.make_async_remote_copy(
            src_ref=self.slots.at[0],
            dst_ref=self.slots.at[far],
            send_sem=self.send_sem.at[far],
            recv_sem=self.recv_sem.at[far],
            device_id=((self.seq + far) % self.count, self.column),
            device_id_type=MESH,
        )

    def loads(self):
        return [
            pltpu.make_async_copy(self.sources[which], (self.taps, self.gain)[which], self.local_sem.at[which])
            for which in range(2)
        ]

    def start(self, late):
        if late:
            return
        for load in self.loads():
            load.start()

    def tile(self, index):
        for load in self.loads():
            load.wait()
        self.slots[0, 0:3, :] = self.taps[0:3, :]
        self.slots[0, 3:4, :] = self.before.outs_v[1][0:1, :]
        self.slots[0, 4:5, :] = self.gain[0:1, :]
        self.slots[0, 5:8, :] = jnp.zeros_like(self.slots[0, 5:8, :])

        def begin(far, carry):
            self.copy(far).start()
            return carry

        lax.fori_loop(1, self.count, begin, 0)

    def finish(self):
        self.total[...] = self.slots[0]

        def add(far, carry):
            self.copy(far).wait_recv()
            self.total[...] += self.slots[far]
            return carry

        lax.fori_loop(1, self.count, add, 0)
        store = pltpu.make_async_copy(self.total, self.target, self.local_sem.at[2])
        store.start()

        def sent(far, carry):
            self.copy(far).wait_send()
            return carry

        lax.fori_loop(1, self.count, sent, 0)
        store.wait()


class Section:
    def __init__(self, ranges, jobs=(), waits=(), rest=1, calls=(), early=True, then=()):
        self.ranges, self.jobs, self.waits, self.rest, self.calls, self.early = ranges, jobs, waits, rest, calls, early
        self.then = then
        self.job = Jobs(*[job for job, _, _ in jobs])

    def run(self, ring, ins, outs):
        job = self.job
        ranges = [(group, low * ring.ticks // 12, high * ring.ticks // 12) for group, low, high in self.ranges]
        total = sum(high - low for _, low, high in ranges)
        rest = self.rest * ring.ticks // 12
        active = total - rest
        each = -(-job.tiles // active)

        def ready():
            for exchange in self.waits:
                exchange.wait()
            for exchange in self.then:
                exchange.start()
            job.start(True)

        def body(*scratch):
            job.bind(ins, outs, list(scratch))
            job.start(False)
            if not self.waits:
                job.start(True)
            done = 0
            for place, (group, low, high) in enumerate(ranges):
                if low == 0 and group > 0 and place > 0:
                    ring.turn(group)
                if place == 0:
                    for call in self.calls:
                        call.start()

                def step(index, carry, group=group, shift=done - low):
                    late = index + shift - rest
                    first, after = late * job.tiles // active, (late + 1) * job.tiles // active
                    if self.waits:
                        pl.when(late == -1)(ready)
                    for inner in range(each):
                        tile = first + inner

                        @pl.when((late >= 0) & (tile < after))
                        def _(tile=tile):
                            job.tile(tile)

                    ring.tick(group, index)
                    return carry

                lax.fori_loop(low, high, step, 0)
                done += high - low
            group, _, high = ranges[-1]
            ends = high == ring.ticks and group + 1 < len(ring.groups)
            if ends and self.early:
                ring.begin(group + 1)
            job.finish()
            if ends and not self.early:
                ring.begin(group + 1)

        pl.run_scoped(body, *job.scratch)
        group, _, high = ranges[-1]
        if high == ring.ticks:
            ring.settle(group)
            ring.settled(group)


class Plan:
    def __init__(self, arrays):
        self.arrays = arrays
        self.shapes = {name: jax.ShapeDtypeStruct(array.shape, array.dtype) for name, array in arrays.items()}
        self.inputs = list(self.shapes)
        self.weights = set()

    def define(self, name, shape, dtype):
        self.shapes[name] = jax.ShapeDtypeStruct(shape, dtype)

    def add(self, job, ins, outs):
        for name, shape in zip(outs, job.out_shapes):
            self.shapes[name] = shape
        return job, ins, outs

    def flat(self, full):
        shape = self.shapes[full].shape
        return jax.ShapeDtypeStruct((shape[0] * shape[1], shape[2]), LOW)

    def run(self, ring, sections, exchanges, peers, name, collective):
        inputs = self.inputs
        outputs = [made for made in self.shapes if made not in inputs]
        kept = [item for section in sections for item in section.job.kept]
        sems = [item for exchange in exchanges for item in exchange.scratch]

        def kernel(*all_refs):
            in_refs, out_refs, ring_scratch, sem_refs, kept_refs = split(
                all_refs, [len(inputs), len(outputs), len(ring.scratch), len(sems), len(kept)]
            )
            refs = dict(zip(inputs + outputs, in_refs + out_refs))
            ring.bind(refs, ring_scratch)
            for place, exchange in enumerate(exchanges):
                exchange.bind(refs, sem_refs[2 * place : 2 * place + 2])
            for section, own in zip(sections, split(kept_refs, [len(section.job.kept) for section in sections])):
                section.job.hold(own)
            ring.prepare()
            greet(peers())
            ring.begin(0)
            ring.settled(-1)
            for section in sections:
                ins = [rows_of(refs[made], made in self.weights) for _, names, _ in section.jobs for made in names]
                outs = [refs[made] for _, _, names in section.jobs for made in names]
                section.run(ring, ins, outs)
            ring.finish()
            for exchange in exchanges:
                exchange.finish()

        flops = ring.flops + sum(section.job.flops for section in sections)
        results = pl.pallas_call(
            kernel,
            out_shape=[self.shapes[made] for made in outputs],
            in_specs=[pl.BlockSpec(memory_space=pl.ANY)] * len(inputs),
            out_specs=[pl.BlockSpec(memory_space=pl.ANY)] * len(outputs),
            scratch_shapes=ring.scratch + sems + kept,
            compiler_params=pltpu.CompilerParams(
                collective_id=collective, has_side_effects=True, vmem_limit_bytes=VMEM_BYTES
            ),
            cost_estimate=pl.CostEstimate(flops=flops, bytes_accessed=10**9, transcendentals=0),
            name=name,
        )(*self.arrays.values())
        named = dict(zip(outputs, results))
        return {made: flat(array) if made in self.weights else array for made, array in named.items()}


def row_and_column_peers():
    seq, column = lax.axis_index("seq"), lax.axis_index("tp")
    devices, columns = lax.axis_size("seq"), lax.axis_size("tp")
    near = [(seq, (column + step) % columns) for step in range(1, columns)]
    return near + [((seq + step) % devices, column) for step in range(1, devices)]


def run_forward(arrays, seen):
    count, columns = lax.axis_size("seq"), lax.axis_size("tp")
    plan = Plan(arrays)
    shapes, add = plan.shapes, plan.add
    rows, own = arrays["tokens"].shape
    for name in ("tokens_blocks", "cot_blocks", "branch_terms", "normed_blocks"):
        plan.define(name, (columns, rows, own), LOW)
    low = ["gate_low0", "up_low0", "gate_low1", "up_low1", "shrink_low0", "shrink_low1"]
    small = add(SmallGatherJob(shapes["small"], seen), ["small"], ["wide"])
    cast = add(CastJob(shapes["pairs"], shapes["shrink"]), ["pairs", "shrink"], low)
    groups = [[("entry_low", "entry_full"), ("exit_low", "exit_full")]]
    groups += [[(name, name.replace("low", "full"))] for name in low]
    for group in groups:
        for shard, full in group:
            plan.define(full, (count,) + shapes[shard].shape, LOW)
            plan.weights.add(full)
    ring = GatherRing(groups, shapes)
    tokens_sent = PeerCopies("tokens", "tokens_blocks")
    cot_sent = PeerCopies("cotangent", "cot_blocks")
    branch_sent = PeerCopies("term", "branch_terms")
    normed_sent = PeerCopies("normed_own", "normed_blocks")

    entry_job = EntryJob(
        shapes["tokens_blocks"], shapes["wide"], plan.flat("entry_full"), plan.flat("exit_full"), shapes["bound"]
    )
    entry_job.then = branch_sent
    entry = add(
        entry_job,
        ["tokens_blocks", "wide", "entry_full", "exit_full", "bound"],
        ["projected", "conv_out", "gated", "halo", "mixer", "term", "scale_one", "normed_one"],
    )
    turn_cot = add(TurnJob(shapes["cot_blocks"]), ["cot_blocks"], ["cot_full"])
    norm_job = NormJob(shapes["tokens"], shapes["branch_terms"], shapes["wide"])
    norm_job.then = normed_sent
    norm = add(norm_job, ["tokens", "branch_terms", "wide"], ["residual", "normed_own", "scale_two"])
    expands = []
    for half in "01":
        job = ExpandJob(shapes["normed_blocks"], plan.flat("gate_full" + half), plan.flat("up_full" + half))
        names = ["normed_blocks", "gate_full" + half, "up_full" + half]
        expands.append(add(job, names, ["gate_rows" + half, "up_rows" + half, "activation" + half]))
    hidden_job = HiddenGradJob(shapes["cot_blocks"], plan.flat("shrink_full0"), shapes["gate_rows0"], shapes["up_rows0"])
    hidden = add(hidden_job, ["cot_blocks", "shrink_full0", "gate_rows0", "up_rows0"], ["gate_grad0", "up_grad0"])
    turn_normed = add(TurnJob(shapes["normed_blocks"]), ["normed_blocks"], ["normed_two"])
    sections = [
        Section([(0, 0, 12)], [small, cast], calls=[tokens_sent], early=False),
        Section([(1, 0, 12)], [entry], [tokens_sent], calls=[cot_sent]),
        Section([(2, 0, 12)], [turn_cot], [cot_sent], rest=3),
        Section([(3, 0, 12)], [norm], [branch_sent], rest=4),
        Section([(4, 0, 12)]),
        Section([(5, 0, 12)], expands, [normed_sent], rest=4),
        Section([(6, 0, 12)], [hidden, turn_normed]),
    ]
    exchanges = [tokens_sent, cot_sent, branch_sent, normed_sent]
    return plan.run(ring, sections, exchanges, row_and_column_peers, "forward", 0)


def run_backward(arrays):
    columns = lax.axis_size("tp")
    plan = Plan(arrays)
    shapes, add = plan.shapes, plan.add
    rows, own = arrays["tokens"].shape
    for name in ("two_terms", "mixed_terms", "branch_blocks", "one_terms"):
        plan.define(name, (columns, rows, own), LOW)
    two_sent = PeerCopies("two_term", "two_terms")
    mixed_sent = PeerCopies("mixed_term", "mixed_terms")
    branch_sent = PeerCopies("branch_own", "branch_blocks")
    one_sent = PeerCopies("one_term", "one_terms")

    hidden = add(
        HiddenGradJob(shapes["cot_blocks"], shapes["shrink_full1"], shapes["gate_rows1"], shapes["up_rows1"]),
        ["cot_blocks", "shrink_full1", "gate_rows1", "up_rows1"],
        ["gate_grad1", "up_grad1"],
    )
    names = [["gate_grad0", "up_grad0", "gate_grad1", "up_grad1"], ["gate_full0", "up_full0", "gate_full1", "up_full1"]]
    two_job = WidthJob(*[[shapes[name] for name in side] for side in names])
    two_job.then = two_sent
    two = add(two_job, names[0] + names[1], ["two_term"])
    names = [["activation0", "activation1"], ["shrink_full0", "shrink_full1"]]
    mixed = add(WidthJob(*[[shapes[name] for name in side] for side in names]), names[0] + names[1], ["mixed_term"])
    back_two = NormBackJob(
        shapes["two_terms"], shapes["residual"], shapes["scale_two"], shapes["wide"], 4, shapes["cotangent"], True
    )
    back_two.then = branch_sent
    names = ["two_terms", "residual", "scale_two", "wide", "cotangent"]
    norm_two = add(back_two, names, ["residual_grad", "gain_two_grad", "branch_own"])
    names = ["branch_blocks", "exit_full", "entry_full", "projected", "conv_out", "gated", "halo", "wide", "bound"]
    mixer_job = MixerGradJob(*[shapes[name] for name in names])
    mixer_job.then = one_sent
    mixer = add(mixer_job, names, ["projected_grad", "one_term", "taps_grad"])
    turn = add(TurnJob(shapes["branch_blocks"]), ["branch_blocks"], ["branch_full"])
    back_one = NormBackJob(
        shapes["one_terms"], shapes["tokens"], shapes["scale_one"], shapes["wide"], 3, shapes["residual_grad"], False
    )
    names = ["one_terms", "tokens", "scale_one", "wide", "residual_grad"]
    norm_one = add(back_one, names, ["tokens_grad", "gain_one_grad"])
    small_job = SmallSumJob(shapes["taps_grad"], shapes["gain_two_grad"], back_one)
    small = add(small_job, ["taps_grad", "gain_two_grad"], ["small_part"])
    total = add(SumJob(shapes["residual"], shapes["mixed_terms"]), ["residual", "mixed_terms"], ["mixed"])

    wide = own
    halves = [("cot_full", "activation0"), ("cot_full", "activation1")]
    halves += [("normed_two", name) for name in ("gate_grad0", "up_grad0", "gate_grad1", "up_grad1")]
    halves += [("normed_one", "projected_grad")]
    groups = [[(left, right, 0), (left, right, wide)] for left, right in halves]
    groups += [[("normed_one", "projected_grad", 2 * wide), ("branch_full", "mixer", 0)]]
    places = {"cot_full": 0, "normed_two": 1, "normed_one": 0, "branch_full": 2}
    ring = ScatterRing(groups, places, shapes, wide)
    sums = ["shrink0", "shrink1", "gate0", "up0", "gate1", "up1", "entry", "entry_exit"]
    for name, shape in zip(sums, ring.out_shapes):
        plan.shapes[name] = shape
    ring.outs = sums
    names = [["shrink_weight", "shrink_first", "shrink_second"], ["shrink0", "shrink1"]]
    shrink_job = AdamJob(shapes["shrink_weight"], [shapes[name] for name in names[1]])
    adam_shrink = add(shrink_job, names[0] + names[1], ["shrink_next", "shrink_first_next", "shrink_second_next"])
    names = [["expand_weight", "expand_first", "expand_second"], ["gate0", "up0", "gate1", "up1"]]
    expand_job = AdamPairsJob(shapes["expand_weight"], [shapes[name] for name in names[1]])
    adam_expand = add(expand_job, names[0] + names[1], ["expand_next", "expand_first_next", "expand_second_next"])
    sections = [
        Section([(0, 0, 5)], [hidden]),
        Section([(0, 5, 12), (1, 0, 4)], [two], rest=2),
        Section([(1, 4, 12), (2, 0, 5)], [mixed]),
        Section([(2, 5, 12)], [norm_two], [two_sent], rest=3),
        Section([(3, 0, 12)], [adam_shrink], rest=2),
        Section([(4, 0, 12)], [mixer], [branch_sent], rest=3, then=[mixed_sent]),
        Section([(5, 0, 12)], [turn]),
        Section([(6, 0, 12)], [norm_one, small, total], [one_sent, mixed_sent], rest=5),
        Section([(7, 0, 12)], [adam_expand], rest=2),
    ]
    exchanges = [two_sent, mixed_sent, branch_sent, one_sent]
    return plan.run(ring, sections, exchanges, row_and_column_peers, "backward", 1)


def rows_of(ref, gathered):
    if not gathered:
        return ref
    count, rows, columns = ref.shape
    return ref.reshape(count * rows, columns)


def flat(full):
    return full.reshape(full.shape[0] * full.shape[1], full.shape[2])


def contract_cols(left, right):
    return lax.dot_general(
        left, right, (((1,), (1,)), ((), ())), preferred_element_type=jnp.float32
    )


def adam_update(weight, first, second, grad, rate, decay):
    first_next = BETA_ONE * first + (1.0 - BETA_ONE) * grad
    second_next = BETA_TWO * second + (1.0 - BETA_TWO) * grad * grad
    corrected = first_next / (1.0 - BETA_ONE**STEP)
    spread = jnp.sqrt(second_next / (1.0 - BETA_TWO**STEP)) + ADAM_EPSILON
    return (weight - rate * (corrected / spread + decay * weight), first_next, second_next)


def adam_mixer_kernel(*refs):
    entries, exits, grads, outs = refs[:3], refs[3:6], refs[6:8], refs[8:]
    planes, _, columns = entries[0].shape
    for plane in range(planes + 1):
        grad = grads[plane // 2][:, plane % 2 * columns : (plane % 2 + 1) * columns]
        state = [ref[plane] for ref in entries] if plane < planes else [ref[...] for ref in exits]
        results = adam_update(*state, grad, RATE_WIDE, WEIGHT_DECAY)
        for place, result in enumerate(results):
            if plane < planes:
                outs[place][plane] = result
            else:
                outs[3 + place][...] = result


def adam_mixer(entries, exits, grad, last):
    rows, planes, columns = entries[0].shape
    block = max(rows // 4, 8)
    entry_spec = pl.BlockSpec((planes, block, columns), lambda step: (0, step, 0))
    exit_spec = pl.BlockSpec((block, columns), lambda step: (step, 0))
    grad_spec = pl.BlockSpec((block, 2 * columns), lambda step: (step, 0))
    size = entries[0].size + exits[0].size
    results = pl.pallas_call(
        adam_mixer_kernel,
        out_shape=[jax.ShapeDtypeStruct((planes, rows, columns), jnp.float32)] * 3
        + [jax.ShapeDtypeStruct((rows, columns), jnp.float32)] * 3,
        grid=(rows // block,),
        in_specs=[entry_spec] * 3 + [exit_spec] * 3 + [grad_spec] * 2,
        out_specs=[entry_spec] * 3 + [exit_spec] * 3,
        compiler_params=pltpu.CompilerParams(vmem_limit_bytes=VMEM_BYTES),
        cost_estimate=pl.CostEstimate(flops=20 * size, bytes_accessed=28 * size, transcendentals=0),
        name="adam_mixer",
    )(*[array.transpose(1, 0, 2) for array in entries], *exits, grad, last)
    return [result.transpose(1, 0, 2) for result in results[:3]] + list(results[3:])


def paired(array):
    rows, _, columns = array.shape
    return array.reshape(rows, 2, columns // LANES, LANES).transpose(0, 2, 1, 3).reshape(-1, LANES)


def unpaired(array, shape):
    rows, _, columns = shape
    return array.reshape(rows, columns // LANES, 2, LANES).transpose(0, 2, 1, 3).reshape(shape)


def shards(
    tokens,
    bounds,
    cotangent,
    entry_weight,
    entry_first,
    entry_second,
    exit_weight,
    exit_first,
    exit_second,
    expand_weight,
    expand_first,
    expand_second,
    shrink_weight,
    shrink_first,
    shrink_second,
    conv_kernel,
    conv_first,
    conv_second,
    norm_gains,
    gain_first,
    gain_second,
):
    channels = tokens.shape[1]
    seen = conv_kernel.shape[1]
    small = jnp.concatenate([conv_kernel, norm_gains], axis=0)
    small = jnp.pad(small, ((0, 16 - small.shape[0]), (0, LANES - seen))).astype(LOW)
    entry_low = entry_weight.reshape(entry_weight.shape[0], 3 * channels).astype(LOW)
    bound = jnp.broadcast_to(bounds[0], (8, 128))
    made = run_forward(
        {
            "entry_low": entry_low,
            "exit_low": exit_weight.astype(LOW),
            "small": small,
            "tokens": tokens,
            "cotangent": cotangent,
            "bound": bound,
            "pairs": paired(expand_weight),
            "shrink": shrink_weight,
        },
        seen,
    )
    names = ["wide", "exit_full", "entry_full", "projected", "conv_out", "gated", "halo", "mixer", "residual"]
    names += ["scale_one", "scale_two", "cot_blocks", "cot_full", "normed_one", "normed_two", "gate_grad0", "up_grad0"]
    names += ["gate_rows1", "up_rows1", "activation0", "activation1"]
    names += [name + half for name in ("gate_full", "up_full", "shrink_full") for half in "01"]
    given = {"tokens": tokens, "cotangent": cotangent, "bound": bound}
    given |= {"shrink_weight": shrink_weight, "shrink_first": shrink_first, "shrink_second": shrink_second}
    given["expand_weight"] = paired(expand_weight)
    given["expand_first"], given["expand_second"] = paired(expand_first), paired(expand_second)
    grads = run_backward(given | {name: made[name] for name in names})
    mixed, tokens_grad = grads["mixed"], grads["tokens_grad"]
    small_part = lax.dynamic_slice_in_dim(grads["small_part"], lax.axis_index("seq") * seen, seen, axis=1)
    kernel_part = small_part[:3]
    gains_part = small_part[3:5]
    (
        entry_next,
        entry_first_next,
        entry_second_next,
        exit_next,
        exit_first_next,
        exit_second_next,
    ) = adam_mixer(
        (entry_weight, entry_first, entry_second),
        (exit_weight, exit_first, exit_second),
        grads["entry"],
        grads["entry_exit"],
    )
    shrink_next, shrink_first_next, shrink_second_next = (
        grads["shrink" + name] for name in ("_next", "_first_next", "_second_next")
    )
    expand_next, expand_first_next, expand_second_next = (
        unpaired(grads["expand" + name], expand_weight.shape) for name in ("_next", "_first_next", "_second_next")
    )
    conv_next, conv_first_next, conv_second_next = adam_update(
        conv_kernel, conv_first, conv_second, kernel_part, RATE_CONV, 0.0
    )
    gains_next, gains_first_next, gains_second_next = adam_update(
        norm_gains, gain_first, gain_second, gains_part, RATE_GAIN, 0.0
    )
    return (
        mixed,
        tokens_grad,
        entry_next,
        entry_first_next,
        entry_second_next,
        exit_next,
        exit_first_next,
        exit_second_next,
        expand_next,
        expand_first_next,
        expand_second_next,
        shrink_next,
        shrink_first_next,
        shrink_second_next,
        conv_next,
        conv_first_next,
        conv_second_next,
        gains_next,
        gains_first_next,
        gains_second_next,
    )


def solution(mesh):
    rows = P("seq", "tp")
    stacked = P("seq", None, "tp")
    small = P(None, ("tp", "seq"))
    return jax.shard_map(
        shards,
        mesh=mesh,
        in_specs=(rows, P("seq"), rows) + (stacked,) * 3 + (rows,) * 3 + (stacked,) * 3 + (rows,) * 3 + (small,) * 6,
        out_specs=(rows, rows) + (stacked,) * 3 + (rows,) * 3 + (stacked,) * 3 + (rows,) * 3 + (small,) * 6,
        check_vma=False,
    )
```

```python
import functools

import jax
import jax.numpy as jnp
from jax import lax
from jax.experimental import pallas as pl
from jax.experimental.pallas import tpu as pltpu
from jax.sharding import PartitionSpec as P

D = 2048
STEP = 10


EPSILON = 1e-05
BETA_ONE = 0.9
BETA_TWO = 0.95
ADAM_EPSILON = 1e-08
WEIGHT_DECAY = 0.1
RATE_WIDE = 0.04
RATE_CONV = 0.5
RATE_GAIN = 0.4

MESH = pl.DeviceIdType.MESH
LOW = jnp.bfloat16
LANES = 128
VMEM_BYTES = 60 * 1024 * 1024


def ring_place(index, count):
    side = index % 2
    level = index // 2
    return level * (1 - side) + (count - 1 - level) * side


def ring_index(place, count):
    back = place // (count // 2)
    return (1 - back) * (2 * place) + back * (2 * (count - 1 - place) + 1)


def ring_ends(count):
    place = ring_place(lax.axis_index("seq"), count)
    ahead = ring_index((place + 1) % count, count)
    behind = ring_index((place + count - 1) % count, count)
    return place, ahead, behind


def greet(peers):
    barrier = pltpu.get_barrier_semaphore()
    for peer in peers:
        pl.semaphore_signal(barrier, inc=1, device_id=peer, device_id_type=MESH)
    pl.semaphore_wait(barrier, len(peers))


def split(items, sizes):
    parts, start = [], 0
    for size in sizes:
        parts.append(items[start : start + size])
        start += size
    return parts


class GatherRing:
    def __init__(self, groups, shapes):
        self.count = lax.axis_size("seq")
        self.groups = groups
        self.rows = {full: shapes[shard].shape[0] for group in groups for shard, full in group}
        self.order = {full: place for place, full in enumerate(self.rows)}
        self.parts = 2 if min(self.rows.values()) % 64 == 0 else 1
        self.ticks = (self.count - 2) * self.parts
        arrays = len(self.rows)
        sems = pltpu.SemaphoreType.DMA((arrays, 2, self.parts, self.count - 1))
        self.scratch = [sems, sems, pltpu.SemaphoreType.DMA((arrays,))]
        self.flops = 0

    def bind(self, refs, scratch):
        self.refs = refs
        self.send_sem, self.recv_sem, self.own_sem = scratch
        self.column = lax.axis_index("tp")
        self.place, self.ahead, self.behind = ring_ends(self.count)

    def copy(self, shard, full, way, part, step, first=False):
        move = (self.place + self.count - step) if way == 0 else (self.place + step)
        owner = ring_index(move % self.count, self.count)
        half = self.rows[full] // 2
        size = half // self.parts
        rows = pl.ds(pl.multiple_of(way * half + part * size, 16), size)
        there = self.refs[full].at[owner, rows]
        return pltpu.make_async_remote_copy(
            src_ref=self.refs[shard].at[rows] if first else there,
            dst_ref=there,
            send_sem=self.send_sem.at[self.order[full], way, part, step],
            recv_sem=self.recv_sem.at[self.order[full], way, part, step],
            device_id=(self.ahead if way == 0 else self.behind, self.column),
            device_id_type=MESH,
        )

    def own(self, shard, full):
        there = self.refs[full].at[lax.axis_index("seq")]
        return pltpu.make_async_copy(self.refs[shard], there, self.own_sem.at[self.order[full]])

    def pieces(self, group):
        return [(shard, full, way) for shard, full in self.groups[group] for way in range(2)]

    def begin(self, group):
        for part in range(self.parts):
            for shard, full, way in self.pieces(group):
                self.copy(shard, full, way, part, 0, True).start()
        for shard, full in self.groups[group]:
            self.own(shard, full).start()

    def tick(self, group, index):
        step, part = 1 + index // self.parts, index % self.parts
        for shard, full, way in self.pieces(group):
            self.copy(shard, full, way, part, step - 1).wait_recv()
            self.copy(shard, full, way, part, step).start()

    def prepare(self):
        pass

    def turn(self, group):
        self.begin(group)
        self.settle(group - 1)

    def settled(self, group):
        pass

    def settle(self, group):
        for part in range(self.parts):
            for shard, full, way in self.pieces(group):
                self.copy(shard, full, way, part, self.count - 2).wait_recv()
        for shard, full in self.groups[group]:
            self.own(shard, full).wait()

    def finish(self):
        def sent(step, carry):
            for group in range(len(self.groups)):
                for part in range(self.parts):
                    for shard, full, way in self.pieces(group):
                        self.copy(shard, full, way, part, step).wait_send()
            return carry

        lax.fori_loop(0, self.count - 1, sent, 0)


class PeerCopies:
    def __init__(self, source, target):
        self.source, self.target = source, target
        columns = lax.axis_size("tp")
        self.scratch = [pltpu.SemaphoreType.DMA((columns,)), pltpu.SemaphoreType.DMA((columns,))]

    def bind(self, refs, scratch):
        self.source_ref, self.target_ref = refs[self.source], refs[self.target]
        self.send_sem, self.recv_sem = scratch
        self.columns = lax.axis_size("tp")
        self.seq, self.column = lax.axis_index("seq"), lax.axis_index("tp")

    def block(self, peer):
        if len(self.source_ref.shape) == len(self.target_ref.shape):
            return self.source_ref.at[peer]
        return self.source_ref

    def own(self):
        return pltpu.make_async_copy(
            self.block(self.column), self.target_ref.at[self.column], self.send_sem.at[0]
        )

    def copy(self, step):
        peer = (self.column + step) % self.columns
        return pltpu.make_async_remote_copy(
            src_ref=self.block(peer),
            dst_ref=self.target_ref.at[self.column],
            send_sem=self.send_sem.at[step],
            recv_sem=self.recv_sem.at[step],
            device_id=(self.seq, peer),
            device_id_type=MESH,
        )

    def start(self):
        for step in range(1, self.columns):
            self.copy(step).start()
        self.own().start()

    def wait(self):
        self.own().wait()
        for step in range(1, self.columns):
            self.copy(step).wait_recv()

    def finish(self):
        for step in range(1, self.columns):
            self.copy(step).wait_send()


class ScatterRing:
    def __init__(self, groups, places, shapes, wide):
        self.count = lax.axis_size("seq")
        self.groups, self.places, self.wide = groups, places, wide
        self.names = list(places)
        left = shapes[self.names[0]]
        features, tokens = left.shape
        self.rows = features // self.count
        self.parts = 2
        self.ticks = (self.count - 2) * self.parts
        sems = pltpu.SemaphoreType.DMA((len(groups), 2, self.parts, self.count - 1))
        buffers = max(places.values()) + 1
        self.scratch = [
            pltpu.VMEM((buffers, features, tokens), LOW),
            pltpu.VMEM((2, 2, tokens, wide), LOW),
            pltpu.VMEM((2, 2, self.count, self.rows, wide), LOW),
            pltpu.VMEM((2, self.rows, 2 * wide), jnp.float32),
            sems,
            sems,
            pltpu.SemaphoreType.DMA((len(self.names),)),
            pltpu.SemaphoreType.DMA((2, 2)),
            pltpu.SemaphoreType.DMA((2,)),
        ]
        self.flops = 4 * len(groups) * features * tokens * wide
        self.out_shapes = [jax.ShapeDtypeStruct((self.rows, 2 * wide), jnp.float32)] * len(groups)

    def bind(self, refs, scratch):
        self.refs, self.out_refs = refs, [refs[name] for name in self.outs]
        self.lefts, self.rights, self.slots, self.finals = scratch[:4]
        self.send_sem, self.recv_sem, self.left_sem, self.right_sem, self.done_sem = scratch[4:]
        self.column = lax.axis_index("tp")
        self.place, self.ahead, self.behind = ring_ends(self.count)

    def left_load(self, name):
        return pltpu.make_async_copy(
            self.refs[name], self.lefts.at[self.places[name]], self.left_sem.at[self.names.index(name)]
        )

    def right_load(self, group, way):
        _, name, start = self.groups[group][way]
        source = self.refs[name].at[:, pl.ds(start, self.wide)]
        return pltpu.make_async_copy(source, self.rights.at[group % 2, way], self.right_sem.at[group % 2, way])

    def fetch(self, group):
        for way in range(2):
            self.right_load(group, way).start()

    def span(self, part):
        width = self.wide // self.parts
        return pl.ds(pl.multiple_of(part * width, 128), width)

    def term(self, group, way, part, step):
        move = (self.place + 2 * self.count - 1 - step) if way == 0 else (self.place + 1 + step)
        owner = ring_index(move % self.count, self.count)
        rows = pl.ds(pl.multiple_of(owner * self.rows, 16), self.rows)
        left = self.lefts[self.places[self.groups[group][way][0]], rows, :]
        right = self.rights[group % 2, way, :, self.span(part)]
        return jnp.dot(left, right, preferred_element_type=jnp.float32)

    def held(self, group, way, part, step):
        return self.slots.at[group % 2, way, step, :, self.span(part)]

    def copy(self, group, way, part, step):
        return pltpu.make_async_remote_copy(
            src_ref=self.held(group, way, part, step),
            dst_ref=self.held(group, way, part, step + 1),
            send_sem=self.send_sem.at[group, way, part, step],
            recv_sem=self.recv_sem.at[group, way, part, step],
            device_id=(self.ahead if way == 0 else self.behind, self.column),
            device_id_type=MESH,
        )

    def store(self, group):
        return pltpu.make_async_copy(self.finals.at[group % 2], self.out_refs[group], self.done_sem.at[group % 2])

    def prepare(self):
        self.left_load("cot_full").start()
        self.fetch(0)
        self.left_load("normed_two").start()

    def turn(self, group):
        self.begin(group)
        self.settle(group - 1)
        self.settled(group - 1)

    def settled(self, group):
        if group + 2 < len(self.groups):
            self.fetch(group + 2)
        if group == 1:
            self.left_load("normed_one").start()
        if group == 5:
            self.left_load("branch_full").start()

    def begin(self, group):
        for name, first in (("cot_full", 0), ("normed_two", 2), ("normed_one", 6), ("branch_full", 7)):
            if group == first:
                self.left_load(name).wait()
        for way in range(2):
            self.right_load(group, way).wait()
        for part in range(self.parts):
            for way in range(2):
                self.held(group, way, part, 0)[...] = self.term(group, way, part, 0).astype(LOW)
                self.copy(group, way, part, 0).start()

    def tick(self, group, index):
        step, part = 1 + index // self.parts, index % self.parts
        for way in range(2):
            mine = self.term(group, way, part, step)
            self.copy(group, way, part, step - 1).wait_recv()
            held = self.held(group, way, part, step)
            held[...] = (held[...].astype(jnp.float32) + mine).astype(LOW)
            self.copy(group, way, part, step).start()

    def settle(self, group):
        last = self.count - 1
        if group >= 1:
            self.store(group - 1).wait()
        for part in range(self.parts):
            for way in range(2):
                mine = self.term(group, way, part, last)
                self.copy(group, way, part, last - 1).wait_recv()
                width = self.wide // self.parts
                start = way * self.wide + part * width
                self.finals[group % 2, :, start : start + width] = (
                    self.held(group, way, part, last)[...].astype(jnp.float32) + mine
                )
        self.store(group).start()

        def sent(step, carry):
            for part in range(self.parts):
                for way in range(2):
                    self.copy(group, way, part, step).wait_send()
            return carry

        lax.fori_loop(0, last, sent, 0)

    def finish(self):
        self.store(len(self.groups) - 1).wait()


class Job:
    wide = 256
    kept = []
    late = ()

    def hold(self, refs):
        pass

    def __init__(self, whole, tiled, outs, tiles, flops):
        self.whole, self.tiled = whole, tiled
        self.inputs = list(whole) + [array for array, axis in tiled]
        self.axes = [axis for array, axis in tiled]
        self.out_shapes = [jax.ShapeDtypeStruct(shape, dtype) for shape, dtype in outs]
        self.tiles = tiles
        self.flops = flops
        self.scratch = (
            [pltpu.VMEM(array.shape, array.dtype) for array in self.inputs]
            + [pltpu.VMEM(shape, dtype) for shape, dtype in outs]
            + [
                pltpu.SemaphoreType.DMA((len(whole),)),
                pltpu.SemaphoreType.DMA((len(tiled), tiles)),
                pltpu.SemaphoreType.DMA((len(outs), tiles)),
            ]
        )

    def bind(self, ins, outs, scratch):
        self.in_refs, self.out_refs = ins, outs
        sizes = [len(self.whole), len(self.tiled), len(outs)]
        self.whole_v, self.tiled_v, self.outs_v = split(scratch, sizes)
        self.whole_sem, self.tiled_sem, self.out_sem = scratch[sum(sizes) :]

    def peers(self):
        return []

    def window(self, axis, index):
        span = pl.ds(pl.multiple_of(index * self.wide, 128), self.wide)
        return (span,) if axis == 0 else (slice(None), span)

    def whole_load(self, which):
        return pltpu.make_async_copy(self.in_refs[which], self.whole_v[which], self.whole_sem.at[which])

    def tiled_load(self, which, index):
        window = self.window(self.axes[which], index)
        there = self.in_refs[len(self.whole) + which].at[window]
        return pltpu.make_async_copy(there, self.tiled_v[which].at[window], self.tiled_sem.at[which, index])

    def out_window(self, index):
        return self.window(1, index)

    def store(self, which, index):
        window = self.out_window(index)
        return pltpu.make_async_copy(
            self.outs_v[which].at[window], self.out_refs[which].at[window], self.out_sem.at[which, index]
        )

    def start(self, late):
        for which in range(len(self.whole)):
            if late == (which in self.late):
                self.whole_load(which).start()

        def begin(index, carry):
            for which in range(len(self.tiled)):
                self.tiled_load(which, index).start()
            return carry

        if not late:
            lax.fori_loop(0, self.tiles, begin, 0)

    def tile(self, index):
        @pl.when(index == 0)
        def _():
            for which in range(len(self.whole)):
                self.whole_load(which).wait()

        for which in range(len(self.tiled)):
            self.tiled_load(which, index).wait()
        tiles = [ref[self.window(axis, index)] for ref, axis in zip(self.tiled_v, self.axes)]
        for which, value in enumerate(self.compute(self.whole_v, tiles)):
            self.outs_v[which][self.out_window(index)] = value
            self.store(which, index).start()

    def finish(self):
        def end(index, carry):
            for which in range(len(self.outs_v)):
                self.store(which, index).wait()
            return carry

        lax.fori_loop(0, self.tiles, end, 0)


def blocks_dot(blocks, weight):
    parts, _, depth = blocks.shape
    total = None
    for part in range(parts):
        term = jnp.dot(blocks[part], weight[part * depth : (part + 1) * depth], preferred_element_type=jnp.float32)
        total = term if total is None else total + term
    return total


class ExpandJob(Job):

    late = (0,)

    def __init__(self, normed, gate_full, up_full):
        rows, width = normed.shape[1], gate_full.shape[1]
        outs = [((rows, width), jnp.float32), ((rows, width), jnp.float32), ((rows, width), LOW)]
        super().__init__(
            [normed], [(gate_full, 1), (up_full, 1)], outs, width // self.wide, 4 * rows * gate_full.size
        )

    def compute(self, whole, tiles):
        gate_rows = blocks_dot(whole[0], tiles[0])
        up_rows = blocks_dot(whole[0], tiles[1])
        return gate_rows, up_rows, (gate_rows * jax.nn.sigmoid(gate_rows) * up_rows).astype(LOW)


class HiddenGradJob(Job):
    def __init__(self, cot, shrink_full, gate_rows, up_rows):
        rows, width = gate_rows.shape
        outs = [((rows, width), LOW), ((rows, width), LOW)]
        tiled = [(shrink_full, 1), (gate_rows, 1), (up_rows, 1)]
        super().__init__([cot], tiled, outs, width // self.wide, 2 * rows * shrink_full.size)

    def compute(self, whole, tiles):
        _, gate_rows, up_rows = tiles
        act_grad = blocks_dot(whole[0], tiles[0])
        sigmoid_gate = jax.nn.sigmoid(gate_rows)
        gate_grad = act_grad * up_rows * sigmoid_gate * (1.0 + gate_rows * (1.0 - sigmoid_gate))
        return gate_grad.astype(LOW), (act_grad * (gate_rows * sigmoid_gate)).astype(LOW)


class WidthJob(Job):
    then = None

    def __init__(self, lefts, weights):
        rows, width = lefts[0].shape[0], weights[0].shape[0]
        flops = 2 * rows * sum(weight.size for weight in weights)
        parts = lax.axis_size("tp")
        self.own = width // parts
        out = ((parts, rows, self.own), LOW)
        super().__init__(lefts, [(weight, 0) for weight in weights], [out], width // self.wide, flops)

    def out_window(self, index):
        each = self.own // self.wide
        return index // each, slice(None), pl.ds(pl.multiple_of(index % each * self.wide, 128), self.wide)

    def compute(self, whole, tiles):
        total = None
        for left, weight in zip(whole, tiles):
            term = contract_cols(left[...], weight)
            total = term if total is None else total + term
        return (total.astype(LOW),)

    def finish(self):
        super().finish()
        if self.then:
            self.then.start()


class MixerJob:
    kept = []
    late = ()

    def hold(self, refs):
        self.kept_refs = refs

    def __init__(self, inputs, outs, extra, phases, flops):
        self.inputs = list(inputs)
        self.out_shapes = [jax.ShapeDtypeStruct(shape, dtype) for shape, dtype in outs]
        self.phases = phases
        self.tiles = sum(phases)
        self.flops = flops
        self.scratch = (
            [pltpu.VMEM(array.shape, array.dtype) for array in self.inputs]
            + [pltpu.VMEM(shape, dtype) for shape, dtype in outs]
            + extra
            + [
                pltpu.SemaphoreType.DMA((len(self.inputs),)),
                pltpu.SemaphoreType.DMA((len(outs),)),
            ]
        )

    def bind(self, ins, outs, scratch):
        self.in_refs, self.out_refs = ins, outs
        extra = len(scratch) - len(ins) - len(outs) - 2
        self.ins_v, self.outs_v, self.extra_v = split(scratch, [len(ins), len(outs), extra])
        self.in_sem, self.out_sem = scratch[-2:]
        self.count = lax.axis_size("seq")
        self.seq = lax.axis_index("seq")
        self.column = lax.axis_index("tp")

    def peers(self):
        after = (self.seq + 1) % self.count
        before = (self.seq + self.count - 1) % self.count
        return [(after, self.column), (before, self.column)]

    def load(self, which):
        return pltpu.make_async_copy(self.in_refs[which], self.ins_v[which], self.in_sem.at[which])

    def store(self, which):
        return pltpu.make_async_copy(self.outs_v[which], self.out_refs[which], self.out_sem.at[which])

    def passing(self, source, target, forward):
        step = 1 if forward else self.count - 1
        return pltpu.make_async_remote_copy(
            src_ref=source,
            dst_ref=target,
            send_sem=self.kept_refs[1].at[0],
            recv_sem=self.kept_refs[1].at[1],
            device_id=((self.seq + step) % self.count, self.column),
            device_id_type=MESH,
        )

    def start(self, late):
        for which in range(len(self.inputs)):
            if late == (which in self.late):
                self.load(which).start()

    def tile(self, index):
        begin = 0
        for phase, tiles in enumerate(self.phases):
            here = index - begin

            @pl.when((here >= 0) & (here < tiles))
            def _(phase=phase, here=here, tiles=tiles):
                @pl.when(here == 0)
                def _():
                    self.before(phase)

                self.work(phase, here)

                @pl.when(here == tiles - 1)
                def _():
                    self.after(phase)

            begin += tiles

    def finish(self):
        for which in range(len(self.out_shapes)):
            self.store(which).wait()


def visible(bound_row, shape):
    position = lax.broadcasted_iota(jnp.int32, shape, 0)
    see_one = position != bound_row
    return position, see_one, see_one & (position - 1 != bound_row)


def lagged(rows, halo, position):
    last, second = halo[15:16].astype(jnp.float32), halo[14:15].astype(jnp.float32)
    one = jnp.where(position == 0, last, pltpu.roll(rows, 1, 0))
    two = jnp.where(position == 0, second, jnp.where(position == 1, last, pltpu.roll(rows, 2, 0)))
    return one, two


class EntryJob(MixerJob):
    then = None
    late = (0,)

    def __init__(self, tokens, wide, entry_full, exit_full, bound):
        parts, rows, own = tokens.shape
        width, columns = exit_full.shape
        self.rows, self.columns, self.own = rows, columns, own
        self.width = width
        outs = [
            ((rows, 3 * columns), jnp.float32),
            ((rows, columns), jnp.float32),
            ((rows, columns), LOW),
            ((16, columns), LOW),
            ((rows, columns), LOW),
            ((parts, rows, own), LOW),
            ((rows, 128), jnp.float32),
            ((width, rows), LOW),
        ]
        phases = [rows // 256, 3 * columns // 256, 1, columns // 128, width // 256]
        flops = 2 * rows * (entry_full.size + exit_full.size)
        super().__init__([tokens, wide, entry_full, exit_full, bound], outs, [], phases, flops)
        self.kept = [pltpu.VMEM((16, columns), LOW), pltpu.SemaphoreType.DMA((2,))]

    def halo(self):
        return self.passing(self.outs_v[2].at[pl.ds(self.rows - 16, 16)], self.kept_refs[0], True)

    def before(self, phase):
        if phase == 0:
            for which in (0, 1):
                self.load(which).wait()
        if phase == 1:
            self.store(6).start()
            self.store(7).start()
            self.load(2).wait()
        if phase == 3:
            self.load(4).wait()
            self.halo().wait_recv()
            self.outs_v[3][...] = self.kept_refs[0][...]
            self.store(3).start()
        if phase == 4:
            self.load(3).wait()

    def after(self, phase):
        if phase == 1:
            self.store(0).start()
        if phase == 2:
            self.halo().start()
            self.store(2).start()
        if phase == 3:
            self.store(1).start()
            self.store(4).start()
        if phase == 4:
            self.store(5).start()

    def finish(self):
        self.store(5).wait()
        if self.then:
            self.then.start()
        self.halo().wait_send()
        for which in (0, 1, 2, 3, 4, 6, 7):
            self.store(which).wait()

    def work(self, phase, index):
        tokens, wide, entry, exits, bound = self.ins_v
        taps = wide.at[self.column]
        projected, conv, gated, halo, mixer, term, scales, turned_rows = self.outs_v
        columns = self.columns
        if phase == 0:
            rows = pl.ds(pl.multiple_of(index * 256, 256), 256)
            values = [tokens[part, rows, :].astype(jnp.float32) for part in range(tokens.shape[0])]
            total = sum(jnp.sum(value * value, axis=1, keepdims=True) for value in values)
            scale = lax.rsqrt(total / D + EPSILON)
            scales[rows, :] = jnp.broadcast_to(scale, (256, 128))
            for part, value in enumerate(values):
                normed = (value * scale * wide[part, 3:4, :]).astype(LOW)
                tokens[part, rows, :] = normed
                turned_rows[part * self.own : (part + 1) * self.own, rows] = normed.T
        if phase == 1:
            span = pl.ds(pl.multiple_of(index * 256, 256), 256)
            projected[:, span] = blocks_dot(tokens, entry[:, span])
        if phase == 2:
            gated[...] = (projected[:, :columns] * projected[:, 2 * columns :]).astype(LOW)
        if phase == 3:
            span = pl.ds(pl.multiple_of(index * 128, 128), 128)
            middle = pl.ds(pl.multiple_of(columns + index * 128, 128), 128)
            rows = gated[:, span].astype(jnp.float32)
            position, see_one, see_two = visible(bound[0:1, :], rows.shape)
            before = halo[:, span].astype(jnp.float32) * jnp.where(self.seq > 0, 1.0, 0.0)
            one, two = lagged(rows, before, position)
            total = (
                taps[2:3, span] * rows
                + taps[1:2, span] * jnp.where(see_one, one, 0.0)
                + taps[0:1, span] * jnp.where(see_two, two, 0.0)
            )
            conv[:, span] = total
            mixer[:, span] = (projected[:, middle] * total).astype(LOW)
        if phase == 4:
            features = pl.ds(pl.multiple_of(index * 256, 256), 256)
            owner, inner = index // (self.own // 256), index % (self.own // 256)
            span = pl.ds(pl.multiple_of(inner * 256, 256), 256)
            term[owner, :, span] = contract_cols(mixer[...], exits[features, :]).astype(LOW)


class MixerGradJob(MixerJob):
    then = None
    late = (0,)

    def __init__(self, branch, exit_full, entry_full, projected, conv, gated, halo, wide, bound):
        parts, rows, own = branch.shape
        width, columns = exit_full.shape
        self.rows, self.columns, self.own = rows, columns, own
        outs = [((rows, 3 * columns), LOW), ((parts, rows, own), LOW), ((8, columns), jnp.float32)]
        extra = [
            pltpu.VMEM((rows, columns), jnp.float32),
            pltpu.VMEM((8, columns), jnp.float32),
        ]
        self.kept = [pltpu.VMEM((8, columns), jnp.float32), pltpu.SemaphoreType.DMA((2,))]
        phases = [columns // 256, 1, columns // 128, width // 256]
        flops = 2 * rows * (entry_full.size + exit_full.size)
        inputs = [branch, exit_full, entry_full, projected, conv, gated, halo, wide, bound]
        super().__init__(inputs, outs, extra, phases, flops)

    def back(self):
        return self.passing(self.extra_v[1], self.kept_refs[0], False)

    def before(self, phase):
        if phase == 0:
            for which in (0, 1, 3, 4):
                self.load(which).wait()
        if phase == 1:
            for which in (7, 8):
                self.load(which).wait()
        if phase == 2:
            for which in (5, 6):
                self.load(which).wait()
            self.back().wait_recv()
        if phase == 3:
            self.load(2).wait()

    def after(self, phase):
        if phase == 1:
            self.back().start()
        if phase == 2:
            self.store(0).start()
            self.store(2).start()
        if phase == 3:
            self.store(1).start()

    def finish(self):
        self.store(1).wait()
        if self.then:
            self.then.start()
        self.back().wait_send()
        for which in (0, 2):
            self.store(which).wait()

    def work(self, phase, index):
        branch, exits, entry, projected, conv, gated, halo, wide, bound = self.ins_v
        taps = wide.at[self.column]
        grads, term, taps_grad = self.outs_v
        conv_grad, sent = self.extra_v
        returned = self.kept_refs[0]
        columns, height = self.columns, self.rows
        if phase == 0:
            span = pl.ds(pl.multiple_of(index * 256, 256), 256)
            middle = pl.ds(pl.multiple_of(columns + index * 256, 256), 256)
            mixer_grad = blocks_dot(branch, exits[:, span])
            grads[:, middle] = (mixer_grad * conv[:, span]).astype(LOW)
            conv_grad[:, span] = mixer_grad * projected[:, middle]
        if phase == 1:
            for start in range(0, columns, 128):
                span = slice(start, start + 128)
                rows = conv_grad[0:8, span]
                position, see_one, see_two = visible(bound[0:1, :], rows.shape)
                one = pltpu.roll(jnp.where(see_one, rows, 0.0) * taps[1:2, span], 1, 0)
                two = jnp.where(see_two, rows, 0.0) * taps[0:1, span]
                sent[:, span] = two + jnp.where(position == 0, 0.0, one)
            taps_grad[...] = jnp.zeros_like(taps_grad)
        if phase == 2:
            span = pl.ds(pl.multiple_of(index * 128, 128), 128)
            last = pl.ds(pl.multiple_of(2 * columns + index * 128, 128), 128)
            rows = conv_grad[:, span]
            position, see_one, see_two = visible(bound[0:1, :], rows.shape)
            seen_one, seen_two = jnp.where(see_one, rows, 0.0), jnp.where(see_two, rows, 0.0)
            one = pltpu.roll(seen_one * taps[1:2, span], height - 1, 0)
            two = pltpu.roll(seen_two * taps[0:1, span], height - 2, 0)
            after = returned[:, span] * jnp.where(self.seq < self.count - 1, 1.0, 0.0)
            gated_grad = (
                rows * taps[2:3, span]
                + jnp.where(position == height - 1, after[1:2], one)
                + jnp.where(position < height - 2, two, jnp.where(position == height - 2, after[0:1], 0.0))
            )
            grads[:, span] = (gated_grad * projected[:, last]).astype(LOW)
            grads[:, last] = (gated_grad * projected[:, span]).astype(LOW)
            own_rows = gated[:, span].astype(jnp.float32)
            before = halo[:, span].astype(jnp.float32) * jnp.where(self.seq > 0, 1.0, 0.0)
            lag_one, lag_two = lagged(own_rows, before, position)
            taps_grad[0:1, span] = jnp.sum(seen_two * lag_two, axis=0, keepdims=True)
            taps_grad[1:2, span] = jnp.sum(seen_one * lag_one, axis=0, keepdims=True)
            taps_grad[2:3, span] = jnp.sum(rows * own_rows, axis=0, keepdims=True)
        if phase == 3:
            features = pl.ds(pl.multiple_of(index * 256, 256), 256)
            owner, inner = index // (self.own // 256), index % (self.own // 256)
            span = pl.ds(pl.multiple_of(inner * 256, 256), 256)
            term[owner, :, span] = contract_cols(grads[...], entry[features, :]).astype(LOW)


class Jobs:
    def __init__(self, *jobs):
        self.jobs = jobs
        self.inputs = [item for job in jobs for item in job.inputs]
        self.out_shapes = [item for job in jobs for item in job.out_shapes]
        self.scratch = [item for job in jobs for item in job.scratch]
        self.kept = [item for job in jobs for item in job.kept]
        self.tiles = sum(job.tiles for job in jobs)
        self.flops = sum(job.flops for job in jobs)

    def hold(self, refs):
        for job, own in zip(self.jobs, split(refs, [len(job.kept) for job in self.jobs])):
            job.hold(own)

    def bind(self, ins, outs, scratch):
        groups = zip(
            self.jobs,
            split(ins, [len(job.inputs) for job in self.jobs]),
            split(outs, [len(job.out_shapes) for job in self.jobs]),
            split(scratch, [len(job.scratch) for job in self.jobs]),
        )
        for job, own_ins, own_outs, own_scratch in groups:
            job.bind(own_ins, own_outs, own_scratch)

    def peers(self):
        return [peer for job in self.jobs for peer in job.peers()]

    def start(self, late):
        for job in self.jobs:
            job.start(late)

    def tile(self, index):
        begin = 0
        for job in self.jobs:
            here = index - begin

            @pl.when((here >= 0) & (here < job.tiles))
            def _(job=job, here=here):
                job.tile(here)

            begin += job.tiles

    def finish(self):
        for job in self.jobs:
            job.finish()


class TurnJob(MixerJob):
    late = (0,)

    def __init__(self, blocks):
        parts, rows, own = blocks.shape
        super().__init__([blocks], [((parts * own, rows), blocks.dtype)], [], [rows // 128], 0)

    def peers(self):
        return []

    def before(self, phase):
        self.load(0).wait()

    def after(self, phase):
        self.store(0).start()

    def work(self, phase, index):
        (blocks,), (target,) = self.ins_v, self.outs_v
        parts, _, own = blocks.shape
        rows = pl.ds(pl.multiple_of(index * 128, 128), 128)
        for part in range(parts):
            target[part * own : (part + 1) * own, rows] = blocks[part, rows, :].T


class CastJob(MixerJob):
    def __init__(self, pairs, plain):
        rows, columns = plain.shape
        lanes = pairs.shape[1]
        self.rows, self.half, self.lanes = rows, columns // 2, lanes
        self.block = max(rows // 8, 16)
        outs = [((rows, columns // 2), LOW)] * 6
        super().__init__([pairs, plain], outs, [], [rows // self.block], 0)
        self.scratch[0] = pltpu.VMEM((pairs.shape[0] + 2 * columns // lanes, lanes), pairs.dtype)
        self.whole_rows = pairs.shape[0]

    def load(self, which):
        target = self.ins_v[which].at[pl.ds(0, self.whole_rows)] if which == 0 else self.ins_v[which]
        return pltpu.make_async_copy(self.in_refs[which], target, self.in_sem.at[which])

    def peers(self):
        return []

    def before(self, phase):
        for which in range(2):
            self.load(which).wait()

    def after(self, phase):
        for which in range(6):
            self.store(which).start()

    def work(self, phase, index):
        pairs, plain = self.ins_v
        block, half, lanes = self.block, self.half, self.lanes
        tiles = half // lanes
        rows = pl.ds(pl.multiple_of(index * block, 16), block)
        start = index * (block * 4 * tiles)
        for which in range(4):
            side, plane = which // 2, which % 2
            for tile in range(tiles):
                place = (side * tiles + tile) * 2 + plane
                picked = pairs[pl.ds(start + place, block, stride=4 * tiles), :]
                self.outs_v[which][rows, tile * lanes : (tile + 1) * lanes] = picked.astype(LOW)
        for side in range(2):
            self.outs_v[4 + side][rows, :] = plain[rows, side * half : (side + 1) * half].astype(LOW)


class SmallGatherJob:
    tiles, flops = 1, 0

    def __init__(self, own, seen):
        self.inputs = [own]
        self.seen = seen
        devices, columns = lax.axis_size("seq"), lax.axis_size("tp")
        wide = (columns, 8, devices * seen)
        self.out_shapes = [jax.ShapeDtypeStruct(wide, jnp.float32)]
        self.scratch = [pltpu.VMEM(wide, jnp.float32), pltpu.SemaphoreType.DMA((2,))]
        self.kept = [
            pltpu.VMEM((devices, columns) + own.shape, own.dtype),
            pltpu.SemaphoreType.DMA((columns,)),
            pltpu.SemaphoreType.DMA((columns,)),
            pltpu.SemaphoreType.DMA((devices,)),
            pltpu.SemaphoreType.DMA((devices,)),
        ]

    def hold(self, refs):
        self.whole, self.near_send, self.near_recv, self.far_send, self.far_recv = refs
        self.devices, self.columns = lax.axis_size("seq"), lax.axis_size("tp")
        self.seq, self.column = lax.axis_index("seq"), lax.axis_index("tp")

    def bind(self, ins, outs, scratch):
        self.source, self.target = ins[0], outs[0]
        self.wide, self.local_sem = scratch

    def peers(self):
        near = [(self.seq, (self.column + step) % self.columns) for step in range(1, self.columns)]
        far = [((self.seq + step) % self.devices, self.column) for step in range(1, self.devices)]
        return near + far

    def near(self, step):
        piece = self.whole.at[self.seq, self.column]
        return pltpu.make_async_remote_copy(
            src_ref=piece,
            dst_ref=piece,
            send_sem=self.near_send.at[step],
            recv_sem=self.near_recv.at[step],
            device_id=(self.seq, (self.column + step) % self.columns),
            device_id_type=MESH,
        )

    def far(self, step):
        piece = self.whole.at[self.seq]
        return pltpu.make_async_remote_copy(
            src_ref=piece,
            dst_ref=piece,
            send_sem=self.far_send.at[step],
            recv_sem=self.far_recv.at[step],
            device_id=((self.seq + step) % self.devices, self.column),
            device_id_type=MESH,
        )

    def start(self, late):
        if late:
            return
        load = pltpu.make_async_copy(self.source, self.whole.at[self.seq, self.column], self.local_sem.at[0])
        load.start()
        load.wait()
        for step in range(1, self.columns):
            self.near(step).start()

    def tile(self, index):
        for step in range(1, self.columns):
            self.near(step).wait()

        def begin(step, carry):
            self.far(step).start()
            return carry

        lax.fori_loop(1, self.devices, begin, 0)

    def finish(self):
        def end(step, carry):
            self.far(step).wait()
            return carry

        lax.fori_loop(1, self.devices, end, 0)
        each = LANES // self.seen
        for column in range(self.columns):
            for start in range(0, self.devices, each):
                total = None
                for inner in range(each):
                    piece = self.whole[start + inner, column, :, :].astype(jnp.float32)[:8]
                    piece = pltpu.roll(piece, inner * self.seen, 1) if inner else piece
                    total = piece if total is None else total + piece
                self.wide[column, :, start * self.seen : start * self.seen + LANES] = total
        store = pltpu.make_async_copy(self.wide, self.target, self.local_sem.at[1])
        store.start()
        store.wait()


class RowSumJob(MixerJob):
    block = 128

    def __init__(self, inputs, outs, extra, rows, flops):
        self.columns = lax.axis_size("tp")
        blocks = rows // self.block
        self.kept = [
            pltpu.VMEM((self.columns, blocks, self.block), jnp.float32),
            pltpu.SemaphoreType.DMA((self.columns,)),
            pltpu.SemaphoreType.DMA((self.columns,)),
        ]
        totals = pltpu.VMEM((blocks, self.block), jnp.float32)
        super().__init__(inputs, outs, [totals] + extra, [blocks, 1, blocks], flops)

    def peers(self):
        return [(self.seq, (self.column + step) % self.columns) for step in range(1, self.columns)]

    def share(self, step):
        return pltpu.make_async_remote_copy(
            src_ref=self.kept_refs[0].at[0],
            dst_ref=self.kept_refs[0].at[step],
            send_sem=self.kept_refs[1].at[step],
            recv_sem=self.kept_refs[2].at[step],
            device_id=(self.seq, (self.column + step) % self.columns),
            device_id_type=MESH,
        )

    def before(self, phase):
        if phase == 0:
            for which in range(len(self.inputs)):
                self.load(which).wait()

    def after(self, phase):
        if phase == 0:
            for step in range(1, self.columns):
                self.share(step).start()
        if phase == 2:
            for which in range(len(self.out_shapes)):
                self.store(which).start()

    def finish(self):
        for step in range(1, self.columns):
            self.share(step).wait_send()
        super().finish()

    def work(self, phase, index):
        block = self.block
        slots, totals = self.kept_refs[0], self.extra_v[0]
        rows = pl.ds(pl.multiple_of(index * block, block), block)
        if phase == 0:
            part = jnp.sum(self.values(rows), axis=1, keepdims=True)
            slots[0, pl.ds(index, 1), :] = jnp.broadcast_to(part, (block, block)).T[0:1, :]
        if phase == 1:
            for step in range(1, self.columns):
                self.share(step).wait_recv()
            totals[...] = sum(slots[step] for step in range(self.columns))
        if phase == 2:
            self.use(rows, jnp.broadcast_to(totals[pl.ds(index, 1), :], (block, block)).T)


class NormJob(RowSumJob):
    then = None
    late = (1,)

    def __init__(self, rows_in, terms, wide):
        rows, own = rows_in.shape
        outs = [((rows, own), jnp.float32), ((rows, own), LOW), ((rows, 128), jnp.float32)]
        super().__init__([rows_in, terms, wide], outs, [], rows, 0)

    def values(self, rows):
        rows_in, terms, _ = self.ins_v
        residual = sum(terms[part, rows, :].astype(jnp.float32) for part in range(self.columns))
        residual = rows_in[rows, :].astype(jnp.float32) + residual
        self.outs_v[0][rows, :] = residual
        return residual * residual

    def use(self, rows, total):
        residual, normed, scales = self.outs_v
        scale = lax.rsqrt(total / D + EPSILON)
        scales[rows, :] = scale
        gain = self.ins_v[2].at[self.column]
        normed[rows, :] = (residual[rows, :] * scale[:, 0:1] * gain[4:5, :]).astype(LOW)

    def finish(self):
        self.store(1).wait()
        if self.then:
            self.then.start()
        for step in range(1, self.columns):
            self.share(step).wait_send()
        for which in (0, 2):
            self.store(which).wait()


class NormBackJob(RowSumJob):
    then = None
    late = (0,)

    def __init__(self, terms, kept, scales, wide, row, base, rounded):
        _, rows, own = terms.shape
        outs = [((rows, own), jnp.float32), ((8, own), jnp.float32)]
        outs = outs + [((rows, own), LOW)] if rounded else outs
        self.row = row
        super().__init__([terms, kept, scales, wide, base], outs, [], rows, 0)

    def parts(self, rows):
        terms, kept, scales, wide, base = self.ins_v
        gain = wide.at[self.column]
        return (
            sum(terms[part, rows, :].astype(jnp.float32) for part in range(self.columns)),
            kept[rows, :].astype(jnp.float32),
            scales[rows, 0:1],
            gain[self.row : self.row + 1, :],
        )

    def before(self, phase):
        super().before(phase)
        if phase == 0:
            self.outs_v[1][...] = jnp.zeros_like(self.outs_v[1])

    def values(self, rows):
        grad, kept, scale, gain = self.parts(rows)
        product = grad * kept
        self.outs_v[1][0:1, :] += jnp.sum(product * scale, axis=0, keepdims=True)
        return product * gain

    def use(self, rows, total):
        grad, kept, scale, gain = self.parts(rows)
        rows_grad = scale * gain * grad - kept * (scale * scale * scale * total[:, 0:1] / D)
        result = self.ins_v[4][rows, :].astype(jnp.float32) + rows_grad
        self.outs_v[0][rows, :] = result
        if len(self.outs_v) > 2:
            self.outs_v[2][rows, :] = result.astype(LOW)

    def finish(self):
        if self.then:
            self.store(2).wait()
            self.then.start()
        for step in range(1, self.columns):
            self.share(step).wait_send()
        for which in range(len(self.out_shapes)):
            if which != 2 or not self.then:
                self.store(which).wait()


class SumJob(MixerJob):
    late = (1,)

    def __init__(self, base, terms):
        rows, own = base.shape
        super().__init__([base, terms], [((rows, own), LOW)], [], [rows // 128], 0)

    def before(self, phase):
        for which in range(2):
            self.load(which).wait()

    def after(self, phase):
        self.store(0).start()

    def work(self, phase, index):
        base, terms = self.ins_v
        rows = pl.ds(pl.multiple_of(index * 128, 128), 128)
        total = sum(terms[part, rows, :].astype(jnp.float32) for part in range(terms.shape[0]))
        self.outs_v[0][rows, :] = (base[rows, :] + total).astype(LOW)


class AdamJob(MixerJob):
    deep = 1

    def __init__(self, weight, grads, extra=()):
        rows = grads[0].shape[0]
        self.block = max(rows // 8, 8)
        tiles = rows // self.block
        outs = [(weight.shape, jnp.float32)] * 3
        super().__init__([weight] * 3 + list(grads), outs, list(extra), [tiles], 0)
        self.scratch[-1] = pltpu.SemaphoreType.DMA((3, tiles))

    def peers(self):
        return []

    def before(self, phase):
        for which in range(len(self.inputs)):
            self.load(which).wait()

    def after(self, phase):
        pass

    def piece(self, which, index):
        size = self.block * self.deep
        rows = pl.ds(pl.multiple_of(index * size, 8), size)
        return pltpu.make_async_copy(
            self.outs_v[which].at[rows], self.out_refs[which].at[rows], self.out_sem.at[which, index]
        )

    def work(self, phase, index):
        rows = pl.ds(pl.multiple_of(index * self.block, 8), self.block)
        start = 0
        for grad in self.ins_v[3:]:
            span = slice(start, start + grad.shape[1])
            start += grad.shape[1]
            state = [ref[rows, span] for ref in self.ins_v[:3]]
            for out, result in zip(self.outs_v, adam_update(*state, grad[rows, :], RATE_WIDE, WEIGHT_DECAY)):
                out[rows, span] = result
        for which in range(3):
            self.piece(which, index).start()

    def finish(self):
        def end(index, carry):
            for which in range(3):
                self.piece(which, index).wait()
            return carry

        lax.fori_loop(0, self.tiles, end, 0)


class AdamPairsJob(AdamJob):
    def __init__(self, weight, grads):
        rows = grads[0].shape[0]
        self.deep = weight.shape[0] // rows
        size = max(rows // 8, 8) * self.deep
        super().__init__(weight, grads, [pltpu.VMEM((size + self.deep, LANES), jnp.float32)])

    def work(self, phase, index):
        size = self.block * self.deep
        rows = pl.ds(pl.multiple_of(index * self.block, 8), self.block)
        seen = pl.ds(pl.multiple_of(index * size, 8), size)
        mixed = self.extra_v[0]
        for which, grad in enumerate(self.ins_v[3:]):
            half, side = which // 2, which % 2
            tiles = grad.shape[1] // LANES
            for tile in range(tiles):
                place = (half * tiles + tile) * 2 + side
                picked = grad[rows, tile * LANES : (tile + 1) * LANES]
                mixed[pl.ds(place, self.block, stride=self.deep), :] = picked
        state = [ref[seen, :] for ref in self.ins_v[:3]]
        for out, result in zip(self.outs_v, adam_update(*state, mixed[0:size, :], RATE_WIDE, WEIGHT_DECAY)):
            out[seen, :] = result
        for which in range(3):
            self.piece(which, index).start()


class SmallSumJob:
    tiles, flops = 1, 0

    def __init__(self, taps_grad, gain_grad, before):
        count = lax.axis_size("seq")
        self.inputs = [taps_grad, gain_grad]
        shape = taps_grad.shape
        self.before = before
        self.out_shapes = [jax.ShapeDtypeStruct(shape, jnp.float32)]
        self.scratch = [pltpu.VMEM(shape, jnp.float32)] * 3 + [pltpu.SemaphoreType.DMA((3,))]
        self.kept = [
            pltpu.VMEM((count,) + shape, jnp.float32),
            pltpu.SemaphoreType.DMA((count,)),
            pltpu.SemaphoreType.DMA((count,)),
        ]

    def hold(self, refs):
        self.slots, self.send_sem, self.recv_sem = refs

    def bind(self, ins, outs, scratch):
        self.sources, self.target = ins, outs[0]
        self.taps, self.gain, self.total, self.local_sem = scratch
        self.count = lax.axis_size("seq")
        self.seq = lax.axis_index("seq")
        self.column = lax.axis_index("tp")

    def peers(self):
        return [((self.seq + far) % self.count, self.column) for far in range(1, self.count)]

    def copy(self, far):
        return pltpu.make_async_remote_copy(
            src_ref=self.slots.at[0],
            dst_ref=self.slots.at[far],
            send_sem=self.send_sem.at[far],
            recv_sem=self.recv_sem.at[far],
            device_id=((self.seq + far) % self.count, self.column),
            device_id_type=MESH,
        )

    def loads(self):
        return [
            pltpu.make_async_copy(self.sources[which], (self.taps, self.gain)[which], self.local_sem.at[which])
            for which in range(2)
        ]

    def start(self, late):
        if late:
            return
        for load in self.loads():
            load.start()

    def tile(self, index):
        for load in self.loads():
            load.wait()
        self.slots[0, 0:3, :] = self.taps[0:3, :]
        self.slots[0, 3:4, :] = self.before.outs_v[1][0:1, :]
        self.slots[0, 4:5, :] = self.gain[0:1, :]
        self.slots[0, 5:8, :] = jnp.zeros_like(self.slots[0, 5:8, :])

        def begin(far, carry):
            self.copy(far).start()
            return carry

        lax.fori_loop(1, self.count, begin, 0)

    def finish(self):
        self.total[...] = self.slots[0]

        def add(far, carry):
            self.copy(far).wait_recv()
            self.total[...] += self.slots[far]
            return carry

        lax.fori_loop(1, self.count, add, 0)
        store = pltpu.make_async_copy(self.total, self.target, self.local_sem.at[2])
        store.start()

        def sent(far, carry):
            self.copy(far).wait_send()
            return carry

        lax.fori_loop(1, self.count, sent, 0)
        store.wait()


class Section:
    def __init__(self, ranges, jobs=(), waits=(), rest=1, calls=(), early=True, then=()):
        self.ranges, self.jobs, self.waits, self.rest, self.calls, self.early = ranges, jobs, waits, rest, calls, early
        self.then = then
        self.job = Jobs(*[job for job, _, _ in jobs])

    def run(self, ring, ins, outs):
        job = self.job
        ranges = [(group, low * ring.ticks // 12, high * ring.ticks // 12) for group, low, high in self.ranges]
        total = sum(high - low for _, low, high in ranges)
        rest = self.rest * ring.ticks // 12
        active = total - rest
        each = -(-job.tiles // active)

        def ready():
            for exchange in self.waits:
                exchange.wait()
            for exchange in self.then:
                exchange.start()
            job.start(True)

        def body(*scratch):
            job.bind(ins, outs, list(scratch))
            job.start(False)
            if not self.waits:
                job.start(True)
            done = 0
            for place, (group, low, high) in enumerate(ranges):
                if low == 0 and group > 0 and place > 0:
                    ring.turn(group)
                if place == 0:
                    for call in self.calls:
                        call.start()

                def step(index, carry, group=group, shift=done - low):
                    late = index + shift - rest
                    first, after = late * job.tiles // active, (late + 1) * job.tiles // active
                    if self.waits:
                        pl.when(late == -1)(ready)
                    for inner in range(each):
                        tile = first + inner

                        @pl.when((late >= 0) & (tile < after))
                        def _(tile=tile):
                            job.tile(tile)

                    ring.tick(group, index)
                    return carry

                lax.fori_loop(low, high, step, 0)
                done += high - low
            group, _, high = ranges[-1]
            ends = high == ring.ticks and group + 1 < len(ring.groups)
            if ends and self.early:
                ring.begin(group + 1)
            job.finish()
            if ends and not self.early:
                ring.begin(group + 1)

        pl.run_scoped(body, *job.scratch)
        group, _, high = ranges[-1]
        if high == ring.ticks:
            ring.settle(group)
            ring.settled(group)


class Plan:
    def __init__(self, arrays):
        self.arrays = arrays
        self.shapes = {name: jax.ShapeDtypeStruct(array.shape, array.dtype) for name, array in arrays.items()}
        self.inputs = list(self.shapes)
        self.weights = set()

    def define(self, name, shape, dtype):
        self.shapes[name] = jax.ShapeDtypeStruct(shape, dtype)

    def add(self, job, ins, outs):
        for name, shape in zip(outs, job.out_shapes):
            self.shapes[name] = shape
        return job, ins, outs

    def flat(self, full):
        shape = self.shapes[full].shape
        return jax.ShapeDtypeStruct((shape[0] * shape[1], shape[2]), LOW)

    def run(self, ring, sections, exchanges, peers, name, collective):
        inputs = self.inputs
        outputs = [made for made in self.shapes if made not in inputs]
        kept = [item for section in sections for item in section.job.kept]
        sems = [item for exchange in exchanges for item in exchange.scratch]

        def kernel(*all_refs):
            in_refs, out_refs, ring_scratch, sem_refs, kept_refs = split(
                all_refs, [len(inputs), len(outputs), len(ring.scratch), len(sems), len(kept)]
            )
            refs = dict(zip(inputs + outputs, in_refs + out_refs))
            ring.bind(refs, ring_scratch)
            for place, exchange in enumerate(exchanges):
                exchange.bind(refs, sem_refs[2 * place : 2 * place + 2])
            for section, own in zip(sections, split(kept_refs, [len(section.job.kept) for section in sections])):
                section.job.hold(own)
            ring.prepare()
            greet(peers())
            ring.begin(0)
            ring.settled(-1)
            for section in sections:
                ins = [rows_of(refs[made], made in self.weights) for _, names, _ in section.jobs for made in names]
                outs = [refs[made] for _, _, names in section.jobs for made in names]
                section.run(ring, ins, outs)
            ring.finish()
            for exchange in exchanges:
                exchange.finish()

        flops = ring.flops + sum(section.job.flops for section in sections)
        results = pl.pallas_call(
            kernel,
            out_shape=[self.shapes[made] for made in outputs],
            in_specs=[pl.BlockSpec(memory_space=pl.ANY)] * len(inputs),
            out_specs=[pl.BlockSpec(memory_space=pl.ANY)] * len(outputs),
            scratch_shapes=ring.scratch + sems + kept,
            compiler_params=pltpu.CompilerParams(
                collective_id=collective, has_side_effects=True, vmem_limit_bytes=VMEM_BYTES
            ),
            cost_estimate=pl.CostEstimate(flops=flops, bytes_accessed=10**9, transcendentals=0),
            name=name,
        )(*self.arrays.values())
        named = dict(zip(outputs, results))
        return {made: flat(array) if made in self.weights else array for made, array in named.items()}


def row_and_column_peers():
    seq, column = lax.axis_index("seq"), lax.axis_index("tp")
    devices, columns = lax.axis_size("seq"), lax.axis_size("tp")
    near = [(seq, (column + step) % columns) for step in range(1, columns)]
    return near + [((seq + step) % devices, column) for step in range(1, devices)]


def run_forward(arrays, seen):
    count, columns = lax.axis_size("seq"), lax.axis_size("tp")
    plan = Plan(arrays)
    shapes, add = plan.shapes, plan.add
    rows, own = arrays["tokens"].shape
    for name in ("tokens_blocks", "cot_blocks", "branch_terms", "normed_blocks"):
        plan.define(name, (columns, rows, own), LOW)
    low = ["gate_low0", "up_low0", "gate_low1", "up_low1", "shrink_low0", "shrink_low1"]
    small = add(SmallGatherJob(shapes["small"], seen), ["small"], ["wide"])
    cast = add(CastJob(shapes["pairs"], shapes["shrink"]), ["pairs", "shrink"], low)
    groups = [[("entry_low", "entry_full"), ("exit_low", "exit_full")]]
    groups += [[(name, name.replace("low", "full"))] for name in low]
    for group in groups:
        for shard, full in group:
            plan.define(full, (count,) + shapes[shard].shape, LOW)
            plan.weights.add(full)
    ring = GatherRing(groups, shapes)
    tokens_sent = PeerCopies("tokens", "tokens_blocks")
    cot_sent = PeerCopies("cotangent", "cot_blocks")
    branch_sent = PeerCopies("term", "branch_terms")
    normed_sent = PeerCopies("normed_own", "normed_blocks")

    entry_job = EntryJob(
        shapes["tokens_blocks"], shapes["wide"], plan.flat("entry_full"), plan.flat("exit_full"), shapes["bound"]
    )
    entry_job.then = branch_sent
    entry = add(
        entry_job,
        ["tokens_blocks", "wide", "entry_full", "exit_full", "bound"],
        ["projected", "conv_out", "gated", "halo", "mixer", "term", "scale_one", "normed_one"],
    )
    turn_cot = add(TurnJob(shapes["cot_blocks"]), ["cot_blocks"], ["cot_full"])
    norm_job = NormJob(shapes["tokens"], shapes["branch_terms"], shapes["wide"])
    norm_job.then = normed_sent
    norm = add(norm_job, ["tokens", "branch_terms", "wide"], ["residual", "normed_own", "scale_two"])
    expands = []
    for half in "01":
        job = ExpandJob(shapes["normed_blocks"], plan.flat("gate_full" + half), plan.flat("up_full" + half))
        names = ["normed_blocks", "gate_full" + half, "up_full" + half]
        expands.append(add(job, names, ["gate_rows" + half, "up_rows" + half, "activation" + half]))
    hidden_job = HiddenGradJob(shapes["cot_blocks"], plan.flat("shrink_full0"), shapes["gate_rows0"], shapes["up_rows0"])
    hidden = add(hidden_job, ["cot_blocks", "shrink_full0", "gate_rows0", "up_rows0"], ["gate_grad0", "up_grad0"])
    turn_normed = add(TurnJob(shapes["normed_blocks"]), ["normed_blocks"], ["normed_two"])
    sections = [
        Section([(0, 0, 12)], [small, cast], calls=[tokens_sent], early=False),
        Section([(1, 0, 12)], [entry], [tokens_sent], calls=[cot_sent]),
        Section([(2, 0, 12)], [turn_cot], [cot_sent], rest=3),
        Section([(3, 0, 12)], [norm], [branch_sent], rest=4),
        Section([(4, 0, 12)]),
        Section([(5, 0, 12)], expands, [normed_sent], rest=4),
        Section([(6, 0, 12)], [hidden, turn_normed]),
    ]
    exchanges = [tokens_sent, cot_sent, branch_sent, normed_sent]
    return plan.run(ring, sections, exchanges, row_and_column_peers, "forward", 0)


def run_backward(arrays):
    columns = lax.axis_size("tp")
    plan = Plan(arrays)
    shapes, add = plan.shapes, plan.add
    rows, own = arrays["tokens"].shape
    for name in ("two_terms", "mixed_terms", "branch_blocks", "one_terms"):
        plan.define(name, (columns, rows, own), LOW)
    two_sent = PeerCopies("two_term", "two_terms")
    mixed_sent = PeerCopies("mixed_term", "mixed_terms")
    branch_sent = PeerCopies("branch_own", "branch_blocks")
    one_sent = PeerCopies("one_term", "one_terms")

    hidden = add(
        HiddenGradJob(shapes["cot_blocks"], shapes["shrink_full1"], shapes["gate_rows1"], shapes["up_rows1"]),
        ["cot_blocks", "shrink_full1", "gate_rows1", "up_rows1"],
        ["gate_grad1", "up_grad1"],
    )
    names = [["gate_grad0", "up_grad0", "gate_grad1", "up_grad1"], ["gate_full0", "up_full0", "gate_full1", "up_full1"]]
    two_job = WidthJob(*[[shapes[name] for name in side] for side in names])
    two_job.then = two_sent
    two = add(two_job, names[0] + names[1], ["two_term"])
    names = [["activation0", "activation1"], ["shrink_full0", "shrink_full1"]]
    mixed = add(WidthJob(*[[shapes[name] for name in side] for side in names]), names[0] + names[1], ["mixed_term"])
    back_two = NormBackJob(
        shapes["two_terms"], shapes["residual"], shapes["scale_two"], shapes["wide"], 4, shapes["cotangent"], True
    )
    back_two.then = branch_sent
    names = ["two_terms", "residual", "scale_two", "wide", "cotangent"]
    norm_two = add(back_two, names, ["residual_grad", "gain_two_grad", "branch_own"])
    names = ["branch_blocks", "exit_full", "entry_full", "projected", "conv_out", "gated", "halo", "wide", "bound"]
    mixer_job = MixerGradJob(*[shapes[name] for name in names])
    mixer_job.then = one_sent
    mixer = add(mixer_job, names, ["projected_grad", "one_term", "taps_grad"])
    turn = add(TurnJob(shapes["branch_blocks"]), ["branch_blocks"], ["branch_full"])
    back_one = NormBackJob(
        shapes["one_terms"], shapes["tokens"], shapes["scale_one"], shapes["wide"], 3, shapes["residual_grad"], False
    )
    names = ["one_terms", "tokens", "scale_one", "wide", "residual_grad"]
    norm_one = add(back_one, names, ["tokens_grad", "gain_one_grad"])
    small_job = SmallSumJob(shapes["taps_grad"], shapes["gain_two_grad"], back_one)
    small = add(small_job, ["taps_grad", "gain_two_grad"], ["small_part"])
    total = add(SumJob(shapes["residual"], shapes["mixed_terms"]), ["residual", "mixed_terms"], ["mixed"])

    wide = own
    halves = [("cot_full", "activation0"), ("cot_full", "activation1")]
    halves += [("normed_two", name) for name in ("gate_grad0", "up_grad0", "gate_grad1", "up_grad1")]
    halves += [("normed_one", "projected_grad")]
    groups = [[(left, right, 0), (left, right, wide)] for left, right in halves]
    groups += [[("normed_one", "projected_grad", 2 * wide), ("branch_full", "mixer", 0)]]
    places = {"cot_full": 0, "normed_two": 1, "normed_one": 0, "branch_full": 2}
    ring = ScatterRing(groups, places, shapes, wide)
    sums = ["shrink0", "shrink1", "gate0", "up0", "gate1", "up1", "entry", "entry_exit"]
    for name, shape in zip(sums, ring.out_shapes):
        plan.shapes[name] = shape
    ring.outs = sums
    names = [["shrink_weight", "shrink_first", "shrink_second"], ["shrink0", "shrink1"]]
    shrink_job = AdamJob(shapes["shrink_weight"], [shapes[name] for name in names[1]])
    adam_shrink = add(shrink_job, names[0] + names[1], ["shrink_next", "shrink_first_next", "shrink_second_next"])
    names = [["expand_weight", "expand_first", "expand_second"], ["gate0", "up0", "gate1", "up1"]]
    expand_job = AdamPairsJob(shapes["expand_weight"], [shapes[name] for name in names[1]])
    adam_expand = add(expand_job, names[0] + names[1], ["expand_next", "expand_first_next", "expand_second_next"])
    sections = [
        Section([(0, 0, 5)], [hidden]),
        Section([(0, 5, 12), (1, 0, 4)], [two], rest=2),
        Section([(1, 4, 12), (2, 0, 5)], [mixed]),
        Section([(2, 5, 12)], [norm_two], [two_sent], rest=3),
        Section([(3, 0, 12)], [adam_shrink], rest=2),
        Section([(4, 0, 12)], [mixer], [branch_sent], rest=3, then=[mixed_sent]),
        Section([(5, 0, 12)], [turn]),
        Section([(6, 0, 12)], [norm_one, small, total], [one_sent, mixed_sent], rest=5),
        Section([(7, 0, 12)], [adam_expand], rest=2),
    ]
    exchanges = [two_sent, mixed_sent, branch_sent, one_sent]
    return plan.run(ring, sections, exchanges, row_and_column_peers, "backward", 1)


def rows_of(ref, gathered):
    if not gathered:
        return ref
    count, rows, columns = ref.shape
    return ref.reshape(count * rows, columns)


def flat(full):
    return full.reshape(full.shape[0] * full.shape[1], full.shape[2])


def contract_cols(left, right):
    return lax.dot_general(
        left, right, (((1,), (1,)), ((), ())), preferred_element_type=jnp.float32
    )


def adam_update(weight, first, second, grad, rate, decay):
    first_next = BETA_ONE * first + (1.0 - BETA_ONE) * grad
    second_next = BETA_TWO * second + (1.0 - BETA_TWO) * grad * grad
    corrected = first_next / (1.0 - BETA_ONE**STEP)
    spread = jnp.sqrt(second_next / (1.0 - BETA_TWO**STEP)) + ADAM_EPSILON
    return (weight - rate * (corrected / spread + decay * weight), first_next, second_next)


def adam_mixer_kernel(*refs):
    entries, exits, grads, outs = refs[:3], refs[3:6], refs[6:8], refs[8:]
    planes, _, columns = entries[0].shape
    for plane in range(planes + 1):
        grad = grads[plane // 2][:, plane % 2 * columns : (plane % 2 + 1) * columns]
        state = [ref[plane] for ref in entries] if plane < planes else [ref[...] for ref in exits]
        results = adam_update(*state, grad, RATE_WIDE, WEIGHT_DECAY)
        for place, result in enumerate(results):
            if plane < planes:
                outs[place][plane] = result
            else:
                outs[3 + place][...] = result


def adam_mixer(entries, exits, grad, last):
    rows, planes, columns = entries[0].shape
    block = max(rows // 4, 8)
    entry_spec = pl.BlockSpec((planes, block, columns), lambda step: (0, step, 0))
    exit_spec = pl.BlockSpec((block, columns), lambda step: (step, 0))
    grad_spec = pl.BlockSpec((block, 2 * columns), lambda step: (step, 0))
    size = entries[0].size + exits[0].size
    results = pl.pallas_call(
        adam_mixer_kernel,
        out_shape=[jax.ShapeDtypeStruct((planes, rows, columns), jnp.float32)] * 3
        + [jax.ShapeDtypeStruct((rows, columns), jnp.float32)] * 3,
        grid=(rows // block,),
        in_specs=[entry_spec] * 3 + [exit_spec] * 3 + [grad_spec] * 2,
        out_specs=[entry_spec] * 3 + [exit_spec] * 3,
        compiler_params=pltpu.CompilerParams(vmem_limit_bytes=VMEM_BYTES),
        cost_estimate=pl.CostEstimate(flops=20 * size, bytes_accessed=28 * size, transcendentals=0),
        name="adam_mixer",
    )(*[array.transpose(1, 0, 2) for array in entries], *exits, grad, last)
    return [result.transpose(1, 0, 2) for result in results[:3]] + list(results[3:])


def paired(array):
    rows, _, columns = array.shape
    return array.reshape(rows, 2, columns // LANES, LANES).transpose(0, 2, 1, 3).reshape(-1, LANES)


def unpaired(array, shape):
    rows, _, columns = shape
    return array.reshape(rows, columns // LANES, 2, LANES).transpose(0, 2, 1, 3).reshape(shape)


def shards(
    tokens,
    bounds,
    cotangent,
    entry_weight,
    entry_first,
    entry_second,
    exit_weight,
    exit_first,
    exit_second,
    expand_weight,
    expand_first,
    expand_second,
    shrink_weight,
    shrink_first,
    shrink_second,
    conv_kernel,
    conv_first,
    conv_second,
    norm_gains,
    gain_first,
    gain_second,
):
    channels = tokens.shape[1]
    seen = conv_kernel.shape[1]
    small = jnp.concatenate([conv_kernel, norm_gains], axis=0)
    small = jnp.pad(small, ((0, 16 - small.shape[0]), (0, LANES - seen))).astype(LOW)
    entry_low = entry_weight.reshape(entry_weight.shape[0], 3 * channels).astype(LOW)
    bound = jnp.broadcast_to(bounds[0], (8, 128))
    made = run_forward(
        {
            "entry_low": entry_low,
            "exit_low": exit_weight.astype(LOW),
            "small": small,
            "tokens": tokens,
            "cotangent": cotangent,
            "bound": bound,
            "pairs": paired(expand_weight),
            "shrink": shrink_weight,
        },
        seen,
    )
    names = ["wide", "exit_full", "entry_full", "projected", "conv_out", "gated", "halo", "mixer", "residual"]
    names += ["scale_one", "scale_two", "cot_blocks", "cot_full", "normed_one", "normed_two", "gate_grad0", "up_grad0"]
    names += ["gate_rows1", "up_rows1", "activation0", "activation1"]
    names += [name + half for name in ("gate_full", "up_full", "shrink_full") for half in "01"]
    given = {"tokens": tokens, "cotangent": cotangent, "bound": bound}
    given |= {"shrink_weight": shrink_weight, "shrink_first": shrink_first, "shrink_second": shrink_second}
    given["expand_weight"] = paired(expand_weight)
    given["expand_first"], given["expand_second"] = paired(expand_first), paired(expand_second)
    grads = run_backward(given | {name: made[name] for name in names})
    mixed, tokens_grad = grads["mixed"], grads["tokens_grad"]
    small_part = lax.dynamic_slice_in_dim(grads["small_part"], lax.axis_index("seq") * seen, seen, axis=1)
    kernel_part = small_part[:3]
    gains_part = small_part[3:5]
    (
        entry_next,
        entry_first_next,
        entry_second_next,
        exit_next,
        exit_first_next,
        exit_second_next,
    ) = adam_mixer(
        (entry_weight, entry_first, entry_second),
        (exit_weight, exit_first, exit_second),
        grads["entry"],
        grads["entry_exit"],
    )
    shrink_next, shrink_first_next, shrink_second_next = (
        grads["shrink" + name] for name in ("_next", "_first_next", "_second_next")
    )
    expand_next, expand_first_next, expand_second_next = (
        unpaired(grads["expand" + name], expand_weight.shape) for name in ("_next", "_first_next", "_second_next")
    )
    conv_next, conv_first_next, conv_second_next = adam_update(
        conv_kernel, conv_first, conv_second, kernel_part, RATE_CONV, 0.0
    )
    gains_next, gains_first_next, gains_second_next = adam_update(
        norm_gains, gain_first, gain_second, gains_part, RATE_GAIN, 0.0
    )
    return (
        mixed,
        tokens_grad,
        entry_next,
        entry_first_next,
        entry_second_next,
        exit_next,
        exit_first_next,
        exit_second_next,
        expand_next,
        expand_first_next,
        expand_second_next,
        shrink_next,
        shrink_first_next,
        shrink_second_next,
        conv_next,
        conv_first_next,
        conv_second_next,
        gains_next,
        gains_first_next,
        gains_second_next,
    )


def solution(mesh):
    rows = P("seq", "tp")
    stacked = P("seq", None, "tp")
    small = P(None, ("tp", "seq"))
    return jax.shard_map(
        shards,
        mesh=mesh,
        in_specs=(rows, P("seq"), rows) + (stacked,) * 3 + (rows,) * 3 + (stacked,) * 3 + (rows,) * 3 + (small,) * 6,
        out_specs=(rows, rows) + (stacked,) * 3 + (rows,) * 3 + (stacked,) * 3 + (rows,) * 3 + (small,) * 6,
        check_vma=False,
    )
```
